32 devices in a mesh: shard: 4 (over y, x), ctx: 2 (over core), tp: 4 (over z).
Axes of the slice: x: 2, y: 2, z: 4, core: 2. Of those that a mesh axis runs over, the one named last changes fastest.
Arguments:
- tokens: bfloat16 [8, 1024, 1024], P('shard', 'ctx'), may hold values from -6 to 6
- proj_in: bfloat16 [1024, 6144], P('shard', 'tp'), may hold values from -0.1875 to 0.1875
- proj_gates: bfloat16 [1024, 16], P('shard', 'tp'), may hold values from -0.1875 to 0.1875
- conv_taps: bfloat16 [4, 4096], P(None, 'tp'), may hold values from -3 to 3
- log_rates: float32 [8], P('tp'), may hold values from -7.5 to -2.5
- rate_bias: float32 [8], P('tp'), may hold values from -1 to 1
- gate_gain: bfloat16 [256], replicated, may hold values from 0.5 to 1.5
- proj_out: bfloat16 [2048, 1024], P('tp', 'shard'), may hold values from -0.26516504 to 0.26516504
- ffn_gate: bfloat16 [1024, 2816], P('shard', 'tp'), may hold values from -0.1875 to 0.1875
- ffn_up: bfloat16 [1024, 2816], P('shard', 'tp'), may hold values from -0.1875 to 0.1875
- ffn_down: bfloat16 [2816, 1024], P('tp', 'shard'), may hold values from -0.113066754 to 0.113066754
- gain_in: bfloat16 [1024], P('shard'), may hold values from 0.5 to 1.5
- gain_ffn: bfloat16 [1024], P('shard'), may hold values from 0.5 to 1.5
- cotangent: bfloat16 [8, 1024, 1024], P('shard', 'ctx'), may hold values from -6 to 6
Outputs:
- layer_out: bfloat16 [8, 1024, 1024], P('shard', ('ctx', 'tp'))
- token_grad: float32 [8, 1024, 1024], P('shard', ('ctx', 'tp'))
- grad_proj_in: float32 [1024, 6144], P('shard', 'tp')
- grad_proj_gates: float32 [1024, 16], P('shard', 'tp')
- grad_conv_taps: float32 [4, 4096], P(None, 'tp')
- grad_log_rates: float32 [8], P('tp')
- grad_rate_bias: float32 [8], P('tp')
- grad_gate_gain: float32 [256], replicated
- grad_proj_out: float32 [2048, 1024], P('tp', 'shard')
- grad_ffn_gate: float32 [1024, 2816], P('shard', 'tp')
- grad_ffn_up: float32 [1024, 2816], P('shard', 'tp')
- grad_ffn_down: float32 [2816, 1024], P('tp', 'shard')
- grad_gain_in: float32 [1024], P('shard')
- grad_gain_ffn: float32 [1024], P('shard')
The draws below stay inside these ranges and needn't reach their ends.
All inputs are finite; a program needn't handle non-finite values.
Results may differ from the reference program's by a relative error of at most 0.024.
Values may be sent and summed in bfloat16 or wider, within the bound.
No kernel may reach another device: no remote copies, remote signals or barrier semaphores. Data moves between devices by JAX's collectives and lax.ppermute only.
A program may use at most 192 MiB of HBM per device.

```python
import jax
import jax.numpy as jnp
from jax import lax

D = 1024
H = 8
DK = 128
DV = 256
FF = 2816
CONV = 4
SPAN = 64
LEN = 1024
SEQS = 8


def draw_tokens(key, part):
    key = jax.random.fold_in(key, 11)
    shape = (SEQS, LEN, D)
    raw = jnp.clip(jax.random.normal(key, shape, jnp.float32), -6.0, 6.0)
    return raw.astype(jnp.bfloat16)


def draw_cotangent(key, part):
    key = jax.random.fold_in(key, 12)
    shape = (SEQS, LEN, D)
    raw = jnp.clip(jax.random.normal(key, shape, jnp.float32), -6.0, 6.0)
    return raw.astype(jnp.bfloat16)


def draw_proj_in(key, part):
    key = jax.random.fold_in(key, 13)
    shape = (D, H * (2 * DK + 2 * DV))
    raw = jnp.clip(jax.random.normal(key, shape, jnp.float32), -6.0, 6.0)
    return (raw * D ** (-0.5)).astype(jnp.bfloat16)


def draw_proj_gates(key, part):
    key = jax.random.fold_in(key, 14)
    shape = (D, 2 * H)
    raw = jnp.clip(jax.random.normal(key, shape, jnp.float32), -6.0, 6.0)
    return (raw * D ** (-0.5)).astype(jnp.bfloat16)


def draw_conv_taps(key, part):
    key = jax.random.fold_in(key, 15)
    shape = (CONV, H * (2 * DK + DV))
    raw = jnp.clip(jax.random.normal(key, shape, jnp.float32), -6.0, 6.0)
    return (raw * CONV ** (-0.5)).astype(jnp.bfloat16)


def draw_proj_out(key, part):
    key = jax.random.fold_in(key, 16)
    shape = (H * DV, D)
    raw = jnp.clip(jax.random.normal(key, shape, jnp.float32), -6.0, 6.0)
    return (raw * (H * DV // 4) ** (-0.5)).astype(jnp.bfloat16)


def draw_ffn_gate(key, part):
    key = jax.random.fold_in(key, 17)
    shape = (D, FF)
    raw = jnp.clip(jax.random.normal(key, shape, jnp.float32), -6.0, 6.0)
    return (raw * D ** (-0.5)).astype(jnp.bfloat16)


def draw_ffn_up(key, part):
    key = jax.random.fold_in(key, 18)
    shape = (D, FF)
    raw = jnp.clip(jax.random.normal(key, shape, jnp.float32), -6.0, 6.0)
    return (raw * D ** (-0.5)).astype(jnp.bfloat16)


def draw_ffn_down(key, part):
    key = jax.random.fold_in(key, 19)
    shape = (FF, D)
    raw = jnp.clip(jax.random.normal(key, shape, jnp.float32), -6.0, 6.0)
    return (raw * FF ** (-0.5)).astype(jnp.bfloat16)


def level_of(rng, shape, split, smallest, high):
    level = 1.0
    for axis_at, shards_of in split:
        heights = jax.random.uniform(jax.random.fold_in(jax.random.fold_in(rng, 6), axis_at), (shards_of,), jnp.float32, smallest / len(split), high / len(split))
        level = level * jnp.repeat(jnp.exp(heights), shape[axis_at] // shards_of).reshape((-1,) + (1,) * (len(shape) - 1 - axis_at))
    return level


def setup_inputs(seed: int = 0) -> dict:
    seeds = jax.random.split(jax.random.key(seed), 15)
    return {
        "tokens": draw_tokens(jax.random.fold_in(seeds[14], 71), 0),
        "proj_in": draw_proj_in(jax.random.fold_in(seeds[14], 71), 0),
        "proj_gates": draw_proj_gates(jax.random.fold_in(seeds[14], 71), 0),
        "conv_taps": draw_conv_taps(jax.random.fold_in(seeds[14], 71), 0),
        "log_rates": jnp.clip(-7.5 + 5.0 * jax.random.uniform(seeds[4], (H,), jnp.float32) ** level_of(seeds[4], (H,), ((0, 4),), -0.2, 0.2), -7.5, -2.5),
        "rate_bias": jnp.clip(jax.random.uniform(seeds[5], (H,), jnp.float32, -1.0, 1.0) * level_of(seeds[5], (H,), ((0, 4),), -0.4, 0.0), -1.0, 1.0),
        "gate_gain": jnp.clip(1.0 + 0.1 * jax.random.normal(seeds[6], (DV,), jnp.float32), 0.5, 1.5).astype(jnp.bfloat16),
        "proj_out": draw_proj_out(jax.random.fold_in(seeds[14], 71), 0),
        "ffn_gate": draw_ffn_gate(jax.random.fold_in(seeds[14], 71), 0),
        "ffn_up": draw_ffn_up(jax.random.fold_in(seeds[14], 71), 0),
        "ffn_down": draw_ffn_down(jax.random.fold_in(seeds[14], 71), 0),
        "gain_in": jnp.clip(1.0 + 0.1 * jax.random.normal(seeds[11], (D,), jnp.float32), 0.5, 1.5).astype(jnp.bfloat16),
        "gain_ffn": jnp.clip(1.0 + 0.1 * jax.random.normal(seeds[12], (D,), jnp.float32), 0.5, 1.5).astype(jnp.bfloat16),
        "cotangent": draw_cotangent(jax.random.fold_in(seeds[14], 71), 0),
    }


epsilon = 1e-06
highest = lax.Precision.HIGHEST

@jax.custom_vjp
def low(v):
    return lax.optimization_barrier(v.astype(jnp.bfloat16)).astype(jnp.float32)

@jax.custom_vjp
def low_back(v):
    return v

def low_keep(v):
    return (low(v), None)

def low_pass(kept, grad):
    return (grad,)

def back_keep(v):
    return (v, None)

def back_low(kept, grad):
    return (low(grad),)
low.defvjp(low_keep, low_pass)
low_back.defvjp(back_keep, back_low)

def product(left, right):
    return jnp.dot(left.astype(jnp.float32), right.astype(jnp.float32), precision=highest, preferred_element_type=jnp.float32)

def span_step(carry_state, block):
    block_queries, block_keys, block_values, block_decay, block_beta = block
    span_len = block_decay.shape[1]
    cumulative = jnp.cumsum(block_decay, axis=1)
    row_index = lax.broadcasted_iota(jnp.int32, (span_len, span_len), 0)
    col_index = lax.broadcasted_iota(jnp.int32, (span_len, span_len), 1)
    lower_mask = row_index >= col_index
    strict_mask = row_index > col_index
    differences = cumulative[:, :, None] - cumulative[:, None, :]
    decay_table = jnp.where(lower_mask, jnp.exp(jnp.where(lower_mask, differences, 0.0)), 0.0)
    key_gram = jnp.einsum('bik,bjk->bij', block_keys, block_keys, precision=highest)
    unit_lower = jnp.where(strict_mask, block_beta[:, :, None] * key_gram * decay_table, 0.0) + jnp.eye(span_len, dtype=jnp.float32)
    value_width = block_values.shape[2]
    right_sides = jnp.concatenate([block_values * block_beta[:, :, None], block_keys * (block_beta * jnp.exp(cumulative))[:, :, None]], axis=2)
    solved = lax.linalg.triangular_solve(unit_lower, right_sides, left_side=True, lower=True, unit_diagonal=True)
    fresh = solved[:, :, :value_width] - jnp.einsum('bik,bkw->biw', solved[:, :, value_width:], carry_state, precision=highest)
    scores = jnp.einsum('bik,bjk->bij', block_queries, block_keys, precision=highest) * decay_table
    block_output = jnp.einsum('bik,bkw->biw', block_queries * jnp.exp(cumulative)[:, :, None], carry_state, precision=highest) + jnp.einsum('bij,bjw->biw', scores, fresh, precision=highest)
    last_decay = cumulative[:, -1]
    next_state = carry_state * jnp.exp(last_decay)[:, None, None] + jnp.einsum('bik,biw->bkw', block_keys * jnp.exp(last_decay[:, None] - cumulative)[:, :, None], fresh, precision=highest)
    return (next_state, block_output)

def run_mixer(queries, key_rows, value_rows, decays, strengths, carry_state):
    batch_size, length = decays.shape
    blocks = length // SPAN

    def split_blocks(tensor_in):
        return jnp.swapaxes(tensor_in.reshape((batch_size, blocks, SPAN) + tensor_in.shape[2:]), 0, 1)
    final_state, outputs = lax.scan(jax.checkpoint(span_step), carry_state, (split_blocks(queries), split_blocks(key_rows), split_blocks(value_rows), split_blocks(decays), split_blocks(strengths)))
    value_width = value_rows.shape[2]
    return (jnp.swapaxes(outputs, 0, 1).reshape(batch_size, length, value_width), final_state)

def layer(tokens_f, proj_in, proj_gates, conv_taps, log_rates, rate_bias, gate_gain, proj_out, ffn_gate, ffn_up, ffn_down, gain_in, gain_ffn):
    length = tokens_f.shape[0]
    qkv_width = 2 * DK + DV
    scale_in = lax.rsqrt(lax.optimization_barrier(jnp.mean(tokens_f * tokens_f, -1, keepdims=True)) + epsilon)
    normed_in = low(tokens_f * scale_in * gain_in)
    projected = low(low_back(product(normed_in, proj_in))).reshape(length, H, qkv_width + DV)
    mixing_in = projected[:, :, :qkv_width].reshape(length, H * qkv_width)
    gate_values = projected[:, :, qkv_width:]
    gate_logits = low_back(product(normed_in, proj_gates)).reshape(length, H, 2)
    padded = jnp.pad(mixing_in, ((CONV - 1, 0), (0, 0)))
    mixed = conv_taps[0] * padded[0:length]
    for offset in range(1, CONV):
        mixed = mixed + conv_taps[offset] * padded[offset:offset + length]
    active = jax.nn.silu(mixed).reshape(length, H, qkv_width)
    queries = active[:, :, :DK]
    key_rows = active[:, :, DK:2 * DK]
    value_rows = active[:, :, 2 * DK:]
    queries = queries * lax.rsqrt(lax.optimization_barrier(jnp.sum(queries * queries, -1, keepdims=True)) + epsilon) * DK ** (-0.5)
    key_rows = key_rows * lax.rsqrt(lax.optimization_barrier(jnp.sum(key_rows * key_rows, -1, keepdims=True)) + epsilon)
    queries = low(queries)
    key_rows = low(key_rows)
    value_rows = low(value_rows)
    decays = -jnp.exp(log_rates) * jax.nn.softplus(gate_logits[:, :, 0] + rate_bias)
    strengths = jax.nn.sigmoid(gate_logits[:, :, 1])
    start_state = jnp.zeros((H, DK, DV), jnp.float32)
    mixer_out, final_state = run_mixer(jnp.swapaxes(queries, 0, 1), jnp.swapaxes(key_rows, 0, 1), jnp.swapaxes(value_rows, 0, 1), jnp.swapaxes(decays, 0, 1), jnp.swapaxes(strengths, 0, 1), start_state)
    mixer_out = jnp.swapaxes(mixer_out, 0, 1)
    scale_rows = lax.rsqrt(lax.optimization_barrier(jnp.mean(mixer_out * mixer_out, -1, keepdims=True)) + epsilon)
    gated = low(mixer_out * scale_rows * gate_gain * jax.nn.silu(gate_values)).reshape(length, H * DV)
    branch = low_back(product(gated, proj_out))
    middle = tokens_f + branch
    scale_mid = lax.rsqrt(lax.optimization_barrier(jnp.mean(middle * middle, -1, keepdims=True)) + epsilon)
    normed_mid = low(middle * scale_mid * gain_ffn)
    gate_act = low_back(product(normed_mid, ffn_gate))
    up_act = low_back(product(normed_mid, ffn_up))
    hidden = low(jax.nn.silu(gate_act) * up_act)
    return middle + low_back(product(hidden, ffn_down))

def reference(tokens, proj_in, proj_gates, conv_taps, log_rates, rate_bias, gate_gain, proj_out, ffn_gate, ffn_up, ffn_down, gain_in, gain_ffn, cotangent):
    weights = tuple((weight_item.astype(jnp.float32) for weight_item in (proj_in, proj_gates, conv_taps, log_rates, rate_bias, gate_gain, proj_out, ffn_gate, ffn_up, ffn_down, gain_in, gain_ffn)))

    def one_sequence(running, seq_pair):
        sequence, incoming = seq_pair
        result, pullback = jax.vjp(layer, sequence.astype(jnp.float32), *weights)
        grad_list = pullback(incoming.astype(jnp.float32))
        running = tuple((total_item + grad_item for total_item, grad_item in zip(running, grad_list[1:])))
        return (running, (result.astype(jnp.bfloat16), grad_list[0]))
    zero_grads = tuple((jnp.zeros(weight_item.shape, jnp.float32) for weight_item in weights))
    totals, (layer_out, token_grad) = lax.scan(one_sequence, zero_grads, (tokens, cotangent))
    return (layer_out, token_grad, totals[0], totals[1], totals[2], totals[3], totals[4], totals[5], totals[6], totals[7], totals[8], totals[9], totals[10], totals[11])
```

```python
import functools

import jax
import jax.numpy as jnp
from jax import lax
from jax.experimental import pallas as pl
from jax.experimental.pallas import tpu as pltpu
from jax.sharding import PartitionSpec as P

DK = 128
DV = 256
QKV = 2 * DK + DV
HEAD = QKV + DV
CONV = 4
CHUNK = 128
HALO = 16
ROWS = 8

epsilon = 1e-06
f32 = jnp.float32
bf16 = jnp.bfloat16


def mm(left, right, contract=(1, 0)):
    return lax.dot_general(
        left.astype(bf16),
        right.astype(bf16),
        (((contract[0],), (contract[1],)), ((), ())),
        preferred_element_type=f32,
    )


def mm_split(left, right):
    left_hi = left.astype(bf16)
    right_hi = right.astype(bf16)
    left_lo = left - left_hi.astype(f32)
    right_lo = right - right_hi.astype(f32)
    return mm(left_hi, right_hi) + (mm(left_hi, right_lo) + mm(left_lo, right_hi))


def mm_exact(left, right):
    return lax.dot_general(
        left,
        right,
        (((1,), (0,)), ((), ())),
        precision=lax.Precision.HIGHEST,
        preferred_element_type=f32,
    )


def iotas():
    row = lax.broadcasted_iota(jnp.int32, (CHUNK, CHUNK), 0)
    col = lax.broadcasted_iota(jnp.int32, (CHUNK, CHUNK), 1)
    return row, col


def pad_rows(block):
    missing = CHUNK - block.shape[0]
    return jnp.concatenate([block, jnp.zeros((missing, block.shape[1]), f32)], axis=0)


def softplus(values):
    return jnp.maximum(values, 0.0) + jnp.log1p(jnp.exp(-jnp.abs(values)))


def sigmoid(values):
    return 1.0 / (1.0 + jnp.exp(-values))


def chunk_rows(logit_ref, head, chunks):
    def stacked(row):
        picked = logit_ref[0, pl.ds(row, 1), :]
        return jnp.concatenate(
            [picked[:, c * CHUNK : (c + 1) * CHUNK] for c in range(chunks)], axis=0
        )

    return stacked(2 * head), stacked(2 * head + 1)


def invert_units(lowers, row, col):
    eye = (row == col).astype(f32)
    same = (row // 16) == (col // 16)
    powers = [jnp.where(same, n, 0.0) for n in lowers]
    inverses = [eye - p for p in powers]
    for _ in range(3):
        powers = [mm_split(p, p) for p in powers]
        inverses = [x + mm_split(x, p) for x, p in zip(inverses, powers)]
    size = 16
    while size < CHUNK:
        joins = ((row // (2 * size)) == (col // (2 * size))) & ((row // size) != (col // size))
        middles = [mm_split(jnp.where(joins, n, 0.0), x) for n, x in zip(lowers, inverses)]
        inverses = [x - mm_split(x, m) for x, m in zip(inverses, middles)]
        size *= 2
    return inverses


def conv_into(scratch, x_qk, x_v, halo_qk, halo_v, taps_qk, taps_v, length):
    scratch[0:ROWS, 0 : 2 * DK] = halo_qk[0, HALO - ROWS :, :].astype(f32)
    scratch[0:ROWS, 2 * DK :] = halo_v[0, HALO - ROWS :, :].astype(f32)
    scratch[ROWS : ROWS + length, 0 : 2 * DK] = x_qk[0].astype(f32)
    scratch[ROWS : ROWS + length, 2 * DK :] = x_v[0].astype(f32)
    taps = jnp.concatenate([taps_qk[...], taps_v[...]], axis=1).astype(f32)
    first = ROWS - CONV + 1
    mixed = taps[0:1, :] * scratch[first : first + length, :]
    for j in range(1, CONV):
        mixed = mixed + taps[j : j + 1, :] * scratch[first + j : first + j + length, :]
    return mixed, taps


def prep_kernel(
    rates, biases, x_qk, x_v, halo_qk, halo_v, logits, taps_qk, taps_v,
    q_out, k_out, v_out, rows_out, t_out, w_out, u_out, qe_out, m_out, b_out, p_out, end_out, map_out,
    scratch,
):
    head = pl.program_id(0)
    length = x_qk.shape[1]
    chunks = length // CHUNK
    mixed, _ = conv_into(
        scratch, x_qk, x_v, halo_qk, halo_v, taps_qk, taps_v, length
    )
    active = mixed * sigmoid(mixed)
    q_act = active[:, :DK]
    k_act = active[:, DK : 2 * DK]
    q_all = (
        q_act * lax.rsqrt(jnp.sum(q_act * q_act, -1, keepdims=True) + epsilon) * DK ** (-0.5)
    ).astype(bf16)
    k_all = (
        k_act * lax.rsqrt(jnp.sum(k_act * k_act, -1, keepdims=True) + epsilon)
    ).astype(bf16)
    v_all = active[:, 2 * DK :].astype(bf16)
    q_out[0, 0] = q_all
    k_out[0, 0] = k_all
    v_out[0, 0] = v_all
    decay_logit, strength_logit = chunk_rows(logits, head, chunks)
    decay = -jnp.exp(rates[head]) * softplus(decay_logit + biases[head])
    row, col = iotas()
    lower = row >= col
    strict = row > col
    total = mm_exact(pad_rows(decay)[: max(8, chunks)], (row <= col).astype(f32))[:chunks]
    strength = sigmoid(strength_logit)
    stacked = jnp.concatenate([total, strength], axis=0)
    rows_out[0, 0] = stacked
    columns = jnp.transpose(pad_rows(stacked))
    units = range(chunks)
    span = [slice(c * CHUNK, (c + 1) * CHUNK) for c in units]
    g_col = [columns[:, c : c + 1] for c in units]
    b_col = [columns[:, chunks + c : chunks + c + 1] for c in units]
    table = [
        jnp.where(lower, jnp.exp(jnp.where(lower, g_col[c] - total[c : c + 1, :], 0.0)), 0.0)
        for c in units
    ]
    q = [q_all[s] for s in span]
    k = [k_all[s] for s in span]
    gram = [mm(k[c], k[c], (1, 1)) for c in units]
    score = [mm(q[c], k[c], (1, 1)) * table[c] for c in units]
    lowers = [jnp.where(strict, b_col[c] * gram[c] * table[c], 0.0) for c in units]
    inverse = invert_units(lowers, row, col)
    grown = [jnp.exp(g_col[c]) for c in units]
    w = [mm(inverse[c], (b_col[c] * grown[c]) * k[c].astype(f32)) for c in units]
    u = [mm(inverse[c], b_col[c] * v_all[span[c]].astype(f32)) for c in units]
    qe = [grown[c] * q[c].astype(f32) - mm(score[c], w[c]) for c in units]
    own = [mm(score[c], u[c]) for c in units]
    last = [g_col[c][CHUNK - 1 :, :] for c in units]
    k_late = [jnp.exp(last[c] - g_col[c]) * k[c].astype(f32) for c in units]
    m = [-mm(k_late[c], w[c], (0, 0)) for c in units]
    b = [mm(k_late[c], u[c], (0, 0)) for c in units]
    state = b[0]
    for c in units:
        t_out[0, 0, c] = inverse[c].astype(bf16)
        w_out[0, 0, c] = w[c].astype(bf16)
        u_out[0, 0, c] = u[c]
        qe_out[0, 0, c] = qe[c].astype(bf16)
        m_out[0, 0, c] = m[c].astype(bf16)
        b_out[0, 0, c] = b[c]
        p_out[0, 0, c] = own[c]
        if c:
            state = jnp.exp(last[c]) * state + mm(m[c], state) + b[c]
    end_out[0, 0] = state
    if map_out is not None:
        chain = (row == col).astype(f32)
        for c in units:
            chain = jnp.exp(last[c]) * chain + mm(m[c], chain)
        map_out[0, 0] = chain


def output_kernel(
    rows, qe, m, b, own, arriving, og, gain,
    gated_out, mixer_out, states_out,
):
    chunks = qe.shape[2]
    last = jnp.exp(rows[0, 0][0:chunks, CHUNK - 1 :])
    state = arriving[0, 0].astype(f32)
    gain_row = gain[...].astype(f32)
    for c in range(chunks):
        s = slice(c * CHUNK, (c + 1) * CHUNK)
        states_out[0, 0, c] = state.astype(bf16)
        out = mm(qe[0, 0, c], state) + own[0, 0, c]
        mixer_out[0, s, :] = out
        scale = lax.rsqrt(jnp.mean(out * out, -1, keepdims=True) + epsilon)
        gate = og[0, s, :].astype(f32)
        gated_out[0, s, :] = (out * scale * gain_row * (gate * sigmoid(gate))).astype(bf16)
        if c < chunks - 1:
            state = last[c : c + 1, :] * state + mm(m[0, 0, c], state) + b[0, 0, c]


def norm_back_kernel(
    rows, d_gated, mixer, og, gain, qe, m,
    d_out, d_og_out, n_out, start_out, gain_out,
):
    seq = pl.program_id(1)
    chunks = qe.shape[2]
    last = jnp.exp(rows[0, 0][0:chunks, CHUNK - 1 :])
    gain_row = gain[...].astype(f32)
    gain_sum = jnp.zeros((8, DV), f32)
    adds = []
    for c in range(chunks):
        s = slice(c * CHUNK, (c + 1) * CHUNK)
        out = mixer[0, s, :]
        gate = og[0, s, :].astype(f32)
        sig = sigmoid(gate)
        swish = gate * sig
        dg = d_gated[0, s, :].astype(f32)
        scale = lax.rsqrt(jnp.mean(out * out, -1, keepdims=True) + epsilon)
        unit = out * scale
        spread = dg * unit
        e = dg * (gain_row * swish)
        d_mix = scale * (e - unit * jnp.mean(e * unit, -1, keepdims=True))
        d_og_out[0, 0, s, :] = (spread * gain_row * (sig * (1.0 + gate * (1.0 - sig)))).astype(bf16)
        gain_sum = gain_sum + jnp.sum((spread * swish).reshape(CHUNK // 8, 8, DV), axis=0)
        d_low = d_mix.astype(bf16)
        d_out[0, 0, c] = d_low
        add = mm(qe[0, 0, c], d_low, (0, 0))
        n_out[0, 0, c] = add
        adds.append(add)
    back = adds[-1]
    for c in reversed(range(chunks - 1)):
        back = last[c : c + 1, :] * back + mm(m[0, 0, c], back, (0, 0)) + adds[c]
    start_out[0, 0] = back

    @pl.when(seq == 0)
    def _():
        gain_out[0] = gain_sum

    @pl.when(seq != 0)
    def _():
        gain_out[0] = gain_out[0] + gain_sum


def grad_kernel(
    rates, biases, x_qk, x_v, halo_qk, halo_v, logits, taps_qk, taps_v,
    q_in, k_in, v_in, rows, t_in, w_in, u_in, m_in, states, d_out, n_in, arriving, d_og,
    d_proj_out, d_halo_out, d_tail_out, d_logit_out, rate_out, taps_out,
    scratch, grads,
):
    head = pl.program_id(0)
    seq = pl.program_id(1)
    length = x_qk.shape[1]
    chunks = length // CHUNK
    units = range(chunks)
    row, col = iotas()
    lower = row >= col
    strict = row > col
    stacked = rows[0, 0]
    total = stacked[0:chunks]
    strength = stacked[chunks : 2 * chunks]
    columns = jnp.transpose(pad_rows(stacked))
    g_col = [columns[:, c : c + 1] for c in units]
    b_col = [columns[:, chunks + c : chunks + c + 1] for c in units]
    last = [g_col[c][CHUNK - 1 :, :] for c in units]
    ends = [None] * chunks
    back = arriving[0, 0].astype(f32)
    for c in reversed(units):
        ends[c] = back
        if c:
            back = jnp.exp(last[c]) * back + mm(m_in[0, 0, c], back, (0, 0)) + n_in[0, 0, c]
    span = [slice(c * CHUNK, (c + 1) * CHUNK) for c in units]
    table = [
        jnp.where(lower, jnp.exp(jnp.where(lower, g_col[c] - total[c : c + 1, :], 0.0)), 0.0)
        for c in units
    ]
    q = [q_in[0, 0, s, :] for s in span]
    k = [k_in[0, 0, s, :] for s in span]
    v = [v_in[0, 0, s, :] for s in span]
    k_f = [k[c].astype(f32) for c in units]
    q_f = [q[c].astype(f32) for c in units]
    t = [t_in[0, 0, c] for c in units]
    w = [w_in[0, 0, c] for c in units]
    u = [u_in[0, 0, c] for c in units]
    s_in = [states[0, 0, c] for c in units]
    d_o = [d_out[0, 0, c] for c in units]
    gram = [mm(k[c], k[c], (1, 1)) * table[c] for c in units]
    score = [mm(q[c], k[c], (1, 1)) * table[c] for c in units]
    grown = [jnp.exp(g_col[c]) for c in units]
    fade = [jnp.exp(last[c] - g_col[c]) for c in units]
    fresh = [u[c] - mm(w[c], s_in[c]) for c in units]
    k_late = [fade[c] * k_f[c] for c in units]
    d_fresh = [mm(score[c], d_o[c], (0, 0)) + mm(k_late[c], ends[c]) for c in units]
    d_score = [jnp.where(lower, mm(d_o[c], fresh[c], (1, 1)), 0.0) for c in units]
    d_q_grown = [mm(d_o[c], s_in[c], (1, 1)) for c in units]
    d_k_late = [mm(fresh[c], ends[c], (1, 1)) for c in units]
    d_w = [-mm(d_fresh[c], s_in[c], (1, 1)) for c in units]
    d_vb = [mm(t[c], d_fresh[c], (0, 0)) for c in units]
    d_kb = [mm(t[c], d_w[c], (0, 0)) for c in units]
    d_lower = [
        jnp.where(strict, -(mm(d_vb[c], u[c], (1, 1)) + mm(d_kb[c], w[c], (1, 1))), 0.0)
        for c in units
    ]
    d_score_t = [d_score[c] * table[c] for c in units]
    d_lower_b = [d_lower[c] * b_col[c] for c in units]
    d_gram = [d_lower_b[c] * table[c] for c in units]
    cols = []
    cols_b = []
    rows_g = []
    for c in units:
        s = span[c]
        paired = d_score[c] * score[c] + d_lower_b[c] * gram[c]
        late = k_late[c] * d_k_late[c]
        k_dot = grown[c] * (d_kb[c] * k_f[c])
        per_row = (
            paired + grown[c] * (q_f[c] * d_q_grown[c]) - late + b_col[c] * k_dot
        )
        cols.append(jnp.sum(per_row, -1, keepdims=True))
        v_f = v[c].astype(f32)
        v_dot = d_vb[c] * v_f
        cols_b.append(
            jnp.sum(
                d_lower[c] * gram[c] + k_dot + v_dot[:, :DK] + v_dot[:, DK:], -1, keepdims=True
            )
        )
        kept = s_in[c].astype(f32) * ends[c]
        whole = jnp.sum(
            jnp.sum(late, 0, keepdims=True)
            + jnp.exp(last[c]) * jnp.sum(kept[:, :DK] + kept[:, DK:], 0, keepdims=True),
            -1,
            keepdims=True,
        )
        rows_g.append((jnp.sum(paired, 0, keepdims=True), whole))
        d_q = mm(d_score_t[c], k[c]) + grown[c] * d_q_grown[c]
        d_k = (
            mm(d_score_t[c], q[c], (0, 0))
            + mm(d_gram[c], k[c])
            + mm(d_gram[c], k[c], (0, 0))
            + fade[c] * d_k_late[c]
            + (b_col[c] * grown[c]) * d_kb[c]
        )
        grads[ROWS + s.start : ROWS + s.stop, 0:DK] = d_q
        grads[ROWS + s.start : ROWS + s.stop, DK : 2 * DK] = d_k
        grads[ROWS + s.start : ROWS + s.stop, 2 * DK :] = b_col[c] * d_vb[c]
    wide = jnp.concatenate(
        cols + cols_b + [jnp.zeros((CHUNK, CHUNK - 2 * chunks), f32)], axis=1
    )
    tall = jnp.transpose(wide)
    d_total = tall[0:chunks] - jnp.concatenate([r for r, _ in rows_g], axis=0)
    d_strength = tall[chunks : 2 * chunks]
    d_decay = mm_exact(pad_rows(d_total)[: max(8, chunks)], lower.astype(f32))[:chunks]
    d_decay = d_decay + jnp.concatenate([w_ for _, w_ in rows_g], axis=0)
    decay_logit, _ = chunk_rows(logits, head, chunks)
    biased = decay_logit + biases[head]
    rate = jnp.exp(rates[head])
    d_logit = -d_decay * rate * sigmoid(biased)
    d_logit_out[0, 0] = jnp.concatenate([d_logit, d_strength * strength * (1.0 - strength)], axis=0)
    rate_out[0, 0] = -d_decay * rate * softplus(biased)

    mixed, taps = conv_into(
        scratch, x_qk, x_v, halo_qk, halo_v, taps_qk, taps_v, length
    )
    sig = sigmoid(mixed)
    active = mixed * sig
    slope = sig * (1.0 + mixed * (1.0 - sig))

    def unnorm(act, grad, factor):
        scale = lax.rsqrt(jnp.sum(act * act, -1, keepdims=True) + epsilon)
        unit = act * scale
        return (factor * scale) * (grad - unit * jnp.sum(unit * grad, -1, keepdims=True))

    body = slice(ROWS, ROWS + length)
    grads[body, 0:DK] = (
        unnorm(active[:, :DK], grads[body, 0:DK], DK ** (-0.5)) * slope[:, :DK]
    )
    grads[body, DK : 2 * DK] = (
        unnorm(active[:, DK : 2 * DK], grads[body, DK : 2 * DK], 1.0) * slope[:, DK : 2 * DK]
    )
    grads[body, 2 * DK :] = grads[body, 2 * DK :] * slope[:, 2 * DK :]
    grads[0:ROWS, :] = jnp.zeros((ROWS, QKV), f32)
    grads[ROWS + length :, :] = jnp.zeros((ROWS, QKV), f32)
    d_x = None
    d_halo = None
    tap_rows = []
    d_conv = grads[body, :]
    first = ROWS - CONV + 1
    for j in range(CONV):
        ahead = CONV - 1 - j
        part = taps[j : j + 1, :] * grads[ROWS + ahead : ROWS + ahead + length, :]
        d_x = part if d_x is None else d_x + part
        edge = taps[j : j + 1, :] * grads[ahead : ahead + ROWS, :]
        d_halo = edge if d_halo is None else d_halo + edge
        tap_rows.append(
            jnp.sum(d_conv * scratch[first + j : first + j + length, :], 0, keepdims=True)
        )
    d_proj_out[0, :, 0:QKV] = d_x.astype(bf16)
    d_proj_out[0, :, QKV:] = d_og[0, 0]
    d_tail_out[0, 0] = d_x[length - ROWS :, :]
    d_halo_out[0, 0] = d_halo
    tap_rows = jnp.concatenate(tap_rows + [jnp.zeros((8 - CONV, QKV), f32)], axis=0)

    @pl.when(seq == 0)
    def _():
        taps_out[0] = tap_rows

    @pl.when(seq != 0)
    def _():
        taps_out[0] = taps_out[0] + tap_rows


def params():
    return pltpu.CompilerParams(
        dimension_semantics=("arbitrary", "arbitrary"), vmem_limit_bytes=56 * 1024 * 1024
    )


def smem():
    return pl.BlockSpec(memory_space=pltpu.SMEM)


def per_unit(*shape):
    zeros = (0,) * len(shape)
    return pl.BlockSpec((1, 1) + shape, lambda h, s: (s, h) + zeros)


def input_specs(length, logit_rows):
    return [
        smem(),
        smem(),
        pl.BlockSpec((1, length, 256), lambda h, s: (s, 0, 3 * h)),
        pl.BlockSpec((1, length, 256), lambda h, s: (s, 0, 3 * h + 1)),
        pl.BlockSpec((1, HALO, 256), lambda h, s: (s, 0, 3 * h)),
        pl.BlockSpec((1, HALO, 256), lambda h, s: (s, 0, 3 * h + 1)),
        pl.BlockSpec((1, logit_rows, length), lambda h, s: (s, 0, 0)),
        pl.BlockSpec((CONV, 256), lambda h, s: (0, 2 * h)),
        pl.BlockSpec((CONV, 256), lambda h, s: (0, 2 * h + 1)),
    ]


def prepare(projected, halo, logits, taps, rates, biases, with_map):
    seqs, length, _ = projected.shape
    heads = rates.shape[0]
    chunks = length // CHUNK

    def out(dtype, *shape):
        return jax.ShapeDtypeStruct((seqs, heads) + shape, dtype), per_unit(*shape)

    outs = [
        out(bf16, length, DK),
        out(bf16, length, DK),
        out(bf16, length, DV),
        out(f32, 2 * chunks, CHUNK),
        out(bf16, chunks, CHUNK, CHUNK),
        out(bf16, chunks, CHUNK, DK),
        out(f32, chunks, CHUNK, DV),
        out(bf16, chunks, CHUNK, DK),
        out(bf16, chunks, DK, DK),
        out(f32, chunks, DK, DV),
        out(f32, chunks, CHUNK, DV),
        out(f32, DK, DV),
    ]
    if with_map:
        outs.append(out(f32, DK, DK))
        kernel = prep_kernel
    else:

        def kernel(*refs):
            prep_kernel(*refs[:-1], None, refs[-1])

    results = pl.pallas_call(
        kernel,
        grid=(heads, seqs),
        in_specs=input_specs(length, 2 * heads),
        out_specs=[spec for _, spec in outs],
        out_shape=[shape for shape, _ in outs],
        scratch_shapes=[pltpu.VMEM((length + ROWS, QKV), f32)],
        compiler_params=params(),
        name="prepare",
    )(rates, biases, projected, projected, halo, halo, logits, taps, taps)
    return results if with_map else list(results) + [None]


def mixer_output(kept, arriving, projected, gain):
    rows, qe, m, b, own = kept
    seqs, heads, chunks = qe.shape[:3]
    length = chunks * CHUNK
    return pl.pallas_call(
        output_kernel,
        grid=(heads, seqs),
        in_specs=[
            per_unit(2 * chunks, CHUNK),
            per_unit(chunks, CHUNK, DK),
            per_unit(chunks, DK, DK),
            per_unit(chunks, DK, DV),
            per_unit(chunks, CHUNK, DV),
            per_unit(DK, DV),
            pl.BlockSpec((1, length, 256), lambda h, s: (s, 0, 3 * h + 2)),
            pl.BlockSpec((1, DV), lambda h, s: (0, 0)),
        ],
        out_specs=[
            pl.BlockSpec((1, length, DV), lambda h, s: (s, 0, h)),
            pl.BlockSpec((1, length, DV), lambda h, s: (s, 0, h)),
            per_unit(chunks, DK, DV),
        ],
        out_shape=[
            jax.ShapeDtypeStruct((seqs, length, heads * DV), bf16),
            jax.ShapeDtypeStruct((seqs, length, heads * DV), f32),
            jax.ShapeDtypeStruct((seqs, heads, chunks, DK, DV), bf16),
        ],
        compiler_params=params(),
        name="mixer_output",
    )(rows, qe, m, b, own, arriving, projected, gain)


def norm_back(rows, d_gated, mixer, projected, gain, qe, m):
    seqs, heads, chunks = qe.shape[:3]
    length = chunks * CHUNK
    return pl.pallas_call(
        norm_back_kernel,
        grid=(heads, seqs),
        in_specs=[
            per_unit(2 * chunks, CHUNK),
            pl.BlockSpec((1, length, DV), lambda h, s: (s, 0, h)),
            pl.BlockSpec((1, length, DV), lambda h, s: (s, 0, h)),
            pl.BlockSpec((1, length, 256), lambda h, s: (s, 0, 3 * h + 2)),
            pl.BlockSpec((1, DV), lambda h, s: (0, 0)),
            per_unit(chunks, CHUNK, DK),
            per_unit(chunks, DK, DK),
        ],
        out_specs=[
            per_unit(chunks, CHUNK, DV),
            per_unit(length, DV),
            per_unit(chunks, DK, DV),
            per_unit(DK, DV),
            pl.BlockSpec((1, 8, DV), lambda h, s: (h, 0, 0)),
        ],
        out_shape=[
            jax.ShapeDtypeStruct((seqs, heads, chunks, CHUNK, DV), bf16),
            jax.ShapeDtypeStruct((seqs, heads, length, DV), bf16),
            jax.ShapeDtypeStruct((seqs, heads, chunks, DK, DV), f32),
            jax.ShapeDtypeStruct((seqs, heads, DK, DV), f32),
            jax.ShapeDtypeStruct((heads, 8, DV), f32),
        ],
        compiler_params=params(),
        name="norm_back",
    )(rows, d_gated, mixer, projected, gain, qe, m)


def mixer_grads(
    projected, halo, logits, taps, rates, biases, q, k, v, rows, t, w, u, m, states, d_out, n, arriving, d_og
):
    seqs, length, width = projected.shape
    heads = rates.shape[0]
    chunks = length // CHUNK
    return pl.pallas_call(
        grad_kernel,
        grid=(heads, seqs),
        in_specs=input_specs(length, 2 * heads)
        + [
            per_unit(length, DK),
            per_unit(length, DK),
            per_unit(length, DV),
            per_unit(2 * chunks, CHUNK),
            per_unit(chunks, CHUNK, CHUNK),
            per_unit(chunks, CHUNK, DK),
            per_unit(chunks, CHUNK, DV),
            per_unit(chunks, DK, DK),
            per_unit(chunks, DK, DV),
            per_unit(chunks, CHUNK, DV),
            per_unit(chunks, DK, DV),
            per_unit(DK, DV),
            per_unit(length, DV),
        ],
        out_specs=[
            pl.BlockSpec((1, length, HEAD), lambda h, s: (s, 0, h)),
            per_unit(ROWS, QKV),
            per_unit(ROWS, QKV),
            per_unit(2 * chunks, CHUNK),
            per_unit(chunks, CHUNK),
            pl.BlockSpec((1, 8, QKV), lambda h, s: (h, 0, 0)),
        ],
        out_shape=[
            jax.ShapeDtypeStruct((seqs, length, width), bf16),
            jax.ShapeDtypeStruct((seqs, heads, ROWS, QKV), f32),
            jax.ShapeDtypeStruct((seqs, heads, ROWS, QKV), f32),
            jax.ShapeDtypeStruct((seqs, heads, 2 * chunks, CHUNK), f32),
            jax.ShapeDtypeStruct((seqs, heads, chunks, CHUNK), f32),
            jax.ShapeDtypeStruct((heads, 8, QKV), f32),
        ],
        scratch_shapes=[
            pltpu.VMEM((length + ROWS, QKV), f32),
            pltpu.VMEM((length + 2 * ROWS, QKV), f32),
        ],
        compiler_params=params(),
        name="mixer_grads",
    )(
        rates, biases, projected, projected, halo, halo, logits, taps, taps,
        q, k, v, rows, t, w, u, m, states, d_out, n, arriving, d_og,
    )


def shifted(block, axis, distance):
    devices = range(lax.axis_size(axis))
    route = [(i - distance, i) for i in devices if i - distance in devices]
    return lax.ppermute(block, axis, route)


def relay(first, maps, distance):
    arriving = shifted(first.astype(bf16), "ctx", distance)
    for _ in range(lax.axis_size("ctx") - 2):
        leaving = first + maps(arriving.astype(f32))
        arriving = shifted(leaving.astype(bf16), "ctx", distance)
    return arriving


def dot(left, right, contract=(1, 0)):
    return lax.dot_general(
        left, right, (((contract[0],), (contract[1],)), ((), ())), preferred_element_type=f32
    )


def local(
    tokens,
    proj_in,
    proj_gates,
    conv_taps,
    log_rates,
    rate_bias,
    gate_gain,
    proj_out,
    ffn_gate,
    ffn_up,
    ffn_down,
    gain_in,
    gain_ffn,
    cotangent,
):
    seqs, length, width = tokens.shape
    row_count = seqs * length
    heads = log_rates.shape[0]
    chunks = length // CHUNK
    tp_count = lax.axis_size("tp")
    tp_place = lax.axis_index("tp")
    share = length // tp_count
    with_map = lax.axis_size("ctx") > 2

    def own(rows):
        return lax.dynamic_slice_in_dim(
            rows.reshape(seqs, length, rows.shape[-1]), tp_place * share, share, 1
        )

    def scatter_sum(partial):
        partial = partial.astype(bf16).reshape(seqs, length, width)
        return lax.psum_scatter(partial, "tp", scatter_dimension=1, tiled=True).astype(f32)

    def gather_rows(rows):
        return lax.all_gather(rows, "tp", axis=1, tiled=True).reshape(row_count, width)

    whole_in = lax.all_gather(proj_in, "shard", axis=0, tiled=True)
    whole_gates = lax.all_gather(proj_gates, "shard", axis=0, tiled=True)
    whole_out = lax.all_gather(proj_out, "shard", axis=1, tiled=True)
    whole_gate = lax.all_gather(ffn_gate, "shard", axis=0, tiled=True)
    whole_up = lax.all_gather(ffn_up, "shard", axis=0, tiled=True)
    whole_down = lax.all_gather(ffn_down, "shard", axis=1, tiled=True)
    gain_in_f = lax.all_gather(gain_in, "shard", axis=0, tiled=True).astype(f32)
    gain_ffn_f = lax.all_gather(gain_ffn, "shard", axis=0, tiled=True).astype(f32)

    inputs_f = tokens.reshape(row_count, width).astype(f32)
    scale_in = lax.rsqrt(jnp.mean(inputs_f * inputs_f, -1, keepdims=True) + epsilon)
    unit_in = inputs_f * scale_in
    normed_in = (unit_in * gain_in_f).astype(bf16)
    projected = dot(normed_in, whole_in).astype(bf16).reshape(seqs, length, heads * HEAD)
    logits = dot(whole_gates, normed_in, (0, 1)).reshape(2 * heads, seqs, length)
    logits = jnp.swapaxes(logits, 0, 1)
    halo = shifted(projected[:, length - HALO :, :], "ctx", 1)
    q, k, v, rows, t, w, u, qe, m, b, own_out, state_end, state_map = prepare(
        projected, halo, logits, conv_taps, log_rates, rate_bias, with_map
    )

    def map_forward(arriving):
        return jnp.einsum("shij,shjk->shik", state_map, arriving)

    def map_back(arriving):
        return jnp.einsum("shji,shjk->shik", state_map, arriving)

    arriving = relay(state_end, map_forward, 1)
    gain_row = gate_gain.reshape(1, DV)
    gated, mixer, states = mixer_output((rows, qe, m, b, own_out), arriving, projected, gain_row)
    gated = gated.reshape(row_count, heads * DV)

    middle = own(inputs_f) + scatter_sum(dot(gated, whole_out))
    scale_mid = lax.rsqrt(jnp.mean(middle * middle, -1, keepdims=True) + epsilon)
    unit_mid = middle * scale_mid
    normed_mid = gather_rows((unit_mid * gain_ffn_f).astype(bf16))
    gate_act = dot(normed_mid, whole_gate)
    up_act = dot(normed_mid, whole_up)
    gate_sig = jax.nn.sigmoid(gate_act)
    gate_silu = gate_act * gate_sig
    hidden = (gate_silu * up_act).astype(bf16)
    d_out = cotangent.reshape(row_count, width)
    d_hidden = dot(d_out, whole_down, (1, 1))
    d_gate = (d_hidden * up_act * gate_sig * (1.0 + gate_act * (1.0 - gate_sig))).astype(bf16)
    d_up = (d_hidden * gate_silu).astype(bf16)
    d_mid_norm = scatter_sum(dot(d_gate, whole_gate, (1, 1)) + dot(d_up, whole_up, (1, 1)))
    layer_rows = middle + scatter_sum(dot(hidden, whole_down))
    grad_down = dot(hidden, d_out, (0, 0))
    grad_gate = dot(normed_mid, d_gate, (0, 0))
    grad_up = dot(normed_mid, d_up, (0, 0))
    gain_ffn_part = jnp.sum(d_mid_norm * unit_mid, (0, 1))
    scaled_mid = d_mid_norm * gain_ffn_f
    d_middle = own(cotangent).astype(f32) + scale_mid * (
        scaled_mid - unit_mid * jnp.mean(scaled_mid * unit_mid, -1, keepdims=True)
    )
    d_branch = gather_rows(d_middle.astype(bf16))
    grad_out = dot(gated, d_branch, (0, 0))
    d_gated = dot(d_branch, whole_out, (1, 1)).reshape(seqs, length, heads * DV)
    d_mixer, d_og, n, d_start, gain_gate_part = norm_back(
        rows, d_gated, mixer, projected, gain_row, qe, m
    )
    arriving_back = relay(d_start, map_back, -1)
    d_projected, d_halo, d_tail, d_logits, rate_rows, tap_rows = mixer_grads(
        projected, halo, logits, conv_taps, log_rates, rate_bias,
        q, k, v, rows, t, w, u, m, states, d_mixer, n, arriving_back, d_og,
    )
    later = shifted(d_halo, "ctx", -1)
    tail = (d_tail + later).astype(bf16)
    for h in range(heads):
        d_projected = lax.dynamic_update_slice(
            d_projected, tail[:, h], (0, length - ROWS, h * HEAD)
        )
    d_projected = d_projected.reshape(row_count, heads * HEAD)
    d_logit_rows = d_logits.reshape(seqs, 2 * heads, length)
    grad_bias = jnp.sum(d_logits[:, :, :chunks], (0, 2, 3))
    grad_rates = jnp.sum(rate_rows, (0, 2, 3))
    d_logit_rows = jnp.swapaxes(d_logit_rows, 0, 1).reshape(2 * heads, row_count).astype(bf16)
    grad_in = dot(normed_in, d_projected, (0, 0))
    grad_gates = dot(normed_in, d_logit_rows, (0, 1))
    in_back = dot(d_projected, whole_in, (1, 1)) + dot(d_logit_rows, whole_gates, (0, 1))
    d_in_norm = scatter_sum(in_back)
    unit_own = own(unit_in)
    scale_own = own(scale_in)
    gain_in_part = jnp.sum(d_in_norm * unit_own, (0, 1))
    scaled_in = d_in_norm * gain_in_f
    token_grad = d_middle + scale_own * (
        scaled_in - unit_own * jnp.mean(scaled_in * unit_own, -1, keepdims=True)
    )
    gain_gate_part = jnp.sum(gain_gate_part, (0, 1))
    grad_taps = jnp.swapaxes(tap_rows[:, :CONV, :], 0, 1).reshape(CONV, heads * QKV)
    grad_gain_gate, grad_gain_in, grad_gain_ffn = lax.psum(
        (gain_gate_part, gain_in_part, gain_ffn_part), "tp"
    )

    def reduced(grad, axis):
        piece = lax.psum_scatter(
            grad.astype(bf16), ("shard", "ctx"), scatter_dimension=axis, tiled=True
        )
        return lax.all_gather(piece, "ctx", axis=axis, tiled=True).astype(f32)

    sum_taps, sum_rates, sum_bias, sum_gain_gate = lax.psum(
        (grad_taps, grad_rates, grad_bias, grad_gain_gate), ("shard", "ctx")
    )
    return (
        layer_rows.astype(bf16),
        token_grad,
        reduced(grad_in, 0),
        reduced(grad_gates, 0),
        sum_taps,
        sum_rates,
        sum_bias,
        sum_gain_gate,
        reduced(grad_out, 1),
        reduced(grad_gate, 0),
        reduced(grad_up, 0),
        reduced(grad_down, 1),
        reduced(grad_gain_in, 0),
        reduced(grad_gain_ffn, 0),
    )


def solution(mesh):
    placed = (
        P("shard", "ctx", None),
        P("shard", "tp"),
        P("shard", "tp"),
        P(None, "tp"),
        P("tp"),
        P("tp"),
        P(),
        P("tp", "shard"),
        P("shard", "tp"),
        P("shard", "tp"),
        P("tp", "shard"),
        P("shard"),
        P("shard"),
        P("shard", "ctx", None),
    )
    return jax.shard_map(
        local,
        mesh=mesh,
        in_specs=placed,
        out_specs=(
            P("shard", ("ctx", "tp"), None),
            P("shard", ("ctx", "tp"), None),
            P("shard", "tp"),
            P("shard", "tp"),
            P(None, "tp"),
            P("tp"),
            P("tp"),
            P(),
            P("tp", "shard"),
            P("shard", "tp"),
            P("shard", "tp"),
            P("tp", "shard"),
            P("shard"),
            P("shard"),
        ),
        check_vma=False,
    )
```

```python
import functools

import jax
import jax.numpy as jnp
from jax import lax
from jax.experimental import pallas as pl
from jax.experimental.pallas import tpu as pltpu
from jax.sharding import PartitionSpec as P

DK = 128
DV = 256
QKV = 2 * DK + DV
HEAD = QKV + DV
CONV = 4
CHUNK = 128
HALO = 16
ROWS = 8

epsilon = 1e-06
f32 = jnp.float32
bf16 = jnp.bfloat16


def mm(left, right, contract=(1, 0)):
    return lax.dot_general(
        left.astype(bf16),
        right.astype(bf16),
        (((contract[0],), (contract[1],)), ((), ())),
        preferred_element_type=f32,
    )


def mm_split(left, right):
    left_hi = left.astype(bf16)
    right_hi = right.astype(bf16)
    left_lo = left - left_hi.astype(f32)
    right_lo = right - right_hi.astype(f32)
    return mm(left_hi, right_hi) + (mm(left_hi, right_lo) + mm(left_lo, right_hi))


def mm_exact(left, right):
    return lax.dot_general(
        left,
        right,
        (((1,), (0,)), ((), ())),
        precision=lax.Precision.HIGHEST,
        preferred_element_type=f32,
    )


def iotas():
    row = lax.broadcasted_iota(jnp.int32, (CHUNK, CHUNK), 0)
    col = lax.broadcasted_iota(jnp.int32, (CHUNK, CHUNK), 1)
    return row, col


def pad_rows(block):
    missing = CHUNK - block.shape[0]
    return jnp.concatenate([block, jnp.zeros((missing, block.shape[1]), f32)], axis=0)


def softplus(values):
    return jnp.maximum(values, 0.0) + jnp.log1p(jnp.exp(-jnp.abs(values)))


def sigmoid(values):
    return 1.0 / (1.0 + jnp.exp(-values))


def place_of(places, c):
    return pl.ds(pl.multiple_of(places[c] * CHUNK, CHUNK), CHUNK)


def chunk_rows(places, logit_ref, chunks):
    def stacked(row):
        return jnp.concatenate(
            [logit_ref[0, row, pl.ds(places[c], 1), :] for c in range(chunks)], axis=0
        )

    return stacked(0), stacked(1)


def invert_units(lowers, row, col):
    eye = (row == col).astype(f32)
    same = (row // 16) == (col // 16)
    powers = [jnp.where(same, n, 0.0) for n in lowers]
    inverses = [eye - p for p in powers]
    for _ in range(3):
        powers = [mm_split(p, p) for p in powers]
        inverses = [x + mm_split(x, p) for x, p in zip(inverses, powers)]
    size = 16
    while size < CHUNK:
        joins = ((row // (2 * size)) == (col // (2 * size))) & ((row // size) != (col // size))
        middles = [mm_split(jnp.where(joins, n, 0.0), x) for n, x in zip(lowers, inverses)]
        inverses = [x - mm_split(x, m) for x, m in zip(inverses, middles)]
        size *= 2
    return inverses


def conv_into(places, scratch, x_qk, x_v, halo_qk, halo_v, taps_qk, taps_v, length):
    scratch[0:ROWS, 0 : 2 * DK] = halo_qk[0, HALO - ROWS :, :].astype(f32)
    scratch[0:ROWS, 2 * DK :] = halo_v[0, HALO - ROWS :, :].astype(f32)
    for c in range(length // CHUNK):
        body = slice(ROWS + c * CHUNK, ROWS + (c + 1) * CHUNK)
        scratch[body, 0 : 2 * DK] = x_qk[0, place_of(places, c), :].astype(f32)
        scratch[body, 2 * DK :] = x_v[0, place_of(places, c), :].astype(f32)
    taps = jnp.concatenate([taps_qk[...], taps_v[...]], axis=1).astype(f32)
    first = ROWS - CONV + 1
    mixed = taps[0:1, :] * scratch[first : first + length, :]
    for j in range(1, CONV):
        mixed = mixed + taps[j : j + 1, :] * scratch[first + j : first + j + length, :]
    return mixed, taps


def prep_kernel(
    places, rates, biases, x_qk, x_v, halo_qk, halo_v, logits, taps_qk, taps_v,
    q_out, k_out, v_out, rows_out, t_out, w_out, u_out, qe_out, m_out, b_out, p_out, end_out, map_out,
    scratch,
):
    head = pl.program_id(0)
    length = x_qk.shape[1]
    chunks = length // CHUNK
    mixed, _ = conv_into(
        places, scratch, x_qk, x_v, halo_qk, halo_v, taps_qk, taps_v, length
    )
    active = mixed * sigmoid(mixed)
    q_act = active[:, :DK]
    k_act = active[:, DK : 2 * DK]
    q_all = (
        q_act * lax.rsqrt(jnp.sum(q_act * q_act, -1, keepdims=True) + epsilon) * DK ** (-0.5)
    ).astype(bf16)
    k_all = (
        k_act * lax.rsqrt(jnp.sum(k_act * k_act, -1, keepdims=True) + epsilon)
    ).astype(bf16)
    v_all = active[:, 2 * DK :].astype(bf16)
    q_out[0, 0] = q_all
    k_out[0, 0] = k_all
    v_out[0, 0] = v_all
    decay_logit, strength_logit = chunk_rows(places, logits, chunks)
    decay = -jnp.exp(rates[head]) * softplus(decay_logit + biases[head])
    row, col = iotas()
    lower = row >= col
    strict = row > col
    total = mm_exact(pad_rows(decay)[: max(8, chunks)], (row <= col).astype(f32))[:chunks]
    strength = sigmoid(strength_logit)
    stacked = jnp.concatenate([total, strength], axis=0)
    rows_out[0, 0] = stacked
    columns = jnp.transpose(pad_rows(stacked))
    units = range(chunks)
    span = [slice(c * CHUNK, (c + 1) * CHUNK) for c in units]
    g_col = [columns[:, c : c + 1] for c in units]
    b_col = [columns[:, chunks + c : chunks + c + 1] for c in units]
    table = [
        jnp.where(lower, jnp.exp(jnp.where(lower, g_col[c] - total[c : c + 1, :], 0.0)), 0.0)
        for c in units
    ]
    q = [q_all[s] for s in span]
    k = [k_all[s] for s in span]
    gram = [mm(k[c], k[c], (1, 1)) for c in units]
    score = [mm(q[c], k[c], (1, 1)) * table[c] for c in units]
    lowers = [jnp.where(strict, b_col[c] * gram[c] * table[c], 0.0) for c in units]
    inverse = invert_units(lowers, row, col)
    grown = [jnp.exp(g_col[c]) for c in units]
    w = [mm(inverse[c], (b_col[c] * grown[c]) * k[c].astype(f32)) for c in units]
    u = [mm(inverse[c], b_col[c] * v_all[span[c]].astype(f32)) for c in units]
    qe = [grown[c] * q[c].astype(f32) - mm(score[c], w[c]) for c in units]
    own = [mm(score[c], u[c]) for c in units]
    last = [g_col[c][CHUNK - 1 :, :] for c in units]
    k_late = [jnp.exp(last[c] - g_col[c]) * k[c].astype(f32) for c in units]
    m = [-mm(k_late[c], w[c], (0, 0)) for c in units]
    b = [mm(k_late[c], u[c], (0, 0)) for c in units]
    state = b[0]
    for c in units:
        t_out[0, 0, c] = inverse[c].astype(bf16)
        w_out[0, 0, c] = w[c].astype(bf16)
        u_out[0, 0, c] = u[c]
        qe_out[0, 0, c] = qe[c].astype(bf16)
        m_out[0, 0, c] = m[c].astype(bf16)
        b_out[0, 0, c] = b[c]
        p_out[0, 0, c] = own[c]
        if c:
            state = jnp.exp(last[c]) * state + mm(m[c], state) + b[c]
    end_out[0, 0] = state
    if map_out is not None:
        chain = (row == col).astype(f32)
        for c in units:
            chain = jnp.exp(last[c]) * chain + mm(m[c], chain)
        map_out[0, 0] = chain


def output_kernel(
    places, rows, qe, m, b, own, arriving, og, gain,
    gated_out, mixer_out, states_out,
):
    chunks = qe.shape[2]
    last = jnp.exp(rows[0, 0][0:chunks, CHUNK - 1 :])
    state = arriving[0, 0].astype(f32)
    gain_row = gain[...].astype(f32)
    for c in range(chunks):
        s = slice(c * CHUNK, (c + 1) * CHUNK)
        states_out[0, 0, c] = state.astype(bf16)
        out = mm(qe[0, 0, c], state) + own[0, 0, c]
        mixer_out[0, s, :] = out
        scale = lax.rsqrt(jnp.mean(out * out, -1, keepdims=True) + epsilon)
        gate = og[0, place_of(places, c), :].astype(f32)
        gated_out[0, place_of(places, c), :] = (out * scale * gain_row * (gate * sigmoid(gate))).astype(bf16)
        if c < chunks - 1:
            state = last[c : c + 1, :] * state + mm(m[0, 0, c], state) + b[0, 0, c]


def norm_back_kernel(
    places, rows, d_gated, mixer, og, gain, qe, m,
    d_out, d_og_out, n_out, start_out, gain_out,
):
    seq = pl.program_id(1)
    chunks = qe.shape[2]
    last = jnp.exp(rows[0, 0][0:chunks, CHUNK - 1 :])
    gain_row = gain[...].astype(f32)
    gain_sum = jnp.zeros((8, DV), f32)
    adds = []
    for c in range(chunks):
        s = slice(c * CHUNK, (c + 1) * CHUNK)
        out = mixer[0, s, :]
        gate = og[0, place_of(places, c), :].astype(f32)
        sig = sigmoid(gate)
        swish = gate * sig
        dg = d_gated[0, place_of(places, c), :].astype(f32)
        scale = lax.rsqrt(jnp.mean(out * out, -1, keepdims=True) + epsilon)
        unit = out * scale
        spread = dg * unit
        e = dg * (gain_row * swish)
        d_mix = scale * (e - unit * jnp.mean(e * unit, -1, keepdims=True))
        d_og_out[0, 0, s, :] = (spread * gain_row * (sig * (1.0 + gate * (1.0 - sig)))).astype(bf16)
        gain_sum = gain_sum + jnp.sum((spread * swish).reshape(CHUNK // 8, 8, DV), axis=0)
        d_low = d_mix.astype(bf16)
        d_out[0, 0, c] = d_low
        add = mm(qe[0, 0, c], d_low, (0, 0))
        n_out[0, 0, c] = add
        adds.append(add)
    back = adds[-1]
    for c in reversed(range(chunks - 1)):
        back = last[c : c + 1, :] * back + mm(m[0, 0, c], back, (0, 0)) + adds[c]
    start_out[0, 0] = back

    @pl.when(seq == 0)
    def _():
        gain_out[0] = gain_sum

    @pl.when(seq != 0)
    def _():
        gain_out[0] = gain_out[0] + gain_sum


def grad_kernel(
    places, rates, biases, x_qk, x_v, halo_qk, halo_v, logits, taps_qk, taps_v,
    q_in, k_in, v_in, rows, t_in, w_in, u_in, m_in, states, d_out, n_in, arriving, d_og,
    d_proj_out, d_halo_out, d_tail_out, d_logit_out, rate_out, taps_out,
    scratch, grads,
):
    head = pl.program_id(0)
    seq = pl.program_id(1)
    length = x_qk.shape[1]
    chunks = length // CHUNK
    units = range(chunks)
    row, col = iotas()
    lower = row >= col
    strict = row > col
    stacked = rows[0, 0]
    total = stacked[0:chunks]
    strength = stacked[chunks : 2 * chunks]
    columns = jnp.transpose(pad_rows(stacked))
    g_col = [columns[:, c : c + 1] for c in units]
    b_col = [columns[:, chunks + c : chunks + c + 1] for c in units]
    last = [g_col[c][CHUNK - 1 :, :] for c in units]
    ends = [None] * chunks
    back = arriving[0, 0].astype(f32)
    for c in reversed(units):
        ends[c] = back
        if c:
            back = jnp.exp(last[c]) * back + mm(m_in[0, 0, c], back, (0, 0)) + n_in[0, 0, c]
    span = [slice(c * CHUNK, (c + 1) * CHUNK) for c in units]
    table = [
        jnp.where(lower, jnp.exp(jnp.where(lower, g_col[c] - total[c : c + 1, :], 0.0)), 0.0)
        for c in units
    ]
    q = [q_in[0, 0, s, :] for s in span]
    k = [k_in[0, 0, s, :] for s in span]
    v = [v_in[0, 0, s, :] for s in span]
    k_f = [k[c].astype(f32) for c in units]
    q_f = [q[c].astype(f32) for c in units]
    t = [t_in[0, 0, c] for c in units]
    w = [w_in[0, 0, c] for c in units]
    u = [u_in[0, 0, c] for c in units]
    s_in = [states[0, 0, c] for c in units]
    d_o = [d_out[0, 0, c] for c in units]
    gram = [mm(k[c], k[c], (1, 1)) * table[c] for c in units]
    score = [mm(q[c], k[c], (1, 1)) * table[c] for c in units]
    grown = [jnp.exp(g_col[c]) for c in units]
    fade = [jnp.exp(last[c] - g_col[c]) for c in units]
    fresh = [u[c] - mm(w[c], s_in[c]) for c in units]
    k_late = [fade[c] * k_f[c] for c in units]
    d_fresh = [mm(score[c], d_o[c], (0, 0)) + mm(k_late[c], ends[c]) for c in units]
    d_score = [jnp.where(lower, mm(d_o[c], fresh[c], (1, 1)), 0.0) for c in units]
    d_q_grown = [mm(d_o[c], s_in[c], (1, 1)) for c in units]
    d_k_late = [mm(fresh[c], ends[c], (1, 1)) for c in units]
    d_w = [-mm(d_fresh[c], s_in[c], (1, 1)) for c in units]
    d_vb = [mm(t[c], d_fresh[c], (0, 0)) for c in units]
    d_kb = [mm(t[c], d_w[c], (0, 0)) for c in units]
    d_lower = [
        jnp.where(strict, -(mm(d_vb[c], u[c], (1, 1)) + mm(d_kb[c], w[c], (1, 1))), 0.0)
        for c in units
    ]
    d_score_t = [d_score[c] * table[c] for c in units]
    d_lower_b = [d_lower[c] * b_col[c] for c in units]
    d_gram = [d_lower_b[c] * table[c] for c in units]
    cols = []
    cols_b = []
    rows_g = []
    for c in units:
        s = span[c]
        paired = d_score[c] * score[c] + d_lower_b[c] * gram[c]
        late = k_late[c] * d_k_late[c]
        k_dot = grown[c] * (d_kb[c] * k_f[c])
        per_row = (
            paired + grown[c] * (q_f[c] * d_q_grown[c]) - late + b_col[c] * k_dot
        )
        cols.append(jnp.sum(per_row, -1, keepdims=True))
        v_f = v[c].astype(f32)
        v_dot = d_vb[c] * v_f
        cols_b.append(
            jnp.sum(
                d_lower[c] * gram[c] + k_dot + v_dot[:, :DK] + v_dot[:, DK:], -1, keepdims=True
            )
        )
        kept = s_in[c].astype(f32) * ends[c]
        whole = jnp.sum(
            jnp.sum(late, 0, keepdims=True)
            + jnp.exp(last[c]) * jnp.sum(kept[:, :DK] + kept[:, DK:], 0, keepdims=True),
            -1,
            keepdims=True,
        )
        rows_g.append((jnp.sum(paired, 0, keepdims=True), whole))
        d_q = mm(d_score_t[c], k[c]) + grown[c] * d_q_grown[c]
        d_k = (
            mm(d_score_t[c], q[c], (0, 0))
            + mm(d_gram[c], k[c])
            + mm(d_gram[c], k[c], (0, 0))
            + fade[c] * d_k_late[c]
            + (b_col[c] * grown[c]) * d_kb[c]
        )
        grads[ROWS + s.start : ROWS + s.stop, 0:DK] = d_q
        grads[ROWS + s.start : ROWS + s.stop, DK : 2 * DK] = d_k
        grads[ROWS + s.start : ROWS + s.stop, 2 * DK :] = b_col[c] * d_vb[c]
    wide = jnp.concatenate(
        cols + cols_b + [jnp.zeros((CHUNK, CHUNK - 2 * chunks), f32)], axis=1
    )
    tall = jnp.transpose(wide)
    d_total = tall[0:chunks] - jnp.concatenate([r for r, _ in rows_g], axis=0)
    d_strength = tall[chunks : 2 * chunks]
    d_decay = mm_exact(pad_rows(d_total)[: max(8, chunks)], lower.astype(f32))[:chunks]
    d_decay = d_decay + jnp.concatenate([w_ for _, w_ in rows_g], axis=0)
    decay_logit, _ = chunk_rows(places, logits, chunks)
    biased = decay_logit + biases[head]
    rate = jnp.exp(rates[head])
    d_logit = -d_decay * rate * sigmoid(biased)
    d_strength_logit = d_strength * strength * (1.0 - strength)
    for c in units:
        d_logit_out[0, 0, pl.ds(places[c], 1), :] = d_logit[c : c + 1, :]
        d_logit_out[0, 1, pl.ds(places[c], 1), :] = d_strength_logit[c : c + 1, :]
    rate_out[0, 0] = -d_decay * rate * softplus(biased)

    mixed, taps = conv_into(
        places, scratch, x_qk, x_v, halo_qk, halo_v, taps_qk, taps_v, length
    )
    sig = sigmoid(mixed)
    active = mixed * sig
    slope = sig * (1.0 + mixed * (1.0 - sig))

    def unnorm(act, grad, factor):
        scale = lax.rsqrt(jnp.sum(act * act, -1, keepdims=True) + epsilon)
        unit = act * scale
        return (factor * scale) * (grad - unit * jnp.sum(unit * grad, -1, keepdims=True))

    body = slice(ROWS, ROWS + length)
    grads[body, 0:DK] = (
        unnorm(active[:, :DK], grads[body, 0:DK], DK ** (-0.5)) * slope[:, :DK]
    )
    grads[body, DK : 2 * DK] = (
        unnorm(active[:, DK : 2 * DK], grads[body, DK : 2 * DK], 1.0) * slope[:, DK : 2 * DK]
    )
    grads[body, 2 * DK :] = grads[body, 2 * DK :] * slope[:, 2 * DK :]
    grads[0:ROWS, :] = jnp.zeros((ROWS, QKV), f32)
    grads[ROWS + length :, :] = jnp.zeros((ROWS, QKV), f32)
    d_x = None
    d_halo = None
    tap_rows = []
    d_conv = grads[body, :]
    first = ROWS - CONV + 1
    for j in range(CONV):
        ahead = CONV - 1 - j
        part = taps[j : j + 1, :] * grads[ROWS + ahead : ROWS + ahead + length, :]
        d_x = part if d_x is None else d_x + part
        edge = taps[j : j + 1, :] * grads[ahead : ahead + ROWS, :]
        d_halo = edge if d_halo is None else d_halo + edge
        tap_rows.append(
            jnp.sum(d_conv * scratch[first + j : first + j + length, :], 0, keepdims=True)
        )
    for c in units:
        d_proj_out[0, place_of(places, c), 0:QKV] = d_x[span[c]].astype(bf16)
        d_proj_out[0, place_of(places, c), QKV:] = d_og[0, 0, span[c], :]
    d_tail_out[0, 0] = d_x[length - ROWS :, :]
    d_halo_out[0, 0] = d_halo
    tap_rows = jnp.concatenate(tap_rows + [jnp.zeros((8 - CONV, QKV), f32)], axis=0)

    @pl.when(seq == 0)
    def _():
        taps_out[0] = tap_rows

    @pl.when(seq != 0)
    def _():
        taps_out[0] = taps_out[0] + tap_rows


def params():
    return pltpu.CompilerParams(
        dimension_semantics=("arbitrary", "arbitrary"), vmem_limit_bytes=56 * 1024 * 1024
    )


def smem():
    return pl.BlockSpec(memory_space=pltpu.SMEM)


def per_unit(*shape):
    zeros = (0,) * len(shape)
    return pl.BlockSpec((1, 1) + shape, lambda h, s: (s, h) + zeros)


def input_specs(length):
    return [
        smem(),
        smem(),
        smem(),
        pl.BlockSpec((1, length, 256), lambda h, s: (s, 0, 3 * h)),
        pl.BlockSpec((1, length, 256), lambda h, s: (s, 0, 3 * h + 1)),
        pl.BlockSpec((1, HALO, 256), lambda h, s: (s, 0, 3 * h)),
        pl.BlockSpec((1, HALO, 256), lambda h, s: (s, 0, 3 * h + 1)),
        pl.BlockSpec((1, 2, length // CHUNK, CHUNK), lambda h, s: (s, h, 0, 0)),
        pl.BlockSpec((CONV, 256), lambda h, s: (0, 2 * h)),
        pl.BlockSpec((CONV, 256), lambda h, s: (0, 2 * h + 1)),
    ]


def prepare(places, projected, halo, logits, taps, rates, biases, with_map):
    seqs, length, _ = projected.shape
    heads = rates.shape[0]
    chunks = length // CHUNK

    def out(dtype, *shape):
        return jax.ShapeDtypeStruct((seqs, heads) + shape, dtype), per_unit(*shape)

    outs = [
        out(bf16, length, DK),
        out(bf16, length, DK),
        out(bf16, length, DV),
        out(f32, 2 * chunks, CHUNK),
        out(bf16, chunks, CHUNK, CHUNK),
        out(bf16, chunks, CHUNK, DK),
        out(f32, chunks, CHUNK, DV),
        out(bf16, chunks, CHUNK, DK),
        out(bf16, chunks, DK, DK),
        out(f32, chunks, DK, DV),
        out(f32, chunks, CHUNK, DV),
        out(f32, DK, DV),
    ]
    if with_map:
        outs.append(out(f32, DK, DK))
        kernel = prep_kernel
    else:

        def kernel(*refs):
            prep_kernel(*refs[:-1], None, refs[-1])

    results = pl.pallas_call(
        kernel,
        grid=(heads, seqs),
        in_specs=input_specs(length),
        out_specs=[spec for _, spec in outs],
        out_shape=[shape for shape, _ in outs],
        scratch_shapes=[pltpu.VMEM((length + ROWS, QKV), f32)],
        compiler_params=params(),
        name="prepare",
    )(places, rates, biases, projected, projected, halo, halo, logits, taps, taps)
    return results if with_map else list(results) + [None]


def mixer_output(places, kept, arriving, projected, gain):
    rows, qe, m, b, own = kept
    seqs, heads, chunks = qe.shape[:3]
    length = chunks * CHUNK
    return pl.pallas_call(
        output_kernel,
        grid=(heads, seqs),
        in_specs=[
            smem(),
            per_unit(2 * chunks, CHUNK),
            per_unit(chunks, CHUNK, DK),
            per_unit(chunks, DK, DK),
            per_unit(chunks, DK, DV),
            per_unit(chunks, CHUNK, DV),
            per_unit(DK, DV),
            pl.BlockSpec((1, length, 256), lambda h, s: (s, 0, 3 * h + 2)),
            pl.BlockSpec((1, DV), lambda h, s: (0, 0)),
        ],
        out_specs=[
            pl.BlockSpec((1, length, DV), lambda h, s: (s, 0, h)),
            pl.BlockSpec((1, length, DV), lambda h, s: (s, 0, h)),
            per_unit(chunks, DK, DV),
        ],
        out_shape=[
            jax.ShapeDtypeStruct((seqs, length, heads * DV), bf16),
            jax.ShapeDtypeStruct((seqs, length, heads * DV), f32),
            jax.ShapeDtypeStruct((seqs, heads, chunks, DK, DV), bf16),
        ],
        compiler_params=params(),
        name="mixer_output",
    )(places, rows, qe, m, b, own, arriving, projected, gain)


def norm_back(places, rows, d_gated, mixer, projected, gain, qe, m):
    seqs, heads, chunks = qe.shape[:3]
    length = chunks * CHUNK
    return pl.pallas_call(
        norm_back_kernel,
        grid=(heads, seqs),
        in_specs=[
            smem(),
            per_unit(2 * chunks, CHUNK),
            pl.BlockSpec((1, length, DV), lambda h, s: (s, 0, h)),
            pl.BlockSpec((1, length, DV), lambda h, s: (s, 0, h)),
            pl.BlockSpec((1, length, 256), lambda h, s: (s, 0, 3 * h + 2)),
            pl.BlockSpec((1, DV), lambda h, s: (0, 0)),
            per_unit(chunks, CHUNK, DK),
            per_unit(chunks, DK, DK),
        ],
        out_specs=[
            per_unit(chunks, CHUNK, DV),
            per_unit(length, DV),
            per_unit(chunks, DK, DV),
            per_unit(DK, DV),
            pl.BlockSpec((1, 8, DV), lambda h, s: (h, 0, 0)),
        ],
        out_shape=[
            jax.ShapeDtypeStruct((seqs, heads, chunks, CHUNK, DV), bf16),
            jax.ShapeDtypeStruct((seqs, heads, length, DV), bf16),
            jax.ShapeDtypeStruct((seqs, heads, chunks, DK, DV), f32),
            jax.ShapeDtypeStruct((seqs, heads, DK, DV), f32),
            jax.ShapeDtypeStruct((heads, 8, DV), f32),
        ],
        compiler_params=params(),
        name="norm_back",
    )(places, rows, d_gated, mixer, projected, gain, qe, m)


def mixer_grads(
    places, projected, halo, logits, taps, rates, biases, q, k, v, rows, t, w, u, m, states, d_out, n, arriving, d_og
):
    seqs, length, width = projected.shape
    heads = rates.shape[0]
    chunks = length // CHUNK
    return pl.pallas_call(
        grad_kernel,
        grid=(heads, seqs),
        in_specs=input_specs(length)
        + [
            per_unit(length, DK),
            per_unit(length, DK),
            per_unit(length, DV),
            per_unit(2 * chunks, CHUNK),
            per_unit(chunks, CHUNK, CHUNK),
            per_unit(chunks, CHUNK, DK),
            per_unit(chunks, CHUNK, DV),
            per_unit(chunks, DK, DK),
            per_unit(chunks, DK, DV),
            per_unit(chunks, CHUNK, DV),
            per_unit(chunks, DK, DV),
            per_unit(DK, DV),
            per_unit(length, DV),
        ],
        out_specs=[
            pl.BlockSpec((1, length, HEAD), lambda h, s: (s, 0, h)),
            per_unit(ROWS, QKV),
            per_unit(ROWS, QKV),
            pl.BlockSpec((1, 2, chunks, CHUNK), lambda h, s: (s, h, 0, 0)),
            per_unit(chunks, CHUNK),
            pl.BlockSpec((1, 8, QKV), lambda h, s: (h, 0, 0)),
        ],
        out_shape=[
            jax.ShapeDtypeStruct((seqs, length, width), bf16),
            jax.ShapeDtypeStruct((seqs, heads, ROWS, QKV), f32),
            jax.ShapeDtypeStruct((seqs, heads, ROWS, QKV), f32),
            jax.ShapeDtypeStruct((seqs, 2 * heads, chunks, CHUNK), f32),
            jax.ShapeDtypeStruct((seqs, heads, chunks, CHUNK), f32),
            jax.ShapeDtypeStruct((heads, 8, QKV), f32),
        ],
        scratch_shapes=[
            pltpu.VMEM((length + ROWS, QKV), f32),
            pltpu.VMEM((length + 2 * ROWS, QKV), f32),
        ],
        compiler_params=params(),
        name="mixer_grads",
    )(
        places, rates, biases, projected, projected, halo, halo, logits, taps, taps,
        q, k, v, rows, t, w, u, m, states, d_out, n, arriving, d_og,
    )


def shifted(block, axis, distance):
    devices = range(lax.axis_size(axis))
    route = [(i - distance, i) for i in devices if i - distance in devices]
    return lax.ppermute(block, axis, route)


def relay(first, maps, distance):
    arriving = shifted(first.astype(bf16), "ctx", distance)
    for _ in range(lax.axis_size("ctx") - 2):
        leaving = first + maps(arriving.astype(f32))
        arriving = shifted(leaving.astype(bf16), "ctx", distance)
    return arriving


def dot(left, right, contract=(1, 0)):
    return lax.dot_general(
        left, right, (((contract[0],), (contract[1],)), ((), ())), preferred_element_type=f32
    )


def local(
    tokens,
    proj_in,
    proj_gates,
    conv_taps,
    log_rates,
    rate_bias,
    gate_gain,
    proj_out,
    ffn_gate,
    ffn_up,
    ffn_down,
    gain_in,
    gain_ffn,
    cotangent,
):
    seqs, length, width = tokens.shape
    row_count = seqs * length
    heads = log_rates.shape[0]
    chunks = length // CHUNK
    tp_count = lax.axis_size("tp")
    tp_place = lax.axis_index("tp")
    share = length // tp_count
    with_map = lax.axis_size("ctx") > 2

    def own(rows):
        return lax.dynamic_slice_in_dim(
            rows.reshape(seqs, length, rows.shape[-1]), tp_place * share, share, 1
        )

    def scatter_sum(partial):
        partial = partial.astype(bf16).reshape(seqs, length, width)
        return lax.psum_scatter(partial, "tp", scatter_dimension=1, tiled=True).astype(f32)

    def gather_rows(rows):
        return lax.all_gather(rows, "tp", axis=1, tiled=True).reshape(row_count, width)

    whole_in = lax.all_gather(proj_in, "shard", axis=0, tiled=True)
    whole_gates = lax.all_gather(proj_gates, "shard", axis=0, tiled=True)
    whole_out = lax.all_gather(proj_out, "shard", axis=1, tiled=True)
    whole_gate = lax.all_gather(ffn_gate, "shard", axis=0, tiled=True)
    whole_up = lax.all_gather(ffn_up, "shard", axis=0, tiled=True)
    whole_down = lax.all_gather(ffn_down, "shard", axis=1, tiled=True)
    gain_in_f = lax.all_gather(gain_in, "shard", axis=0, tiled=True).astype(f32)
    gain_ffn_f = lax.all_gather(gain_ffn, "shard", axis=0, tiled=True).astype(f32)

    inputs_f = tokens.reshape(row_count, width).astype(f32)
    scale_in = lax.rsqrt(jnp.mean(inputs_f * inputs_f, -1, keepdims=True) + epsilon)
    unit_in = inputs_f * scale_in
    normed_in = (unit_in * gain_in_f).astype(bf16)
    projected = dot(normed_in, whole_in).astype(bf16).reshape(seqs, length, heads * HEAD)
    logits = dot(whole_gates, normed_in, (0, 1)).reshape(
        2 * heads, seqs, chunks, CHUNK
    )
    logits = jnp.swapaxes(logits, 0, 1)
    halo = shifted(projected[:, length - HALO :, :], "ctx", 1)
    places = jnp.arange(chunks, dtype=jnp.int32)
    q, k, v, rows, t, w, u, qe, m, b, own_out, state_end, state_map = prepare(
        places, projected, halo, logits, conv_taps, log_rates, rate_bias, with_map
    )

    def map_forward(arriving):
        return jnp.einsum("shij,shjk->shik", state_map, arriving)

    def map_back(arriving):
        return jnp.einsum("shji,shjk->shik", state_map, arriving)

    arriving = relay(state_end, map_forward, 1)
    gain_row = gate_gain.reshape(1, DV)
    gated, mixer, states = mixer_output(
        places, (rows, qe, m, b, own_out), arriving, projected, gain_row
    )
    gated = gated.reshape(row_count, heads * DV)

    middle = own(inputs_f) + scatter_sum(dot(gated, whole_out))
    scale_mid = lax.rsqrt(jnp.mean(middle * middle, -1, keepdims=True) + epsilon)
    unit_mid = middle * scale_mid
    normed_mid = gather_rows((unit_mid * gain_ffn_f).astype(bf16))
    gate_act = dot(normed_mid, whole_gate)
    up_act = dot(normed_mid, whole_up)
    gate_sig = jax.nn.sigmoid(gate_act)
    gate_silu = gate_act * gate_sig
    hidden = (gate_silu * up_act).astype(bf16)
    d_out = cotangent.reshape(row_count, width)
    d_hidden = dot(d_out, whole_down, (1, 1))
    d_gate = (d_hidden * up_act * gate_sig * (1.0 + gate_act * (1.0 - gate_sig))).astype(bf16)
    d_up = (d_hidden * gate_silu).astype(bf16)
    d_mid_norm = scatter_sum(dot(d_gate, whole_gate, (1, 1)) + dot(d_up, whole_up, (1, 1)))
    layer_rows = middle + scatter_sum(dot(hidden, whole_down))
    grad_down = dot(hidden, d_out, (0, 0))
    grad_gate = dot(normed_mid, d_gate, (0, 0))
    grad_up = dot(normed_mid, d_up, (0, 0))
    gain_ffn_part = jnp.sum(d_mid_norm * unit_mid, (0, 1))
    scaled_mid = d_mid_norm * gain_ffn_f
    d_middle = own(cotangent).astype(f32) + scale_mid * (
        scaled_mid - unit_mid * jnp.mean(scaled_mid * unit_mid, -1, keepdims=True)
    )
    d_branch = gather_rows(d_middle.astype(bf16))
    grad_out = dot(gated, d_branch, (0, 0))
    d_gated = dot(d_branch, whole_out, (1, 1)).reshape(seqs, length, heads * DV)
    d_mixer, d_og, n, d_start, gain_gate_part = norm_back(
        places, rows, d_gated, mixer, projected, gain_row, qe, m
    )
    arriving_back = relay(d_start, map_back, -1)
    d_projected, d_halo, d_tail, d_logits, rate_rows, tap_rows = mixer_grads(
        places, projected, halo, logits, conv_taps, log_rates, rate_bias,
        q, k, v, rows, t, w, u, m, states, d_mixer, n, arriving_back, d_og,
    )
    later = shifted(d_halo, "ctx", -1)
    tail = (d_tail + later).astype(bf16)
    for h in range(heads):
        d_projected = lax.dynamic_update_slice(
            d_projected, tail[:, h], (0, length - ROWS, h * HEAD)
        )
    d_projected = d_projected.reshape(row_count, heads * HEAD)
    grad_bias = jnp.sum(d_logits[:, 0::2], (0, 2, 3))
    grad_rates = jnp.sum(rate_rows, (0, 2, 3))
    d_logit_rows = jnp.swapaxes(d_logits, 0, 1).reshape(2 * heads, row_count).astype(bf16)
    grad_in = dot(normed_in, d_projected, (0, 0))
    grad_gates = dot(normed_in, d_logit_rows, (0, 1))
    in_back = dot(d_projected, whole_in, (1, 1)) + dot(d_logit_rows, whole_gates, (0, 1))
    d_in_norm = scatter_sum(in_back)
    unit_own = own(unit_in)
    scale_own = own(scale_in)
    gain_in_part = jnp.sum(d_in_norm * unit_own, (0, 1))
    scaled_in = d_in_norm * gain_in_f
    token_grad = d_middle + scale_own * (
        scaled_in - unit_own * jnp.mean(scaled_in * unit_own, -1, keepdims=True)
    )
    gain_gate_part = jnp.sum(gain_gate_part, (0, 1))
    grad_taps = jnp.swapaxes(tap_rows[:, :CONV, :], 0, 1).reshape(CONV, heads * QKV)
    grad_gain_gate, grad_gain_in, grad_gain_ffn = lax.psum(
        (gain_gate_part, gain_in_part, gain_ffn_part), "tp"
    )

    def reduced(grad, axis):
        piece = lax.psum_scatter(
            grad.astype(bf16), ("shard", "ctx"), scatter_dimension=axis, tiled=True
        )
        return lax.all_gather(piece, "ctx", axis=axis, tiled=True).astype(f32)

    sum_taps, sum_rates, sum_bias, sum_gain_gate = lax.psum(
        (grad_taps, grad_rates, grad_bias, grad_gain_gate), ("shard", "ctx")
    )
    return (
        layer_rows.astype(bf16),
        token_grad,
        reduced(grad_in, 0),
        reduced(grad_gates, 0),
        sum_taps,
        sum_rates,
        sum_bias,
        sum_gain_gate,
        reduced(grad_out, 1),
        reduced(grad_gate, 0),
        reduced(grad_up, 0),
        reduced(grad_down, 1),
        reduced(grad_gain_in, 0),
        reduced(grad_gain_ffn, 0),
    )


def ffn_kernel(rows, d_rows, weights, hidden_out, d_pair_out, back_out, down_out):
    units = weights.shape[1] // 3
    acts = mm(rows[...], weights[:, : 2 * units])
    gate_act = acts[:, :units]
    up_act = acts[:, units:]
    d_hidden = mm(d_rows[...], weights[:, 2 * units :])
    sig = sigmoid(gate_act)
    swish = gate_act * sig
    hidden = (swish * up_act).astype(bf16)
    d_gate = (d_hidden * up_act * sig * (1.0 + gate_act * (1.0 - sig))).astype(bf16)
    d_up = (d_hidden * swish).astype(bf16)
    hidden_out[...] = hidden
    d_pair = jnp.concatenate([d_gate, d_up], axis=1)
    d_pair_out[...] = d_pair
    back_out[...] = mm(d_pair, weights[:, : 2 * units], (1, 1)).astype(bf16)
    down_out[...] = mm(hidden, weights[:, 2 * units :], (1, 1)).astype(bf16)


def feed_forward(rows, d_rows, weights):
    count, width = rows.shape
    units = weights.shape[1] // 3
    tile = min(256, count)

    def tiled(columns):
        return pl.BlockSpec((tile, columns), lambda i: (i, 0))

    widths = (units, 2 * units, width, width)
    return pl.pallas_call(
        ffn_kernel,
        grid=(count // tile,),
        in_specs=[tiled(width), tiled(width), pl.BlockSpec(weights.shape, lambda i: (0, 0))],
        out_specs=[tiled(columns) for columns in widths],
        out_shape=[jax.ShapeDtypeStruct((count, columns), bf16) for columns in widths],
        compiler_params=pltpu.CompilerParams(
            dimension_semantics=("arbitrary",), vmem_limit_bytes=56 * 1024 * 1024
        ),
        name="feed_forward",
    )(rows, d_rows, weights)


def widened(block):
    return jnp.pad(block, ((0, 0), (0, -block.shape[1] % 128)))


def local_paired(
    tokens,
    proj_in,
    proj_gates,
    conv_taps,
    log_rates,
    rate_bias,
    gate_gain,
    proj_out,
    ffn_gate,
    ffn_up,
    ffn_down,
    gain_in,
    gain_ffn,
    cotangent,
):
    seqs, length, width = tokens.shape
    heads = log_rates.shape[0]
    units = ffn_gate.shape[1]
    inner = heads * HEAD
    core = lax.axis_index("ctx")
    place = lax.axis_index("tp")
    tp_count = lax.axis_size("tp")
    seq = place // 2
    half = place % 2
    quarter = length // 2
    share = length // tp_count
    full = 2 * length
    chunks = full // CHUNK
    pairs = [(i, i ^ 1) for i in range(tp_count)]
    route = []
    for j in range(tp_count):
        route.append((j, (j % 2) * tp_count + j // 2))
        route.append((tp_count + j, (j % 2) * tp_count + 2 + j // 2))
    route_back = [(b, a) for a, b in route]

    def swap_core(block):
        return lax.ppermute(block, "ctx", [(0, 1), (1, 0)])

    def swap_chip(block):
        return lax.ppermute(block, "tp", pairs)

    def to_users(block):
        return lax.ppermute(block, ("ctx", "tp"), route)

    def to_owners(block):
        mine = lax.ppermute(block, ("ctx", "tp"), route_back)
        return mine.astype(f32) + swap_core(mine).astype(f32)

    def group_rows(rows):
        sequence = lax.dynamic_index_in_dim(rows, seq, 0, keepdims=False)
        mine = lax.dynamic_slice_in_dim(sequence, half * quarter, quarter, 0)
        other = lax.dynamic_slice_in_dim(sequence, (1 - half) * quarter, quarter, 0)
        got = swap_core(jnp.concatenate([mine, other], axis=0))
        return jnp.concatenate([mine, got[:quarter], other, got[quarter:]], axis=0)

    def scatter_sum(near, far):
        far_got = swap_core(far[quarter:])
        far_sum = (far[:quarter].astype(f32) + far_got.astype(f32)).astype(bf16)
        far_sum = swap_chip(far_sum)
        near_got = swap_core(near[quarter:])
        return near[:quarter].astype(f32) + near_got.astype(f32) + far_sum.astype(f32)

    def gather_rows(mine):
        far = swap_chip(mine)
        near = jnp.concatenate([mine, swap_core(mine)], axis=0)
        return near, jnp.concatenate([far, swap_core(far)], axis=0)

    even = half == 0
    first = seq == 0
    send_a = [(0, 0), (1, 2), (2, 1), (3, 3)]
    send_b = [(0, 1), (1, 3), (2, 0), (3, 2)]

    def to_outputs(mine):
        low, high = mine[:share], mine[share:]
        got_a = lax.ppermute(jnp.where(first, low, high), "tp", send_a)
        got_b = lax.ppermute(jnp.where(first, high, low), "tp", send_b)
        return jnp.stack([jnp.where(even, got_a, got_b), jnp.where(even, got_b, got_a)])

    def gathered(block):
        return lax.all_gather(to_users(block), "shard", axis=0, tiled=True)

    weights_in = gathered(jnp.concatenate([proj_in, widened(proj_gates)], axis=1))
    whole_out = gathered(proj_out.T)
    weights_ffn = gathered(
        jnp.concatenate([widened(ffn_gate), widened(ffn_up), widened(ffn_down.T)], axis=1)
    )
    whole_in = weights_in[:, :inner]
    whole_gates = weights_in[:, inner : inner + 2 * heads]
    gains = lax.all_gather(jnp.stack([gain_in, gain_ffn]), "shard", axis=1, tiled=True).astype(f32)
    gain_in_f, gain_ffn_f = gains[0:1], gains[1:2]
    small = jnp.concatenate([conv_taps, jnp.zeros((4, conv_taps.shape[1]), bf16)], axis=0)
    taps = to_users(small)[:CONV]
    rates = to_users(jnp.pad(jnp.stack([log_rates, rate_bias]), ((0, 6), (0, 128 - heads))))
    log_rates_here, rate_bias_here = rates[0, :heads], rates[1, :heads]

    inputs_f = group_rows(tokens).astype(f32)
    d_out = group_rows(cotangent)
    scale_in = lax.rsqrt(jnp.mean(inputs_f * inputs_f, -1, keepdims=True) + epsilon)
    normed_in = (inputs_f * scale_in * gain_in_f).astype(bf16)
    projected = dot(normed_in, whole_in).astype(bf16).reshape(1, full, inner)
    logits = dot(whole_gates, normed_in, (0, 1)).reshape(1, 2 * heads, chunks, CHUNK)
    halo = jnp.zeros((1, HALO, inner), bf16)
    chunk = jnp.arange(chunks, dtype=jnp.int32)
    per_quarter = quarter // CHUNK
    true_quarter = chunk // per_quarter
    places = (
        2 * ((true_quarter % 2) ^ half) + ((true_quarter // 2) ^ core)
    ) * per_quarter + chunk % per_quarter
    q, k, v, rows, t, w, u, qe, m, b, own_out, _, _ = prepare(
        places, projected, halo, logits, taps, log_rates_here, rate_bias_here, False
    )
    no_state = jnp.zeros((1, heads, DK, DV), f32)
    gain_row = gate_gain.reshape(1, DV)
    gated, mixer, states = mixer_output(
        places, (rows, qe, m, b, own_out), no_state, projected, gain_row
    )
    gated = gated.reshape(full, heads * DV)
    far_part = dot(gated[length:], whole_out, (1, 1)).astype(bf16)
    near_part = dot(gated[:length], whole_out, (1, 1)).astype(bf16)
    middle = inputs_f[:quarter] + scatter_sum(near_part, far_part)
    scale_mid = lax.rsqrt(jnp.mean(middle * middle, -1, keepdims=True) + epsilon)
    unit_mid = middle * scale_mid
    near_mid, far_mid = gather_rows((unit_mid * gain_ffn_f).astype(bf16))
    near_ffn = feed_forward(near_mid, d_out[:length], weights_ffn)
    far_ffn = feed_forward(far_mid, d_out[length:], weights_ffn)
    d_mid_norm = scatter_sum(near_ffn[2], far_ffn[2])
    layer_rows = middle + scatter_sum(near_ffn[3], far_ffn[3])
    layer_out = to_outputs(layer_rows.astype(bf16))
    normed_mid = jnp.concatenate([near_mid, far_mid], axis=0)
    hidden = jnp.concatenate([near_ffn[0], far_ffn[0]], axis=0)
    d_pair = jnp.concatenate([near_ffn[1], far_ffn[1]], axis=0)

    def reduced(grad):
        return to_owners(lax.psum_scatter(grad, "shard", scatter_dimension=0, tiled=True))

    sum_ffn = reduced(
        jnp.concatenate(
            [
                dot(normed_mid, d_pair, (0, 0)).astype(bf16),
                dot(d_out, hidden, (0, 0)).astype(bf16),
            ],
            axis=1,
        )
    )
    padded = sum_ffn.shape[1] // 3
    sum_gate = sum_ffn[:, :units]
    sum_up = sum_ffn[:, padded : padded + units]
    sum_down = sum_ffn[:, 2 * padded : 2 * padded + units].T

    scaled_mid = d_mid_norm * gain_ffn_f
    d_middle = d_out[:quarter].astype(f32) + scale_mid * (
        scaled_mid - unit_mid * jnp.mean(scaled_mid * unit_mid, -1, keepdims=True)
    )
    d_low = d_middle.astype(bf16)
    d_branch = jnp.concatenate(gather_rows(d_low), axis=0)
    d_middle_out = to_outputs(d_low)
    d_gated = dot(d_branch, whole_out).reshape(1, full, heads * DV)
    sum_out = reduced(dot(d_branch, gated, (0, 0)).astype(bf16)).T
    d_mixer, d_og, n, _, gain_gate_part = norm_back(
        places, rows, d_gated, mixer, projected, gain_row, qe, m
    )
    d_projected, _, _, d_logits, rate_rows, tap_rows = mixer_grads(
        places, projected, halo, logits, taps, log_rates_here, rate_bias_here,
        q, k, v, rows, t, w, u, m, states, d_mixer, n, no_state, d_og,
    )
    d_projected = d_projected.reshape(full, inner)
    d_logit_rows = d_logits.reshape(2 * heads, full).astype(bf16)
    far_back = dot(d_projected[length:], whole_in, (1, 1)) + dot(
        d_logit_rows[:, length:], whole_gates, (0, 1)
    )
    near_back = dot(d_projected[:length], whole_in, (1, 1)) + dot(
        d_logit_rows[:, :length], whole_gates, (0, 1)
    )
    d_in_norm = to_outputs(scatter_sum(near_back.astype(bf16), far_back.astype(bf16)).astype(bf16))
    sum_in = reduced(
        jnp.concatenate(
            [
                dot(normed_in, d_projected, (0, 0)).astype(bf16),
                widened(dot(normed_in, d_logit_rows, (0, 1)).astype(bf16)),
            ],
            axis=1,
        )
    )
    sum_gates = sum_in[:, inner : inner + 2 * heads]
    sum_in = sum_in[:, :inner]

    last = lax.dynamic_slice_in_dim(tokens, place * share, share, 1).astype(f32)
    scale_last = lax.rsqrt(jnp.mean(last * last, -1, keepdims=True) + epsilon)
    unit_last = last * scale_last
    scaled_in = d_in_norm.astype(f32) * gain_in_f
    token_grad = d_middle_out.astype(f32) + scale_last * (
        scaled_in - unit_last * jnp.mean(scaled_in * unit_last, -1, keepdims=True)
    )

    tap_count = CONV * heads * QKV
    parts = [
        jnp.swapaxes(tap_rows[:, :CONV, :], 0, 1).reshape(tap_count),
        jnp.sum(gain_gate_part, (0, 1)),
        jnp.sum(rate_rows, (0, 2, 3)),
        jnp.sum(d_logits[0, 0::2], (1, 2)),
    ]
    packed = jnp.concatenate(parts)
    packed = jnp.pad(packed, (0, -packed.shape[0] % 1024)).reshape(-1, 128)
    packed = to_owners(jnp.sum(lax.all_gather(packed, "shard"), 0)).reshape(-1)
    sum_taps = packed[:tap_count].reshape(CONV, heads * QKV)
    gain_end = tap_count + DV
    sum_rates = packed[gain_end : gain_end + heads]
    sum_bias = packed[gain_end + heads : gain_end + 2 * heads]

    def along(weight, grad):
        return jnp.sum(weight.astype(f32) * grad, 1)

    part_in = along(proj_in, sum_in) + along(proj_gates, sum_gates)
    part_ffn = along(ffn_gate, sum_gate) + along(ffn_up, sum_up)
    gain_sums = lax.psum(
        jnp.concatenate([packed[tap_count:gain_end], part_in, part_ffn]), "tp"
    )
    rows_here = gain_in.shape[0]
    return (
        layer_out,
        token_grad,
        sum_in,
        sum_gates,
        sum_taps,
        sum_rates,
        sum_bias,
        gain_sums[:DV],
        sum_out,
        sum_gate,
        sum_up,
        sum_down,
        gain_sums[DV : DV + rows_here] / gain_in.astype(f32),
        gain_sums[DV + rows_here :] / gain_ffn.astype(f32),
    )


def solution(mesh):
    placed = (
        P("shard", "ctx", None),
        P("shard", "tp"),
        P("shard", "tp"),
        P(None, "tp"),
        P("tp"),
        P("tp"),
        P(),
        P("tp", "shard"),
        P("shard", "tp"),
        P("shard", "tp"),
        P("tp", "shard"),
        P("shard"),
        P("shard"),
        P("shard", "ctx", None),
    )
    shape = dict(mesh.shape)
    paired = (shape["shard"], shape["ctx"], shape["tp"]) == (4, 2, 4)

    def body(*arrays):
        seqs, length, _ = arrays[0].shape
        if paired and seqs == 2 and length % (2 * CHUNK) == 0:
            return local_paired(*arrays)
        return local(*arrays)

    return jax.shard_map(
        body,
        mesh=mesh,
        in_specs=placed,
        out_specs=(
            P("shard", ("ctx", "tp"), None),
            P("shard", ("ctx", "tp"), None),
            P("shard", "tp"),
            P("shard", "tp"),
            P(None, "tp"),
            P("tp"),
            P("tp"),
            P(),
            P("tp", "shard"),
            P("shard", "tp"),
            P("shard", "tp"),
            P("tp", "shard"),
            P("shard"),
            P("shard"),
        ),
        check_vma=False,
    )
```

```python
import functools

import jax
import jax.numpy as jnp
from jax import lax
from jax.experimental import pallas as pl
from jax.experimental.pallas import tpu as pltpu
from jax.sharding import PartitionSpec as P

DK = 128
DV = 256
QKV = 2 * DK + DV
HEAD = QKV + DV
CONV = 4
CHUNK = 128
HALO = 16
ROWS = 8

epsilon = 1e-06
f32 = jnp.float32
bf16 = jnp.bfloat16


def mm(left, right, contract=(1, 0)):
    return lax.dot_general(
        left.astype(bf16),
        right.astype(bf16),
        (((contract[0],), (contract[1],)), ((), ())),
        preferred_element_type=f32,
    )


def mm_split(left, right):
    left_hi = left.astype(bf16)
    right_hi = right.astype(bf16)
    left_lo = left - left_hi.astype(f32)
    right_lo = right - right_hi.astype(f32)
    return mm(left_hi, right_hi) + (mm(left_hi, right_lo) + mm(left_lo, right_hi))


def mm_exact(left, right):
    return lax.dot_general(
        left,
        right,
        (((1,), (0,)), ((), ())),
        precision=lax.Precision.HIGHEST,
        preferred_element_type=f32,
    )


def iotas():
    row = lax.broadcasted_iota(jnp.int32, (CHUNK, CHUNK), 0)
    col = lax.broadcasted_iota(jnp.int32, (CHUNK, CHUNK), 1)
    return row, col


def pad_rows(block):
    missing = CHUNK - block.shape[0]
    return jnp.concatenate([block, jnp.zeros((missing, block.shape[1]), f32)], axis=0)


def softplus(values):
    return jnp.maximum(values, 0.0) + jnp.log1p(jnp.exp(-jnp.abs(values)))


def sigmoid(values):
    return 1.0 / (1.0 + jnp.exp(-values))


def place_of(places, c):
    return pl.ds(pl.multiple_of(places[c] * CHUNK, CHUNK), CHUNK)


def chunk_rows(places, logit_ref, chunks):
    def stacked(row):
        return jnp.concatenate(
            [logit_ref[0, row, pl.ds(places[c], 1), :] for c in range(chunks)], axis=0
        )

    return stacked(0), stacked(1)


def invert_units(lowers, row, col):
    eye = (row == col).astype(f32)
    same = (row // 16) == (col // 16)
    powers = [jnp.where(same, n, 0.0) for n in lowers]
    inverses = [eye - p for p in powers]
    for _ in range(3):
        powers = [mm_split(p, p) for p in powers]
        inverses = [x + mm_split(x, p) for x, p in zip(inverses, powers)]
    size = 16
    while size < CHUNK:
        joins = ((row // (2 * size)) == (col // (2 * size))) & ((row // size) != (col // size))
        middles = [mm_split(jnp.where(joins, n, 0.0), x) for n, x in zip(lowers, inverses)]
        inverses = [x - mm_split(x, m) for x, m in zip(inverses, middles)]
        size *= 2
    return inverses


def conv_into(places, scratch, x_qk, x_v, halo_qk, halo_v, taps_qk, taps_v, length):
    scratch[0:ROWS, 0 : 2 * DK] = halo_qk[0, HALO - ROWS :, :].astype(f32)
    scratch[0:ROWS, 2 * DK :] = halo_v[0, HALO - ROWS :, :].astype(f32)
    for c in range(length // CHUNK):
        body = slice(ROWS + c * CHUNK, ROWS + (c + 1) * CHUNK)
        scratch[body, 0 : 2 * DK] = x_qk[0, place_of(places, c), :].astype(f32)
        scratch[body, 2 * DK :] = x_v[0, place_of(places, c), :].astype(f32)
    taps = jnp.concatenate([taps_qk[...], taps_v[...]], axis=1).astype(f32)
    first = ROWS - CONV + 1
    mixed = taps[0:1, :] * scratch[first : first + length, :]
    for j in range(1, CONV):
        mixed = mixed + taps[j : j + 1, :] * scratch[first + j : first + j + length, :]
    return mixed, taps


def prep_kernel(
    places, rates, biases, x_qk, x_v, halo_qk, halo_v, logits, taps_qk, taps_v,
    q_out, k_out, v_out, rows_out, t_out, w_out, u_out, qe_out, m_out, b_out, p_out, end_out, map_out,
    scratch,
):
    head = pl.program_id(0)
    length = x_qk.shape[1]
    chunks = length // CHUNK
    mixed, _ = conv_into(
        places, scratch, x_qk, x_v, halo_qk, halo_v, taps_qk, taps_v, length
    )
    active = mixed * sigmoid(mixed)
    q_act = active[:, :DK]
    k_act = active[:, DK : 2 * DK]
    q_all = (
        q_act * lax.rsqrt(jnp.sum(q_act * q_act, -1, keepdims=True) + epsilon) * DK ** (-0.5)
    ).astype(bf16)
    k_all = (
        k_act * lax.rsqrt(jnp.sum(k_act * k_act, -1, keepdims=True) + epsilon)
    ).astype(bf16)
    v_all = active[:, 2 * DK :].astype(bf16)
    q_out[0, 0] = q_all
    k_out[0, 0] = k_all
    v_out[0, 0] = v_all
    decay_logit, strength_logit = chunk_rows(places, logits, chunks)
    decay = -jnp.exp(rates[head]) * softplus(decay_logit + biases[head])
    row, col = iotas()
    lower = row >= col
    strict = row > col
    total = mm_exact(pad_rows(decay)[: max(8, chunks)], (row <= col).astype(f32))[:chunks]
    strength = sigmoid(strength_logit)
    stacked = jnp.concatenate([total, strength], axis=0)
    rows_out[0, 0] = stacked
    columns = jnp.transpose(pad_rows(stacked))
    units = range(chunks)
    span = [slice(c * CHUNK, (c + 1) * CHUNK) for c in units]
    g_col = [columns[:, c : c + 1] for c in units]
    b_col = [columns[:, chunks + c : chunks + c + 1] for c in units]
    table = [
        jnp.where(lower, jnp.exp(jnp.where(lower, g_col[c] - total[c : c + 1, :], 0.0)), 0.0)
        for c in units
    ]
    q = [q_all[s] for s in span]
    k = [k_all[s] for s in span]
    gram = [mm(k[c], k[c], (1, 1)) for c in units]
    score = [mm(q[c], k[c], (1, 1)) * table[c] for c in units]
    lowers = [jnp.where(strict, b_col[c] * gram[c] * table[c], 0.0) for c in units]
    inverse = invert_units(lowers, row, col)
    grown = [jnp.exp(g_col[c]) for c in units]
    w = [mm(inverse[c], (b_col[c] * grown[c]) * k[c].astype(f32)) for c in units]
    u = [mm(inverse[c], b_col[c] * v_all[span[c]].astype(f32)) for c in units]
    qe = [grown[c] * q[c].astype(f32) - mm(score[c], w[c]) for c in units]
    own = [mm(score[c], u[c]) for c in units]
    last = [g_col[c][CHUNK - 1 :, :] for c in units]
    k_late = [jnp.exp(last[c] - g_col[c]) * k[c].astype(f32) for c in units]
    m = [-mm(k_late[c], w[c], (0, 0)) for c in units]
    b = [mm(k_late[c], u[c], (0, 0)) for c in units]
    state = b[0]
    for c in units:
        t_out[0, 0, c] = inverse[c].astype(bf16)
        w_out[0, 0, c] = w[c].astype(bf16)
        u_out[0, 0, c] = u[c]
        qe_out[0, 0, c] = qe[c].astype(bf16)
        m_out[0, 0, c] = m[c].astype(bf16)
        b_out[0, 0, c] = b[c]
        p_out[0, 0, c] = own[c]
        if c:
            state = jnp.exp(last[c]) * state + mm(m[c], state) + b[c]
    end_out[0, 0] = state
    if map_out is not None:
        chain = (row == col).astype(f32)
        for c in units:
            chain = jnp.exp(last[c]) * chain + mm(m[c], chain)
        map_out[0, 0] = chain


def output_kernel(
    places, rows, qe, m, b, own, arriving, og, gain,
    gated_out, mixer_out, states_out,
):
    chunks = qe.shape[2]
    last = jnp.exp(rows[0, 0][0:chunks, CHUNK - 1 :])
    state = arriving[0, 0].astype(f32)
    gain_row = gain[...].astype(f32)
    for c in range(chunks):
        s = slice(c * CHUNK, (c + 1) * CHUNK)
        states_out[0, 0, c] = state.astype(bf16)
        out = mm(qe[0, 0, c], state) + own[0, 0, c]
        mixer_out[0, s, :] = out
        scale = lax.rsqrt(jnp.mean(out * out, -1, keepdims=True) + epsilon)
        gate = og[0, place_of(places, c), :].astype(f32)
        gated_out[0, place_of(places, c), :] = (out * scale * gain_row * (gate * sigmoid(gate))).astype(bf16)
        if c < chunks - 1:
            state = last[c : c + 1, :] * state + mm(m[0, 0, c], state) + b[0, 0, c]


def norm_back_kernel(
    places, rows, d_gated, mixer, og, gain, qe, m,
    d_out, d_og_out, n_out, start_out, gain_out,
):
    seq = pl.program_id(1)
    chunks = qe.shape[2]
    last = jnp.exp(rows[0, 0][0:chunks, CHUNK - 1 :])
    gain_row = gain[...].astype(f32)
    gain_sum = jnp.zeros((8, DV), f32)
    adds = []
    for c in range(chunks):
        s = slice(c * CHUNK, (c + 1) * CHUNK)
        out = mixer[0, s, :]
        gate = og[0, place_of(places, c), :].astype(f32)
        sig = sigmoid(gate)
        swish = gate * sig
        dg = d_gated[0, place_of(places, c), :].astype(f32)
        scale = lax.rsqrt(jnp.mean(out * out, -1, keepdims=True) + epsilon)
        unit = out * scale
        spread = dg * unit
        e = dg * (gain_row * swish)
        d_mix = scale * (e - unit * jnp.mean(e * unit, -1, keepdims=True))
        d_og_out[0, 0, s, :] = (spread * gain_row * (sig * (1.0 + gate * (1.0 - sig)))).astype(bf16)
        gain_sum = gain_sum + jnp.sum((spread * swish).reshape(CHUNK // 8, 8, DV), axis=0)
        d_low = d_mix.astype(bf16)
        d_out[0, 0, c] = d_low
        add = mm(qe[0, 0, c], d_low, (0, 0))
        n_out[0, 0, c] = add
        adds.append(add)
    back = adds[-1]
    for c in reversed(range(chunks - 1)):
        back = last[c : c + 1, :] * back + mm(m[0, 0, c], back, (0, 0)) + adds[c]
    start_out[0, 0] = back

    @pl.when(seq == 0)
    def _():
        gain_out[0] = gain_sum

    @pl.when(seq != 0)
    def _():
        gain_out[0] = gain_out[0] + gain_sum


def grad_kernel(
    start, places, rates, biases, x_qk, x_v, halo_qk, halo_v, logits, taps_qk, taps_v,
    q_in, k_in, v_in, rows, t_in, w_in, u_in, m_in, states, d_out, n_in, arriving, d_og,
    d_proj_out, d_halo_out, d_tail_out, d_logit_out, rate_out, taps_out,
    scratch, grads,
):
    head = pl.program_id(0) + start
    seq = pl.program_id(1)
    length = x_qk.shape[1]
    chunks = length // CHUNK
    units = range(chunks)
    row, col = iotas()
    lower = row >= col
    strict = row > col
    stacked = rows[0, 0]
    total = stacked[0:chunks]
    strength = stacked[chunks : 2 * chunks]
    columns = jnp.transpose(pad_rows(stacked))
    g_col = [columns[:, c : c + 1] for c in units]
    b_col = [columns[:, chunks + c : chunks + c + 1] for c in units]
    last = [g_col[c][CHUNK - 1 :, :] for c in units]
    ends = [None] * chunks
    back = arriving[0, 0].astype(f32)
    for c in reversed(units):
        ends[c] = back
        if c:
            back = jnp.exp(last[c]) * back + mm(m_in[0, 0, c], back, (0, 0)) + n_in[0, 0, c]
    span = [slice(c * CHUNK, (c + 1) * CHUNK) for c in units]
    table = [
        jnp.where(lower, jnp.exp(jnp.where(lower, g_col[c] - total[c : c + 1, :], 0.0)), 0.0)
        for c in units
    ]
    q = [q_in[0, 0, s, :] for s in span]
    k = [k_in[0, 0, s, :] for s in span]
    v = [v_in[0, 0, s, :] for s in span]
    k_f = [k[c].astype(f32) for c in units]
    q_f = [q[c].astype(f32) for c in units]
    t = [t_in[0, 0, c] for c in units]
    w = [w_in[0, 0, c] for c in units]
    u = [u_in[0, 0, c] for c in units]
    s_in = [states[0, 0, c] for c in units]
    d_o = [d_out[0, 0, c] for c in units]
    gram = [mm(k[c], k[c], (1, 1)) * table[c] for c in units]
    score = [mm(q[c], k[c], (1, 1)) * table[c] for c in units]
    grown = [jnp.exp(g_col[c]) for c in units]
    fade = [jnp.exp(last[c] - g_col[c]) for c in units]
    fresh = [u[c] - mm(w[c], s_in[c]) for c in units]
    k_late = [fade[c] * k_f[c] for c in units]
    d_fresh = [mm(score[c], d_o[c], (0, 0)) + mm(k_late[c], ends[c]) for c in units]
    d_score = [jnp.where(lower, mm(d_o[c], fresh[c], (1, 1)), 0.0) for c in units]
    d_q_grown = [mm(d_o[c], s_in[c], (1, 1)) for c in units]
    d_k_late = [mm(fresh[c], ends[c], (1, 1)) for c in units]
    d_w = [-mm(d_fresh[c], s_in[c], (1, 1)) for c in units]
    d_vb = [mm(t[c], d_fresh[c], (0, 0)) for c in units]
    d_kb = [mm(t[c], d_w[c], (0, 0)) for c in units]
    d_lower = [
        jnp.where(strict, -(mm(d_vb[c], u[c], (1, 1)) + mm(d_kb[c], w[c], (1, 1))), 0.0)
        for c in units
    ]
    d_score_t = [d_score[c] * table[c] for c in units]
    d_lower_b = [d_lower[c] * b_col[c] for c in units]
    d_gram = [d_lower_b[c] * table[c] for c in units]
    cols = []
    cols_b = []
    rows_g = []
    for c in units:
        s = span[c]
        paired = d_score[c] * score[c] + d_lower_b[c] * gram[c]
        late = k_late[c] * d_k_late[c]
        k_dot = grown[c] * (d_kb[c] * k_f[c])
        per_row = (
            paired + grown[c] * (q_f[c] * d_q_grown[c]) - late + b_col[c] * k_dot
        )
        cols.append(jnp.sum(per_row, -1, keepdims=True))
        v_f = v[c].astype(f32)
        v_dot = d_vb[c] * v_f
        cols_b.append(
            jnp.sum(
                d_lower[c] * gram[c] + k_dot + v_dot[:, :DK] + v_dot[:, DK:], -1, keepdims=True
            )
        )
        kept = s_in[c].astype(f32) * ends[c]
        whole = jnp.sum(
            jnp.sum(late, 0, keepdims=True)
            + jnp.exp(last[c]) * jnp.sum(kept[:, :DK] + kept[:, DK:], 0, keepdims=True),
            -1,
            keepdims=True,
        )
        rows_g.append((jnp.sum(paired, 0, keepdims=True), whole))
        d_q = mm(d_score_t[c], k[c]) + grown[c] * d_q_grown[c]
        d_k = (
            mm(d_score_t[c], q[c], (0, 0))
            + mm(d_gram[c], k[c])
            + mm(d_gram[c], k[c], (0, 0))
            + fade[c] * d_k_late[c]
            + (b_col[c] * grown[c]) * d_kb[c]
        )
        grads[ROWS + s.start : ROWS + s.stop, 0:DK] = d_q
        grads[ROWS + s.start : ROWS + s.stop, DK : 2 * DK] = d_k
        grads[ROWS + s.start : ROWS + s.stop, 2 * DK :] = b_col[c] * d_vb[c]
    wide = jnp.concatenate(
        cols + cols_b + [jnp.zeros((CHUNK, CHUNK - 2 * chunks), f32)], axis=1
    )
    tall = jnp.transpose(wide)
    d_total = tall[0:chunks] - jnp.concatenate([r for r, _ in rows_g], axis=0)
    d_strength = tall[chunks : 2 * chunks]
    d_decay = mm_exact(pad_rows(d_total)[: max(8, chunks)], lower.astype(f32))[:chunks]
    d_decay = d_decay + jnp.concatenate([w_ for _, w_ in rows_g], axis=0)
    decay_logit, _ = chunk_rows(places, logits, chunks)
    biased = decay_logit + biases[head]
    rate = jnp.exp(rates[head])
    d_logit = -d_decay * rate * sigmoid(biased)
    d_strength_logit = d_strength * strength * (1.0 - strength)
    for c in units:
        d_logit_out[0, 0, pl.ds(places[c], 1), :] = d_logit[c : c + 1, :]
        d_logit_out[0, 1, pl.ds(places[c], 1), :] = d_strength_logit[c : c + 1, :]
    rate_out[0, 0] = -d_decay * rate * softplus(biased)

    mixed, taps = conv_into(
        places, scratch, x_qk, x_v, halo_qk, halo_v, taps_qk, taps_v, length
    )
    sig = sigmoid(mixed)
    active = mixed * sig
    slope = sig * (1.0 + mixed * (1.0 - sig))

    def unnorm(act, grad, factor):
        scale = lax.rsqrt(jnp.sum(act * act, -1, keepdims=True) + epsilon)
        unit = act * scale
        return (factor * scale) * (grad - unit * jnp.sum(unit * grad, -1, keepdims=True))

    body = slice(ROWS, ROWS + length)
    grads[body, 0:DK] = (
        unnorm(active[:, :DK], grads[body, 0:DK], DK ** (-0.5)) * slope[:, :DK]
    )
    grads[body, DK : 2 * DK] = (
        unnorm(active[:, DK : 2 * DK], grads[body, DK : 2 * DK], 1.0) * slope[:, DK : 2 * DK]
    )
    grads[body, 2 * DK :] = grads[body, 2 * DK :] * slope[:, 2 * DK :]
    grads[0:ROWS, :] = jnp.zeros((ROWS, QKV), f32)
    grads[ROWS + length :, :] = jnp.zeros((ROWS, QKV), f32)
    d_x = None
    d_halo = None
    tap_rows = []
    d_conv = grads[body, :]
    first = ROWS - CONV + 1
    for j in range(CONV):
        ahead = CONV - 1 - j
        part = taps[j : j + 1, :] * grads[ROWS + ahead : ROWS + ahead + length, :]
        d_x = part if d_x is None else d_x + part
        edge = taps[j : j + 1, :] * grads[ahead : ahead + ROWS, :]
        d_halo = edge if d_halo is None else d_halo + edge
        tap_rows.append(
            jnp.sum(d_conv * scratch[first + j : first + j + length, :], 0, keepdims=True)
        )
    for c in units:
        d_proj_out[0, place_of(places, c), 0:QKV] = d_x[span[c]].astype(bf16)
        d_proj_out[0, place_of(places, c), QKV:] = d_og[0, 0, span[c], :]
    d_tail_out[0, 0] = d_x[length - ROWS :, :]
    d_halo_out[0, 0] = d_halo
    tap_rows = jnp.concatenate(tap_rows + [jnp.zeros((8 - CONV, QKV), f32)], axis=0)

    @pl.when(seq == 0)
    def _():
        taps_out[0] = tap_rows

    @pl.when(seq != 0)
    def _():
        taps_out[0] = taps_out[0] + tap_rows


def cost(micros):
    return pl.CostEstimate(
        flops=int(micros * 1e9), bytes_accessed=int(micros * 3e6), transcendentals=0
    )


def params():
    return pltpu.CompilerParams(
        dimension_semantics=("arbitrary", "arbitrary"), vmem_limit_bytes=56 * 1024 * 1024
    )


def smem():
    return pl.BlockSpec(memory_space=pltpu.SMEM)


def per_unit(*shape, start=0):
    zeros = (0,) * len(shape)
    return pl.BlockSpec((1, 1) + shape, lambda h, s: (s, h + start) + zeros)


def input_specs(length, start=0):
    return [
        smem(),
        smem(),
        smem(),
        pl.BlockSpec((1, length, 256), lambda h, s: (s, 0, 3 * (h + start))),
        pl.BlockSpec((1, length, 256), lambda h, s: (s, 0, 3 * (h + start) + 1)),
        pl.BlockSpec((1, HALO, 256), lambda h, s: (s, 0, 3 * (h + start))),
        pl.BlockSpec((1, HALO, 256), lambda h, s: (s, 0, 3 * (h + start) + 1)),
        pl.BlockSpec((1, 2, length // CHUNK, CHUNK), lambda h, s: (s, h + start, 0, 0)),
        pl.BlockSpec((CONV, 256), lambda h, s: (0, 2 * (h + start))),
        pl.BlockSpec((CONV, 256), lambda h, s: (0, 2 * (h + start) + 1)),
    ]


def prepare(places, projected, halo, logits, taps, rates, biases, with_map):
    seqs, length, _ = projected.shape
    heads = rates.shape[0]
    chunks = length // CHUNK

    def out(dtype, *shape):
        return jax.ShapeDtypeStruct((seqs, heads) + shape, dtype), per_unit(*shape)

    outs = [
        out(bf16, length, DK),
        out(bf16, length, DK),
        out(bf16, length, DV),
        out(f32, 2 * chunks, CHUNK),
        out(bf16, chunks, CHUNK, CHUNK),
        out(bf16, chunks, CHUNK, DK),
        out(f32, chunks, CHUNK, DV),
        out(bf16, chunks, CHUNK, DK),
        out(bf16, chunks, DK, DK),
        out(f32, chunks, DK, DV),
        out(f32, chunks, CHUNK, DV),
        out(f32, DK, DV),
    ]
    if with_map:
        outs.append(out(f32, DK, DK))
        kernel = prep_kernel
    else:

        def kernel(*refs):
            prep_kernel(*refs[:-1], None, refs[-1])

    results = pl.pallas_call(
        kernel,
        grid=(heads, seqs),
        in_specs=input_specs(length),
        out_specs=[spec for _, spec in outs],
        out_shape=[shape for shape, _ in outs],
        scratch_shapes=[pltpu.VMEM((length + ROWS, QKV), f32)],
        compiler_params=params(),
        cost_estimate=cost(9.0 * heads * seqs * chunks / 8),
        name="prepare",
    )(places, rates, biases, projected, projected, halo, halo, logits, taps, taps)
    return results if with_map else list(results) + [None]


def mixer_output(places, kept, arriving, projected, gain):
    rows, qe, m, b, own = kept
    seqs, heads, chunks = qe.shape[:3]
    length = chunks * CHUNK
    return pl.pallas_call(
        output_kernel,
        grid=(heads, seqs),
        in_specs=[
            smem(),
            per_unit(2 * chunks, CHUNK),
            per_unit(chunks, CHUNK, DK),
            per_unit(chunks, DK, DK),
            per_unit(chunks, DK, DV),
            per_unit(chunks, CHUNK, DV),
            per_unit(DK, DV),
            pl.BlockSpec((1, length, 256), lambda h, s: (s, 0, 3 * h + 2)),
            pl.BlockSpec((1, DV), lambda h, s: (0, 0)),
        ],
        out_specs=[
            pl.BlockSpec((1, length, DV), lambda h, s: (s, 0, h)),
            pl.BlockSpec((1, length, DV), lambda h, s: (s, 0, h)),
            per_unit(chunks, DK, DV),
        ],
        out_shape=[
            jax.ShapeDtypeStruct((seqs, length, heads * DV), bf16),
            jax.ShapeDtypeStruct((seqs, length, heads * DV), f32),
            jax.ShapeDtypeStruct((seqs, heads, chunks, DK, DV), bf16),
        ],
        compiler_params=params(),
        cost_estimate=cost(4.0 * heads * seqs * chunks / 8),
        name="mixer_output",
    )(places, rows, qe, m, b, own, arriving, projected, gain)


def norm_back(places, rows, d_gated, mixer, projected, gain, qe, m, start=0, count=None):
    seqs, heads, chunks = qe.shape[:3]
    length = chunks * CHUNK
    heads = count or heads
    return pl.pallas_call(
        norm_back_kernel,
        grid=(heads, seqs),
        in_specs=[
            smem(),
            per_unit(2 * chunks, CHUNK, start=start),
            pl.BlockSpec((1, length, DV), lambda h, s: (s, 0, h + start)),
            pl.BlockSpec((1, length, DV), lambda h, s: (s, 0, h + start)),
            pl.BlockSpec((1, length, 256), lambda h, s: (s, 0, 3 * (h + start) + 2)),
            pl.BlockSpec((1, DV), lambda h, s: (0, 0)),
            per_unit(chunks, CHUNK, DK, start=start),
            per_unit(chunks, DK, DK, start=start),
        ],
        out_specs=[
            per_unit(chunks, CHUNK, DV),
            per_unit(length, DV),
            per_unit(chunks, DK, DV),
            per_unit(DK, DV),
            pl.BlockSpec((1, 8, DV), lambda h, s: (h, 0, 0)),
        ],
        out_shape=[
            jax.ShapeDtypeStruct((seqs, heads, chunks, CHUNK, DV), bf16),
            jax.ShapeDtypeStruct((seqs, heads, length, DV), bf16),
            jax.ShapeDtypeStruct((seqs, heads, chunks, DK, DV), f32),
            jax.ShapeDtypeStruct((seqs, heads, DK, DV), f32),
            jax.ShapeDtypeStruct((heads, 8, DV), f32),
        ],
        compiler_params=params(),
        cost_estimate=cost(4.0 * heads * seqs * chunks / 8),
        name="norm_back",
    )(places, rows, d_gated, mixer, projected, gain, qe, m)


def mixer_grads(
    places, projected, halo, logits, taps, rates, biases, q, k, v, rows, t, w, u, m, states, d_out, n, arriving, d_og,
    start=0, count=None,
):
    seqs, length, _ = projected.shape
    heads = count or rates.shape[0]
    chunks = length // CHUNK
    return pl.pallas_call(
        functools.partial(grad_kernel, start),
        grid=(heads, seqs),
        in_specs=input_specs(length, start)
        + [
            per_unit(length, DK, start=start),
            per_unit(length, DK, start=start),
            per_unit(length, DV, start=start),
            per_unit(2 * chunks, CHUNK, start=start),
            per_unit(chunks, CHUNK, CHUNK, start=start),
            per_unit(chunks, CHUNK, DK, start=start),
            per_unit(chunks, CHUNK, DV, start=start),
            per_unit(chunks, DK, DK, start=start),
            per_unit(chunks, DK, DV, start=start),
            per_unit(chunks, CHUNK, DV, start=start),
            per_unit(chunks, DK, DV, start=start),
            per_unit(DK, DV, start=start),
            per_unit(length, DV, start=start),
        ],
        out_specs=[
            pl.BlockSpec((1, length, HEAD), lambda h, s: (s, 0, h)),
            per_unit(ROWS, QKV),
            per_unit(ROWS, QKV),
            pl.BlockSpec((1, 2, chunks, CHUNK), lambda h, s: (s, h, 0, 0)),
            per_unit(chunks, CHUNK),
            pl.BlockSpec((1, 8, QKV), lambda h, s: (h, 0, 0)),
        ],
        out_shape=[
            jax.ShapeDtypeStruct((seqs, length, heads * HEAD), bf16),
            jax.ShapeDtypeStruct((seqs, heads, ROWS, QKV), f32),
            jax.ShapeDtypeStruct((seqs, heads, ROWS, QKV), f32),
            jax.ShapeDtypeStruct((seqs, 2 * heads, chunks, CHUNK), f32),
            jax.ShapeDtypeStruct((seqs, heads, chunks, CHUNK), f32),
            jax.ShapeDtypeStruct((heads, 8, QKV), f32),
        ],
        scratch_shapes=[
            pltpu.VMEM((length + ROWS, QKV), f32),
            pltpu.VMEM((length + 2 * ROWS, QKV), f32),
        ],
        compiler_params=params(),
        cost_estimate=cost(10.0 * heads * seqs * chunks / 8),
        name="mixer_grads",
    )(
        places, rates, biases, projected, projected, halo, halo, logits, taps, taps,
        q, k, v, rows, t, w, u, m, states, d_out, n, arriving, d_og,
    )


def shifted(block, axis, distance):
    devices = range(lax.axis_size(axis))
    route = [(i - distance, i) for i in devices if i - distance in devices]
    return lax.ppermute(block, axis, route)


def relay(first, maps, distance):
    arriving = shifted(first.astype(bf16), "ctx", distance)
    for _ in range(lax.axis_size("ctx") - 2):
        leaving = first + maps(arriving.astype(f32))
        arriving = shifted(leaving.astype(bf16), "ctx", distance)
    return arriving


def dot(left, right, contract=(1, 0)):
    return lax.dot_general(
        left, right, (((contract[0],), (contract[1],)), ((), ())), preferred_element_type=f32
    )


def local(
    tokens,
    proj_in,
    proj_gates,
    conv_taps,
    log_rates,
    rate_bias,
    gate_gain,
    proj_out,
    ffn_gate,
    ffn_up,
    ffn_down,
    gain_in,
    gain_ffn,
    cotangent,
):
    seqs, length, width = tokens.shape
    row_count = seqs * length
    heads = log_rates.shape[0]
    chunks = length // CHUNK
    tp_count = lax.axis_size("tp")
    tp_place = lax.axis_index("tp")
    share = length // tp_count
    with_map = lax.axis_size("ctx") > 2

    def own(rows):
        return lax.dynamic_slice_in_dim(
            rows.reshape(seqs, length, rows.shape[-1]), tp_place * share, share, 1
        )

    def scatter_sum(partial):
        partial = partial.astype(bf16).reshape(seqs, length, width)
        return lax.psum_scatter(partial, "tp", scatter_dimension=1, tiled=True).astype(f32)

    def gather_rows(rows):
        return lax.all_gather(rows, "tp", axis=1, tiled=True).reshape(row_count, width)

    whole_in = lax.all_gather(proj_in, "shard", axis=0, tiled=True)
    whole_gates = lax.all_gather(proj_gates, "shard", axis=0, tiled=True)
    whole_out = lax.all_gather(proj_out, "shard", axis=1, tiled=True)
    whole_gate = lax.all_gather(ffn_gate, "shard", axis=0, tiled=True)
    whole_up = lax.all_gather(ffn_up, "shard", axis=0, tiled=True)
    whole_down = lax.all_gather(ffn_down, "shard", axis=1, tiled=True)
    gain_in_f = lax.all_gather(gain_in, "shard", axis=0, tiled=True).astype(f32)
    gain_ffn_f = lax.all_gather(gain_ffn, "shard", axis=0, tiled=True).astype(f32)

    inputs_f = tokens.reshape(row_count, width).astype(f32)
    scale_in = lax.rsqrt(jnp.mean(inputs_f * inputs_f, -1, keepdims=True) + epsilon)
    unit_in = inputs_f * scale_in
    normed_in = (unit_in * gain_in_f).astype(bf16)
    projected = dot(normed_in, whole_in).astype(bf16).reshape(seqs, length, heads * HEAD)
    logits = dot(whole_gates, normed_in, (0, 1)).reshape(
        2 * heads, seqs, chunks, CHUNK
    )
    logits = jnp.swapaxes(logits, 0, 1)
    halo = shifted(projected[:, length - HALO :, :], "ctx", 1)
    places = jnp.arange(chunks, dtype=jnp.int32)
    q, k, v, rows, t, w, u, qe, m, b, own_out, state_end, state_map = prepare(
        places, projected, halo, logits, conv_taps, log_rates, rate_bias, with_map
    )

    def map_forward(arriving):
        return jnp.einsum("shij,shjk->shik", state_map, arriving)

    def map_back(arriving):
        return jnp.einsum("shji,shjk->shik", state_map, arriving)

    arriving = relay(state_end, map_forward, 1)
    gain_row = gate_gain.reshape(1, DV)
    gated, mixer, states = mixer_output(
        places, (rows, qe, m, b, own_out), arriving, projected, gain_row
    )
    gated = gated.reshape(row_count, heads * DV)

    middle = own(inputs_f) + scatter_sum(dot(gated, whole_out))
    scale_mid = lax.rsqrt(jnp.mean(middle * middle, -1, keepdims=True) + epsilon)
    unit_mid = middle * scale_mid
    normed_mid = gather_rows((unit_mid * gain_ffn_f).astype(bf16))
    gate_act = dot(normed_mid, whole_gate)
    up_act = dot(normed_mid, whole_up)
    gate_sig = jax.nn.sigmoid(gate_act)
    gate_silu = gate_act * gate_sig
    hidden = (gate_silu * up_act).astype(bf16)
    d_out = cotangent.reshape(row_count, width)
    d_hidden = dot(d_out, whole_down, (1, 1))
    d_gate = (d_hidden * up_act * gate_sig * (1.0 + gate_act * (1.0 - gate_sig))).astype(bf16)
    d_up = (d_hidden * gate_silu).astype(bf16)
    d_mid_norm = scatter_sum(dot(d_gate, whole_gate, (1, 1)) + dot(d_up, whole_up, (1, 1)))
    layer_rows = middle + scatter_sum(dot(hidden, whole_down))
    grad_down = dot(hidden, d_out, (0, 0))
    grad_gate = dot(normed_mid, d_gate, (0, 0))
    grad_up = dot(normed_mid, d_up, (0, 0))
    gain_ffn_part = jnp.sum(d_mid_norm * unit_mid, (0, 1))
    scaled_mid = d_mid_norm * gain_ffn_f
    d_middle = own(cotangent).astype(f32) + scale_mid * (
        scaled_mid - unit_mid * jnp.mean(scaled_mid * unit_mid, -1, keepdims=True)
    )
    d_branch = gather_rows(d_middle.astype(bf16))
    grad_out = dot(gated, d_branch, (0, 0))
    d_gated = dot(d_branch, whole_out, (1, 1)).reshape(seqs, length, heads * DV)
    d_mixer, d_og, n, d_start, gain_gate_part = norm_back(
        places, rows, d_gated, mixer, projected, gain_row, qe, m
    )
    arriving_back = relay(d_start, map_back, -1)
    d_projected, d_halo, d_tail, d_logits, rate_rows, tap_rows = mixer_grads(
        places, projected, halo, logits, conv_taps, log_rates, rate_bias,
        q, k, v, rows, t, w, u, m, states, d_mixer, n, arriving_back, d_og,
    )
    later = shifted(d_halo, "ctx", -1)
    tail = (d_tail + later).astype(bf16)
    for h in range(heads):
        d_projected = lax.dynamic_update_slice(
            d_projected, tail[:, h], (0, length - ROWS, h * HEAD)
        )
    d_projected = d_projected.reshape(row_count, heads * HEAD)
    grad_bias = jnp.sum(d_logits[:, 0::2], (0, 2, 3))
    grad_rates = jnp.sum(rate_rows, (0, 2, 3))
    d_logit_rows = jnp.swapaxes(d_logits, 0, 1).reshape(2 * heads, row_count).astype(bf16)
    grad_in = dot(normed_in, d_projected, (0, 0))
    grad_gates = dot(normed_in, d_logit_rows, (0, 1))
    in_back = dot(d_projected, whole_in, (1, 1)) + dot(d_logit_rows, whole_gates, (0, 1))
    d_in_norm = scatter_sum(in_back)
    unit_own = own(unit_in)
    scale_own = own(scale_in)
    gain_in_part = jnp.sum(d_in_norm * unit_own, (0, 1))
    scaled_in = d_in_norm * gain_in_f
    token_grad = d_middle + scale_own * (
        scaled_in - unit_own * jnp.mean(scaled_in * unit_own, -1, keepdims=True)
    )
    gain_gate_part = jnp.sum(gain_gate_part, (0, 1))
    grad_taps = jnp.swapaxes(tap_rows[:, :CONV, :], 0, 1).reshape(CONV, heads * QKV)
    grad_gain_gate, grad_gain_in, grad_gain_ffn = lax.psum(
        (gain_gate_part, gain_in_part, gain_ffn_part), "tp"
    )

    def reduced(grad, axis):
        piece = lax.psum_scatter(
            grad.astype(bf16), ("shard", "ctx"), scatter_dimension=axis, tiled=True
        )
        return lax.all_gather(piece, "ctx", axis=axis, tiled=True).astype(f32)

    sum_taps, sum_rates, sum_bias, sum_gain_gate = lax.psum(
        (grad_taps, grad_rates, grad_bias, grad_gain_gate), ("shard", "ctx")
    )
    return (
        layer_rows.astype(bf16),
        token_grad,
        reduced(grad_in, 0),
        reduced(grad_gates, 0),
        sum_taps,
        sum_rates,
        sum_bias,
        sum_gain_gate,
        reduced(grad_out, 1),
        reduced(grad_gate, 0),
        reduced(grad_up, 0),
        reduced(grad_down, 1),
        reduced(grad_gain_in, 0),
        reduced(grad_gain_ffn, 0),
    )


def ffn_kernel(
    rows, d_rows, pair, down, hidden_out, d_pair_out, back_a, back_b, down_a, down_b
):
    units = down.shape[1]
    acts = mm(rows[...], pair[...])
    gate_act = acts[:, :units]
    up_act = acts[:, units:]
    d_hidden = mm(d_rows[...], down[...])
    sig = sigmoid(gate_act)
    swish = gate_act * sig
    hidden = (swish * up_act).astype(bf16)
    d_gate = (d_hidden * up_act * sig * (1.0 + gate_act * (1.0 - sig))).astype(bf16)
    d_up = (d_hidden * swish).astype(bf16)
    hidden_out[...] = hidden
    d_pair = jnp.concatenate([d_gate, d_up], axis=1)
    d_pair_out[...] = d_pair
    back = mm(d_pair, pair[...], (1, 1)).astype(bf16)
    through = mm(hidden, down[...], (1, 1)).astype(bf16)

    @pl.when(pl.program_id(0) == 0)
    def _():
        back_a[...] = back
        down_a[...] = through

    @pl.when(pl.program_id(0) == 1)
    def _():
        back_b[...] = back
        down_b[...] = through


def feed_forward(rows, d_rows, pair, down):
    count, width = rows.shape
    units = down.shape[1]
    tile = count // 2

    def tiled(columns):
        return pl.BlockSpec((tile, columns), lambda i: (i, 0))

    def whole(shape):
        return pl.BlockSpec(shape, lambda i: (0, 0))

    return pl.pallas_call(
        ffn_kernel,
        grid=(2,),
        in_specs=[tiled(width), tiled(width), whole(pair.shape), whole(down.shape)],
        out_specs=[tiled(units), tiled(2 * units)] + [whole((tile, width))] * 4,
        out_shape=[
            jax.ShapeDtypeStruct((count, units), bf16),
            jax.ShapeDtypeStruct((count, 2 * units), bf16),
        ]
        + [jax.ShapeDtypeStruct((tile, width), bf16)] * 4,
        compiler_params=pltpu.CompilerParams(
            dimension_semantics=("arbitrary",), vmem_limit_bytes=56 * 1024 * 1024
        ),
        cost_estimate=cost(9.0 * count / 512),
        name="feed_forward",
    )(rows, d_rows, pair, down)


def branch_back_kernel(
    places, rows, part_0, part_1, part_2, part_3, weights, mixer, og, gain, qe, m,
    d_out, d_og_out, n_out, start_out, gain_out, d_gated,
):
    count = part_0.shape[0]
    for i, part in enumerate((part_0, part_1, part_2, part_3)):
        d_gated[0, i * count : (i + 1) * count, :] = mm(part[...], weights[...])
    norm_back_kernel(
        places, rows, d_gated, mixer, og, gain, qe, m, d_out, d_og_out, n_out, start_out, gain_out
    )


def branch_back(places, rows, parts, weights, mixer, projected, gain, qe, m):
    seqs, heads, chunks = qe.shape[:3]
    length = chunks * CHUNK
    count, width = parts[0].shape
    return pl.pallas_call(
        branch_back_kernel,
        grid=(heads, seqs),
        in_specs=[
            smem(),
            per_unit(2 * chunks, CHUNK),
        ]
        + [pl.BlockSpec((count, width), lambda h, s: (0, 0))] * 4
        + [
            pl.BlockSpec((width, DV), lambda h, s: (0, h)),
            pl.BlockSpec((1, length, DV), lambda h, s: (s, 0, h)),
            pl.BlockSpec((1, length, 256), lambda h, s: (s, 0, 3 * h + 2)),
            pl.BlockSpec((1, DV), lambda h, s: (0, 0)),
            per_unit(chunks, CHUNK, DK),
            per_unit(chunks, DK, DK),
        ],
        out_specs=[
            per_unit(chunks, CHUNK, DV),
            per_unit(length, DV),
            per_unit(chunks, DK, DV),
            per_unit(DK, DV),
            pl.BlockSpec((1, 8, DV), lambda h, s: (h, 0, 0)),
        ],
        out_shape=[
            jax.ShapeDtypeStruct((seqs, heads, chunks, CHUNK, DV), bf16),
            jax.ShapeDtypeStruct((seqs, heads, length, DV), bf16),
            jax.ShapeDtypeStruct((seqs, heads, chunks, DK, DV), f32),
            jax.ShapeDtypeStruct((seqs, heads, DK, DV), f32),
            jax.ShapeDtypeStruct((heads, 8, DV), f32),
        ],
        scratch_shapes=[pltpu.VMEM((1, length, DV), f32)],
        compiler_params=params(),
        cost_estimate=cost(5.0 * heads),
        name="branch_back",
    )(places, rows, *parts, weights, mixer, projected, gain, qe, m)


def widened(block):
    return jnp.pad(block, ((0, 0), (0, -block.shape[1] % 128)))


def local_paired(
    tokens,
    proj_in,
    proj_gates,
    conv_taps,
    log_rates,
    rate_bias,
    gate_gain,
    proj_out,
    ffn_gate,
    ffn_up,
    ffn_down,
    gain_in,
    gain_ffn,
    cotangent,
):
    seqs, length, width = tokens.shape
    heads = log_rates.shape[0]
    units = ffn_gate.shape[1]
    core = lax.axis_index("ctx")
    place = lax.axis_index("tp")
    shard = lax.axis_index("shard")
    tp_count = lax.axis_size("tp")
    shards = lax.axis_size("shard")
    seq = place // 2
    half = place % 2
    quarter = length // 2
    share = length // tp_count
    full = 2 * length
    chunks = full // CHUNK
    route = []
    for j in range(tp_count):
        route.append((j, (j % 2) * tp_count + j // 2))
        route.append((tp_count + j, (j % 2) * tp_count + 2 + j // 2))
    route_back = [(b, a) for a, b in route]
    pairs = [(i, i ^ 1) for i in range(tp_count)]
    pairs_x = [(i, i ^ 1) for i in range(shards)]
    pairs_y = [(i, i ^ 2) for i in range(shards)]
    odd_x = shard % 2 == 1
    odd_y = shard // 2 == 1

    def hold(*values):
        return lax.optimization_barrier(values)

    def swap_core(block):
        with jax.named_scope("swap_core"):
            return lax.ppermute(block, "ctx", [(0, 1), (1, 0)])

    def swap_chip(block):
        with jax.named_scope("swap_chip"):
            return lax.ppermute(block, "tp", pairs)

    def swap_x(block):
        with jax.named_scope("swap_x"):
            return lax.ppermute(block, "shard", pairs_x)

    def swap_y(block):
        with jax.named_scope("swap_y"):
            return lax.ppermute(block, "shard", pairs_y)

    def to_users(block):
        with jax.named_scope("to_users"):
            return lax.ppermute(block, ("ctx", "tp"), route)

    def to_owners(block):
        with jax.named_scope("to_owners"):
            return lax.ppermute(block, ("ctx", "tp"), route_back)

    def both_cores(block):
        return block.astype(f32) + swap_core(block).astype(f32)

    def add(kept, got):
        return (kept.astype(f32) + got.astype(f32)).astype(bf16)

    def group_rows(mine, got):
        return jnp.concatenate(
            [mine[:quarter], got[:quarter], mine[quarter:], got[quarter:]], axis=0
        )

    def own_rows(rows):
        sequence = lax.dynamic_index_in_dim(rows, seq, 0, keepdims=False)
        mine = lax.dynamic_slice_in_dim(sequence, half * quarter, quarter, 0)
        other = lax.dynamic_slice_in_dim(sequence, (1 - half) * quarter, quarter, 0)
        return jnp.concatenate([mine, other], axis=0)

    def swap_sides(mine):
        return swap_x(mine), swap_y(mine)

    def swap_fourth(from_x, from_y):
        count = from_x.shape[0] // 2
        return swap_x(from_y[:count]), swap_y(from_x[count:])

    def ordered(odd, mine, theirs):
        return jnp.concatenate([jnp.where(odd, theirs, mine), jnp.where(odd, mine, theirs)], axis=0)

    def assembled(mine, sides, fourth):
        across = jnp.concatenate(fourth, axis=0)
        return ordered(
            odd_y, ordered(odd_x, mine, sides[0]), ordered(odd_x, sides[1], across)
        )

    def blocks(grad, *places_xor):
        rows = grad.shape[0] // shards
        return jnp.concatenate(
            [lax.dynamic_slice_in_dim(grad, (shard ^ p) * rows, rows, 0) for p in places_xor],
            axis=0,
        )

    def scatter_first(grad):
        cut = grad.shape[1] // 256 * 128
        left, right = grad[:, :cut], grad[:, cut:]
        return (
            blocks(left, 0, 2),
            swap_x(blocks(left, 1, 3)),
            blocks(right, 0, 1),
            swap_y(blocks(right, 2, 3)),
        )

    def scatter_second(left, left_got, right, right_got):
        rows = left.shape[0] // 2
        left = add(left, left_got)
        right = add(right, right_got)
        return left[:rows], swap_y(left[rows:]), right[:rows], swap_x(right[rows:])

    def scatter_end(left, left_got, right, right_got):
        return jnp.concatenate([add(left, left_got), add(right, right_got)], axis=1)

    def quarters(rows, weights, contract, extra=None):
        out = []
        for i in (3, 2, 1, 0):
            span = slice(i * quarter, (i + 1) * quarter)
            out.append(sum(dot(r[span], w, contract) for r, w in zip(rows, weights)))
        return out

    small = jnp.concatenate(
        [
            conv_taps.astype(f32),
            jnp.pad(jnp.stack([log_rates, rate_bias]), ((0, 2), (0, conv_taps.shape[1] - heads))),
        ],
        axis=0,
    )
    mine_in = to_users(jnp.concatenate([proj_in, widened(proj_gates)], axis=1))
    mine_rows = own_rows(tokens)
    got_rows = swap_core(mine_rows)
    gains = lax.all_gather(jnp.stack([gain_in, gain_ffn]), "shard", axis=1, tiled=True)
    mine_d = own_rows(cotangent)
    got_d = swap_core(mine_d)
    mine_pair = jnp.concatenate([widened(ffn_gate), widened(ffn_up)], axis=1)
    mine_down = widened(ffn_down.T)
    (
        mine_in, mine_rows, got_rows, gains, mine_d, got_d, small, mine_out, mine_pair, mine_down,
    ) = hold(
        mine_in, mine_rows, got_rows, gains, mine_d, got_d, small, proj_out.T, mine_pair, mine_down,
    )
    in_sides = swap_sides(mine_in)
    small = to_users(small)
    mine_out = to_users(mine_out)
    gains = gains.astype(f32)
    gain_in_f, gain_ffn_f = gains[0:1], gains[1:2]
    inputs_f = group_rows(mine_rows, got_rows).astype(f32)
    scale_in = lax.rsqrt(jnp.mean(inputs_f * inputs_f, -1, keepdims=True) + epsilon)
    normed_in = (inputs_f * scale_in * gain_in_f).astype(bf16)
    d_out = group_rows(mine_d, got_d)
    in_sides, small, mine_out, normed_in, d_out, mine_pair = hold(
        in_sides, small, mine_out, normed_in, d_out, mine_pair
    )
    in_fourth = swap_fourth(*in_sides)
    mine_pair = to_users(mine_pair)
    whole_out = lax.all_gather(mine_out, "shard", axis=0, tiled=True)
    in_fourth, mine_down = hold(in_fourth, mine_down)
    inner = heads * HEAD
    weights_in = assembled(mine_in, in_sides, in_fourth)
    whole_in = weights_in[:, :inner]
    whole_gates = weights_in[:, inner : inner + 2 * heads]
    projected = dot(normed_in, whole_in).astype(bf16).reshape(1, full, inner)
    logits = dot(whole_gates, normed_in, (0, 1)).reshape(1, 2 * heads, chunks, CHUNK)
    projected, logits, mine_pair, mine_down = hold(projected, logits, mine_pair, mine_down)
    whole_pair = lax.all_gather(mine_pair, "shard", axis=0, tiled=True)
    mine_down = to_users(mine_down)

    taps = small[:CONV]
    log_rates_here, rate_bias_here = small[CONV, :heads], small[CONV + 1, :heads]
    halo = jnp.zeros((1, HALO, inner), bf16)
    chunk = jnp.arange(chunks, dtype=jnp.int32)
    per_quarter = quarter // CHUNK
    true_quarter = chunk // per_quarter
    places = (
        2 * ((true_quarter % 2) ^ half) + ((true_quarter // 2) ^ core)
    ) * per_quarter + chunk % per_quarter
    no_state = jnp.zeros((1, heads, DK, DV), f32)
    gain_row = gate_gain.reshape(1, DV)
    source = (projected, halo, logits, taps, log_rates_here, rate_bias_here)
    q, k, v, rows, t, w, u, qe, m, b, own_out, _, _ = prepare(places, *source, False)
    own_out, mine_down = hold(own_out, mine_down)
    down_sides = swap_sides(mine_down)
    gated, mixer, states = mixer_output(
        places, (rows, qe, m, b, own_out), no_state, projected, gain_row
    )
    gated = gated.reshape(full, heads * DV)
    far_b, far_a, near_b, near_a = quarters([gated], [whole_out], (1, 1))
    far_got = swap_core(far_b.astype(bf16))
    near_got = swap_core(near_b.astype(bf16))
    far_sum, near_a, near_got, down_sides = hold(
        add(far_a, far_got), near_a, near_got, down_sides
    )
    far_sum = swap_chip(far_sum)
    down_fourth = swap_fourth(*down_sides)
    far_sum, near_a, near_got, down_fourth = hold(far_sum, near_a, near_got, down_fourth)
    middle = inputs_f[:quarter] + (near_a + near_got.astype(f32) + far_sum.astype(f32))
    scale_mid = lax.rsqrt(jnp.mean(middle * middle, -1, keepdims=True) + epsilon)
    unit_mid = middle * scale_mid

    mine_mid = (unit_mid * gain_ffn_f).astype(bf16)
    far_mid = swap_chip(mine_mid)
    near_mid = jnp.concatenate([mine_mid, swap_core(mine_mid)], axis=0)
    whole_down = assembled(mine_down, down_sides, down_fourth)
    near_hidden, near_d_pair, near_a, near_b, near_down_a, near_down_b = feed_forward(
        near_mid, d_out[:length], whole_pair, whole_down
    )
    far_mid, near_b = hold(far_mid, near_b)
    far_mid = jnp.concatenate([far_mid, swap_core(far_mid)], axis=0)
    near_got = swap_core(near_b)
    far_hidden, far_d_pair, far_a, far_b, far_down_a, far_down_b = feed_forward(
        far_mid, d_out[length:], whole_pair, whole_down
    )
    far_got = swap_core(far_b)
    normed_mid = jnp.concatenate([near_mid, far_mid], axis=0)
    hidden = jnp.concatenate([near_hidden, far_hidden], axis=0)
    d_pair = jnp.concatenate([near_d_pair, far_d_pair], axis=0)
    far_sum, near_got, normed_mid, hidden, d_pair = hold(
        add(far_a, far_got), near_got, normed_mid, hidden, d_pair
    )
    far_sum = swap_chip(far_sum)
    far_down_got = swap_core(far_down_b)
    near_down_got = swap_core(near_down_b)
    grad_pair = dot(normed_mid, d_pair, (0, 0)).astype(bf16)
    grad_down = dot(d_out, hidden, (0, 0)).astype(bf16)
    far_sum, grad_pair, grad_down, far_down_got, near_down_got = hold(
        far_sum, grad_pair, grad_down, far_down_got, near_down_got
    )
    piece_pair = lax.psum_scatter(grad_pair, "shard", scatter_dimension=0, tiled=True)
    d_mid_norm = near_a.astype(f32) + near_got.astype(f32) + far_sum.astype(f32)
    scaled_mid = d_mid_norm * gain_ffn_f
    d_middle = d_out[:quarter].astype(f32) + scale_mid * (
        scaled_mid - unit_mid * jnp.mean(scaled_mid * unit_mid, -1, keepdims=True)
    )
    d_low = d_middle.astype(bf16)
    far_low = swap_chip(d_low)
    near_low = swap_core(d_low)
    steps_down = scatter_first(grad_down)
    far_low, near_low, steps_down = hold(far_low, near_low, steps_down)
    d_parts = (d_low, near_low, far_low, swap_core(far_low))

    far_down_sum = swap_chip(add(far_down_a, far_down_got))
    steps_down = scatter_second(*steps_down)
    d_mixer, d_og, n, _, gain_gate_part = branch_back(
        places, rows, d_parts, whole_out, mixer, projected, gain_row, qe, m
    )
    far_down_sum, steps_down, d_mixer, gated = hold(far_down_sum, steps_down, d_mixer, gated)

    def head_grads(h, d_mixer):
        d_projected, _, _, d_logits, rate_rows, tap_rows = mixer_grads(
            places, *source, q, k, v, rows, t, w, u, m, states, d_mixer, n, no_state, d_og,
            start=h, count=1,
        )
        return d_projected.reshape(full, HEAD), d_logits.reshape(2, full), rate_rows, tap_rows

    piece_down = to_owners(scatter_end(*steps_down))
    rows_first, logits_first, rate_first, taps_first = head_grads(0, d_mixer)
    grad_first = dot(normed_in, rows_first, (0, 0)).astype(bf16)
    grad_out = dot(jnp.concatenate(d_parts, axis=0), gated, (0, 0)).astype(bf16)
    grad_first, grad_out, piece_pair, piece_down, d_mixer = hold(
        grad_first, grad_out, piece_pair, piece_down, d_mixer
    )
    steps = scatter_first(grad_first)
    owned_pair = to_owners(piece_pair)
    piece_out = lax.psum_scatter(grad_out, "shard", scatter_dimension=0, tiled=True)
    rows_last, logits_last, rate_last, taps_last = head_grads(1, d_mixer)
    steps, rows_last = hold(steps, rows_last)

    steps_first = scatter_second(*steps)
    grad_last = dot(normed_in, rows_last, (0, 0)).astype(bf16)
    steps_first, grad_last, rows_last, logits_last = hold(
        steps_first, grad_last, rows_last, logits_last
    )
    steps_last = scatter_first(grad_last)
    piece_first = to_owners(scatter_end(*steps_first))
    d_logit_rows = jnp.concatenate([logits_first, logits_last], axis=0).astype(bf16)
    in_rows = [rows_first, rows_last]
    in_weights = [whole_in[:, :HEAD], whole_in[:, HEAD:]]

    def gates_back(i):
        return dot(d_logit_rows[:, i * quarter : (i + 1) * quarter], whole_gates, (0, 1))

    far_b, far_a, near_b, near_a = quarters(in_rows, in_weights, (1, 1))
    far_got = swap_core((far_b + gates_back(3)).astype(bf16))
    far_sum = far_a + gates_back(2)
    steps_last, far_sum, far_got, near_b, near_a = hold(
        steps_last, far_sum, far_got, near_b, near_a
    )
    steps_last = scatter_second(*steps_last)
    far_sum = swap_chip(add(far_sum, far_got))
    near_got = swap_core((near_b + gates_back(1)).astype(bf16))
    near_a = near_a + gates_back(0)
    layer_rows = (
        middle
        + near_down_a.astype(f32)
        + near_down_got.astype(f32)
        + far_down_sum.astype(f32)
    ).astype(bf16)

    grad_gates = dot(d_logit_rows, normed_in)
    part_in = jnp.sum(whole_in[:, :HEAD].astype(f32) * grad_first.astype(f32), 1)
    part_in = part_in + jnp.sum(whole_in[:, HEAD:].astype(f32) * grad_last.astype(f32), 1)
    part_in = part_in + jnp.sum(whole_gates.astype(f32) * grad_gates.T, 1)
    tap_count = CONV * heads * QKV
    sizes = [tap_count, DV, width, 2 * heads * width, 2 * heads]
    packed = jnp.concatenate(
        [
            jnp.concatenate([taps_first[0, :CONV], taps_last[0, :CONV]], axis=1).reshape(tap_count),
            jnp.sum(gain_gate_part, (0, 1)),
            part_in,
            grad_gates.reshape(2 * heads * width),
            jnp.stack(
                [
                    jnp.sum(rate_first),
                    jnp.sum(rate_last),
                    jnp.sum(logits_first[0]),
                    jnp.sum(logits_last[0]),
                ]
            ),
        ]
    )
    packed = jnp.pad(packed, (0, -packed.shape[0] % 1024)).reshape(-1, 128)
    packed = packed + swap_x(packed)
    steps_last, far_sum, near_got, near_a, packed, piece_first = hold(
        steps_last, far_sum, near_got, near_a, packed, piece_first
    )
    piece_last = to_owners(scatter_end(*steps_last))
    d_in_norm = near_a + near_got.astype(f32) + far_sum.astype(f32)
    unit_in = (inputs_f * scale_in)[:quarter]
    scaled_in = d_in_norm * gain_in_f
    token_rows = d_middle + scale_in[:quarter] * (
        scaled_in - unit_in * jnp.mean(scaled_in * unit_in, -1, keepdims=True)
    )

    even = half == 0
    first = seq == 0
    send_a = [(0, 0), (1, 2), (2, 1), (3, 3)]
    send_b = [(0, 1), (1, 3), (2, 0), (3, 2)]

    def to_outputs(mine):
        low, high = mine[:share], mine[share:]
        with jax.named_scope("to_outputs"):
            got_a = lax.ppermute(jnp.where(first, low, high), "tp", send_a)
            got_b = lax.ppermute(jnp.where(first, high, low), "tp", send_b)
        return got_a, got_b

    def stacked(got_a, got_b):
        return jnp.stack([jnp.where(even, got_a, got_b), jnp.where(even, got_b, got_a)])

    token_got = to_outputs(token_rows.astype(bf16))
    packed = packed + swap_y(packed)
    owned_out = to_owners(piece_out)
    sum_pair = both_cores(owned_pair)
    sum_down = both_cores(piece_down)[:, :units].T
    sum_first = both_cores(piece_first)
    layer_got = to_outputs(layer_rows)
    packed = both_cores(to_owners(packed)).reshape(-1)
    sum_out = both_cores(owned_out).T
    sum_last = both_cores(piece_last)

    sum_gate = sum_pair[:, :units]
    sum_up = sum_pair[:, sum_pair.shape[1] // 2 :][:, :units]
    part_ffn = jnp.sum(ffn_gate.astype(f32) * sum_gate + ffn_up.astype(f32) * sum_up, 1)
    starts = [sum(sizes[:i]) for i in range(len(sizes))]
    sum_taps, sum_gain, part_in, sum_gates, sum_rates = (
        packed[start : start + size] for start, size in zip(starts, sizes)
    )
    rows_here = gain_in.shape[0]

    def own_block(rows_of):
        return lax.dynamic_slice_in_dim(rows_of, shard * rows_here, rows_here, -1)

    over_blocks = jnp.concatenate([sum_gain, own_block(part_in), part_ffn])
    over_blocks = jnp.pad(over_blocks, (0, -over_blocks.shape[0] % 1024)).reshape(-1, 128)
    over_blocks = over_blocks + swap_chip(over_blocks)
    with jax.named_scope("swap_pair"):
        other_pair = lax.ppermute(over_blocks, "tp", [(i, i ^ 2) for i in range(tp_count)])
    over_blocks = (over_blocks + other_pair).reshape(-1)
    return (
        stacked(*layer_got),
        stacked(*token_got).astype(f32),
        jnp.concatenate([sum_first, sum_last], axis=1),
        own_block(sum_gates.reshape(2 * heads, width)).T,
        sum_taps.reshape(CONV, heads * QKV),
        sum_rates[:heads],
        sum_rates[heads:],
        over_blocks[:DV],
        sum_out,
        sum_gate,
        sum_up,
        sum_down,
        over_blocks[DV : DV + rows_here] / gain_in.astype(f32),
        over_blocks[DV + rows_here : DV + 2 * rows_here] / gain_ffn.astype(f32),
    )


def solution(mesh):
    placed = (
        P("shard", "ctx", None),
        P("shard", "tp"),
        P("shard", "tp"),
        P(None, "tp"),
        P("tp"),
        P("tp"),
        P(),
        P("tp", "shard"),
        P("shard", "tp"),
        P("shard", "tp"),
        P("tp", "shard"),
        P("shard"),
        P("shard"),
        P("shard", "ctx", None),
    )
    shape = dict(mesh.shape)
    paired = (shape["shard"], shape["ctx"], shape["tp"]) == (4, 2, 4)

    def body(*arrays):
        seqs, length, _ = arrays[0].shape
        heads = arrays[4].shape[0]
        if paired and seqs == 2 and heads == 2 and length % (2 * CHUNK) == 0:
            return local_paired(*arrays)
        return local(*arrays)

    return jax.shard_map(
        body,
        mesh=mesh,
        in_specs=placed,
        out_specs=(
            P("shard", ("ctx", "tp"), None),
            P("shard", ("ctx", "tp"), None),
            P("shard", "tp"),
            P("shard", "tp"),
            P(None, "tp"),
            P("tp"),
            P("tp"),
            P(),
            P("tp", "shard"),
            P("shard", "tp"),
            P("shard", "tp"),
            P("tp", "shard"),
            P("shard"),
            P("shard"),
        ),
        check_vma=False,
    )
```

```python
import functools

import jax
import jax.numpy as jnp
from jax import lax
from jax.experimental import pallas as pl
from jax.experimental.pallas import tpu as pltpu
from jax.sharding import PartitionSpec as P

DK = 128
DV = 256
QKV = 2 * DK + DV
HEAD = QKV + DV
CONV = 4
CHUNK = 128
HALO = 16
ROWS = 8

epsilon = 1e-06
f32 = jnp.float32
bf16 = jnp.bfloat16


def mm(left, right, contract=(1, 0)):
    return lax.dot_general(
        left.astype(bf16),
        right.astype(bf16),
        (((contract[0],), (contract[1],)), ((), ())),
        preferred_element_type=f32,
    )


def mm_split(left, right):
    left_hi = left.astype(bf16)
    right_hi = right.astype(bf16)
    left_lo = left - left_hi.astype(f32)
    right_lo = right - right_hi.astype(f32)
    return mm(left_hi, right_hi) + (mm(left_hi, right_lo) + mm(left_lo, right_hi))


def mm_exact(left, right):
    return lax.dot_general(
        left,
        right,
        (((1,), (0,)), ((), ())),
        precision=lax.Precision.HIGHEST,
        preferred_element_type=f32,
    )


def iotas():
    row = lax.broadcasted_iota(jnp.int32, (CHUNK, CHUNK), 0)
    col = lax.broadcasted_iota(jnp.int32, (CHUNK, CHUNK), 1)
    return row, col


def pad_rows(block):
    missing = CHUNK - block.shape[0]
    return jnp.concatenate([block, jnp.zeros((missing, block.shape[1]), f32)], axis=0)


def softplus(values):
    return jnp.maximum(values, 0.0) + jnp.log1p(jnp.exp(-jnp.abs(values)))


def sigmoid(values):
    return 1.0 / (1.0 + jnp.exp(-values))


def place_of(places, c):
    return pl.ds(pl.multiple_of(places[c] * CHUNK, CHUNK), CHUNK)


def chunk_rows(places, logit_ref, chunks):
    def stacked(row):
        return jnp.concatenate(
            [logit_ref[0, row, pl.ds(places[c], 1), :] for c in range(chunks)], axis=0
        )

    return stacked(0), stacked(1)


def invert_units(lowers, row, col):
    eye = (row == col).astype(f32)
    same = (row // 16) == (col // 16)
    powers = [jnp.where(same, n, 0.0) for n in lowers]
    inverses = [eye - p for p in powers]
    for _ in range(3):
        powers = [mm_split(p, p) for p in powers]
        inverses = [x + mm_split(x, p) for x, p in zip(inverses, powers)]
    size = 16
    while size < CHUNK:
        joins = ((row // (2 * size)) == (col // (2 * size))) & ((row // size) != (col // size))
        middles = [mm_split(jnp.where(joins, n, 0.0), x) for n, x in zip(lowers, inverses)]
        inverses = [x - mm_split(x, m) for x, m in zip(inverses, middles)]
        size *= 2
    return inverses


def conv_into(places, scratch, x_qk, x_v, halo_qk, halo_v, taps_qk, taps_v, length):
    scratch[0:ROWS, 0 : 2 * DK] = halo_qk[0, HALO - ROWS :, :].astype(f32)
    scratch[0:ROWS, 2 * DK :] = halo_v[0, HALO - ROWS :, :].astype(f32)
    for c in range(length // CHUNK):
        body = slice(ROWS + c * CHUNK, ROWS + (c + 1) * CHUNK)
        scratch[body, 0 : 2 * DK] = x_qk[0, place_of(places, c), :].astype(f32)
        scratch[body, 2 * DK :] = x_v[0, place_of(places, c), :].astype(f32)
    taps = jnp.concatenate([taps_qk[...], taps_v[...]], axis=1).astype(f32)
    first = ROWS - CONV + 1
    mixed = taps[0:1, :] * scratch[first : first + length, :]
    for j in range(1, CONV):
        mixed = mixed + taps[j : j + 1, :] * scratch[first + j : first + j + length, :]
    return mixed, taps


def prep_kernel(
    places, rates, biases, x_qk, x_v, halo_qk, halo_v, logits, taps_qk, taps_v,
    q_out, k_out, v_out, rows_out, t_out, w_out, u_out, qe_out, m_out, b_out, p_out, end_out, map_out,
    scratch,
):
    head = pl.program_id(0)
    length = x_qk.shape[1]
    chunks = length // CHUNK
    mixed, _ = conv_into(
        places, scratch, x_qk, x_v, halo_qk, halo_v, taps_qk, taps_v, length
    )
    active = mixed * sigmoid(mixed)
    q_act = active[:, :DK]
    k_act = active[:, DK : 2 * DK]
    q_all = (
        q_act * lax.rsqrt(jnp.sum(q_act * q_act, -1, keepdims=True) + epsilon) * DK ** (-0.5)
    ).astype(bf16)
    k_all = (
        k_act * lax.rsqrt(jnp.sum(k_act * k_act, -1, keepdims=True) + epsilon)
    ).astype(bf16)
    v_all = active[:, 2 * DK :].astype(bf16)
    q_out[0, 0] = q_all
    k_out[0, 0] = k_all
    v_out[0, 0] = v_all
    decay_logit, strength_logit = chunk_rows(places, logits, chunks)
    decay = -jnp.exp(rates[head]) * softplus(decay_logit + biases[head])
    row, col = iotas()
    lower = row >= col
    strict = row > col
    total = mm_exact(pad_rows(decay)[: max(8, chunks)], (row <= col).astype(f32))[:chunks]
    strength = sigmoid(strength_logit)
    stacked = jnp.concatenate([total, strength], axis=0)
    rows_out[0, 0] = stacked
    columns = jnp.transpose(pad_rows(stacked))
    units = range(chunks)
    span = [slice(c * CHUNK, (c + 1) * CHUNK) for c in units]
    g_col = [columns[:, c : c + 1] for c in units]
    b_col = [columns[:, chunks + c : chunks + c + 1] for c in units]
    table = [
        jnp.where(lower, jnp.exp(jnp.where(lower, g_col[c] - total[c : c + 1, :], 0.0)), 0.0)
        for c in units
    ]
    q = [q_all[s] for s in span]
    k = [k_all[s] for s in span]
    gram = [mm(k[c], k[c], (1, 1)) for c in units]
    score = [mm(q[c], k[c], (1, 1)) * table[c] for c in units]
    lowers = [jnp.where(strict, b_col[c] * gram[c] * table[c], 0.0) for c in units]
    inverse = invert_units(lowers, row, col)
    grown = [jnp.exp(g_col[c]) for c in units]
    w = [mm(inverse[c], (b_col[c] * grown[c]) * k[c].astype(f32)) for c in units]
    u = [mm(inverse[c], b_col[c] * v_all[span[c]].astype(f32)) for c in units]
    qe = [grown[c] * q[c].astype(f32) - mm(score[c], w[c]) for c in units]
    own = [mm(score[c], u[c]) for c in units]
    last = [g_col[c][CHUNK - 1 :, :] for c in units]
    k_late = [jnp.exp(last[c] - g_col[c]) * k[c].astype(f32) for c in units]
    m = [-mm(k_late[c], w[c], (0, 0)) for c in units]
    b = [mm(k_late[c], u[c], (0, 0)) for c in units]
    state = b[0]
    for c in units:
        t_out[0, 0, c] = inverse[c].astype(bf16)
        w_out[0, 0, c] = w[c].astype(bf16)
        u_out[0, 0, c] = u[c]
        qe_out[0, 0, c] = qe[c].astype(bf16)
        m_out[0, 0, c] = m[c].astype(bf16)
        b_out[0, 0, c] = b[c]
        p_out[0, 0, c] = own[c]
        if c:
            state = jnp.exp(last[c]) * state + mm(m[c], state) + b[c]
    end_out[0, 0] = state
    if map_out is not None:
        chain = (row == col).astype(f32)
        for c in units:
            chain = jnp.exp(last[c]) * chain + mm(m[c], chain)
        map_out[0, 0] = chain


def output_kernel(
    places, rows, qe, m, b, own, arriving, og, gain,
    gated_out, mixer_out, states_out,
):
    chunks = qe.shape[2]
    last = jnp.exp(rows[0, 0][0:chunks, CHUNK - 1 :])
    state = arriving[0, 0].astype(f32)
    gain_row = gain[...].astype(f32)
    for c in range(chunks):
        s = slice(c * CHUNK, (c + 1) * CHUNK)
        states_out[0, 0, c] = state.astype(bf16)
        out = mm(qe[0, 0, c], state) + own[0, 0, c]
        mixer_out[0, s, :] = out
        scale = lax.rsqrt(jnp.mean(out * out, -1, keepdims=True) + epsilon)
        gate = og[0, place_of(places, c), :].astype(f32)
        gated_out[0, place_of(places, c), :] = (out * scale * gain_row * (gate * sigmoid(gate))).astype(bf16)
        if c < chunks - 1:
            state = last[c : c + 1, :] * state + mm(m[0, 0, c], state) + b[0, 0, c]


def norm_back_kernel(
    places, rows, d_gated, mixer, og, gain, qe, m,
    d_out, d_og_out, n_out, start_out, gain_out,
):
    seq = pl.program_id(1)
    chunks = qe.shape[2]
    last = jnp.exp(rows[0, 0][0:chunks, CHUNK - 1 :])
    gain_row = gain[...].astype(f32)
    gain_sum = jnp.zeros((8, DV), f32)
    adds = []
    for c in range(chunks):
        s = slice(c * CHUNK, (c + 1) * CHUNK)
        out = mixer[0, s, :]
        gate = og[0, place_of(places, c), :].astype(f32)
        sig = sigmoid(gate)
        swish = gate * sig
        dg = d_gated[0, place_of(places, c), :].astype(f32)
        scale = lax.rsqrt(jnp.mean(out * out, -1, keepdims=True) + epsilon)
        unit = out * scale
        spread = dg * unit
        e = dg * (gain_row * swish)
        d_mix = scale * (e - unit * jnp.mean(e * unit, -1, keepdims=True))
        d_og_out[0, 0, s, :] = (spread * gain_row * (sig * (1.0 + gate * (1.0 - sig)))).astype(bf16)
        gain_sum = gain_sum + jnp.sum((spread * swish).reshape(CHUNK // 8, 8, DV), axis=0)
        d_low = d_mix.astype(bf16)
        d_out[0, 0, c] = d_low
        add = mm(qe[0, 0, c], d_low, (0, 0))
        n_out[0, 0, c] = add
        adds.append(add)
    back = adds[-1]
    for c in reversed(range(chunks - 1)):
        back = last[c : c + 1, :] * back + mm(m[0, 0, c], back, (0, 0)) + adds[c]
    start_out[0, 0] = back

    @pl.when(seq == 0)
    def _():
        gain_out[0] = gain_sum

    @pl.when(seq != 0)
    def _():
        gain_out[0] = gain_out[0] + gain_sum


def grad_kernel(
    start, places, rates, biases, x_qk, x_v, halo_qk, halo_v, logits, taps_qk, taps_v,
    q_in, k_in, v_in, rows, t_in, w_in, u_in, m_in, states, d_out, n_in, arriving, d_og,
    d_proj_out, d_halo_out, d_tail_out, d_logit_out, rate_out, taps_out,
    scratch, grads,
):
    head = pl.program_id(0) + start
    seq = pl.program_id(1)
    length = x_qk.shape[1]
    chunks = length // CHUNK
    units = range(chunks)
    row, col = iotas()
    lower = row >= col
    strict = row > col
    stacked = rows[0, 0]
    total = stacked[0:chunks]
    strength = stacked[chunks : 2 * chunks]
    columns = jnp.transpose(pad_rows(stacked))
    g_col = [columns[:, c : c + 1] for c in units]
    b_col = [columns[:, chunks + c : chunks + c + 1] for c in units]
    last = [g_col[c][CHUNK - 1 :, :] for c in units]
    ends = [None] * chunks
    back = arriving[0, 0].astype(f32)
    for c in reversed(units):
        ends[c] = back
        if c:
            back = jnp.exp(last[c]) * back + mm(m_in[0, 0, c], back, (0, 0)) + n_in[0, 0, c]
    span = [slice(c * CHUNK, (c + 1) * CHUNK) for c in units]
    table = [
        jnp.where(lower, jnp.exp(jnp.where(lower, g_col[c] - total[c : c + 1, :], 0.0)), 0.0)
        for c in units
    ]
    q = [q_in[0, 0, s, :] for s in span]
    k = [k_in[0, 0, s, :] for s in span]
    v = [v_in[0, 0, s, :] for s in span]
    k_f = [k[c].astype(f32) for c in units]
    q_f = [q[c].astype(f32) for c in units]
    t = [t_in[0, 0, c] for c in units]
    w = [w_in[0, 0, c] for c in units]
    u = [u_in[0, 0, c] for c in units]
    s_in = [states[0, 0, c] for c in units]
    d_o = [d_out[0, 0, c] for c in units]
    gram = [mm(k[c], k[c], (1, 1)) * table[c] for c in units]
    score = [mm(q[c], k[c], (1, 1)) * table[c] for c in units]
    grown = [jnp.exp(g_col[c]) for c in units]
    fade = [jnp.exp(last[c] - g_col[c]) for c in units]
    fresh = [u[c] - mm(w[c], s_in[c]) for c in units]
    k_late = [fade[c] * k_f[c] for c in units]
    d_fresh = [mm(score[c], d_o[c], (0, 0)) + mm(k_late[c], ends[c]) for c in units]
    d_score = [jnp.where(lower, mm(d_o[c], fresh[c], (1, 1)), 0.0) for c in units]
    d_q_grown = [mm(d_o[c], s_in[c], (1, 1)) for c in units]
    d_k_late = [mm(fresh[c], ends[c], (1, 1)) for c in units]
    d_w = [-mm(d_fresh[c], s_in[c], (1, 1)) for c in units]
    d_vb = [mm(t[c], d_fresh[c], (0, 0)) for c in units]
    d_kb = [mm(t[c], d_w[c], (0, 0)) for c in units]
    d_lower = [
        jnp.where(strict, -(mm(d_vb[c], u[c], (1, 1)) + mm(d_kb[c], w[c], (1, 1))), 0.0)
        for c in units
    ]
    d_score_t = [d_score[c] * table[c] for c in units]
    d_lower_b = [d_lower[c] * b_col[c] for c in units]
    d_gram = [d_lower_b[c] * table[c] for c in units]
    cols = []
    cols_b = []
    rows_g = []
    for c in units:
        s = span[c]
        paired = d_score[c] * score[c] + d_lower_b[c] * gram[c]
        late = k_late[c] * d_k_late[c]
        k_dot = grown[c] * (d_kb[c] * k_f[c])
        per_row = (
            paired + grown[c] * (q_f[c] * d_q_grown[c]) - late + b_col[c] * k_dot
        )
        cols.append(jnp.sum(per_row, -1, keepdims=True))
        v_f = v[c].astype(f32)
        v_dot = d_vb[c] * v_f
        cols_b.append(
            jnp.sum(
                d_lower[c] * gram[c] + k_dot + v_dot[:, :DK] + v_dot[:, DK:], -1, keepdims=True
            )
        )
        kept = s_in[c].astype(f32) * ends[c]
        whole = jnp.sum(
            jnp.sum(late, 0, keepdims=True)
            + jnp.exp(last[c]) * jnp.sum(kept[:, :DK] + kept[:, DK:], 0, keepdims=True),
            -1,
            keepdims=True,
        )
        rows_g.append((jnp.sum(paired, 0, keepdims=True), whole))
        d_q = mm(d_score_t[c], k[c]) + grown[c] * d_q_grown[c]
        d_k = (
            mm(d_score_t[c], q[c], (0, 0))
            + mm(d_gram[c], k[c])
            + mm(d_gram[c], k[c], (0, 0))
            + fade[c] * d_k_late[c]
            + (b_col[c] * grown[c]) * d_kb[c]
        )
        grads[ROWS + s.start : ROWS + s.stop, 0:DK] = d_q
        grads[ROWS + s.start : ROWS + s.stop, DK : 2 * DK] = d_k
        grads[ROWS + s.start : ROWS + s.stop, 2 * DK :] = b_col[c] * d_vb[c]
    wide = jnp.concatenate(
        cols + cols_b + [jnp.zeros((CHUNK, CHUNK - 2 * chunks), f32)], axis=1
    )
    tall = jnp.transpose(wide)
    d_total = tall[0:chunks] - jnp.concatenate([r for r, _ in rows_g], axis=0)
    d_strength = tall[chunks : 2 * chunks]
    d_decay = mm_exact(pad_rows(d_total)[: max(8, chunks)], lower.astype(f32))[:chunks]
    d_decay = d_decay + jnp.concatenate([w_ for _, w_ in rows_g], axis=0)
    decay_logit, _ = chunk_rows(places, logits, chunks)
    biased = decay_logit + biases[head]
    rate = jnp.exp(rates[head])
    d_logit = -d_decay * rate * sigmoid(biased)
    d_strength_logit = d_strength * strength * (1.0 - strength)
    for c in units:
        d_logit_out[0, 0, pl.ds(places[c], 1), :] = d_logit[c : c + 1, :]
        d_logit_out[0, 1, pl.ds(places[c], 1), :] = d_strength_logit[c : c + 1, :]
    rate_out[0, 0] = -d_decay * rate * softplus(biased)

    mixed, taps = conv_into(
        places, scratch, x_qk, x_v, halo_qk, halo_v, taps_qk, taps_v, length
    )
    sig = sigmoid(mixed)
    active = mixed * sig
    slope = sig * (1.0 + mixed * (1.0 - sig))

    def unnorm(act, grad, factor):
        scale = lax.rsqrt(jnp.sum(act * act, -1, keepdims=True) + epsilon)
        unit = act * scale
        return (factor * scale) * (grad - unit * jnp.sum(unit * grad, -1, keepdims=True))

    body = slice(ROWS, ROWS + length)
    grads[body, 0:DK] = (
        unnorm(active[:, :DK], grads[body, 0:DK], DK ** (-0.5)) * slope[:, :DK]
    )
    grads[body, DK : 2 * DK] = (
        unnorm(active[:, DK : 2 * DK], grads[body, DK : 2 * DK], 1.0) * slope[:, DK : 2 * DK]
    )
    grads[body, 2 * DK :] = grads[body, 2 * DK :] * slope[:, 2 * DK :]
    grads[0:ROWS, :] = jnp.zeros((ROWS, QKV), f32)
    grads[ROWS + length :, :] = jnp.zeros((ROWS, QKV), f32)
    d_x = None
    d_halo = None
    tap_rows = []
    d_conv = grads[body, :]
    first = ROWS - CONV + 1
    for j in range(CONV):
        ahead = CONV - 1 - j
        part = taps[j : j + 1, :] * grads[ROWS + ahead : ROWS + ahead + length, :]
        d_x = part if d_x is None else d_x + part
        edge = taps[j : j + 1, :] * grads[ahead : ahead + ROWS, :]
        d_halo = edge if d_halo is None else d_halo + edge
        tap_rows.append(
            jnp.sum(d_conv * scratch[first + j : first + j + length, :], 0, keepdims=True)
        )
    for c in units:
        d_proj_out[0, place_of(places, c), 0:QKV] = d_x[span[c]].astype(bf16)
        d_proj_out[0, place_of(places, c), QKV:] = d_og[0, 0, span[c], :]
    d_tail_out[0, 0] = d_x[length - ROWS :, :]
    d_halo_out[0, 0] = d_halo
    tap_rows = jnp.concatenate(tap_rows + [jnp.zeros((8 - CONV, QKV), f32)], axis=0)

    @pl.when(seq == 0)
    def _():
        taps_out[0] = tap_rows

    @pl.when(seq != 0)
    def _():
        taps_out[0] = taps_out[0] + tap_rows


def cost(micros):
    return pl.CostEstimate(
        flops=int(micros * 1e8), bytes_accessed=int(micros * 1e5), transcendentals=0
    )


def params():
    return pltpu.CompilerParams(
        dimension_semantics=("arbitrary", "arbitrary"), vmem_limit_bytes=56 * 1024 * 1024
    )


def smem():
    return pl.BlockSpec(memory_space=pltpu.SMEM)


def per_unit(*shape, start=0):
    zeros = (0,) * len(shape)
    return pl.BlockSpec((1, 1) + shape, lambda h, s: (s, h + start) + zeros)


def input_specs(length, start=0):
    return [
        smem(),
        smem(),
        smem(),
        pl.BlockSpec((1, length, 256), lambda h, s: (s, 0, 3 * (h + start))),
        pl.BlockSpec((1, length, 256), lambda h, s: (s, 0, 3 * (h + start) + 1)),
        pl.BlockSpec((1, HALO, 256), lambda h, s: (s, 0, 3 * (h + start))),
        pl.BlockSpec((1, HALO, 256), lambda h, s: (s, 0, 3 * (h + start) + 1)),
        pl.BlockSpec((1, 2, length // CHUNK, CHUNK), lambda h, s: (s, h + start, 0, 0)),
        pl.BlockSpec((CONV, 256), lambda h, s: (0, 2 * (h + start))),
        pl.BlockSpec((CONV, 256), lambda h, s: (0, 2 * (h + start) + 1)),
    ]


def prepare(places, projected, halo, logits, taps, rates, biases, with_map):
    seqs, length, _ = projected.shape
    heads = rates.shape[0]
    chunks = length // CHUNK

    def out(dtype, *shape):
        return jax.ShapeDtypeStruct((seqs, heads) + shape, dtype), per_unit(*shape)

    outs = [
        out(bf16, length, DK),
        out(bf16, length, DK),
        out(bf16, length, DV),
        out(f32, 2 * chunks, CHUNK),
        out(bf16, chunks, CHUNK, CHUNK),
        out(bf16, chunks, CHUNK, DK),
        out(f32, chunks, CHUNK, DV),
        out(bf16, chunks, CHUNK, DK),
        out(bf16, chunks, DK, DK),
        out(f32, chunks, DK, DV),
        out(f32, chunks, CHUNK, DV),
        out(f32, DK, DV),
    ]
    if with_map:
        outs.append(out(f32, DK, DK))
        kernel = prep_kernel
    else:

        def kernel(*refs):
            prep_kernel(*refs[:-1], None, refs[-1])

    results = pl.pallas_call(
        kernel,
        grid=(heads, seqs),
        in_specs=input_specs(length),
        out_specs=[spec for _, spec in outs],
        out_shape=[shape for shape, _ in outs],
        scratch_shapes=[pltpu.VMEM((length + ROWS, QKV), f32)],
        compiler_params=params(),
        cost_estimate=cost(9.0 * heads * seqs * chunks / 8),
        name="prepare",
    )(places, rates, biases, projected, projected, halo, halo, logits, taps, taps)
    return results if with_map else list(results) + [None]


def mixer_output(places, kept, arriving, projected, gain):
    rows, qe, m, b, own = kept
    seqs, heads, chunks = qe.shape[:3]
    length = chunks * CHUNK
    return pl.pallas_call(
        output_kernel,
        grid=(heads, seqs),
        in_specs=[
            smem(),
            per_unit(2 * chunks, CHUNK),
            per_unit(chunks, CHUNK, DK),
            per_unit(chunks, DK, DK),
            per_unit(chunks, DK, DV),
            per_unit(chunks, CHUNK, DV),
            per_unit(DK, DV),
            pl.BlockSpec((1, length, 256), lambda h, s: (s, 0, 3 * h + 2)),
            pl.BlockSpec((1, DV), lambda h, s: (0, 0)),
        ],
        out_specs=[
            pl.BlockSpec((1, length, DV), lambda h, s: (s, 0, h)),
            pl.BlockSpec((1, length, DV), lambda h, s: (s, 0, h)),
            per_unit(chunks, DK, DV),
        ],
        out_shape=[
            jax.ShapeDtypeStruct((seqs, length, heads * DV), bf16),
            jax.ShapeDtypeStruct((seqs, length, heads * DV), f32),
            jax.ShapeDtypeStruct((seqs, heads, chunks, DK, DV), bf16),
        ],
        compiler_params=params(),
        cost_estimate=cost(4.0 * heads * seqs * chunks / 8),
        name="mixer_output",
    )(places, rows, qe, m, b, own, arriving, projected, gain)


def norm_back(places, rows, d_gated, mixer, projected, gain, qe, m, start=0, count=None):
    seqs, heads, chunks = qe.shape[:3]
    length = chunks * CHUNK
    heads = count or heads
    return pl.pallas_call(
        norm_back_kernel,
        grid=(heads, seqs),
        in_specs=[
            smem(),
            per_unit(2 * chunks, CHUNK, start=start),
            pl.BlockSpec((1, length, DV), lambda h, s: (s, 0, h + start)),
            pl.BlockSpec((1, length, DV), lambda h, s: (s, 0, h + start)),
            pl.BlockSpec((1, length, 256), lambda h, s: (s, 0, 3 * (h + start) + 2)),
            pl.BlockSpec((1, DV), lambda h, s: (0, 0)),
            per_unit(chunks, CHUNK, DK, start=start),
            per_unit(chunks, DK, DK, start=start),
        ],
        out_specs=[
            per_unit(chunks, CHUNK, DV),
            per_unit(length, DV),
            per_unit(chunks, DK, DV),
            per_unit(DK, DV),
            pl.BlockSpec((1, 8, DV), lambda h, s: (h, 0, 0)),
        ],
        out_shape=[
            jax.ShapeDtypeStruct((seqs, heads, chunks, CHUNK, DV), bf16),
            jax.ShapeDtypeStruct((seqs, heads, length, DV), bf16),
            jax.ShapeDtypeStruct((seqs, heads, chunks, DK, DV), f32),
            jax.ShapeDtypeStruct((seqs, heads, DK, DV), f32),
            jax.ShapeDtypeStruct((heads, 8, DV), f32),
        ],
        compiler_params=params(),
        cost_estimate=cost(4.0 * heads * seqs * chunks / 8),
        name="norm_back",
    )(places, rows, d_gated, mixer, projected, gain, qe, m)


def mixer_grads(
    places, projected, halo, logits, taps, rates, biases, q, k, v, rows, t, w, u, m, states, d_out, n, arriving, d_og,
    start=0, count=None,
):
    seqs, length, _ = projected.shape
    heads = count or rates.shape[0]
    chunks = length // CHUNK
    return pl.pallas_call(
        functools.partial(grad_kernel, start),
        grid=(heads, seqs),
        in_specs=input_specs(length, start)
        + [
            per_unit(length, DK, start=start),
            per_unit(length, DK, start=start),
            per_unit(length, DV, start=start),
            per_unit(2 * chunks, CHUNK, start=start),
            per_unit(chunks, CHUNK, CHUNK, start=start),
            per_unit(chunks, CHUNK, DK, start=start),
            per_unit(chunks, CHUNK, DV, start=start),
            per_unit(chunks, DK, DK, start=start),
            per_unit(chunks, DK, DV, start=start),
            per_unit(chunks, CHUNK, DV, start=start),
            per_unit(chunks, DK, DV, start=start),
            per_unit(DK, DV, start=start),
            per_unit(length, DV, start=start),
        ],
        out_specs=[
            pl.BlockSpec((1, length, HEAD), lambda h, s: (s, 0, h)),
            per_unit(ROWS, QKV),
            per_unit(ROWS, QKV),
            pl.BlockSpec((1, 2, chunks, CHUNK), lambda h, s: (s, h, 0, 0)),
            per_unit(chunks, CHUNK),
            pl.BlockSpec((1, 8, QKV), lambda h, s: (h, 0, 0)),
        ],
        out_shape=[
            jax.ShapeDtypeStruct((seqs, length, heads * HEAD), bf16),
            jax.ShapeDtypeStruct((seqs, heads, ROWS, QKV), f32),
            jax.ShapeDtypeStruct((seqs, heads, ROWS, QKV), f32),
            jax.ShapeDtypeStruct((seqs, 2 * heads, chunks, CHUNK), f32),
            jax.ShapeDtypeStruct((seqs, heads, chunks, CHUNK), f32),
            jax.ShapeDtypeStruct((heads, 8, QKV), f32),
        ],
        scratch_shapes=[
            pltpu.VMEM((length + ROWS, QKV), f32),
            pltpu.VMEM((length + 2 * ROWS, QKV), f32),
        ],
        compiler_params=params(),
        cost_estimate=cost(10.0 * heads * seqs * chunks / 8),
        name="mixer_grads",
    )(
        places, rates, biases, projected, projected, halo, halo, logits, taps, taps,
        q, k, v, rows, t, w, u, m, states, d_out, n, arriving, d_og,
    )


def shifted(block, axis, distance):
    devices = range(lax.axis_size(axis))
    route = [(i - distance, i) for i in devices if i - distance in devices]
    return lax.ppermute(block, axis, route)


def relay(first, maps, distance):
    arriving = shifted(first.astype(bf16), "ctx", distance)
    for _ in range(lax.axis_size("ctx") - 2):
        leaving = first + maps(arriving.astype(f32))
        arriving = shifted(leaving.astype(bf16), "ctx", distance)
    return arriving


def dot(left, right, contract=(1, 0)):
    return lax.dot_general(
        left, right, (((contract[0],), (contract[1],)), ((), ())), preferred_element_type=f32
    )


def local(
    tokens,
    proj_in,
    proj_gates,
    conv_taps,
    log_rates,
    rate_bias,
    gate_gain,
    proj_out,
    ffn_gate,
    ffn_up,
    ffn_down,
    gain_in,
    gain_ffn,
    cotangent,
):
    seqs, length, width = tokens.shape
    row_count = seqs * length
    heads = log_rates.shape[0]
    chunks = length // CHUNK
    tp_count = lax.axis_size("tp")
    tp_place = lax.axis_index("tp")
    share = length // tp_count
    with_map = lax.axis_size("ctx") > 2

    def own(rows):
        return lax.dynamic_slice_in_dim(
            rows.reshape(seqs, length, rows.shape[-1]), tp_place * share, share, 1
        )

    def scatter_sum(partial):
        partial = partial.astype(bf16).reshape(seqs, length, width)
        return lax.psum_scatter(partial, "tp", scatter_dimension=1, tiled=True).astype(f32)

    def gather_rows(rows):
        return lax.all_gather(rows, "tp", axis=1, tiled=True).reshape(row_count, width)

    whole_in = lax.all_gather(proj_in, "shard", axis=0, tiled=True)
    whole_gates = lax.all_gather(proj_gates, "shard", axis=0, tiled=True)
    whole_out = lax.all_gather(proj_out, "shard", axis=1, tiled=True)
    whole_gate = lax.all_gather(ffn_gate, "shard", axis=0, tiled=True)
    whole_up = lax.all_gather(ffn_up, "shard", axis=0, tiled=True)
    whole_down = lax.all_gather(ffn_down, "shard", axis=1, tiled=True)
    gain_in_f = lax.all_gather(gain_in, "shard", axis=0, tiled=True).astype(f32)
    gain_ffn_f = lax.all_gather(gain_ffn, "shard", axis=0, tiled=True).astype(f32)

    inputs_f = tokens.reshape(row_count, width).astype(f32)
    scale_in = lax.rsqrt(jnp.mean(inputs_f * inputs_f, -1, keepdims=True) + epsilon)
    unit_in = inputs_f * scale_in
    normed_in = (unit_in * gain_in_f).astype(bf16)
    projected = dot(normed_in, whole_in).astype(bf16).reshape(seqs, length, heads * HEAD)
    logits = dot(whole_gates, normed_in, (0, 1)).reshape(
        2 * heads, seqs, chunks, CHUNK
    )
    logits = jnp.swapaxes(logits, 0, 1)
    halo = shifted(projected[:, length - HALO :, :], "ctx", 1)
    places = jnp.arange(chunks, dtype=jnp.int32)
    q, k, v, rows, t, w, u, qe, m, b, own_out, state_end, state_map = prepare(
        places, projected, halo, logits, conv_taps, log_rates, rate_bias, with_map
    )

    def map_forward(arriving):
        return jnp.einsum("shij,shjk->shik", state_map, arriving)

    def map_back(arriving):
        return jnp.einsum("shji,shjk->shik", state_map, arriving)

    arriving = relay(state_end, map_forward, 1)
    gain_row = gate_gain.reshape(1, DV)
    gated, mixer, states = mixer_output(
        places, (rows, qe, m, b, own_out), arriving, projected, gain_row
    )
    gated = gated.reshape(row_count, heads * DV)

    middle = own(inputs_f) + scatter_sum(dot(gated, whole_out))
    scale_mid = lax.rsqrt(jnp.mean(middle * middle, -1, keepdims=True) + epsilon)
    unit_mid = middle * scale_mid
    normed_mid = gather_rows((unit_mid * gain_ffn_f).astype(bf16))
    gate_act = dot(normed_mid, whole_gate)
    up_act = dot(normed_mid, whole_up)
    gate_sig = jax.nn.sigmoid(gate_act)
    gate_silu = gate_act * gate_sig
    hidden = (gate_silu * up_act).astype(bf16)
    d_out = cotangent.reshape(row_count, width)
    d_hidden = dot(d_out, whole_down, (1, 1))
    d_gate = (d_hidden * up_act * gate_sig * (1.0 + gate_act * (1.0 - gate_sig))).astype(bf16)
    d_up = (d_hidden * gate_silu).astype(bf16)
    d_mid_norm = scatter_sum(dot(d_gate, whole_gate, (1, 1)) + dot(d_up, whole_up, (1, 1)))
    layer_rows = middle + scatter_sum(dot(hidden, whole_down))
    grad_down = dot(hidden, d_out, (0, 0))
    grad_gate = dot(normed_mid, d_gate, (0, 0))
    grad_up = dot(normed_mid, d_up, (0, 0))
    gain_ffn_part = jnp.sum(d_mid_norm * unit_mid, (0, 1))
    scaled_mid = d_mid_norm * gain_ffn_f
    d_middle = own(cotangent).astype(f32) + scale_mid * (
        scaled_mid - unit_mid * jnp.mean(scaled_mid * unit_mid, -1, keepdims=True)
    )
    d_branch = gather_rows(d_middle.astype(bf16))
    grad_out = dot(gated, d_branch, (0, 0))
    d_gated = dot(d_branch, whole_out, (1, 1)).reshape(seqs, length, heads * DV)
    d_mixer, d_og, n, d_start, gain_gate_part = norm_back(
        places, rows, d_gated, mixer, projected, gain_row, qe, m
    )
    arriving_back = relay(d_start, map_back, -1)
    d_projected, d_halo, d_tail, d_logits, rate_rows, tap_rows = mixer_grads(
        places, projected, halo, logits, conv_taps, log_rates, rate_bias,
        q, k, v, rows, t, w, u, m, states, d_mixer, n, arriving_back, d_og,
    )
    later = shifted(d_halo, "ctx", -1)
    tail = (d_tail + later).astype(bf16)
    for h in range(heads):
        d_projected = lax.dynamic_update_slice(
            d_projected, tail[:, h], (0, length - ROWS, h * HEAD)
        )
    d_projected = d_projected.reshape(row_count, heads * HEAD)
    grad_bias = jnp.sum(d_logits[:, 0::2], (0, 2, 3))
    grad_rates = jnp.sum(rate_rows, (0, 2, 3))
    d_logit_rows = jnp.swapaxes(d_logits, 0, 1).reshape(2 * heads, row_count).astype(bf16)
    grad_in = dot(normed_in, d_projected, (0, 0))
    grad_gates = dot(normed_in, d_logit_rows, (0, 1))
    in_back = dot(d_projected, whole_in, (1, 1)) + dot(d_logit_rows, whole_gates, (0, 1))
    d_in_norm = scatter_sum(in_back)
    unit_own = own(unit_in)
    scale_own = own(scale_in)
    gain_in_part = jnp.sum(d_in_norm * unit_own, (0, 1))
    scaled_in = d_in_norm * gain_in_f
    token_grad = d_middle + scale_own * (
        scaled_in - unit_own * jnp.mean(scaled_in * unit_own, -1, keepdims=True)
    )
    gain_gate_part = jnp.sum(gain_gate_part, (0, 1))
    grad_taps = jnp.swapaxes(tap_rows[:, :CONV, :], 0, 1).reshape(CONV, heads * QKV)
    grad_gain_gate, grad_gain_in, grad_gain_ffn = lax.psum(
        (gain_gate_part, gain_in_part, gain_ffn_part), "tp"
    )

    def reduced(grad, axis):
        piece = lax.psum_scatter(
            grad.astype(bf16), ("shard", "ctx"), scatter_dimension=axis, tiled=True
        )
        return lax.all_gather(piece, "ctx", axis=axis, tiled=True).astype(f32)

    sum_taps, sum_rates, sum_bias, sum_gain_gate = lax.psum(
        (grad_taps, grad_rates, grad_bias, grad_gain_gate), ("shard", "ctx")
    )
    return (
        layer_rows.astype(bf16),
        token_grad,
        reduced(grad_in, 0),
        reduced(grad_gates, 0),
        sum_taps,
        sum_rates,
        sum_bias,
        sum_gain_gate,
        reduced(grad_out, 1),
        reduced(grad_gate, 0),
        reduced(grad_up, 0),
        reduced(grad_down, 1),
        reduced(grad_gain_in, 0),
        reduced(grad_gain_ffn, 0),
    )


def ffn_kernel(part_a, part_b, d_rows, weights, *refs):
    rows_out, hidden_out, d_pair_out, back_a, back_b, down_a, down_b = refs[-7:]
    units = weights.shape[1] // 3
    pair, down = weights.at[:, : 2 * units], weights.at[:, 2 * units :]
    half = part_a.shape[0]
    rows = jnp.concatenate([part_a[...], part_b[...]], axis=0)
    rows_out[...] = rows
    acts = mm(rows, pair[...])
    gate_act = acts[:, :units]
    up_act = acts[:, units:]
    d_hidden = mm(d_rows[...], down[...])
    sig = sigmoid(gate_act)
    swish = gate_act * sig
    hidden = (swish * up_act).astype(bf16)
    d_gate = (d_hidden * up_act * sig * (1.0 + gate_act * (1.0 - sig))).astype(bf16)
    d_up = (d_hidden * swish).astype(bf16)
    hidden_out[...] = hidden
    d_pair = jnp.concatenate([d_gate, d_up], axis=1)
    d_pair_out[...] = d_pair
    back = mm(d_pair, pair[...], (1, 1)).astype(bf16)
    through = mm(hidden, down[...], (1, 1)).astype(bf16)
    back_a[...] = back[:half]
    back_b[...] = back[half:]
    down_a[...] = through[:half]
    down_b[...] = through[half:]


def feed_forward(part_a, part_b, d_rows, weights, carried):
    half, width = part_a.shape
    units = weights.shape[1] // 3
    index = 1 if carried else 0

    def whole(*shape):
        return pl.BlockSpec(shape, lambda i: (0, 0))

    def placed(columns):
        return pl.BlockSpec((2 * half, columns), lambda i: (index, 0))

    return pl.pallas_call(
        ffn_kernel,
        grid=(1,),
        in_specs=[
            whole(half, width), whole(half, width), placed(width), whole(*weights.shape),
        ]
        + [pl.BlockSpec(memory_space=pl.ANY)] * len(carried),
        out_specs=[placed(width), placed(units), placed(2 * units)] + [whole(half, width)] * 4,
        out_shape=[
            jax.ShapeDtypeStruct((4 * half, columns), bf16) for columns in (width, units, 2 * units)
        ]
        + [jax.ShapeDtypeStruct((half, width), bf16)] * 4,
        input_output_aliases={4 + i: i for i in range(len(carried))},
        compiler_params=pltpu.CompilerParams(
            dimension_semantics=("arbitrary",), vmem_limit_bytes=56 * 1024 * 1024
        ),
        cost_estimate=cost(9.0),
        name="feed_forward",
    )(part_a, part_b, d_rows, weights, *carried)


def input_back_kernel(d_first, d_last, d_logits, weights, gates, *outs):
    split = d_first.shape[1]
    total = (
        mm(d_first[...], weights[:, :split], (1, 1))
        + mm(d_last[...], weights[:, split : 2 * split], (1, 1))
        + mm(d_logits[...], gates[...], (0, 0))
    ).astype(bf16)
    for i, out in enumerate(outs):

        @pl.when(pl.program_id(0) == i)
        def _(out=out):
            out[...] = total


def input_back(d_first, d_last, d_logits, weights, gates):
    full = d_first.shape[0]
    count = full // 4
    width = weights.shape[0]

    def whole(array):
        return pl.BlockSpec(array.shape, lambda i: (0, 0))

    return pl.pallas_call(
        input_back_kernel,
        grid=(4,),
        in_specs=[
            pl.BlockSpec((count, d_first.shape[1]), lambda i: (i, 0)),
            pl.BlockSpec((count, d_last.shape[1]), lambda i: (i, 0)),
            pl.BlockSpec((d_logits.shape[0], count), lambda i: (0, i)),
            whole(weights),
            whole(gates),
        ],
        out_specs=[pl.BlockSpec((count, width), lambda i: (0, 0))] * 4,
        out_shape=[jax.ShapeDtypeStruct((count, width), bf16)] * 4,
        compiler_params=pltpu.CompilerParams(
            dimension_semantics=("arbitrary",), vmem_limit_bytes=56 * 1024 * 1024
        ),
        cost_estimate=cost(5.0),
        name="input_back",
    )(d_first, d_last, d_logits, weights, gates)


def project_kernel(rows, weights, out):
    out[...] = mm(rows[...], weights[...]).astype(bf16)


def project(rows, weights):
    count, width = rows.shape
    columns = weights.shape[1]
    tile = count // 4
    return pl.pallas_call(
        project_kernel,
        grid=(4,),
        in_specs=[
            pl.BlockSpec((tile, width), lambda i: (i, 0)),
            pl.BlockSpec((width, columns), lambda i: (0, 0)),
        ],
        out_specs=pl.BlockSpec((tile, columns), lambda i: (i, 0)),
        out_shape=jax.ShapeDtypeStruct((count, columns), bf16),
        compiler_params=pltpu.CompilerParams(
            dimension_semantics=("arbitrary",), vmem_limit_bytes=56 * 1024 * 1024
        ),
        cost_estimate=cost(5.0),
        name="project",
    )(rows, weights)


def both_grads_kernel(rows, d_rows, weights, part_0, part_1, part_2, part_3, gated, out, sums):
    grad = mm(rows[...], d_rows[...], (0, 0))
    columns = jnp.sum(grad * weights[...].astype(f32), -1, keepdims=True)
    lanes = jnp.concatenate([columns, jnp.zeros((columns.shape[0], 127), f32)], axis=1)
    sums[...] = jnp.transpose(lanes)[0:8]
    branch = jnp.concatenate([part_0[...], part_1[...], part_2[...], part_3[...]], axis=0)
    out[...] = jnp.concatenate([grad, mm(branch, gated[...], (0, 0))], axis=1).astype(bf16)


def both_grads(rows, d_rows, weights, parts, gated):
    full, width = rows.shape
    columns = d_rows.shape[1]
    count = width // 4
    wide = columns + gated.shape[1]
    return pl.pallas_call(
        both_grads_kernel,
        grid=(4,),
        in_specs=[
            pl.BlockSpec((full, count), lambda i: (0, i)),
            pl.BlockSpec((full, columns), lambda i: (0, 0)),
            pl.BlockSpec((count, columns), lambda i: (i, 0)),
        ]
        + [pl.BlockSpec((parts[0].shape[0], count), lambda i: (0, i))] * 4
        + [pl.BlockSpec(gated.shape, lambda i: (0, 0))],
        out_specs=[
            pl.BlockSpec((count, wide), lambda i: (i, 0)),
            pl.BlockSpec((8, count), lambda i: (0, i)),
        ],
        out_shape=[
            jax.ShapeDtypeStruct((width, wide), bf16),
            jax.ShapeDtypeStruct((8, width), f32),
        ],
        compiler_params=pltpu.CompilerParams(
            dimension_semantics=("arbitrary",), vmem_limit_bytes=56 * 1024 * 1024
        ),
        cost_estimate=cost(8.0),
        name="both_grads",
    )(rows, d_rows, weights, *parts, gated)


def input_grad_kernel(
    shard, rows, d_rows, weights, left_a, left_b, left_send, right_a, right_b, right_send, part
):
    grad = mm(rows[...], d_rows[...], (0, 0))
    sums = jnp.sum(grad * weights[...].astype(f32), -1, keepdims=True)
    lanes = jnp.concatenate([sums, jnp.zeros((sums.shape[0], 127), f32)], axis=1)
    part[...] = jnp.transpose(lanes)[0:8]
    low = grad.astype(bf16)
    count = low.shape[0]
    cut = left_a.shape[1]
    left, right = low[:, :cut], low[:, cut:]
    step = pl.program_id(0)

    @pl.when(step == 0)
    def _():
        left_a[...] = left
        right_a[...] = right

    @pl.when(step == 1)
    def _():
        left_send[:count] = left
        right_b[...] = right

    @pl.when(step == 2)
    def _():
        left_b[...] = left
        right_send[:count] = right

    @pl.when(step == 3)
    def _():
        left_send[count:] = left
        right_send[count:] = right


def input_grad(shard, rows, d_rows, weights, head):
    full, width = rows.shape
    columns = d_rows.shape[1]
    count = width // 4
    cut = columns // 256 * 128

    def whole(*shape):
        return pl.BlockSpec(shape, lambda i, place: (0, 0))

    shapes = [
        (count, cut), (count, cut), (2 * count, cut),
        (count, columns - cut), (count, columns - cut), (2 * count, columns - cut),
    ]
    return pl.pallas_call(
        input_grad_kernel,
        grid_spec=pltpu.PrefetchScalarGridSpec(
            num_scalar_prefetch=1,
            grid=(4,),
            in_specs=[
                pl.BlockSpec((full, count), lambda i, place: (0, place[0] ^ i)),
                whole(full, columns),
                pl.BlockSpec((count, columns), lambda i, place: (place[0] ^ i, head)),
            ],
            out_specs=[whole(*shape) for shape in shapes]
            + [pl.BlockSpec((8, count), lambda i, place: (0, place[0] ^ i))],
        ),
        out_shape=[jax.ShapeDtypeStruct(shape, bf16) for shape in shapes]
        + [jax.ShapeDtypeStruct((8, width), f32)],
        compiler_params=pltpu.CompilerParams(
            dimension_semantics=("arbitrary",), vmem_limit_bytes=56 * 1024 * 1024
        ),
        cost_estimate=cost(4.0),
        name="input_grad",
    )(shard, rows, d_rows, weights)


def branch_back_kernel(
    places, rows, part_0, part_1, part_2, part_3, weights, mixer, og, gain, qe, m,
    d_out, d_og_out, n_out, start_out, gain_out, d_gated,
):
    count = part_0.shape[0]
    for i, part in enumerate((part_0, part_1, part_2, part_3)):
        d_gated[0, i * count : (i + 1) * count, :] = mm(part[...], weights[...])
    norm_back_kernel(
        places, rows, d_gated, mixer, og, gain, qe, m, d_out, d_og_out, n_out, start_out, gain_out
    )


def branch_back(places, rows, parts, weights, mixer, projected, gain, qe, m):
    seqs, heads, chunks = qe.shape[:3]
    length = chunks * CHUNK
    count, width = parts[0].shape
    return pl.pallas_call(
        branch_back_kernel,
        grid=(heads, seqs),
        in_specs=[
            smem(),
            per_unit(2 * chunks, CHUNK),
        ]
        + [pl.BlockSpec((count, width), lambda h, s: (0, 0))] * 4
        + [
            pl.BlockSpec((width, DV), lambda h, s: (0, h)),
            pl.BlockSpec((1, length, DV), lambda h, s: (s, 0, h)),
            pl.BlockSpec((1, length, 256), lambda h, s: (s, 0, 3 * h + 2)),
            pl.BlockSpec((1, DV), lambda h, s: (0, 0)),
            per_unit(chunks, CHUNK, DK),
            per_unit(chunks, DK, DK),
        ],
        out_specs=[
            per_unit(chunks, CHUNK, DV),
            per_unit(length, DV),
            per_unit(chunks, DK, DV),
            per_unit(DK, DV),
            pl.BlockSpec((1, 8, DV), lambda h, s: (h, 0, 0)),
        ],
        out_shape=[
            jax.ShapeDtypeStruct((seqs, heads, chunks, CHUNK, DV), bf16),
            jax.ShapeDtypeStruct((seqs, heads, length, DV), bf16),
            jax.ShapeDtypeStruct((seqs, heads, chunks, DK, DV), f32),
            jax.ShapeDtypeStruct((seqs, heads, DK, DV), f32),
            jax.ShapeDtypeStruct((heads, 8, DV), f32),
        ],
        scratch_shapes=[pltpu.VMEM((1, length, DV), f32)],
        compiler_params=params(),
        cost_estimate=cost(5.0 * heads),
        name="branch_back",
    )(places, rows, *parts, weights, mixer, projected, gain, qe, m)


def widened(block):
    return jnp.pad(block, ((0, 0), (0, -block.shape[1] % 128)))


def local_paired(
    tokens,
    proj_in,
    proj_gates,
    conv_taps,
    log_rates,
    rate_bias,
    gate_gain,
    proj_out,
    ffn_gate,
    ffn_up,
    ffn_down,
    gain_in,
    gain_ffn,
    cotangent,
):
    seqs, length, width = tokens.shape
    heads = log_rates.shape[0]
    units = ffn_gate.shape[1]
    core = lax.axis_index("ctx")
    place = lax.axis_index("tp")
    shard = lax.axis_index("shard")
    tp_count = lax.axis_size("tp")
    shards = lax.axis_size("shard")
    seq = place // 2
    half = place % 2
    quarter = length // 2
    share = length // tp_count
    full = 2 * length
    chunks = full // CHUNK
    route = []
    for j in range(tp_count):
        route.append((j, (j % 2) * tp_count + j // 2))
        route.append((tp_count + j, (j % 2) * tp_count + 2 + j // 2))
    route_back = [(b, a) for a, b in route]
    pairs = [(i, i ^ 1) for i in range(tp_count)]
    pairs_x = [(i, i ^ 1) for i in range(shards)]
    pairs_y = [(i, i ^ 2) for i in range(shards)]
    odd_x = shard % 2 == 1
    odd_y = shard // 2 == 1

    def hold(*values):
        return lax.optimization_barrier(values)

    def swap_core(block):
        with jax.named_scope("swap_core"):
            return lax.ppermute(block, "ctx", [(0, 1), (1, 0)])

    def swap_chip(block):
        with jax.named_scope("swap_chip"):
            return lax.ppermute(block, "tp", pairs)

    def swap_x(block):
        with jax.named_scope("swap_x"):
            return lax.ppermute(block, "shard", pairs_x)

    def swap_y(block):
        with jax.named_scope("swap_y"):
            return lax.ppermute(block, "shard", pairs_y)

    def to_users(block):
        with jax.named_scope("to_users"):
            return lax.ppermute(block, ("ctx", "tp"), route)

    def to_owners(block):
        with jax.named_scope("to_owners"):
            return lax.ppermute(block, ("ctx", "tp"), route_back)

    def both_cores(block):
        return block.astype(f32) + swap_core(block).astype(f32)

    def add(kept, got):
        return (kept.astype(f32) + got.astype(f32)).astype(bf16)

    def group_rows(mine, got):
        return jnp.concatenate(
            [mine[:quarter], got[:quarter], mine[quarter:], got[quarter:]], axis=0
        )

    def own_rows(rows):
        sequence = lax.dynamic_index_in_dim(rows, seq, 0, keepdims=False)
        mine = lax.dynamic_slice_in_dim(sequence, half * quarter, quarter, 0)
        other = lax.dynamic_slice_in_dim(sequence, (1 - half) * quarter, quarter, 0)
        return jnp.concatenate([mine, other], axis=0)

    def swap_sides(mine):
        return swap_x(mine), swap_y(mine)

    def swap_fourth(from_x, from_y):
        count = from_x.shape[0] // 2
        return swap_x(from_y[:count]), swap_y(from_x[count:])

    def ordered(odd, mine, theirs):
        return jnp.concatenate([jnp.where(odd, theirs, mine), jnp.where(odd, mine, theirs)], axis=0)

    def assembled(mine, sides, fourth):
        across = jnp.concatenate(fourth, axis=0)
        return ordered(
            odd_y, ordered(odd_x, mine, sides[0]), ordered(odd_x, sides[1], across)
        )

    def blocks(grad, *places_xor):
        rows = grad.shape[0] // shards
        return jnp.concatenate(
            [lax.dynamic_slice_in_dim(grad, (shard ^ p) * rows, rows, 0) for p in places_xor],
            axis=0,
        )

    def scatter_first(grad):
        cut = grad.shape[1] // 256 * 128
        left, right = grad[:, :cut], grad[:, cut:]
        return (
            blocks(left, 0, 2),
            swap_x(blocks(left, 1, 3)),
            blocks(right, 0, 1),
            swap_y(blocks(right, 2, 3)),
        )

    def scatter_second(left, left_got, right, right_got):
        rows = left.shape[0] // 2
        left = add(left, left_got)
        right = add(right, right_got)
        return left[:rows], swap_y(left[rows:]), right[:rows], swap_x(right[rows:])

    def scatter_end(left, left_got, right, right_got):
        return jnp.concatenate([add(left, left_got), add(right, right_got)], axis=1)

    def quarters(rows, weights):
        return [
            dot(rows[i * quarter : (i + 1) * quarter], weights, (1, 1)) for i in (3, 2, 1, 0)
        ]

    def piece_first(left_a, left_b, left_send, right_a, right_b, right_send):
        return left_a, left_b, swap_x(left_send), right_a, right_b, swap_y(right_send)

    def piece_second(left_a, left_b, left_got, right_a, right_b, right_got):
        rows = left_a.shape[0]
        left_on = swap_y(add(left_b, left_got[rows:]))
        right_on = swap_x(add(right_b, right_got[rows:]))
        return left_a, left_got, left_on, right_a, right_got, right_on

    def piece_end(left_a, left_got, left_on, right_a, right_got, right_on):
        rows = left_a.shape[0]

        def total(mine, got, on):
            return (mine.astype(f32) + got[:rows].astype(f32) + on.astype(f32)).astype(bf16)

        return jnp.concatenate(
            [total(left_a, left_got, left_on), total(right_a, right_got, right_on)], axis=1
        )

    small = jnp.concatenate(
        [
            conv_taps.astype(f32),
            jnp.pad(jnp.stack([log_rates, rate_bias]), ((0, 2), (0, conv_taps.shape[1] - heads))),
        ],
        axis=0,
    )
    inner = heads * HEAD
    block = proj_in.shape[0]
    gates_block = jnp.pad(
        proj_gates.T, ((0, 16 - 2 * heads), (0, inner - block))
    )
    mine_in = to_users(jnp.concatenate([proj_in, gates_block], axis=0))
    mine_rows = own_rows(tokens)
    got_rows = swap_core(mine_rows)
    gains = lax.all_gather(jnp.stack([gain_in, gain_ffn]), "shard", axis=1, tiled=True)
    mine_d = own_rows(cotangent)
    got_d = swap_core(mine_d)
    mine_pair = jnp.concatenate([widened(ffn_gate), widened(ffn_up)], axis=1)
    mine_in, mine_rows, got_rows, gains, mine_d, got_d, small, mine_out, mine_pair, mine_down = hold(
        mine_in, mine_rows, got_rows, gains, mine_d, got_d, small, proj_out.T, mine_pair,
        widened(ffn_down.T),
    )
    in_sides = swap_sides(mine_in)
    small = to_users(small)
    mine_out = to_users(mine_out)
    mine_down = to_users(mine_down)
    gains = gains.astype(f32)
    gain_in_f, gain_ffn_f = gains[0:1], gains[1:2]
    inputs_f = group_rows(mine_rows, got_rows).astype(f32)
    scale_in = lax.rsqrt(jnp.mean(inputs_f * inputs_f, -1, keepdims=True) + epsilon)
    normed_in = (inputs_f * scale_in * gain_in_f).astype(bf16)
    d_out = group_rows(mine_d, got_d)
    in_sides, small, mine_out, normed_in, d_out, mine_pair, mine_down = hold(
        in_sides, small, mine_out, normed_in, d_out, mine_pair, mine_down
    )
    in_fourth = swap_fourth(*in_sides)
    mine_pair = to_users(mine_pair)
    whole_out = lax.all_gather(mine_out, "shard", axis=0, tiled=True)
    in_fourth, normed_in = hold(in_fourth, normed_in)
    whole_in = assembled(
        mine_in[:block],
        [side[:block] for side in in_sides],
        [jnp.concatenate(in_fourth, axis=0)[:block]],
    )
    gate_rows = [
        rows_of[block : block + 8, :block]
        for rows_of in (mine_in, *in_sides, jnp.concatenate(in_fourth, axis=0))
    ]

    def side_by_side(odd, mine, theirs):
        return jnp.concatenate(
            [jnp.where(odd, theirs, mine), jnp.where(odd, mine, theirs)], axis=1
        )

    gates_rows = side_by_side(
        odd_y,
        side_by_side(odd_x, gate_rows[0], gate_rows[1]),
        side_by_side(odd_x, gate_rows[2], gate_rows[3]),
    )
    projected = dot(normed_in, whole_in).astype(bf16).reshape(1, full, inner)
    logits = dot(gates_rows, normed_in, (1, 1))[: 2 * heads]
    logits = logits.reshape(1, 2 * heads, chunks, CHUNK)
    projected, logits, gates_rows, mine_ffn = hold(
        projected, logits, gates_rows, jnp.concatenate([mine_pair, mine_down], axis=1)
    )
    weights_ffn = lax.all_gather(mine_ffn, "shard", axis=0, tiled=True)

    taps = small[:CONV]
    log_rates_here, rate_bias_here = small[CONV, :heads], small[CONV + 1, :heads]
    halo = jnp.zeros((1, HALO, inner), bf16)
    chunk = jnp.arange(chunks, dtype=jnp.int32)
    per_quarter = quarter // CHUNK
    true_quarter = chunk // per_quarter
    places = (
        2 * ((true_quarter % 2) ^ half) + ((true_quarter // 2) ^ core)
    ) * per_quarter + chunk % per_quarter
    no_state = jnp.zeros((1, heads, DK, DV), f32)
    gain_row = gate_gain.reshape(1, DV)
    source = (projected, halo, logits, taps, log_rates_here, rate_bias_here)
    prepared = prepare(places, *source, False)[:11]
    q, k, v, rows, t, w, u, qe, m, b, own_out = prepared
    gated, mixer, states = mixer_output(
        places, (rows, qe, m, b, own_out), no_state, projected, gain_row
    )
    gated = gated.reshape(full, heads * DV)
    far_b, far_a, near_b, near_a = quarters(gated, whole_out)
    far_got = swap_core(far_b.astype(bf16))
    near_got = swap_core(near_b.astype(bf16))
    far_sum, near_a, near_got = hold(add(far_a, far_got), near_a, near_got)
    far_sum = swap_chip(far_sum)
    middle = inputs_f[:quarter] + (near_a + near_got.astype(f32) + far_sum.astype(f32))
    scale_mid = lax.rsqrt(jnp.mean(middle * middle, -1, keepdims=True) + epsilon)
    unit_mid = middle * scale_mid

    mine_mid = (unit_mid * gain_ffn_f).astype(bf16)
    far_mid = swap_chip(mine_mid)
    near_mid = swap_core(mine_mid)
    near = feed_forward(mine_mid, near_mid, d_out, weights_ffn, ())
    far_mid, near = hold(far_mid, near)
    near_a, near_b, near_down_a, near_down_b = near[3:]
    near_got = swap_core(near_b)
    far = feed_forward(
        far_mid, swap_core(far_mid), d_out, weights_ffn, tuple(near[:3])
    )
    normed_mid, hidden, d_pair, far_a, far_b, far_down_a, far_down_b = far
    far_got = swap_core(far_b)
    far_sum, near_got, normed_mid, hidden, d_pair = hold(
        add(far_a, far_got), near_got, normed_mid, hidden, d_pair
    )
    far_sum = swap_chip(far_sum)
    far_down_got = swap_core(far_down_b)
    near_down_got = swap_core(near_down_b)
    grad_pair = dot(normed_mid, d_pair, (0, 0)).astype(bf16)
    grad_down = dot(d_out, hidden, (0, 0)).astype(bf16)
    grad_ffn = jnp.concatenate([grad_pair, grad_down], axis=1)
    far_sum, grad_ffn, far_down_got, near_down_got = hold(
        far_sum, grad_ffn, far_down_got, near_down_got
    )
    piece_ffn = lax.psum_scatter(grad_ffn, "shard", scatter_dimension=0, tiled=True)
    d_mid_norm = near_a.astype(f32) + near_got.astype(f32) + far_sum.astype(f32)
    scaled_mid = d_mid_norm * gain_ffn_f
    d_middle = d_out[:quarter].astype(f32) + scale_mid * (
        scaled_mid - unit_mid * jnp.mean(scaled_mid * unit_mid, -1, keepdims=True)
    )
    d_low = d_middle.astype(bf16)
    far_low = swap_chip(d_low)
    near_low = swap_core(d_low)
    far_low, near_low, far_down_a, far_down_got = hold(
        far_low, near_low, far_down_a, far_down_got
    )
    d_parts = (d_low, near_low, far_low, swap_core(far_low))

    far_down_sum = swap_chip(add(far_down_a, far_down_got))
    branch = branch_back(places, rows, d_parts, whole_out, mixer, projected, gain_row, qe, m)
    branch, gated = hold(branch, gated)
    d_mixer, d_og, n, _, gain_gate_part = branch

    def head_grads(h, d_mixer):
        d_projected, _, _, d_logits, rate_rows, tap_rows = mixer_grads(
            places, *source, q, k, v, rows, t, w, u, m, states, d_mixer, n, no_state, d_og,
            start=h, count=1,
        )
        return d_projected.reshape(full, HEAD), d_logits, rate_rows, tap_rows

    even = half == 0
    first = seq == 0
    send_a = [(0, 0), (1, 2), (2, 1), (3, 3)]
    send_b = [(0, 1), (1, 3), (2, 0), (3, 2)]

    def to_outputs(mine):
        low, high = mine[:share], mine[share:]
        with jax.named_scope("to_outputs"):
            got_a = lax.ppermute(jnp.where(first, low, high), "tp", send_a)
            got_b = lax.ppermute(jnp.where(first, high, low), "tp", send_b)
        return got_a, got_b

    def stacked(got_a, got_b):
        return jnp.stack([jnp.where(even, got_a, got_b), jnp.where(even, got_b, got_a)])

    place_x = shard.reshape(1).astype(jnp.int32)
    first_head = head_grads(0, d_mixer)
    first_head, d_mixer, far_down_sum = hold(first_head, d_mixer, far_down_sum)
    grad_both, part_first = both_grads(normed_in, first_head[0], whole_in, d_parts, gated)
    grad_both, part_first, d_mixer, piece_ffn = hold(grad_both, part_first, d_mixer, piece_ffn)
    owned_pair = to_owners(piece_ffn[:, : 2 * hidden.shape[1]])
    piece_both = lax.psum_scatter(grad_both, "shard", scatter_dimension=0, tiled=True)
    layer_rows = (
        middle
        + near_down_a.astype(f32)
        + near_down_got.astype(f32)
        + far_down_sum.astype(f32)
    ).astype(bf16)

    last_head, owned_pair = hold(head_grads(1, d_mixer), owned_pair)

    owned_down = to_owners(piece_ffn[:, 2 * hidden.shape[1] :])
    *sent, part_last = input_grad(place_x, normed_in, last_head[0], whole_in, 1)
    sent, part_last, last_head, owned_down, layer_rows = hold(
        sent, part_last, last_head, owned_down, layer_rows
    )
    steps_last = piece_first(*sent)
    layer_got = to_outputs(layer_rows)
    logits_first = first_head[1].reshape(2, full)
    logits_last = last_head[1].reshape(2, full)
    d_logit_rows = jnp.concatenate(
        [logits_first, logits_last, jnp.zeros((8 - 2 * heads, full), f32)], axis=0
    ).astype(bf16)
    grad_gates = dot(d_logit_rows, normed_in)
    packed = jnp.concatenate(
        [
            jnp.concatenate([first_head[3][0], last_head[3][0]], axis=1),
            grad_gates,
            part_first + part_last + gates_rows.astype(f32) * grad_gates,
            jnp.concatenate(
                [
                    gain_gate_part[0], gain_gate_part[1], first_head[2][0, 0], last_head[2][0, 0],
                    first_head[1][0, 0], last_head[1][0, 0],
                ],
                axis=1,
            ),
        ],
        axis=0,
    )
    packed_got = swap_x(packed)
    backs = input_back(first_head[0], last_head[0], d_logit_rows, whole_in, gates_rows)
    backs, steps_last, layer_got, packed, packed_got, piece_both = hold(
        backs, steps_last, layer_got, packed, packed_got, piece_both
    )
    owned_both = to_owners(piece_both)
    near_a, near_b, far_a, far_b = backs
    far_got = swap_core(far_b)
    near_got = swap_core(near_b)
    steps_last = piece_second(*steps_last)
    packed = packed + packed_got
    packed_got = swap_y(packed)
    far_sum, near_got, near_a, steps_last, packed, packed_got, owned_pair, owned_down = hold(
        add(far_a, far_got), near_got, near_a, steps_last, packed, packed_got, owned_pair,
        owned_down,
    )
    far_sum = swap_chip(far_sum)
    piece_last = to_owners(piece_end(*steps_last))
    packed = to_owners(packed + packed_got)
    sum_pair = both_cores(owned_pair)
    sum_gate = sum_pair[:, :units]
    sum_up = sum_pair[:, sum_pair.shape[1] // 2 :][:, :units]
    sum_down = both_cores(owned_down)[:, :units].T
    layer_out = stacked(*layer_got)
    far_sum, packed, sum_gate, sum_up, sum_down, layer_out, owned_both, near_a = hold(
        far_sum, packed, sum_gate, sum_up, sum_down, layer_out, owned_both, near_a
    )
    d_in_norm = near_a.astype(f32) + near_got.astype(f32) + far_sum.astype(f32)
    unit_in = (inputs_f * scale_in)[:quarter]
    scaled_in = d_in_norm * gain_in_f
    token_rows = d_middle + scale_in[:quarter] * (
        scaled_in - unit_in * jnp.mean(scaled_in * unit_in, -1, keepdims=True)
    )
    token_got = to_outputs(token_rows.astype(bf16))
    packed = both_cores(packed)
    sum_both = both_cores(owned_both)
    sum_out = sum_both[:, HEAD:].T
    sum_last = both_cores(piece_last)

    part_ffn = jnp.sum(ffn_gate.astype(f32) * sum_gate + ffn_up.astype(f32) * sum_up, 1)
    sum_taps, sum_gates, part_in, rest = (packed[8 * i : 8 * i + 8] for i in range(4))
    sum_gain = jnp.sum(rest[:, :DV] + rest[:, DV : 2 * DV], 0)
    sum_rates = jnp.sum(rest[:, 2 * DV :].reshape(8, 2 * heads, CHUNK), (0, 2))
    rows_here = gain_in.shape[0]

    def own_block(rows_of):
        return lax.dynamic_slice_in_dim(rows_of, shard * rows_here, rows_here, -1)

    over_blocks = jnp.concatenate([sum_gain, jnp.sum(own_block(part_in), 0), part_ffn])
    over_blocks = jnp.pad(over_blocks, (0, -over_blocks.shape[0] % 1024)).reshape(-1, 128)
    over_blocks = over_blocks + swap_chip(over_blocks)
    with jax.named_scope("swap_pair"):
        other_pair = lax.ppermute(over_blocks, "tp", [(i, i ^ 2) for i in range(tp_count)])
    over_blocks = (over_blocks + other_pair).reshape(-1)
    return (
        layer_out,
        stacked(*token_got).astype(f32),
        jnp.concatenate([sum_both[:, :HEAD], sum_last], axis=1),
        own_block(sum_gates)[: 2 * heads].T,
        sum_taps[:CONV],
        sum_rates[:heads],
        sum_rates[heads:],
        over_blocks[:DV],
        sum_out,
        sum_gate,
        sum_up,
        sum_down,
        over_blocks[DV : DV + rows_here] / gain_in.astype(f32),
        over_blocks[DV + rows_here : DV + 2 * rows_here] / gain_ffn.astype(f32),
    )


def solution(mesh):
    placed = (
        P("shard", "ctx", None),
        P("shard", "tp"),
        P("shard", "tp"),
        P(None, "tp"),
        P("tp"),
        P("tp"),
        P(),
        P("tp", "shard"),
        P("shard", "tp"),
        P("shard", "tp"),
        P("tp", "shard"),
        P("shard"),
        P("shard"),
        P("shard", "ctx", None),
    )
    shape = dict(mesh.shape)
    paired = (shape["shard"], shape["ctx"], shape["tp"]) == (4, 2, 4)

    def body(*arrays):
        seqs, length, _ = arrays[0].shape
        heads = arrays[4].shape[0]
        if paired and seqs == 2 and heads == 2 and length % (2 * CHUNK) == 0:
            return local_paired(*arrays)
        return local(*arrays)

    return jax.shard_map(
        body,
        mesh=mesh,
        in_specs=placed,
        out_specs=(
            P("shard", ("ctx", "tp"), None),
            P("shard", ("ctx", "tp"), None),
            P("shard", "tp"),
            P("shard", "tp"),
            P(None, "tp"),
            P("tp"),
            P("tp"),
            P(),
            P("tp", "shard"),
            P("shard", "tp"),
            P("shard", "tp"),
            P("tp", "shard"),
            P("shard"),
            P("shard"),
        ),
        check_vma=False,
    )
```

```python
import functools

import jax
import jax.numpy as jnp
from jax import lax
from jax.experimental import pallas as pl
from jax.experimental.pallas import tpu as pltpu
from jax.sharding import PartitionSpec as P

DK = 128
DV = 256
QKV = 2 * DK + DV
HEAD = QKV + DV
CONV = 4
CHUNK = 128
HALO = 16
ROWS = 8

epsilon = 1e-06
f32 = jnp.float32
bf16 = jnp.bfloat16


def mm(left, right, contract=(1, 0)):
    return lax.dot_general(
        left.astype(bf16),
        right.astype(bf16),
        (((contract[0],), (contract[1],)), ((), ())),
        preferred_element_type=f32,
    )


def mm_split(left, right):
    left_hi = left.astype(bf16)
    right_hi = right.astype(bf16)
    left_lo = left - left_hi.astype(f32)
    right_lo = right - right_hi.astype(f32)
    return mm(left_hi, right_hi) + (mm(left_hi, right_lo) + mm(left_lo, right_hi))


def mm_exact(left, right):
    return lax.dot_general(
        left,
        right,
        (((1,), (0,)), ((), ())),
        precision=lax.Precision.HIGHEST,
        preferred_element_type=f32,
    )


def iotas():
    row = lax.broadcasted_iota(jnp.int32, (CHUNK, CHUNK), 0)
    col = lax.broadcasted_iota(jnp.int32, (CHUNK, CHUNK), 1)
    return row, col


def pad_rows(block):
    missing = CHUNK - block.shape[0]
    return jnp.concatenate([block, jnp.zeros((missing, block.shape[1]), f32)], axis=0)


def softplus(values):
    return jnp.maximum(values, 0.0) + jnp.log1p(jnp.exp(-jnp.abs(values)))


def sigmoid(values):
    return 1.0 / (1.0 + jnp.exp(-values))


def place_of(places, c):
    return pl.ds(pl.multiple_of(places[c] * CHUNK, CHUNK), CHUNK)


def chunk_rows(places, logit_ref, chunks):
    def stacked(row):
        return jnp.concatenate(
            [logit_ref[0, row, pl.ds(places[c], 1), :] for c in range(chunks)], axis=0
        )

    return stacked(0), stacked(1)


def invert_units(lowers, row, col):
    eye = (row == col).astype(f32)
    same = (row // 16) == (col // 16)
    powers = [jnp.where(same, n, 0.0) for n in lowers]
    inverses = [eye - p for p in powers]
    for _ in range(3):
        powers = [mm_split(p, p) for p in powers]
        inverses = [x + mm_split(x, p) for x, p in zip(inverses, powers)]
    size = 16
    while size < CHUNK:
        joins = ((row // (2 * size)) == (col // (2 * size))) & ((row // size) != (col // size))
        middles = [mm_split(jnp.where(joins, n, 0.0), x) for n, x in zip(lowers, inverses)]
        inverses = [x - mm_split(x, m) for x, m in zip(inverses, middles)]
        size *= 2
    return inverses


def conv_into(places, scratch, x_qk, x_v, halo_qk, halo_v, taps_qk, taps_v, length):
    scratch[0:ROWS, 0 : 2 * DK] = halo_qk[0, HALO - ROWS :, :].astype(f32)
    scratch[0:ROWS, 2 * DK :] = halo_v[0, HALO - ROWS :, :].astype(f32)
    for c in range(length // CHUNK):
        body = slice(ROWS + c * CHUNK, ROWS + (c + 1) * CHUNK)
        scratch[body, 0 : 2 * DK] = x_qk[0, place_of(places, c), :].astype(f32)
        scratch[body, 2 * DK :] = x_v[0, place_of(places, c), :].astype(f32)
    taps = jnp.concatenate([taps_qk[...], taps_v[...]], axis=1).astype(f32)
    first = ROWS - CONV + 1
    mixed = taps[0:1, :] * scratch[first : first + length, :]
    for j in range(1, CONV):
        mixed = mixed + taps[j : j + 1, :] * scratch[first + j : first + j + length, :]
    return mixed, taps


def prep_kernel(
    places, rates, biases, x_qk, x_v, halo_qk, halo_v, logits, taps_qk, taps_v,
    q_out, k_out, v_out, rows_out, t_out, w_out, u_out, qe_out, m_out, b_out, p_out, end_out, map_out,
    scratch,
):
    head = pl.program_id(0)
    length = x_qk.shape[1]
    chunks = length // CHUNK
    mixed, _ = conv_into(
        places, scratch, x_qk, x_v, halo_qk, halo_v, taps_qk, taps_v, length
    )
    active = mixed * sigmoid(mixed)
    q_act = active[:, :DK]
    k_act = active[:, DK : 2 * DK]
    q_all = (
        q_act * lax.rsqrt(jnp.sum(q_act * q_act, -1, keepdims=True) + epsilon) * DK ** (-0.5)
    ).astype(bf16)
    k_all = (
        k_act * lax.rsqrt(jnp.sum(k_act * k_act, -1, keepdims=True) + epsilon)
    ).astype(bf16)
    v_all = active[:, 2 * DK :].astype(bf16)
    q_out[0, 0] = q_all
    k_out[0, 0] = k_all
    v_out[0, 0] = v_all
    decay_logit, strength_logit = chunk_rows(places, logits, chunks)
    decay = -jnp.exp(rates[head]) * softplus(decay_logit + biases[head])
    row, col = iotas()
    lower = row >= col
    strict = row > col
    total = mm_exact(pad_rows(decay)[: max(8, chunks)], (row <= col).astype(f32))[:chunks]
    strength = sigmoid(strength_logit)
    stacked = jnp.concatenate([total, strength], axis=0)
    rows_out[0, 0] = stacked
    columns = jnp.transpose(pad_rows(stacked))
    units = range(chunks)
    span = [slice(c * CHUNK, (c + 1) * CHUNK) for c in units]
    g_col = [columns[:, c : c + 1] for c in units]
    b_col = [columns[:, chunks + c : chunks + c + 1] for c in units]
    table = [
        jnp.where(lower, jnp.exp(jnp.where(lower, g_col[c] - total[c : c + 1, :], 0.0)), 0.0)
        for c in units
    ]
    q = [q_all[s] for s in span]
    k = [k_all[s] for s in span]
    gram = [mm(k[c], k[c], (1, 1)) for c in units]
    score = [mm(q[c], k[c], (1, 1)) * table[c] for c in units]
    lowers = [jnp.where(strict, b_col[c] * gram[c] * table[c], 0.0) for c in units]
    inverse = invert_units(lowers, row, col)
    grown = [jnp.exp(g_col[c]) for c in units]
    w = [mm(inverse[c], (b_col[c] * grown[c]) * k[c].astype(f32)) for c in units]
    u = [mm(inverse[c], b_col[c] * v_all[span[c]].astype(f32)) for c in units]
    qe = [grown[c] * q[c].astype(f32) - mm(score[c], w[c]) for c in units]
    own = [mm(score[c], u[c]) for c in units]
    last = [g_col[c][CHUNK - 1 :, :] for c in units]
    k_late = [jnp.exp(last[c] - g_col[c]) * k[c].astype(f32) for c in units]
    m = [-mm(k_late[c], w[c], (0, 0)) for c in units]
    b = [mm(k_late[c], u[c], (0, 0)) for c in units]
    state = b[0]
    for c in units:
        t_out[0, 0, c] = inverse[c].astype(bf16)
        w_out[0, 0, c] = w[c].astype(bf16)
        u_out[0, 0, c] = u[c]
        qe_out[0, 0, c] = qe[c].astype(bf16)
        m_out[0, 0, c] = m[c].astype(bf16)
        b_out[0, 0, c] = b[c]
        p_out[0, 0, c] = own[c]
        if c:
            state = jnp.exp(last[c]) * state + mm(m[c], state) + b[c]
    end_out[0, 0] = state
    if map_out is not None:
        chain = (row == col).astype(f32)
        for c in units:
            chain = jnp.exp(last[c]) * chain + mm(m[c], chain)
        map_out[0, 0] = chain


def output_kernel(
    places, rows, qe, m, b, own, arriving, og, gain,
    gated_out, mixer_out, states_out,
):
    chunks = qe.shape[2]
    last = jnp.exp(rows[0, 0][0:chunks, CHUNK - 1 :])
    state = arriving[0, 0].astype(f32)
    gain_row = gain[...].astype(f32)
    for c in range(chunks):
        s = slice(c * CHUNK, (c + 1) * CHUNK)
        states_out[0, 0, c] = state.astype(bf16)
        out = mm(qe[0, 0, c], state) + own[0, 0, c]
        mixer_out[0, s, :] = out
        scale = lax.rsqrt(jnp.mean(out * out, -1, keepdims=True) + epsilon)
        gate = og[0, place_of(places, c), :].astype(f32)
        gated_out[0, place_of(places, c), :] = (out * scale * gain_row * (gate * sigmoid(gate))).astype(bf16)
        if c < chunks - 1:
            state = last[c : c + 1, :] * state + mm(m[0, 0, c], state) + b[0, 0, c]


def norm_back_kernel(
    places, rows, d_gated, mixer, og, gain, qe, m,
    d_out, d_og_out, n_out, start_out, gain_out,
):
    seq = pl.program_id(1)
    chunks = qe.shape[2]
    last = jnp.exp(rows[0, 0][0:chunks, CHUNK - 1 :])
    gain_row = gain[...].astype(f32)
    gain_sum = jnp.zeros((8, DV), f32)
    adds = []
    for c in range(chunks):
        s = slice(c * CHUNK, (c + 1) * CHUNK)
        out = mixer[0, s, :]
        gate = og[0, place_of(places, c), :].astype(f32)
        sig = sigmoid(gate)
        swish = gate * sig
        dg = d_gated[0, place_of(places, c), :].astype(f32)
        scale = lax.rsqrt(jnp.mean(out * out, -1, keepdims=True) + epsilon)
        unit = out * scale
        spread = dg * unit
        e = dg * (gain_row * swish)
        d_mix = scale * (e - unit * jnp.mean(e * unit, -1, keepdims=True))
        d_og_out[0, 0, s, :] = (spread * gain_row * (sig * (1.0 + gate * (1.0 - sig)))).astype(bf16)
        gain_sum = gain_sum + jnp.sum((spread * swish).reshape(CHUNK // 8, 8, DV), axis=0)
        d_low = d_mix.astype(bf16)
        d_out[0, 0, c] = d_low
        add = mm(qe[0, 0, c], d_low, (0, 0))
        n_out[0, 0, c] = add
        adds.append(add)
    back = adds[-1]
    for c in reversed(range(chunks - 1)):
        back = last[c : c + 1, :] * back + mm(m[0, 0, c], back, (0, 0)) + adds[c]
    start_out[0, 0] = back

    @pl.when(seq == 0)
    def _():
        gain_out[0] = gain_sum

    @pl.when(seq != 0)
    def _():
        gain_out[0] = gain_out[0] + gain_sum


def grad_kernel(
    start, places, rates, biases, x_qk, x_v, halo_qk, halo_v, logits, taps_qk, taps_v,
    q_in, k_in, v_in, rows, t_in, w_in, u_in, m_in, states, d_out, n_in, arriving, d_og,
    d_proj_out, d_halo_out, d_tail_out, d_logit_out, rate_out, taps_out,
    scratch, grads,
):
    head = pl.program_id(0) + start
    seq = pl.program_id(1)
    length = x_qk.shape[1]
    chunks = length // CHUNK
    units = range(chunks)
    row, col = iotas()
    lower = row >= col
    strict = row > col
    stacked = rows[0, 0]
    total = stacked[0:chunks]
    strength = stacked[chunks : 2 * chunks]
    columns = jnp.transpose(pad_rows(stacked))
    g_col = [columns[:, c : c + 1] for c in units]
    b_col = [columns[:, chunks + c : chunks + c + 1] for c in units]
    last = [g_col[c][CHUNK - 1 :, :] for c in units]
    ends = [None] * chunks
    back = arriving[0, 0].astype(f32)
    for c in reversed(units):
        ends[c] = back
        if c:
            back = jnp.exp(last[c]) * back + mm(m_in[0, 0, c], back, (0, 0)) + n_in[0, 0, c]
    span = [slice(c * CHUNK, (c + 1) * CHUNK) for c in units]
    table = [
        jnp.where(lower, jnp.exp(jnp.where(lower, g_col[c] - total[c : c + 1, :], 0.0)), 0.0)
        for c in units
    ]
    q = [q_in[0, 0, s, :] for s in span]
    k = [k_in[0, 0, s, :] for s in span]
    v = [v_in[0, 0, s, :] for s in span]
    k_f = [k[c].astype(f32) for c in units]
    q_f = [q[c].astype(f32) for c in units]
    t = [t_in[0, 0, c] for c in units]
    w = [w_in[0, 0, c] for c in units]
    u = [u_in[0, 0, c] for c in units]
    s_in = [states[0, 0, c] for c in units]
    d_o = [d_out[0, 0, c] for c in units]
    gram = [mm(k[c], k[c], (1, 1)) * table[c] for c in units]
    score = [mm(q[c], k[c], (1, 1)) * table[c] for c in units]
    grown = [jnp.exp(g_col[c]) for c in units]
    fade = [jnp.exp(last[c] - g_col[c]) for c in units]
    fresh = [u[c] - mm(w[c], s_in[c]) for c in units]
    k_late = [fade[c] * k_f[c] for c in units]
    d_fresh = [mm(score[c], d_o[c], (0, 0)) + mm(k_late[c], ends[c]) for c in units]
    d_score = [jnp.where(lower, mm(d_o[c], fresh[c], (1, 1)), 0.0) for c in units]
    d_q_grown = [mm(d_o[c], s_in[c], (1, 1)) for c in units]
    d_k_late = [mm(fresh[c], ends[c], (1, 1)) for c in units]
    d_w = [-mm(d_fresh[c], s_in[c], (1, 1)) for c in units]
    d_vb = [mm(t[c], d_fresh[c], (0, 0)) for c in units]
    d_kb = [mm(t[c], d_w[c], (0, 0)) for c in units]
    d_lower = [
        jnp.where(strict, -(mm(d_vb[c], u[c], (1, 1)) + mm(d_kb[c], w[c], (1, 1))), 0.0)
        for c in units
    ]
    d_score_t = [d_score[c] * table[c] for c in units]
    d_lower_b = [d_lower[c] * b_col[c] for c in units]
    d_gram = [d_lower_b[c] * table[c] for c in units]
    cols = []
    cols_b = []
    rows_g = []
    for c in units:
        s = span[c]
        paired = d_score[c] * score[c] + d_lower_b[c] * gram[c]
        late = k_late[c] * d_k_late[c]
        k_dot = grown[c] * (d_kb[c] * k_f[c])
        per_row = (
            paired + grown[c] * (q_f[c] * d_q_grown[c]) - late + b_col[c] * k_dot
        )
        cols.append(jnp.sum(per_row, -1, keepdims=True))
        v_f = v[c].astype(f32)
        v_dot = d_vb[c] * v_f
        cols_b.append(
            jnp.sum(
                d_lower[c] * gram[c] + k_dot + v_dot[:, :DK] + v_dot[:, DK:], -1, keepdims=True
            )
        )
        kept = s_in[c].astype(f32) * ends[c]
        whole = jnp.sum(
            jnp.sum(late, 0, keepdims=True)
            + jnp.exp(last[c]) * jnp.sum(kept[:, :DK] + kept[:, DK:], 0, keepdims=True),
            -1,
            keepdims=True,
        )
        rows_g.append((jnp.sum(paired, 0, keepdims=True), whole))
        d_q = mm(d_score_t[c], k[c]) + grown[c] * d_q_grown[c]
        d_k = (
            mm(d_score_t[c], q[c], (0, 0))
            + mm(d_gram[c], k[c])
            + mm(d_gram[c], k[c], (0, 0))
            + fade[c] * d_k_late[c]
            + (b_col[c] * grown[c]) * d_kb[c]
        )
        grads[ROWS + s.start : ROWS + s.stop, 0:DK] = d_q
        grads[ROWS + s.start : ROWS + s.stop, DK : 2 * DK] = d_k
        grads[ROWS + s.start : ROWS + s.stop, 2 * DK :] = b_col[c] * d_vb[c]
    wide = jnp.concatenate(
        cols + cols_b + [jnp.zeros((CHUNK, CHUNK - 2 * chunks), f32)], axis=1
    )
    tall = jnp.transpose(wide)
    d_total = tall[0:chunks] - jnp.concatenate([r for r, _ in rows_g], axis=0)
    d_strength = tall[chunks : 2 * chunks]
    d_decay = mm_exact(pad_rows(d_total)[: max(8, chunks)], lower.astype(f32))[:chunks]
    d_decay = d_decay + jnp.concatenate([w_ for _, w_ in rows_g], axis=0)
    decay_logit, _ = chunk_rows(places, logits, chunks)
    biased = decay_logit + biases[head]
    rate = jnp.exp(rates[head])
    d_logit = -d_decay * rate * sigmoid(biased)
    d_strength_logit = d_strength * strength * (1.0 - strength)
    for c in units:
        d_logit_out[0, 0, pl.ds(places[c], 1), :] = d_logit[c : c + 1, :]
        d_logit_out[0, 1, pl.ds(places[c], 1), :] = d_strength_logit[c : c + 1, :]
    rate_out[0, 0] = -d_decay * rate * softplus(biased)

    mixed, taps = conv_into(
        places, scratch, x_qk, x_v, halo_qk, halo_v, taps_qk, taps_v, length
    )
    sig = sigmoid(mixed)
    active = mixed * sig
    slope = sig * (1.0 + mixed * (1.0 - sig))

    def unnorm(act, grad, factor):
        scale = lax.rsqrt(jnp.sum(act * act, -1, keepdims=True) + epsilon)
        unit = act * scale
        return (factor * scale) * (grad - unit * jnp.sum(unit * grad, -1, keepdims=True))

    body = slice(ROWS, ROWS + length)
    grads[body, 0:DK] = (
        unnorm(active[:, :DK], grads[body, 0:DK], DK ** (-0.5)) * slope[:, :DK]
    )
    grads[body, DK : 2 * DK] = (
        unnorm(active[:, DK : 2 * DK], grads[body, DK : 2 * DK], 1.0) * slope[:, DK : 2 * DK]
    )
    grads[body, 2 * DK :] = grads[body, 2 * DK :] * slope[:, 2 * DK :]
    grads[0:ROWS, :] = jnp.zeros((ROWS, QKV), f32)
    grads[ROWS + length :, :] = jnp.zeros((ROWS, QKV), f32)
    d_x = None
    d_halo = None
    tap_rows = []
    d_conv = grads[body, :]
    first = ROWS - CONV + 1
    for j in range(CONV):
        ahead = CONV - 1 - j
        part = taps[j : j + 1, :] * grads[ROWS + ahead : ROWS + ahead + length, :]
        d_x = part if d_x is None else d_x + part
        edge = taps[j : j + 1, :] * grads[ahead : ahead + ROWS, :]
        d_halo = edge if d_halo is None else d_halo + edge
        tap_rows.append(
            jnp.sum(d_conv * scratch[first + j : first + j + length, :], 0, keepdims=True)
        )
    for c in units:
        d_proj_out[0, place_of(places, c), 0:QKV] = d_x[span[c]].astype(bf16)
        d_proj_out[0, place_of(places, c), QKV:] = d_og[0, 0, span[c], :]
    d_tail_out[0, 0] = d_x[length - ROWS :, :]
    d_halo_out[0, 0] = d_halo
    tap_rows = jnp.concatenate(tap_rows + [jnp.zeros((8 - CONV, QKV), f32)], axis=0)

    @pl.when(seq == 0)
    def _():
        taps_out[0] = tap_rows

    @pl.when(seq != 0)
    def _():
        taps_out[0] = taps_out[0] + tap_rows


def cost(micros):
    return pl.CostEstimate(
        flops=int(micros * 1e8), bytes_accessed=int(micros * 1e5), transcendentals=0
    )


def params():
    return pltpu.CompilerParams(
        dimension_semantics=("arbitrary", "arbitrary"), vmem_limit_bytes=56 * 1024 * 1024
    )


def smem():
    return pl.BlockSpec(memory_space=pltpu.SMEM)


def per_unit(*shape, start=0):
    zeros = (0,) * len(shape)
    return pl.BlockSpec((1, 1) + shape, lambda h, s: (s, h + start) + zeros)


def input_specs(length, start=0):
    return [
        smem(),
        smem(),
        smem(),
        pl.BlockSpec((1, length, 256), lambda h, s: (s, 0, 3 * (h + start))),
        pl.BlockSpec((1, length, 256), lambda h, s: (s, 0, 3 * (h + start) + 1)),
        pl.BlockSpec((1, HALO, 256), lambda h, s: (s, 0, 3 * (h + start))),
        pl.BlockSpec((1, HALO, 256), lambda h, s: (s, 0, 3 * (h + start) + 1)),
        pl.BlockSpec((1, 2, length // CHUNK, CHUNK), lambda h, s: (s, h + start, 0, 0)),
        pl.BlockSpec((CONV, 256), lambda h, s: (0, 2 * (h + start))),
        pl.BlockSpec((CONV, 256), lambda h, s: (0, 2 * (h + start) + 1)),
    ]


def prepare(places, projected, halo, logits, taps, rates, biases, with_map):
    seqs, length, _ = projected.shape
    heads = rates.shape[0]
    chunks = length // CHUNK

    def out(dtype, *shape):
        return jax.ShapeDtypeStruct((seqs, heads) + shape, dtype), per_unit(*shape)

    outs = [
        out(bf16, length, DK),
        out(bf16, length, DK),
        out(bf16, length, DV),
        out(f32, 2 * chunks, CHUNK),
        out(bf16, chunks, CHUNK, CHUNK),
        out(bf16, chunks, CHUNK, DK),
        out(f32, chunks, CHUNK, DV),
        out(bf16, chunks, CHUNK, DK),
        out(bf16, chunks, DK, DK),
        out(f32, chunks, DK, DV),
        out(f32, chunks, CHUNK, DV),
        out(f32, DK, DV),
    ]
    if with_map:
        outs.append(out(f32, DK, DK))
        kernel = prep_kernel
    else:

        def kernel(*refs):
            prep_kernel(*refs[:-1], None, refs[-1])

    results = pl.pallas_call(
        kernel,
        grid=(heads, seqs),
        in_specs=input_specs(length),
        out_specs=[spec for _, spec in outs],
        out_shape=[shape for shape, _ in outs],
        scratch_shapes=[pltpu.VMEM((length + ROWS, QKV), f32)],
        compiler_params=params(),
        cost_estimate=cost(9.0 * heads * seqs * chunks / 8),
        name="prepare",
    )(places, rates, biases, projected, projected, halo, halo, logits, taps, taps)
    return results if with_map else list(results) + [None]


def mixer_output(places, kept, arriving, projected, gain):
    rows, qe, m, b, own = kept
    seqs, heads, chunks = qe.shape[:3]
    length = chunks * CHUNK
    return pl.pallas_call(
        output_kernel,
        grid=(heads, seqs),
        in_specs=[
            smem(),
            per_unit(2 * chunks, CHUNK),
            per_unit(chunks, CHUNK, DK),
            per_unit(chunks, DK, DK),
            per_unit(chunks, DK, DV),
            per_unit(chunks, CHUNK, DV),
            per_unit(DK, DV),
            pl.BlockSpec((1, length, 256), lambda h, s: (s, 0, 3 * h + 2)),
            pl.BlockSpec((1, DV), lambda h, s: (0, 0)),
        ],
        out_specs=[
            pl.BlockSpec((1, length, DV), lambda h, s: (s, 0, h)),
            pl.BlockSpec((1, length, DV), lambda h, s: (s, 0, h)),
            per_unit(chunks, DK, DV),
        ],
        out_shape=[
            jax.ShapeDtypeStruct((seqs, length, heads * DV), bf16),
            jax.ShapeDtypeStruct((seqs, length, heads * DV), f32),
            jax.ShapeDtypeStruct((seqs, heads, chunks, DK, DV), bf16),
        ],
        compiler_params=params(),
        cost_estimate=cost(4.0 * heads * seqs * chunks / 8),
        name="mixer_output",
    )(places, rows, qe, m, b, own, arriving, projected, gain)


def norm_back(places, rows, d_gated, mixer, projected, gain, qe, m, start=0, count=None):
    seqs, heads, chunks = qe.shape[:3]
    length = chunks * CHUNK
    heads = count or heads
    return pl.pallas_call(
        norm_back_kernel,
        grid=(heads, seqs),
        in_specs=[
            smem(),
            per_unit(2 * chunks, CHUNK, start=start),
            pl.BlockSpec((1, length, DV), lambda h, s: (s, 0, h + start)),
            pl.BlockSpec((1, length, DV), lambda h, s: (s, 0, h + start)),
            pl.BlockSpec((1, length, 256), lambda h, s: (s, 0, 3 * (h + start) + 2)),
            pl.BlockSpec((1, DV), lambda h, s: (0, 0)),
            per_unit(chunks, CHUNK, DK, start=start),
            per_unit(chunks, DK, DK, start=start),
        ],
        out_specs=[
            per_unit(chunks, CHUNK, DV),
            per_unit(length, DV),
            per_unit(chunks, DK, DV),
            per_unit(DK, DV),
            pl.BlockSpec((1, 8, DV), lambda h, s: (h, 0, 0)),
        ],
        out_shape=[
            jax.ShapeDtypeStruct((seqs, heads, chunks, CHUNK, DV), bf16),
            jax.ShapeDtypeStruct((seqs, heads, length, DV), bf16),
            jax.ShapeDtypeStruct((seqs, heads, chunks, DK, DV), f32),
            jax.ShapeDtypeStruct((seqs, heads, DK, DV), f32),
            jax.ShapeDtypeStruct((heads, 8, DV), f32),
        ],
        compiler_params=params(),
        cost_estimate=cost(4.0 * heads * seqs * chunks / 8),
        name="norm_back",
    )(places, rows, d_gated, mixer, projected, gain, qe, m)


def mixer_grads(
    places, projected, halo, logits, taps, rates, biases, q, k, v, rows, t, w, u, m, states, d_out, n, arriving, d_og,
    start=0, count=None,
):
    seqs, length, _ = projected.shape
    heads = count or rates.shape[0]
    chunks = length // CHUNK
    return pl.pallas_call(
        functools.partial(grad_kernel, start),
        grid=(heads, seqs),
        in_specs=input_specs(length, start)
        + [
            per_unit(length, DK, start=start),
            per_unit(length, DK, start=start),
            per_unit(length, DV, start=start),
            per_unit(2 * chunks, CHUNK, start=start),
            per_unit(chunks, CHUNK, CHUNK, start=start),
            per_unit(chunks, CHUNK, DK, start=start),
            per_unit(chunks, CHUNK, DV, start=start),
            per_unit(chunks, DK, DK, start=start),
            per_unit(chunks, DK, DV, start=start),
            per_unit(chunks, CHUNK, DV, start=start),
            per_unit(chunks, DK, DV, start=start),
            per_unit(DK, DV, start=start),
            per_unit(length, DV, start=start),
        ],
        out_specs=[
            pl.BlockSpec((1, length, HEAD), lambda h, s: (s, 0, h)),
            per_unit(ROWS, QKV),
            per_unit(ROWS, QKV),
            pl.BlockSpec((1, 2, chunks, CHUNK), lambda h, s: (s, h, 0, 0)),
            per_unit(chunks, CHUNK),
            pl.BlockSpec((1, 8, QKV), lambda h, s: (h, 0, 0)),
        ],
        out_shape=[
            jax.ShapeDtypeStruct((seqs, length, heads * HEAD), bf16),
            jax.ShapeDtypeStruct((seqs, heads, ROWS, QKV), f32),
            jax.ShapeDtypeStruct((seqs, heads, ROWS, QKV), f32),
            jax.ShapeDtypeStruct((seqs, 2 * heads, chunks, CHUNK), f32),
            jax.ShapeDtypeStruct((seqs, heads, chunks, CHUNK), f32),
            jax.ShapeDtypeStruct((heads, 8, QKV), f32),
        ],
        scratch_shapes=[
            pltpu.VMEM((length + ROWS, QKV), f32),
            pltpu.VMEM((length + 2 * ROWS, QKV), f32),
        ],
        compiler_params=params(),
        cost_estimate=cost(10.0 * heads * seqs * chunks / 8),
        name="mixer_grads",
    )(
        places, rates, biases, projected, projected, halo, halo, logits, taps, taps,
        q, k, v, rows, t, w, u, m, states, d_out, n, arriving, d_og,
    )


def shifted(block, axis, distance):
    devices = range(lax.axis_size(axis))
    route = [(i - distance, i) for i in devices if i - distance in devices]
    return lax.ppermute(block, axis, route)


def relay(first, maps, distance):
    arriving = shifted(first.astype(bf16), "ctx", distance)
    for _ in range(lax.axis_size("ctx") - 2):
        leaving = first + maps(arriving.astype(f32))
        arriving = shifted(leaving.astype(bf16), "ctx", distance)
    return arriving


def dot(left, right, contract=(1, 0)):
    return lax.dot_general(
        left, right, (((contract[0],), (contract[1],)), ((), ())), preferred_element_type=f32
    )


def local(
    tokens,
    proj_in,
    proj_gates,
    conv_taps,
    log_rates,
    rate_bias,
    gate_gain,
    proj_out,
    ffn_gate,
    ffn_up,
    ffn_down,
    gain_in,
    gain_ffn,
    cotangent,
):
    seqs, length, width = tokens.shape
    row_count = seqs * length
    heads = log_rates.shape[0]
    chunks = length // CHUNK
    tp_count = lax.axis_size("tp")
    tp_place = lax.axis_index("tp")
    share = length // tp_count
    with_map = lax.axis_size("ctx") > 2

    def own(rows):
        return lax.dynamic_slice_in_dim(
            rows.reshape(seqs, length, rows.shape[-1]), tp_place * share, share, 1
        )

    def scatter_sum(partial):
        partial = partial.astype(bf16).reshape(seqs, length, width)
        return lax.psum_scatter(partial, "tp", scatter_dimension=1, tiled=True).astype(f32)

    def gather_rows(rows):
        return lax.all_gather(rows, "tp", axis=1, tiled=True).reshape(row_count, width)

    whole_in = lax.all_gather(proj_in, "shard", axis=0, tiled=True)
    whole_gates = lax.all_gather(proj_gates, "shard", axis=0, tiled=True)
    whole_out = lax.all_gather(proj_out, "shard", axis=1, tiled=True)
    whole_gate = lax.all_gather(ffn_gate, "shard", axis=0, tiled=True)
    whole_up = lax.all_gather(ffn_up, "shard", axis=0, tiled=True)
    whole_down = lax.all_gather(ffn_down, "shard", axis=1, tiled=True)
    gain_in_f = lax.all_gather(gain_in, "shard", axis=0, tiled=True).astype(f32)
    gain_ffn_f = lax.all_gather(gain_ffn, "shard", axis=0, tiled=True).astype(f32)

    inputs_f = tokens.reshape(row_count, width).astype(f32)
    scale_in = lax.rsqrt(jnp.mean(inputs_f * inputs_f, -1, keepdims=True) + epsilon)
    unit_in = inputs_f * scale_in
    normed_in = (unit_in * gain_in_f).astype(bf16)
    projected = dot(normed_in, whole_in).astype(bf16).reshape(seqs, length, heads * HEAD)
    logits = dot(whole_gates, normed_in, (0, 1)).reshape(
        2 * heads, seqs, chunks, CHUNK
    )
    logits = jnp.swapaxes(logits, 0, 1)
    halo = shifted(projected[:, length - HALO :, :], "ctx", 1)
    places = jnp.arange(chunks, dtype=jnp.int32)
    q, k, v, rows, t, w, u, qe, m, b, own_out, state_end, state_map = prepare(
        places, projected, halo, logits, conv_taps, log_rates, rate_bias, with_map
    )

    def map_forward(arriving):
        return jnp.einsum("shij,shjk->shik", state_map, arriving)

    def map_back(arriving):
        return jnp.einsum("shji,shjk->shik", state_map, arriving)

    arriving = relay(state_end, map_forward, 1)
    gain_row = gate_gain.reshape(1, DV)
    gated, mixer, states = mixer_output(
        places, (rows, qe, m, b, own_out), arriving, projected, gain_row
    )
    gated = gated.reshape(row_count, heads * DV)

    middle = own(inputs_f) + scatter_sum(dot(gated, whole_out))
    scale_mid = lax.rsqrt(jnp.mean(middle * middle, -1, keepdims=True) + epsilon)
    unit_mid = middle * scale_mid
    normed_mid = gather_rows((unit_mid * gain_ffn_f).astype(bf16))
    gate_act = dot(normed_mid, whole_gate)
    up_act = dot(normed_mid, whole_up)
    gate_sig = jax.nn.sigmoid(gate_act)
    gate_silu = gate_act * gate_sig
    hidden = (gate_silu * up_act).astype(bf16)
    d_out = cotangent.reshape(row_count, width)
    d_hidden = dot(d_out, whole_down, (1, 1))
    d_gate = (d_hidden * up_act * gate_sig * (1.0 + gate_act * (1.0 - gate_sig))).astype(bf16)
    d_up = (d_hidden * gate_silu).astype(bf16)
    d_mid_norm = scatter_sum(dot(d_gate, whole_gate, (1, 1)) + dot(d_up, whole_up, (1, 1)))
    layer_rows = middle + scatter_sum(dot(hidden, whole_down))
    grad_down = dot(hidden, d_out, (0, 0))
    grad_gate = dot(normed_mid, d_gate, (0, 0))
    grad_up = dot(normed_mid, d_up, (0, 0))
    gain_ffn_part = jnp.sum(d_mid_norm * unit_mid, (0, 1))
    scaled_mid = d_mid_norm * gain_ffn_f
    d_middle = own(cotangent).astype(f32) + scale_mid * (
        scaled_mid - unit_mid * jnp.mean(scaled_mid * unit_mid, -1, keepdims=True)
    )
    d_branch = gather_rows(d_middle.astype(bf16))
    grad_out = dot(gated, d_branch, (0, 0))
    d_gated = dot(d_branch, whole_out, (1, 1)).reshape(seqs, length, heads * DV)
    d_mixer, d_og, n, d_start, gain_gate_part = norm_back(
        places, rows, d_gated, mixer, projected, gain_row, qe, m
    )
    arriving_back = relay(d_start, map_back, -1)
    d_projected, d_halo, d_tail, d_logits, rate_rows, tap_rows = mixer_grads(
        places, projected, halo, logits, conv_taps, log_rates, rate_bias,
        q, k, v, rows, t, w, u, m, states, d_mixer, n, arriving_back, d_og,
    )
    later = shifted(d_halo, "ctx", -1)
    tail = (d_tail + later).astype(bf16)
    for h in range(heads):
        d_projected = lax.dynamic_update_slice(
            d_projected, tail[:, h], (0, length - ROWS, h * HEAD)
        )
    d_projected = d_projected.reshape(row_count, heads * HEAD)
    grad_bias = jnp.sum(d_logits[:, 0::2], (0, 2, 3))
    grad_rates = jnp.sum(rate_rows, (0, 2, 3))
    d_logit_rows = jnp.swapaxes(d_logits, 0, 1).reshape(2 * heads, row_count).astype(bf16)
    grad_in = dot(normed_in, d_projected, (0, 0))
    grad_gates = dot(normed_in, d_logit_rows, (0, 1))
    in_back = dot(d_projected, whole_in, (1, 1)) + dot(d_logit_rows, whole_gates, (0, 1))
    d_in_norm = scatter_sum(in_back)
    unit_own = own(unit_in)
    scale_own = own(scale_in)
    gain_in_part = jnp.sum(d_in_norm * unit_own, (0, 1))
    scaled_in = d_in_norm * gain_in_f
    token_grad = d_middle + scale_own * (
        scaled_in - unit_own * jnp.mean(scaled_in * unit_own, -1, keepdims=True)
    )
    gain_gate_part = jnp.sum(gain_gate_part, (0, 1))
    grad_taps = jnp.swapaxes(tap_rows[:, :CONV, :], 0, 1).reshape(CONV, heads * QKV)
    grad_gain_gate, grad_gain_in, grad_gain_ffn = lax.psum(
        (gain_gate_part, gain_in_part, gain_ffn_part), "tp"
    )

    def reduced(grad, axis):
        piece = lax.psum_scatter(
            grad.astype(bf16), ("shard", "ctx"), scatter_dimension=axis, tiled=True
        )
        return lax.all_gather(piece, "ctx", axis=axis, tiled=True).astype(f32)

    sum_taps, sum_rates, sum_bias, sum_gain_gate = lax.psum(
        (grad_taps, grad_rates, grad_bias, grad_gain_gate), ("shard", "ctx")
    )
    return (
        layer_rows.astype(bf16),
        token_grad,
        reduced(grad_in, 0),
        reduced(grad_gates, 0),
        sum_taps,
        sum_rates,
        sum_bias,
        sum_gain_gate,
        reduced(grad_out, 1),
        reduced(grad_gate, 0),
        reduced(grad_up, 0),
        reduced(grad_down, 1),
        reduced(grad_gain_in, 0),
        reduced(grad_gain_ffn, 0),
    )


def ffn_kernel(part_a, part_b, d_rows, weights, *refs):
    rows_out, hidden_out, d_pair_out, back_a, back_b, down_a, down_b = refs[-7:]
    units = weights.shape[1] // 3
    main = units // 128 * 128
    pair, down = weights.at[:, : 2 * units], weights.at[:, 2 * units :]
    half = part_a.shape[0]
    rows = jnp.concatenate([part_a[...], part_b[...]], axis=0)
    rows_out[...] = rows
    acts = mm(rows, pair[...])
    d_hidden = mm(d_rows[...], down[...])

    def through_gate(gate_act, up_act, d_act):
        sig = sigmoid(gate_act)
        swish = gate_act * sig
        d_gate = d_act * up_act * sig * (1.0 + gate_act * (1.0 - sig))
        return (swish * up_act).astype(bf16), d_gate.astype(bf16), (d_act * swish).astype(bf16)

    hidden, d_gate, d_up = through_gate(acts[:, :main], acts[:, main : 2 * main], d_hidden[:, :main])
    d_pair = [d_gate, d_up]
    if units > main:
        last = 2 * main + units - main
        tail, d_gate, d_up = through_gate(
            acts[:, 2 * main : last], acts[:, last:], d_hidden[:, main:]
        )
        hidden = jnp.concatenate([hidden, tail], axis=1)
        d_pair = d_pair + [d_gate, d_up]
    hidden_out[...] = hidden
    d_pair = jnp.concatenate(d_pair, axis=1)
    d_pair_out[...] = d_pair
    back = mm(d_pair, pair[...], (1, 1)).astype(bf16)
    through = mm(hidden, down[...], (1, 1)).astype(bf16)
    back_a[...] = back[:half]
    back_b[...] = back[half:]
    down_a[...] = through[:half]
    down_b[...] = through[half:]


def paired(gate, up):
    main = gate.shape[1] // 128 * 128
    return jnp.concatenate([gate[:, :main], up[:, :main], gate[:, main:], up[:, main:]], axis=1)


def unpaired(pair):
    units = pair.shape[1] // 2
    main = units // 128 * 128
    last = main + units
    gate = jnp.concatenate([pair[:, :main], pair[:, 2 * main : last]], axis=1)
    return gate, jnp.concatenate([pair[:, main : 2 * main], pair[:, last:]], axis=1)


def feed_forward(part_a, part_b, d_rows, weights, carried):
    half, width = part_a.shape
    units = weights.shape[1] // 3
    index = 1 if carried else 0

    def whole(*shape):
        return pl.BlockSpec(shape, lambda i: (0, 0))

    def placed(columns):
        return pl.BlockSpec((2 * half, columns), lambda i: (index, 0))

    return pl.pallas_call(
        ffn_kernel,
        grid=(1,),
        in_specs=[
            whole(half, width), whole(half, width), placed(width), whole(*weights.shape),
        ]
        + [pl.BlockSpec(memory_space=pl.ANY)] * len(carried),
        out_specs=[placed(width), placed(units), placed(2 * units)] + [whole(half, width)] * 4,
        out_shape=[
            jax.ShapeDtypeStruct((4 * half, columns), bf16) for columns in (width, units, 2 * units)
        ]
        + [jax.ShapeDtypeStruct((half, width), bf16)] * 4,
        input_output_aliases={4 + i: i for i in range(len(carried))},
        compiler_params=pltpu.CompilerParams(
            dimension_semantics=("arbitrary",), vmem_limit_bytes=56 * 1024 * 1024
        ),
        cost_estimate=cost(9.0),
        name="feed_forward",
    )(part_a, part_b, d_rows, weights, *carried)


def input_back_kernel(d_first, d_last, d_logits, weights, gates, *outs):
    split = d_first.shape[1]
    total = (
        mm(d_first[...], weights[:, :split], (1, 1))
        + mm(d_last[...], weights[:, split : 2 * split], (1, 1))
        + mm(d_logits[...], gates[...], (0, 0))
    ).astype(bf16)
    for i, out in enumerate(outs):

        @pl.when(pl.program_id(0) == i)
        def _(out=out):
            out[...] = total


def input_back(d_first, d_last, d_logits, weights, gates):
    full = d_first.shape[0]
    count = full // 4
    width = weights.shape[0]

    def whole(array):
        return pl.BlockSpec(array.shape, lambda i: (0, 0))

    return pl.pallas_call(
        input_back_kernel,
        grid=(4,),
        in_specs=[
            pl.BlockSpec((count, d_first.shape[1]), lambda i: (i, 0)),
            pl.BlockSpec((count, d_last.shape[1]), lambda i: (i, 0)),
            pl.BlockSpec((d_logits.shape[0], count), lambda i: (0, i)),
            whole(weights),
            whole(gates),
        ],
        out_specs=[pl.BlockSpec((count, width), lambda i: (0, 0))] * 4,
        out_shape=[jax.ShapeDtypeStruct((count, width), bf16)] * 4,
        compiler_params=pltpu.CompilerParams(
            dimension_semantics=("arbitrary",), vmem_limit_bytes=56 * 1024 * 1024
        ),
        cost_estimate=cost(5.0),
        name="input_back",
    )(d_first, d_last, d_logits, weights, gates)


def ffn_grads_kernel(rows, d_pair, d_rows, hidden, out):
    out[...] = jnp.concatenate(
        [mm(rows[...], d_pair[...], (0, 0)), mm(d_rows[...], hidden[...], (0, 0))], axis=1
    ).astype(bf16)


def ffn_grads(rows, d_pair, d_rows, hidden):
    full, width = rows.shape
    count = width // 4
    wide = d_pair.shape[1] + hidden.shape[1]

    def columns():
        return pl.BlockSpec((full, count), lambda i: (0, i))

    def whole(array):
        return pl.BlockSpec(array.shape, lambda i: (0, 0))

    return pl.pallas_call(
        ffn_grads_kernel,
        grid=(4,),
        in_specs=[columns(), whole(d_pair), columns(), whole(hidden)],
        out_specs=pl.BlockSpec((count, wide), lambda i: (i, 0)),
        out_shape=jax.ShapeDtypeStruct((width, wide), bf16),
        compiler_params=pltpu.CompilerParams(
            dimension_semantics=("arbitrary",), vmem_limit_bytes=56 * 1024 * 1024
        ),
        cost_estimate=cost(10.0),
        name="ffn_grads",
    )(rows, d_pair, d_rows, hidden)


def both_grads_kernel(rows, d_rows, weights, part_0, part_1, part_2, part_3, gated, out, sums):
    grad = mm(rows[...], d_rows[...], (0, 0))
    columns = jnp.sum(grad * weights[...].astype(f32), -1, keepdims=True)
    lanes = jnp.concatenate([columns, jnp.zeros((columns.shape[0], 127), f32)], axis=1)
    sums[...] = jnp.transpose(lanes)[0:8]
    branch = jnp.concatenate([part_0[...], part_1[...], part_2[...], part_3[...]], axis=0)
    out[...] = jnp.concatenate([grad, mm(branch, gated[...], (0, 0))], axis=1).astype(bf16)


def both_grads(rows, d_rows, weights, parts, gated):
    full, width = rows.shape
    columns = d_rows.shape[1]
    count = width // 4
    wide = columns + gated.shape[1]
    return pl.pallas_call(
        both_grads_kernel,
        grid=(4,),
        in_specs=[
            pl.BlockSpec((full, count), lambda i: (0, i)),
            pl.BlockSpec((full, columns), lambda i: (0, 0)),
            pl.BlockSpec((count, columns), lambda i: (i, 0)),
        ]
        + [pl.BlockSpec((parts[0].shape[0], count), lambda i: (0, i))] * 4
        + [pl.BlockSpec(gated.shape, lambda i: (0, 0))],
        out_specs=[
            pl.BlockSpec((count, wide), lambda i: (i, 0)),
            pl.BlockSpec((8, count), lambda i: (0, i)),
        ],
        out_shape=[
            jax.ShapeDtypeStruct((width, wide), bf16),
            jax.ShapeDtypeStruct((8, width), f32),
        ],
        compiler_params=pltpu.CompilerParams(
            dimension_semantics=("arbitrary",), vmem_limit_bytes=56 * 1024 * 1024
        ),
        cost_estimate=cost(8.0),
        name="both_grads",
    )(rows, d_rows, weights, *parts, gated)


def input_grad_kernel(
    shard, rows, d_rows, weights, left_a, left_b, left_send, right_a, right_b, right_send, part
):
    grad = mm(rows[...], d_rows[...], (0, 0))
    sums = jnp.sum(grad * weights[...].astype(f32), -1, keepdims=True)
    lanes = jnp.concatenate([sums, jnp.zeros((sums.shape[0], 127), f32)], axis=1)
    part[...] = jnp.transpose(lanes)[0:8]
    low = grad.astype(bf16)
    count = low.shape[0]
    cut = left_a.shape[1]
    left, right = low[:, :cut], low[:, cut:]
    step = pl.program_id(0)

    @pl.when(step == 0)
    def _():
        left_a[...] = left
        right_a[...] = right

    @pl.when(step == 1)
    def _():
        left_send[:count] = left
        right_b[...] = right

    @pl.when(step == 2)
    def _():
        left_b[...] = left
        right_send[:count] = right

    @pl.when(step == 3)
    def _():
        left_send[count:] = left
        right_send[count:] = right


def input_grad(shard, rows, d_rows, weights, head):
    full, width = rows.shape
    columns = d_rows.shape[1]
    count = width // 4
    cut = columns // 256 * 128

    def whole(*shape):
        return pl.BlockSpec(shape, lambda i, place: (0, 0))

    shapes = [
        (count, cut), (count, cut), (2 * count, cut),
        (count, columns - cut), (count, columns - cut), (2 * count, columns - cut),
    ]
    return pl.pallas_call(
        input_grad_kernel,
        grid_spec=pltpu.PrefetchScalarGridSpec(
            num_scalar_prefetch=1,
            grid=(4,),
            in_specs=[
                pl.BlockSpec((full, count), lambda i, place: (0, place[0] ^ i)),
                whole(full, columns),
                pl.BlockSpec((count, columns), lambda i, place: (place[0] ^ i, head)),
            ],
            out_specs=[whole(*shape) for shape in shapes]
            + [pl.BlockSpec((8, count), lambda i, place: (0, place[0] ^ i))],
        ),
        out_shape=[jax.ShapeDtypeStruct(shape, bf16) for shape in shapes]
        + [jax.ShapeDtypeStruct((8, width), f32)],
        compiler_params=pltpu.CompilerParams(
            dimension_semantics=("arbitrary",), vmem_limit_bytes=56 * 1024 * 1024
        ),
        cost_estimate=cost(4.0),
        name="input_grad",
    )(shard, rows, d_rows, weights)


def branch_back_kernel(
    places, rows, part_0, part_1, part_2, part_3, weights, mixer, og, gain, qe, m,
    d_out, d_og_out, n_out, start_out, gain_out, d_gated,
):
    count = part_0.shape[0]
    for i, part in enumerate((part_0, part_1, part_2, part_3)):
        d_gated[0, i * count : (i + 1) * count, :] = mm(part[...], weights[...])
    norm_back_kernel(
        places, rows, d_gated, mixer, og, gain, qe, m, d_out, d_og_out, n_out, start_out, gain_out
    )


def branch_back(places, rows, parts, weights, mixer, projected, gain, qe, m):
    seqs, heads, chunks = qe.shape[:3]
    length = chunks * CHUNK
    count, width = parts[0].shape
    return pl.pallas_call(
        branch_back_kernel,
        grid=(heads, seqs),
        in_specs=[
            smem(),
            per_unit(2 * chunks, CHUNK),
        ]
        + [pl.BlockSpec((count, width), lambda h, s: (0, 0))] * 4
        + [
            pl.BlockSpec((width, DV), lambda h, s: (0, h)),
            pl.BlockSpec((1, length, DV), lambda h, s: (s, 0, h)),
            pl.BlockSpec((1, length, 256), lambda h, s: (s, 0, 3 * h + 2)),
            pl.BlockSpec((1, DV), lambda h, s: (0, 0)),
            per_unit(chunks, CHUNK, DK),
            per_unit(chunks, DK, DK),
        ],
        out_specs=[
            per_unit(chunks, CHUNK, DV),
            per_unit(length, DV),
            per_unit(chunks, DK, DV),
            per_unit(DK, DV),
            pl.BlockSpec((1, 8, DV), lambda h, s: (h, 0, 0)),
        ],
        out_shape=[
            jax.ShapeDtypeStruct((seqs, heads, chunks, CHUNK, DV), bf16),
            jax.ShapeDtypeStruct((seqs, heads, length, DV), bf16),
            jax.ShapeDtypeStruct((seqs, heads, chunks, DK, DV), f32),
            jax.ShapeDtypeStruct((seqs, heads, DK, DV), f32),
            jax.ShapeDtypeStruct((heads, 8, DV), f32),
        ],
        scratch_shapes=[pltpu.VMEM((1, length, DV), f32)],
        compiler_params=params(),
        cost_estimate=cost(5.0 * heads),
        name="branch_back",
    )(places, rows, *parts, weights, mixer, projected, gain, qe, m)


def widened(block):
    return jnp.pad(block, ((0, 0), (0, -block.shape[1] % 128)))


def local_paired(
    tokens,
    proj_in,
    proj_gates,
    conv_taps,
    log_rates,
    rate_bias,
    gate_gain,
    proj_out,
    ffn_gate,
    ffn_up,
    ffn_down,
    gain_in,
    gain_ffn,
    cotangent,
):
    seqs, length, width = tokens.shape
    heads = log_rates.shape[0]
    units = ffn_gate.shape[1]
    core = lax.axis_index("ctx")
    place = lax.axis_index("tp")
    shard = lax.axis_index("shard")
    tp_count = lax.axis_size("tp")
    shards = lax.axis_size("shard")
    seq = place // 2
    half = place % 2
    quarter = length // 2
    share = length // tp_count
    full = 2 * length
    chunks = full // CHUNK
    route = []
    for j in range(tp_count):
        route.append((j, (j % 2) * tp_count + j // 2))
        route.append((tp_count + j, (j % 2) * tp_count + 2 + j // 2))
    route_back = [(b, a) for a, b in route]
    pairs = [(i, i ^ 1) for i in range(tp_count)]
    pairs_x = [(i, i ^ 1) for i in range(shards)]
    pairs_y = [(i, i ^ 2) for i in range(shards)]
    odd_x = shard % 2 == 1
    odd_y = shard // 2 == 1

    def hold(*values):
        return lax.optimization_barrier(values)

    def swap_core(block):
        with jax.named_scope("swap_core"):
            return lax.ppermute(block, "ctx", [(0, 1), (1, 0)])

    def swap_chip(block):
        with jax.named_scope("swap_chip"):
            return lax.ppermute(block, "tp", pairs)

    def swap_x(block):
        with jax.named_scope("swap_x"):
            return lax.ppermute(block, "shard", pairs_x)

    def swap_y(block):
        with jax.named_scope("swap_y"):
            return lax.ppermute(block, "shard", pairs_y)

    def to_users(block):
        with jax.named_scope("to_users"):
            return lax.ppermute(block, ("ctx", "tp"), route)

    def to_owners(block):
        with jax.named_scope("to_owners"):
            return lax.ppermute(block, ("ctx", "tp"), route_back)

    def both_cores(block):
        return block.astype(f32) + swap_core(block).astype(f32)

    def add(kept, got):
        return (kept.astype(f32) + got.astype(f32)).astype(bf16)

    def group_rows(mine, got):
        return jnp.concatenate(
            [mine[:quarter], got[:quarter], mine[quarter:], got[quarter:]], axis=0
        )

    def own_rows(rows):
        sequence = lax.dynamic_index_in_dim(rows, seq, 0, keepdims=False)
        mine = lax.dynamic_slice_in_dim(sequence, half * quarter, quarter, 0)
        other = lax.dynamic_slice_in_dim(sequence, (1 - half) * quarter, quarter, 0)
        return jnp.concatenate([mine, other], axis=0)

    def swap_sides(mine):
        return swap_x(mine), swap_y(mine)

    def swap_fourth(from_x, from_y):
        count = from_x.shape[0] // 2
        return swap_x(from_y[:count]), swap_y(from_x[count:])

    def ordered(odd, mine, theirs):
        return jnp.concatenate([jnp.where(odd, theirs, mine), jnp.where(odd, mine, theirs)], axis=0)

    def assembled(mine, sides, fourth):
        across = jnp.concatenate(fourth, axis=0)
        return ordered(
            odd_y, ordered(odd_x, mine, sides[0]), ordered(odd_x, sides[1], across)
        )

    def blocks(grad, *places_xor):
        rows = grad.shape[0] // shards
        return jnp.concatenate(
            [lax.dynamic_slice_in_dim(grad, (shard ^ p) * rows, rows, 0) for p in places_xor],
            axis=0,
        )

    def scatter_first(grad):
        cut = grad.shape[1] // 256 * 128
        left, right = grad[:, :cut], grad[:, cut:]
        return (
            blocks(left, 0, 2),
            swap_x(blocks(left, 1, 3)),
            blocks(right, 0, 1),
            swap_y(blocks(right, 2, 3)),
        )

    def scatter_second(left, left_got, right, right_got):
        rows = left.shape[0] // 2
        left = add(left, left_got)
        right = add(right, right_got)
        return left[:rows], swap_y(left[rows:]), right[:rows], swap_x(right[rows:])

    def scatter_end(left, left_got, right, right_got):
        return jnp.concatenate([add(left, left_got), add(right, right_got)], axis=1)

    def quarters(rows, weights):
        return [
            dot(rows[i * quarter : (i + 1) * quarter], weights, (1, 1)) for i in (3, 2, 1, 0)
        ]

    def piece_first(left_a, left_b, left_send, right_a, right_b, right_send):
        return left_a, left_b, swap_x(left_send), right_a, right_b, swap_y(right_send)

    def piece_second(left_a, left_b, left_got, right_a, right_b, right_got):
        rows = left_a.shape[0]
        left_on = swap_y(add(left_b, left_got[rows:]))
        right_on = swap_x(add(right_b, right_got[rows:]))
        return left_a, left_got, left_on, right_a, right_got, right_on

    def piece_end(left_a, left_got, left_on, right_a, right_got, right_on):
        rows = left_a.shape[0]

        def total(mine, got, on):
            return (mine.astype(f32) + got[:rows].astype(f32) + on.astype(f32)).astype(bf16)

        return jnp.concatenate(
            [total(left_a, left_got, left_on), total(right_a, right_got, right_on)], axis=1
        )

    small = jnp.concatenate(
        [
            conv_taps.astype(f32),
            jnp.pad(jnp.stack([log_rates, rate_bias]), ((0, 2), (0, conv_taps.shape[1] - heads))),
        ],
        axis=0,
    )
    inner = heads * HEAD
    block = proj_in.shape[0]
    gates_block = jnp.pad(
        proj_gates.T, ((0, 16 - 2 * heads), (0, inner - block))
    )
    mine_in = to_users(jnp.concatenate([proj_in, gates_block], axis=0))
    mine_rows = own_rows(tokens)
    got_rows = swap_core(mine_rows)
    gains = lax.all_gather(jnp.stack([gain_in, gain_ffn]), "shard", axis=1, tiled=True)
    mine_d = own_rows(cotangent)
    got_d = swap_core(mine_d)
    mine_pair = paired(ffn_gate, ffn_up)
    mine_in, mine_rows, got_rows, gains, mine_d, got_d, small, mine_out, mine_pair, mine_down = hold(
        mine_in, mine_rows, got_rows, gains, mine_d, got_d, small, proj_out.T, mine_pair,
        ffn_down.T,
    )
    in_sides = swap_sides(mine_in)
    small = to_users(small)
    mine_out = to_users(mine_out)
    mine_down = to_users(mine_down)
    gains = gains.astype(f32)
    gain_in_f, gain_ffn_f = gains[0:1], gains[1:2]
    inputs_f = group_rows(mine_rows, got_rows).astype(f32)
    scale_in = lax.rsqrt(jnp.mean(inputs_f * inputs_f, -1, keepdims=True) + epsilon)
    normed_in = (inputs_f * scale_in * gain_in_f).astype(bf16)
    d_out = group_rows(mine_d, got_d)
    in_sides, small, mine_out, normed_in, d_out, mine_pair, mine_down = hold(
        in_sides, small, mine_out, normed_in, d_out, mine_pair, mine_down
    )
    in_fourth = swap_fourth(*in_sides)
    mine_pair = to_users(mine_pair)
    whole_out = lax.all_gather(mine_out, "shard", axis=0, tiled=True)
    in_fourth, normed_in = hold(in_fourth, normed_in)
    whole_in = assembled(
        mine_in[:block],
        [side[:block] for side in in_sides],
        [jnp.concatenate(in_fourth, axis=0)[:block]],
    )
    gate_rows = [
        rows_of[block : block + 8, :block]
        for rows_of in (mine_in, *in_sides, jnp.concatenate(in_fourth, axis=0))
    ]

    def side_by_side(odd, mine, theirs):
        return jnp.concatenate(
            [jnp.where(odd, theirs, mine), jnp.where(odd, mine, theirs)], axis=1
        )

    gates_rows = side_by_side(
        odd_y,
        side_by_side(odd_x, gate_rows[0], gate_rows[1]),
        side_by_side(odd_x, gate_rows[2], gate_rows[3]),
    )
    projected = dot(normed_in, whole_in).astype(bf16).reshape(1, full, inner)
    logits = dot(gates_rows, normed_in, (1, 1))[: 2 * heads]
    logits = logits.reshape(1, 2 * heads, chunks, CHUNK)
    projected, logits, gates_rows, mine_ffn = hold(
        projected, logits, gates_rows, jnp.concatenate([mine_pair, mine_down], axis=1)
    )
    weights_ffn = lax.all_gather(mine_ffn, "shard", axis=0, tiled=True)

    taps = small[:CONV]
    log_rates_here, rate_bias_here = small[CONV, :heads], small[CONV + 1, :heads]
    halo = jnp.zeros((1, HALO, inner), bf16)
    chunk = jnp.arange(chunks, dtype=jnp.int32)
    per_quarter = quarter // CHUNK
    true_quarter = chunk // per_quarter
    places = (
        2 * ((true_quarter % 2) ^ half) + ((true_quarter // 2) ^ core)
    ) * per_quarter + chunk % per_quarter
    no_state = jnp.zeros((1, heads, DK, DV), f32)
    gain_row = gate_gain.reshape(1, DV)
    source = (projected, halo, logits, taps, log_rates_here, rate_bias_here)
    prepared = prepare(places, *source, False)[:11]
    q, k, v, rows, t, w, u, qe, m, b, own_out = prepared
    gated, mixer, states = mixer_output(
        places, (rows, qe, m, b, own_out), no_state, projected, gain_row
    )
    gated = gated.reshape(full, heads * DV)
    far_b, far_a, near_b, near_a = quarters(gated, whole_out)
    far_got = swap_core(far_b.astype(bf16))
    near_got = swap_core(near_b.astype(bf16))
    far_sum, near_a, near_got = hold(add(far_a, far_got), near_a, near_got)
    far_sum = swap_chip(far_sum)
    middle = inputs_f[:quarter] + (near_a + near_got.astype(f32) + far_sum.astype(f32))
    scale_mid = lax.rsqrt(jnp.mean(middle * middle, -1, keepdims=True) + epsilon)
    unit_mid = middle * scale_mid

    mine_mid = (unit_mid * gain_ffn_f).astype(bf16)
    far_mid = swap_chip(mine_mid)
    near_mid = swap_core(mine_mid)
    near = feed_forward(mine_mid, near_mid, d_out, weights_ffn, ())
    far_mid, near = hold(far_mid, near)
    near_a, near_b, near_down_a, near_down_b = near[3:]
    near_got = swap_core(near_b)
    far = feed_forward(
        far_mid, swap_core(far_mid), d_out, weights_ffn, tuple(near[:3])
    )
    normed_mid, hidden, d_pair, far_a, far_b, far_down_a, far_down_b = far
    far_got = swap_core(far_b)
    far_sum, near_got, normed_mid, hidden, d_pair = hold(
        add(far_a, far_got), near_got, normed_mid, hidden, d_pair
    )
    far_sum = swap_chip(far_sum)
    far_down_got = swap_core(far_down_b)
    near_down_got = swap_core(near_down_b)
    grad_ffn = ffn_grads(normed_mid, d_pair, d_out, hidden)
    far_sum, grad_ffn, far_down_got, near_down_got = hold(
        far_sum, grad_ffn, far_down_got, near_down_got
    )
    piece_ffn = lax.psum_scatter(grad_ffn, "shard", scatter_dimension=0, tiled=True)
    d_mid_norm = near_a.astype(f32) + near_got.astype(f32) + far_sum.astype(f32)
    scaled_mid = d_mid_norm * gain_ffn_f
    d_middle = d_out[:quarter].astype(f32) + scale_mid * (
        scaled_mid - unit_mid * jnp.mean(scaled_mid * unit_mid, -1, keepdims=True)
    )
    d_low = d_middle.astype(bf16)
    far_low = swap_chip(d_low)
    near_low = swap_core(d_low)
    far_low, near_low, far_down_a, far_down_got = hold(
        far_low, near_low, far_down_a, far_down_got
    )
    d_parts = (d_low, near_low, far_low, swap_core(far_low))

    far_down_sum = swap_chip(add(far_down_a, far_down_got))
    branch = branch_back(places, rows, d_parts, whole_out, mixer, projected, gain_row, qe, m)
    branch, gated = hold(branch, gated)
    d_mixer, d_og, n, _, gain_gate_part = branch

    def head_grads(h, d_mixer):
        d_projected, _, _, d_logits, rate_rows, tap_rows = mixer_grads(
            places, *source, q, k, v, rows, t, w, u, m, states, d_mixer, n, no_state, d_og,
            start=h, count=1,
        )
        return d_projected.reshape(full, HEAD), d_logits, rate_rows, tap_rows

    even = half == 0
    first = seq == 0
    send_a = [(0, 0), (1, 2), (2, 1), (3, 3)]
    send_b = [(0, 1), (1, 3), (2, 0), (3, 2)]

    def to_outputs(mine):
        low, high = mine[:share], mine[share:]
        with jax.named_scope("to_outputs"):
            got_a = lax.ppermute(jnp.where(first, low, high), "tp", send_a)
            got_b = lax.ppermute(jnp.where(first, high, low), "tp", send_b)
        return got_a, got_b

    def stacked(got_a, got_b):
        return jnp.stack([jnp.where(even, got_a, got_b), jnp.where(even, got_b, got_a)])

    place_x = shard.reshape(1).astype(jnp.int32)
    first_head = head_grads(0, d_mixer)
    first_head, d_mixer, far_down_sum = hold(first_head, d_mixer, far_down_sum)
    grad_both, part_first = both_grads(normed_in, first_head[0], whole_in, d_parts, gated)
    grad_both, part_first, d_mixer, piece_ffn = hold(grad_both, part_first, d_mixer, piece_ffn)
    owned_pair = to_owners(piece_ffn[:, : 2 * hidden.shape[1]])
    piece_both = lax.psum_scatter(grad_both, "shard", scatter_dimension=0, tiled=True)
    layer_rows = (
        middle
        + near_down_a.astype(f32)
        + near_down_got.astype(f32)
        + far_down_sum.astype(f32)
    ).astype(bf16)

    last_head, owned_pair = hold(head_grads(1, d_mixer), owned_pair)

    owned_down = to_owners(piece_ffn[:, 2 * hidden.shape[1] :])
    *sent, part_last = input_grad(place_x, normed_in, last_head[0], whole_in, 1)
    sent, part_last, last_head, owned_down, layer_rows = hold(
        sent, part_last, last_head, owned_down, layer_rows
    )
    steps_last = piece_first(*sent)
    layer_got = to_outputs(layer_rows)
    logits_first = first_head[1].reshape(2, full)
    logits_last = last_head[1].reshape(2, full)
    d_logit_rows = jnp.concatenate(
        [logits_first, logits_last, jnp.zeros((8 - 2 * heads, full), f32)], axis=0
    ).astype(bf16)
    grad_gates = dot(d_logit_rows, normed_in)
    packed = jnp.concatenate(
        [
            jnp.concatenate([first_head[3][0], last_head[3][0]], axis=1),
            grad_gates,
            part_first + part_last + gates_rows.astype(f32) * grad_gates,
            jnp.concatenate(
                [
                    gain_gate_part[0], gain_gate_part[1], first_head[2][0, 0], last_head[2][0, 0],
                    first_head[1][0, 0], last_head[1][0, 0],
                ],
                axis=1,
            ),
        ],
        axis=0,
    )
    packed_got = swap_x(packed)
    backs = input_back(first_head[0], last_head[0], d_logit_rows, whole_in, gates_rows)
    backs, steps_last, layer_got, packed, packed_got, piece_both = hold(
        backs, steps_last, layer_got, packed, packed_got, piece_both
    )
    owned_both = to_owners(piece_both)
    near_a, near_b, far_a, far_b = backs
    far_got = swap_core(far_b)
    near_got = swap_core(near_b)
    steps_last = piece_second(*steps_last)
    packed = packed + packed_got
    packed_got = swap_y(packed)
    (
        far_sum, near_got, near_a, steps_last, packed, packed_got, owned_pair, owned_down, owned_both,
    ) = hold(
        add(far_a, far_got), near_got, near_a, steps_last, packed, packed_got, owned_pair,
        owned_down, owned_both,
    )
    far_sum = swap_chip(far_sum)
    piece_last = piece_end(*steps_last)
    packed = packed + packed_got
    sum_pair = both_cores(owned_pair)
    sum_gate, sum_up = unpaired(sum_pair)
    far_sum, sum_gate, sum_up, near_a, owned_down, layer_got, piece_last, packed, owned_both = hold(
        far_sum, sum_gate, sum_up, near_a, owned_down, layer_got, piece_last, packed, owned_both
    )
    piece_last = to_owners(piece_last)
    packed = to_owners(packed)
    d_in_norm = near_a.astype(f32) + near_got.astype(f32) + far_sum.astype(f32)
    unit_in = (inputs_f * scale_in)[:quarter]
    scaled_in = d_in_norm * gain_in_f
    token_rows = d_middle + scale_in[:quarter] * (
        scaled_in - unit_in * jnp.mean(scaled_in * unit_in, -1, keepdims=True)
    )
    token_got = to_outputs(token_rows.astype(bf16))
    packed = both_cores(packed)
    sum_down = both_cores(owned_down).T
    layer_out = stacked(*layer_got)
    sum_both = both_cores(owned_both)
    sum_out = sum_both[:, HEAD:].T
    sum_last = both_cores(piece_last)

    part_ffn = jnp.sum(ffn_gate.astype(f32) * sum_gate + ffn_up.astype(f32) * sum_up, 1)
    sum_taps, sum_gates, part_in, rest = (packed[8 * i : 8 * i + 8] for i in range(4))
    sum_gain = jnp.sum(rest[:, :DV] + rest[:, DV : 2 * DV], 0)
    sum_rates = jnp.sum(rest[:, 2 * DV :].reshape(8, 2 * heads, CHUNK), (0, 2))
    rows_here = gain_in.shape[0]

    def own_block(rows_of):
        return lax.dynamic_slice_in_dim(rows_of, shard * rows_here, rows_here, -1)

    over_blocks = jnp.concatenate([sum_gain, jnp.sum(own_block(part_in), 0), part_ffn])
    over_blocks = jnp.pad(over_blocks, (0, -over_blocks.shape[0] % 1024)).reshape(-1, 128)
    over_blocks = over_blocks + swap_chip(over_blocks)
    with jax.named_scope("swap_pair"):
        other_pair = lax.ppermute(over_blocks, "tp", [(i, i ^ 2) for i in range(tp_count)])
    over_blocks = (over_blocks + other_pair).reshape(-1)
    return (
        layer_out,
        stacked(*token_got).astype(f32),
        jnp.concatenate([sum_both[:, :HEAD], sum_last], axis=1),
        own_block(sum_gates)[: 2 * heads].T,
        sum_taps[:CONV],
        sum_rates[:heads],
        sum_rates[heads:],
        over_blocks[:DV],
        sum_out,
        sum_gate,
        sum_up,
        sum_down,
        over_blocks[DV : DV + rows_here] / gain_in.astype(f32),
        over_blocks[DV + rows_here : DV + 2 * rows_here] / gain_ffn.astype(f32),
    )


def solution(mesh):
    placed = (
        P("shard", "ctx", None),
        P("shard", "tp"),
        P("shard", "tp"),
        P(None, "tp"),
        P("tp"),
        P("tp"),
        P(),
        P("tp", "shard"),
        P("shard", "tp"),
        P("shard", "tp"),
        P("tp", "shard"),
        P("shard"),
        P("shard"),
        P("shard", "ctx", None),
    )
    shape = dict(mesh.shape)
    paired = (shape["shard"], shape["ctx"], shape["tp"]) == (4, 2, 4)

    def body(*arrays):
        seqs, length, _ = arrays[0].shape
        heads = arrays[4].shape[0]
        if paired and seqs == 2 and heads == 2 and length % (2 * CHUNK) == 0:
            return local_paired(*arrays)
        return local(*arrays)

    return jax.shard_map(
        body,
        mesh=mesh,
        in_specs=placed,
        out_specs=(
            P("shard", ("ctx", "tp"), None),
            P("shard", ("ctx", "tp"), None),
            P("shard", "tp"),
            P("shard", "tp"),
            P(None, "tp"),
            P("tp"),
            P("tp"),
            P(),
            P("tp", "shard"),
            P("shard", "tp"),
            P("shard", "tp"),
            P("tp", "shard"),
            P("shard"),
            P("shard"),
        ),
        check_vma=False,
    )
```

```python
import functools

import jax
import jax.numpy as jnp
from jax import lax
from jax.experimental import pallas as pl
from jax.experimental.pallas import tpu as pltpu
from jax.sharding import PartitionSpec as P

DK = 128
DV = 256
QKV = 2 * DK + DV
HEAD = QKV + DV
CONV = 4
CHUNK = 128
HALO = 16
ROWS = 8

epsilon = 1e-06
f32 = jnp.float32
bf16 = jnp.bfloat16


def mm(left, right, contract=(1, 0)):
    return lax.dot_general(
        left.astype(bf16),
        right.astype(bf16),
        (((contract[0],), (contract[1],)), ((), ())),
        preferred_element_type=f32,
    )


def mm_split(left, right):
    left_hi = left.astype(bf16)
    right_hi = right.astype(bf16)
    left_lo = left - left_hi.astype(f32)
    right_lo = right - right_hi.astype(f32)
    return mm(left_hi, right_hi) + (mm(left_hi, right_lo) + mm(left_lo, right_hi))


def mm_exact(left, right):
    return lax.dot_general(
        left,
        right,
        (((1,), (0,)), ((), ())),
        precision=lax.Precision.HIGHEST,
        preferred_element_type=f32,
    )


def iotas():
    row = lax.broadcasted_iota(jnp.int32, (CHUNK, CHUNK), 0)
    col = lax.broadcasted_iota(jnp.int32, (CHUNK, CHUNK), 1)
    return row, col


def pad_rows(block):
    missing = CHUNK - block.shape[0]
    return jnp.concatenate([block, jnp.zeros((missing, block.shape[1]), f32)], axis=0)


def softplus(values):
    return jnp.maximum(values, 0.0) + jnp.log1p(jnp.exp(-jnp.abs(values)))


def sigmoid(values):
    return 1.0 / (1.0 + jnp.exp(-values))


def place_of(places, c):
    return pl.ds(pl.multiple_of(places[c] * CHUNK, CHUNK), CHUNK)


def chunk_rows(places, logit_ref, chunks):
    def stacked(row):
        return jnp.concatenate(
            [logit_ref[0, row, pl.ds(places[c], 1), :] for c in range(chunks)], axis=0
        )

    return stacked(0), stacked(1)


def invert_units(lowers, row, col):
    eye = (row == col).astype(f32)
    same = (row // 16) == (col // 16)
    powers = [jnp.where(same, n, 0.0) for n in lowers]
    inverses = [eye - p for p in powers]
    for _ in range(3):
        powers = [mm_split(p, p) for p in powers]
        inverses = [x + mm_split(x, p) for x, p in zip(inverses, powers)]
    size = 16
    while size < CHUNK:
        joins = ((row // (2 * size)) == (col // (2 * size))) & ((row // size) != (col // size))
        middles = [mm_split(jnp.where(joins, n, 0.0), x) for n, x in zip(lowers, inverses)]
        inverses = [x - mm_split(x, m) for x, m in zip(inverses, middles)]
        size *= 2
    return inverses


def conv_into(places, scratch, x_qk, x_v, halo_qk, halo_v, taps_qk, taps_v, length):
    scratch[0:ROWS, 0 : 2 * DK] = halo_qk[0, HALO - ROWS :, :].astype(f32)
    scratch[0:ROWS, 2 * DK :] = halo_v[0, HALO - ROWS :, :].astype(f32)
    for c in range(length // CHUNK):
        body = slice(ROWS + c * CHUNK, ROWS + (c + 1) * CHUNK)
        scratch[body, 0 : 2 * DK] = x_qk[0, place_of(places, c), :].astype(f32)
        scratch[body, 2 * DK :] = x_v[0, place_of(places, c), :].astype(f32)
    taps = jnp.concatenate([taps_qk[...], taps_v[...]], axis=1).astype(f32)
    first = ROWS - CONV + 1
    mixed = taps[0:1, :] * scratch[first : first + length, :]
    for j in range(1, CONV):
        mixed = mixed + taps[j : j + 1, :] * scratch[first + j : first + j + length, :]
    return mixed, taps


def prep_kernel(
    places, rates, biases, x_qk, x_v, halo_qk, halo_v, logits, taps_qk, taps_v,
    q_out, k_out, v_out, rows_out, t_out, w_out, u_out, qe_out, m_out, b_out, p_out, end_out, map_out,
    scratch,
):
    head = pl.program_id(0)
    length = x_qk.shape[1]
    chunks = length // CHUNK
    mixed, _ = conv_into(
        places, scratch, x_qk, x_v, halo_qk, halo_v, taps_qk, taps_v, length
    )
    active = mixed * sigmoid(mixed)
    q_act = active[:, :DK]
    k_act = active[:, DK : 2 * DK]
    q_all = (
        q_act * lax.rsqrt(jnp.sum(q_act * q_act, -1, keepdims=True) + epsilon) * DK ** (-0.5)
    ).astype(bf16)
    k_all = (
        k_act * lax.rsqrt(jnp.sum(k_act * k_act, -1, keepdims=True) + epsilon)
    ).astype(bf16)
    v_all = active[:, 2 * DK :].astype(bf16)
    q_out[0, 0] = q_all
    k_out[0, 0] = k_all
    v_out[0, 0] = v_all
    decay_logit, strength_logit = chunk_rows(places, logits, chunks)
    decay = -jnp.exp(rates[head]) * softplus(decay_logit + biases[head])
    row, col = iotas()
    lower = row >= col
    strict = row > col
    total = mm_exact(pad_rows(decay)[: max(8, chunks)], (row <= col).astype(f32))[:chunks]
    strength = sigmoid(strength_logit)
    stacked = jnp.concatenate([total, strength], axis=0)
    rows_out[0, 0] = stacked
    columns = jnp.transpose(pad_rows(stacked))
    units = range(chunks)
    span = [slice(c * CHUNK, (c + 1) * CHUNK) for c in units]
    g_col = [columns[:, c : c + 1] for c in units]
    b_col = [columns[:, chunks + c : chunks + c + 1] for c in units]
    table = [
        jnp.where(lower, jnp.exp(jnp.where(lower, g_col[c] - total[c : c + 1, :], 0.0)), 0.0)
        for c in units
    ]
    q = [q_all[s] for s in span]
    k = [k_all[s] for s in span]
    gram = [mm(k[c], k[c], (1, 1)) for c in units]
    score = [mm(q[c], k[c], (1, 1)) * table[c] for c in units]
    lowers = [jnp.where(strict, b_col[c] * gram[c] * table[c], 0.0) for c in units]
    inverse = invert_units(lowers, row, col)
    grown = [jnp.exp(g_col[c]) for c in units]
    w = [mm(inverse[c], (b_col[c] * grown[c]) * k[c].astype(f32)) for c in units]
    u = [mm(inverse[c], b_col[c] * v_all[span[c]].astype(f32)) for c in units]
    qe = [grown[c] * q[c].astype(f32) - mm(score[c], w[c]) for c in units]
    own = [mm(score[c], u[c]) for c in units]
    last = [g_col[c][CHUNK - 1 :, :] for c in units]
    k_late = [jnp.exp(last[c] - g_col[c]) * k[c].astype(f32) for c in units]
    m = [-mm(k_late[c], w[c], (0, 0)) for c in units]
    b = [mm(k_late[c], u[c], (0, 0)) for c in units]
    state = b[0]
    for c in units:
        t_out[0, 0, c] = inverse[c].astype(bf16)
        w_out[0, 0, c] = w[c].astype(bf16)
        u_out[0, 0, c] = u[c]
        qe_out[0, 0, c] = qe[c].astype(bf16)
        m_out[0, 0, c] = m[c].astype(bf16)
        b_out[0, 0, c] = b[c]
        p_out[0, 0, c] = own[c]
        if c:
            state = jnp.exp(last[c]) * state + mm(m[c], state) + b[c]
    end_out[0, 0] = state
    if map_out is not None:
        chain = (row == col).astype(f32)
        for c in units:
            chain = jnp.exp(last[c]) * chain + mm(m[c], chain)
        map_out[0, 0] = chain


def output_kernel(
    places, rows, qe, m, b, own, arriving, og, gain,
    gated_out, mixer_out, states_out,
):
    chunks = qe.shape[2]
    last = jnp.exp(rows[0, 0][0:chunks, CHUNK - 1 :])
    state = arriving[0, 0].astype(f32)
    gain_row = gain[...].astype(f32)
    for c in range(chunks):
        s = slice(c * CHUNK, (c + 1) * CHUNK)
        states_out[0, 0, c] = state.astype(bf16)
        out = mm(qe[0, 0, c], state) + own[0, 0, c]
        mixer_out[0, s, :] = out
        scale = lax.rsqrt(jnp.mean(out * out, -1, keepdims=True) + epsilon)
        gate = og[0, place_of(places, c), :].astype(f32)
        gated_out[0, place_of(places, c), :] = (out * scale * gain_row * (gate * sigmoid(gate))).astype(bf16)
        if c < chunks - 1:
            state = last[c : c + 1, :] * state + mm(m[0, 0, c], state) + b[0, 0, c]


def norm_back_kernel(
    places, rows, d_gated, mixer, og, gain, qe, m,
    d_out, d_og_out, n_out, start_out, gain_out,
):
    seq = pl.program_id(1)
    chunks = qe.shape[2]
    last = jnp.exp(rows[0, 0][0:chunks, CHUNK - 1 :])
    gain_row = gain[...].astype(f32)
    gain_sum = jnp.zeros((8, DV), f32)
    adds = []
    for c in range(chunks):
        s = slice(c * CHUNK, (c + 1) * CHUNK)
        out = mixer[0, s, :]
        gate = og[0, place_of(places, c), :].astype(f32)
        sig = sigmoid(gate)
        swish = gate * sig
        dg = d_gated[0, place_of(places, c), :].astype(f32)
        scale = lax.rsqrt(jnp.mean(out * out, -1, keepdims=True) + epsilon)
        unit = out * scale
        spread = dg * unit
        e = dg * (gain_row * swish)
        d_mix = scale * (e - unit * jnp.mean(e * unit, -1, keepdims=True))
        d_og_out[0, 0, s, :] = (spread * gain_row * (sig * (1.0 + gate * (1.0 - sig)))).astype(bf16)
        gain_sum = gain_sum + jnp.sum((spread * swish).reshape(CHUNK // 8, 8, DV), axis=0)
        d_low = d_mix.astype(bf16)
        d_out[0, 0, c] = d_low
        add = mm(qe[0, 0, c], d_low, (0, 0))
        n_out[0, 0, c] = add
        adds.append(add)
    back = adds[-1]
    for c in reversed(range(chunks - 1)):
        back = last[c : c + 1, :] * back + mm(m[0, 0, c], back, (0, 0)) + adds[c]
    start_out[0, 0] = back

    @pl.when(seq == 0)
    def _():
        gain_out[0] = gain_sum

    @pl.when(seq != 0)
    def _():
        gain_out[0] = gain_out[0] + gain_sum


def grad_kernel(
    start, places, rates, biases, x_qk, x_v, halo_qk, halo_v, logits, taps_qk, taps_v,
    q_in, k_in, v_in, rows, t_in, w_in, u_in, m_in, states, d_out, n_in, arriving, d_og,
    d_proj_out, d_halo_out, d_tail_out, d_logit_out, rate_out, taps_out,
    scratch, grads,
):
    head = pl.program_id(0) + start
    seq = pl.program_id(1)
    length = x_qk.shape[1]
    chunks = length // CHUNK
    units = range(chunks)
    row, col = iotas()
    lower = row >= col
    strict = row > col
    stacked = rows[0, 0]
    total = stacked[0:chunks]
    strength = stacked[chunks : 2 * chunks]
    columns = jnp.transpose(pad_rows(stacked))
    g_col = [columns[:, c : c + 1] for c in units]
    b_col = [columns[:, chunks + c : chunks + c + 1] for c in units]
    last = [g_col[c][CHUNK - 1 :, :] for c in units]
    ends = [None] * chunks
    back = arriving[0, 0].astype(f32)
    for c in reversed(units):
        ends[c] = back
        if c:
            back = jnp.exp(last[c]) * back + mm(m_in[0, 0, c], back, (0, 0)) + n_in[0, 0, c]
    span = [slice(c * CHUNK, (c + 1) * CHUNK) for c in units]
    table = [
        jnp.where(lower, jnp.exp(jnp.where(lower, g_col[c] - total[c : c + 1, :], 0.0)), 0.0)
        for c in units
    ]
    q = [q_in[0, 0, s, :] for s in span]
    k = [k_in[0, 0, s, :] for s in span]
    v = [v_in[0, 0, s, :] for s in span]
    k_f = [k[c].astype(f32) for c in units]
    q_f = [q[c].astype(f32) for c in units]
    t = [t_in[0, 0, c] for c in units]
    w = [w_in[0, 0, c] for c in units]
    u = [u_in[0, 0, c] for c in units]
    s_in = [states[0, 0, c] for c in units]
    d_o = [d_out[0, 0, c] for c in units]
    gram = [mm(k[c], k[c], (1, 1)) * table[c] for c in units]
    score = [mm(q[c], k[c], (1, 1)) * table[c] for c in units]
    grown = [jnp.exp(g_col[c]) for c in units]
    fade = [jnp.exp(last[c] - g_col[c]) for c in units]
    fresh = [u[c] - mm(w[c], s_in[c]) for c in units]
    k_late = [fade[c] * k_f[c] for c in units]
    d_fresh = [mm(score[c], d_o[c], (0, 0)) + mm(k_late[c], ends[c]) for c in units]
    d_score = [jnp.where(lower, mm(d_o[c], fresh[c], (1, 1)), 0.0) for c in units]
    d_q_grown = [mm(d_o[c], s_in[c], (1, 1)) for c in units]
    d_k_late = [mm(fresh[c], ends[c], (1, 1)) for c in units]
    d_w = [-mm(d_fresh[c], s_in[c], (1, 1)) for c in units]
    d_vb = [mm(t[c], d_fresh[c], (0, 0)) for c in units]
    d_kb = [mm(t[c], d_w[c], (0, 0)) for c in units]
    d_lower = [
        jnp.where(strict, -(mm(d_vb[c], u[c], (1, 1)) + mm(d_kb[c], w[c], (1, 1))), 0.0)
        for c in units
    ]
    d_score_t = [d_score[c] * table[c] for c in units]
    d_lower_b = [d_lower[c] * b_col[c] for c in units]
    d_gram = [d_lower_b[c] * table[c] for c in units]
    cols = []
    cols_b = []
    rows_g = []
    for c in units:
        s = span[c]
        paired = d_score[c] * score[c] + d_lower_b[c] * gram[c]
        late = k_late[c] * d_k_late[c]
        k_dot = grown[c] * (d_kb[c] * k_f[c])
        per_row = (
            paired + grown[c] * (q_f[c] * d_q_grown[c]) - late + b_col[c] * k_dot
        )
        cols.append(jnp.sum(per_row, -1, keepdims=True))
        v_f = v[c].astype(f32)
        v_dot = d_vb[c] * v_f
        cols_b.append(
            jnp.sum(
                d_lower[c] * gram[c] + k_dot + v_dot[:, :DK] + v_dot[:, DK:], -1, keepdims=True
            )
        )
        kept = s_in[c].astype(f32) * ends[c]
        whole = jnp.sum(
            jnp.sum(late, 0, keepdims=True)
            + jnp.exp(last[c]) * jnp.sum(kept[:, :DK] + kept[:, DK:], 0, keepdims=True),
            -1,
            keepdims=True,
        )
        rows_g.append((jnp.sum(paired, 0, keepdims=True), whole))
        d_q = mm(d_score_t[c], k[c]) + grown[c] * d_q_grown[c]
        d_k = (
            mm(d_score_t[c], q[c], (0, 0))
            + mm(d_gram[c], k[c])
            + mm(d_gram[c], k[c], (0, 0))
            + fade[c] * d_k_late[c]
            + (b_col[c] * grown[c]) * d_kb[c]
        )
        grads[ROWS + s.start : ROWS + s.stop, 0:DK] = d_q
        grads[ROWS + s.start : ROWS + s.stop, DK : 2 * DK] = d_k
        grads[ROWS + s.start : ROWS + s.stop, 2 * DK :] = b_col[c] * d_vb[c]
    wide = jnp.concatenate(
        cols + cols_b + [jnp.zeros((CHUNK, CHUNK - 2 * chunks), f32)], axis=1
    )
    tall = jnp.transpose(wide)
    d_total = tall[0:chunks] - jnp.concatenate([r for r, _ in rows_g], axis=0)
    d_strength = tall[chunks : 2 * chunks]
    d_decay = mm_exact(pad_rows(d_total)[: max(8, chunks)], lower.astype(f32))[:chunks]
    d_decay = d_decay + jnp.concatenate([w_ for _, w_ in rows_g], axis=0)
    decay_logit, _ = chunk_rows(places, logits, chunks)
    biased = decay_logit + biases[head]
    rate = jnp.exp(rates[head])
    d_logit = -d_decay * rate * sigmoid(biased)
    d_strength_logit = d_strength * strength * (1.0 - strength)
    for c in units:
        d_logit_out[0, 0, pl.ds(places[c], 1), :] = d_logit[c : c + 1, :]
        d_logit_out[0, 1, pl.ds(places[c], 1), :] = d_strength_logit[c : c + 1, :]
    rate_out[0, 0] = -d_decay * rate * softplus(biased)

    mixed, taps = conv_into(
        places, scratch, x_qk, x_v, halo_qk, halo_v, taps_qk, taps_v, length
    )
    sig = sigmoid(mixed)
    active = mixed * sig
    slope = sig * (1.0 + mixed * (1.0 - sig))

    def unnorm(act, grad, factor):
        scale = lax.rsqrt(jnp.sum(act * act, -1, keepdims=True) + epsilon)
        unit = act * scale
        return (factor * scale) * (grad - unit * jnp.sum(unit * grad, -1, keepdims=True))

    body = slice(ROWS, ROWS + length)
    grads[body, 0:DK] = (
        unnorm(active[:, :DK], grads[body, 0:DK], DK ** (-0.5)) * slope[:, :DK]
    )
    grads[body, DK : 2 * DK] = (
        unnorm(active[:, DK : 2 * DK], grads[body, DK : 2 * DK], 1.0) * slope[:, DK : 2 * DK]
    )
    grads[body, 2 * DK :] = grads[body, 2 * DK :] * slope[:, 2 * DK :]
    grads[0:ROWS, :] = jnp.zeros((ROWS, QKV), f32)
    grads[ROWS + length :, :] = jnp.zeros((ROWS, QKV), f32)
    d_x = None
    d_halo = None
    tap_rows = []
    d_conv = grads[body, :]
    first = ROWS - CONV + 1
    for j in range(CONV):
        ahead = CONV - 1 - j
        part = taps[j : j + 1, :] * grads[ROWS + ahead : ROWS + ahead + length, :]
        d_x = part if d_x is None else d_x + part
        edge = taps[j : j + 1, :] * grads[ahead : ahead + ROWS, :]
        d_halo = edge if d_halo is None else d_halo + edge
        tap_rows.append(
            jnp.sum(d_conv * scratch[first + j : first + j + length, :], 0, keepdims=True)
        )
    for c in units:
        d_proj_out[0, place_of(places, c), 0:QKV] = d_x[span[c]].astype(bf16)
        d_proj_out[0, place_of(places, c), QKV:] = d_og[0, 0, span[c], :]
    d_tail_out[0, 0] = d_x[length - ROWS :, :]
    d_halo_out[0, 0] = d_halo
    tap_rows = jnp.concatenate(tap_rows + [jnp.zeros((8 - CONV, QKV), f32)], axis=0)

    @pl.when(seq == 0)
    def _():
        taps_out[0] = tap_rows

    @pl.when(seq != 0)
    def _():
        taps_out[0] = taps_out[0] + tap_rows


def cost(micros):
    return pl.CostEstimate(
        flops=int(micros * 1e8), bytes_accessed=int(micros * 1e5), transcendentals=0
    )


def params():
    return pltpu.CompilerParams(
        dimension_semantics=("arbitrary", "arbitrary"), vmem_limit_bytes=56 * 1024 * 1024
    )


def smem():
    return pl.BlockSpec(memory_space=pltpu.SMEM)


def per_unit(*shape, start=0):
    zeros = (0,) * len(shape)
    return pl.BlockSpec((1, 1) + shape, lambda h, s: (s, h + start) + zeros)


def input_specs(length, start=0):
    return [
        smem(),
        smem(),
        smem(),
        pl.BlockSpec((1, length, 256), lambda h, s: (s, 0, 3 * (h + start))),
        pl.BlockSpec((1, length, 256), lambda h, s: (s, 0, 3 * (h + start) + 1)),
        pl.BlockSpec((1, HALO, 256), lambda h, s: (s, 0, 3 * (h + start))),
        pl.BlockSpec((1, HALO, 256), lambda h, s: (s, 0, 3 * (h + start) + 1)),
        pl.BlockSpec((1, 2, length // CHUNK, CHUNK), lambda h, s: (s, h + start, 0, 0)),
        pl.BlockSpec((CONV, 256), lambda h, s: (0, 2 * (h + start))),
        pl.BlockSpec((CONV, 256), lambda h, s: (0, 2 * (h + start) + 1)),
    ]


def prepare(places, projected, halo, logits, taps, rates, biases, with_map):
    seqs, length, _ = projected.shape
    heads = rates.shape[0]
    chunks = length // CHUNK

    def out(dtype, *shape):
        return jax.ShapeDtypeStruct((seqs, heads) + shape, dtype), per_unit(*shape)

    outs = [
        out(bf16, length, DK),
        out(bf16, length, DK),
        out(bf16, length, DV),
        out(f32, 2 * chunks, CHUNK),
        out(bf16, chunks, CHUNK, CHUNK),
        out(bf16, chunks, CHUNK, DK),
        out(f32, chunks, CHUNK, DV),
        out(bf16, chunks, CHUNK, DK),
        out(bf16, chunks, DK, DK),
        out(f32, chunks, DK, DV),
        out(f32, chunks, CHUNK, DV),
        out(f32, DK, DV),
    ]
    if with_map:
        outs.append(out(f32, DK, DK))
        kernel = prep_kernel
    else:

        def kernel(*refs):
            prep_kernel(*refs[:-1], None, refs[-1])

    results = pl.pallas_call(
        kernel,
        grid=(heads, seqs),
        in_specs=input_specs(length),
        out_specs=[spec for _, spec in outs],
        out_shape=[shape for shape, _ in outs],
        scratch_shapes=[pltpu.VMEM((length + ROWS, QKV), f32)],
        compiler_params=params(),
        cost_estimate=cost(9.0 * heads * seqs * chunks / 8),
        name="prepare",
    )(places, rates, biases, projected, projected, halo, halo, logits, taps, taps)
    return results if with_map else list(results) + [None]


def mixer_output(places, kept, arriving, projected, gain):
    rows, qe, m, b, own = kept
    seqs, heads, chunks = qe.shape[:3]
    length = chunks * CHUNK
    return pl.pallas_call(
        output_kernel,
        grid=(heads, seqs),
        in_specs=[
            smem(),
            per_unit(2 * chunks, CHUNK),
            per_unit(chunks, CHUNK, DK),
            per_unit(chunks, DK, DK),
            per_unit(chunks, DK, DV),
            per_unit(chunks, CHUNK, DV),
            per_unit(DK, DV),
            pl.BlockSpec((1, length, 256), lambda h, s: (s, 0, 3 * h + 2)),
            pl.BlockSpec((1, DV), lambda h, s: (0, 0)),
        ],
        out_specs=[
            pl.BlockSpec((1, length, DV), lambda h, s: (s, 0, h)),
            pl.BlockSpec((1, length, DV), lambda h, s: (s, 0, h)),
            per_unit(chunks, DK, DV),
        ],
        out_shape=[
            jax.ShapeDtypeStruct((seqs, length, heads * DV), bf16),
            jax.ShapeDtypeStruct((seqs, length, heads * DV), f32),
            jax.ShapeDtypeStruct((seqs, heads, chunks, DK, DV), bf16),
        ],
        compiler_params=params(),
        cost_estimate=cost(4.0 * heads * seqs * chunks / 8),
        name="mixer_output",
    )(places, rows, qe, m, b, own, arriving, projected, gain)


def norm_back(places, rows, d_gated, mixer, projected, gain, qe, m, start=0, count=None):
    seqs, heads, chunks = qe.shape[:3]
    length = chunks * CHUNK
    heads = count or heads
    return pl.pallas_call(
        norm_back_kernel,
        grid=(heads, seqs),
        in_specs=[
            smem(),
            per_unit(2 * chunks, CHUNK, start=start),
            pl.BlockSpec((1, length, DV), lambda h, s: (s, 0, h + start)),
            pl.BlockSpec((1, length, DV), lambda h, s: (s, 0, h + start)),
            pl.BlockSpec((1, length, 256), lambda h, s: (s, 0, 3 * (h + start) + 2)),
            pl.BlockSpec((1, DV), lambda h, s: (0, 0)),
            per_unit(chunks, CHUNK, DK, start=start),
            per_unit(chunks, DK, DK, start=start),
        ],
        out_specs=[
            per_unit(chunks, CHUNK, DV),
            per_unit(length, DV),
            per_unit(chunks, DK, DV),
            per_unit(DK, DV),
            pl.BlockSpec((1, 8, DV), lambda h, s: (h, 0, 0)),
        ],
        out_shape=[
            jax.ShapeDtypeStruct((seqs, heads, chunks, CHUNK, DV), bf16),
            jax.ShapeDtypeStruct((seqs, heads, length, DV), bf16),
            jax.ShapeDtypeStruct((seqs, heads, chunks, DK, DV), f32),
            jax.ShapeDtypeStruct((seqs, heads, DK, DV), f32),
            jax.ShapeDtypeStruct((heads, 8, DV), f32),
        ],
        compiler_params=params(),
        cost_estimate=cost(4.0 * heads * seqs * chunks / 8),
        name="norm_back",
    )(places, rows, d_gated, mixer, projected, gain, qe, m)


def mixer_grads(
    places, projected, halo, logits, taps, rates, biases, q, k, v, rows, t, w, u, m, states, d_out, n, arriving, d_og,
    start=0, count=None,
):
    seqs, length, _ = projected.shape
    heads = count or rates.shape[0]
    chunks = length // CHUNK
    return pl.pallas_call(
        functools.partial(grad_kernel, start),
        grid=(heads, seqs),
        in_specs=input_specs(length, start)
        + [
            per_unit(length, DK, start=start),
            per_unit(length, DK, start=start),
            per_unit(length, DV, start=start),
            per_unit(2 * chunks, CHUNK, start=start),
            per_unit(chunks, CHUNK, CHUNK, start=start),
            per_unit(chunks, CHUNK, DK, start=start),
            per_unit(chunks, CHUNK, DV, start=start),
            per_unit(chunks, DK, DK, start=start),
            per_unit(chunks, DK, DV, start=start),
            per_unit(chunks, CHUNK, DV, start=start),
            per_unit(chunks, DK, DV, start=start),
            per_unit(DK, DV, start=start),
            per_unit(length, DV, start=start),
        ],
        out_specs=[
            pl.BlockSpec((1, length, HEAD), lambda h, s: (s, 0, h)),
            per_unit(ROWS, QKV),
            per_unit(ROWS, QKV),
            pl.BlockSpec((1, 2, chunks, CHUNK), lambda h, s: (s, h, 0, 0)),
            per_unit(chunks, CHUNK),
            pl.BlockSpec((1, 8, QKV), lambda h, s: (h, 0, 0)),
        ],
        out_shape=[
            jax.ShapeDtypeStruct((seqs, length, heads * HEAD), bf16),
            jax.ShapeDtypeStruct((seqs, heads, ROWS, QKV), f32),
            jax.ShapeDtypeStruct((seqs, heads, ROWS, QKV), f32),
            jax.ShapeDtypeStruct((seqs, 2 * heads, chunks, CHUNK), f32),
            jax.ShapeDtypeStruct((seqs, heads, chunks, CHUNK), f32),
            jax.ShapeDtypeStruct((heads, 8, QKV), f32),
        ],
        scratch_shapes=[
            pltpu.VMEM((length + ROWS, QKV), f32),
            pltpu.VMEM((length + 2 * ROWS, QKV), f32),
        ],
        compiler_params=params(),
        cost_estimate=cost(10.0 * heads * seqs * chunks / 8),
        name="mixer_grads",
    )(
        places, rates, biases, projected, projected, halo, halo, logits, taps, taps,
        q, k, v, rows, t, w, u, m, states, d_out, n, arriving, d_og,
    )


def shifted(block, axis, distance):
    devices = range(lax.axis_size(axis))
    route = [(i - distance, i) for i in devices if i - distance in devices]
    return lax.ppermute(block, axis, route)


def relay(first, maps, distance):
    arriving = shifted(first.astype(bf16), "ctx", distance)
    for _ in range(lax.axis_size("ctx") - 2):
        leaving = first + maps(arriving.astype(f32))
        arriving = shifted(leaving.astype(bf16), "ctx", distance)
    return arriving


def dot(left, right, contract=(1, 0)):
    return lax.dot_general(
        left, right, (((contract[0],), (contract[1],)), ((), ())), preferred_element_type=f32
    )


def local(
    tokens,
    proj_in,
    proj_gates,
    conv_taps,
    log_rates,
    rate_bias,
    gate_gain,
    proj_out,
    ffn_gate,
    ffn_up,
    ffn_down,
    gain_in,
    gain_ffn,
    cotangent,
):
    seqs, length, width = tokens.shape
    row_count = seqs * length
    heads = log_rates.shape[0]
    chunks = length // CHUNK
    tp_count = lax.axis_size("tp")
    tp_place = lax.axis_index("tp")
    share = length // tp_count
    with_map = lax.axis_size("ctx") > 2

    def own(rows):
        return lax.dynamic_slice_in_dim(
            rows.reshape(seqs, length, rows.shape[-1]), tp_place * share, share, 1
        )

    def scatter_sum(partial):
        partial = partial.astype(bf16).reshape(seqs, length, width)
        return lax.psum_scatter(partial, "tp", scatter_dimension=1, tiled=True).astype(f32)

    def gather_rows(rows):
        return lax.all_gather(rows, "tp", axis=1, tiled=True).reshape(row_count, width)

    whole_in = lax.all_gather(proj_in, "shard", axis=0, tiled=True)
    whole_gates = lax.all_gather(proj_gates, "shard", axis=0, tiled=True)
    whole_out = lax.all_gather(proj_out, "shard", axis=1, tiled=True)
    whole_gate = lax.all_gather(ffn_gate, "shard", axis=0, tiled=True)
    whole_up = lax.all_gather(ffn_up, "shard", axis=0, tiled=True)
    whole_down = lax.all_gather(ffn_down, "shard", axis=1, tiled=True)
    gain_in_f = lax.all_gather(gain_in, "shard", axis=0, tiled=True).astype(f32)
    gain_ffn_f = lax.all_gather(gain_ffn, "shard", axis=0, tiled=True).astype(f32)

    inputs_f = tokens.reshape(row_count, width).astype(f32)
    scale_in = lax.rsqrt(jnp.mean(inputs_f * inputs_f, -1, keepdims=True) + epsilon)
    unit_in = inputs_f * scale_in
    normed_in = (unit_in * gain_in_f).astype(bf16)
    projected = dot(normed_in, whole_in).astype(bf16).reshape(seqs, length, heads * HEAD)
    logits = dot(whole_gates, normed_in, (0, 1)).reshape(
        2 * heads, seqs, chunks, CHUNK
    )
    logits = jnp.swapaxes(logits, 0, 1)
    halo = shifted(projected[:, length - HALO :, :], "ctx", 1)
    places = jnp.arange(chunks, dtype=jnp.int32)
    q, k, v, rows, t, w, u, qe, m, b, own_out, state_end, state_map = prepare(
        places, projected, halo, logits, conv_taps, log_rates, rate_bias, with_map
    )

    def map_forward(arriving):
        return jnp.einsum("shij,shjk->shik", state_map, arriving)

    def map_back(arriving):
        return jnp.einsum("shji,shjk->shik", state_map, arriving)

    arriving = relay(state_end, map_forward, 1)
    gain_row = gate_gain.reshape(1, DV)
    gated, mixer, states = mixer_output(
        places, (rows, qe, m, b, own_out), arriving, projected, gain_row
    )
    gated = gated.reshape(row_count, heads * DV)

    middle = own(inputs_f) + scatter_sum(dot(gated, whole_out))
    scale_mid = lax.rsqrt(jnp.mean(middle * middle, -1, keepdims=True) + epsilon)
    unit_mid = middle * scale_mid
    normed_mid = gather_rows((unit_mid * gain_ffn_f).astype(bf16))
    gate_act = dot(normed_mid, whole_gate)
    up_act = dot(normed_mid, whole_up)
    gate_sig = jax.nn.sigmoid(gate_act)
    gate_silu = gate_act * gate_sig
    hidden = (gate_silu * up_act).astype(bf16)
    d_out = cotangent.reshape(row_count, width)
    d_hidden = dot(d_out, whole_down, (1, 1))
    d_gate = (d_hidden * up_act * gate_sig * (1.0 + gate_act * (1.0 - gate_sig))).astype(bf16)
    d_up = (d_hidden * gate_silu).astype(bf16)
    d_mid_norm = scatter_sum(dot(d_gate, whole_gate, (1, 1)) + dot(d_up, whole_up, (1, 1)))
    layer_rows = middle + scatter_sum(dot(hidden, whole_down))
    grad_down = dot(hidden, d_out, (0, 0))
    grad_gate = dot(normed_mid, d_gate, (0, 0))
    grad_up = dot(normed_mid, d_up, (0, 0))
    gain_ffn_part = jnp.sum(d_mid_norm * unit_mid, (0, 1))
    scaled_mid = d_mid_norm * gain_ffn_f
    d_middle = own(cotangent).astype(f32) + scale_mid * (
        scaled_mid - unit_mid * jnp.mean(scaled_mid * unit_mid, -1, keepdims=True)
    )
    d_branch = gather_rows(d_middle.astype(bf16))
    grad_out = dot(gated, d_branch, (0, 0))
    d_gated = dot(d_branch, whole_out, (1, 1)).reshape(seqs, length, heads * DV)
    d_mixer, d_og, n, d_start, gain_gate_part = norm_back(
        places, rows, d_gated, mixer, projected, gain_row, qe, m
    )
    arriving_back = relay(d_start, map_back, -1)
    d_projected, d_halo, d_tail, d_logits, rate_rows, tap_rows = mixer_grads(
        places, projected, halo, logits, conv_taps, log_rates, rate_bias,
        q, k, v, rows, t, w, u, m, states, d_mixer, n, arriving_back, d_og,
    )
    later = shifted(d_halo, "ctx", -1)
    tail = (d_tail + later).astype(bf16)
    for h in range(heads):
        d_projected = lax.dynamic_update_slice(
            d_projected, tail[:, h], (0, length - ROWS, h * HEAD)
        )
    d_projected = d_projected.reshape(row_count, heads * HEAD)
    grad_bias = jnp.sum(d_logits[:, 0::2], (0, 2, 3))
    grad_rates = jnp.sum(rate_rows, (0, 2, 3))
    d_logit_rows = jnp.swapaxes(d_logits, 0, 1).reshape(2 * heads, row_count).astype(bf16)
    grad_in = dot(normed_in, d_projected, (0, 0))
    grad_gates = dot(normed_in, d_logit_rows, (0, 1))
    in_back = dot(d_projected, whole_in, (1, 1)) + dot(d_logit_rows, whole_gates, (0, 1))
    d_in_norm = scatter_sum(in_back)
    unit_own = own(unit_in)
    scale_own = own(scale_in)
    gain_in_part = jnp.sum(d_in_norm * unit_own, (0, 1))
    scaled_in = d_in_norm * gain_in_f
    token_grad = d_middle + scale_own * (
        scaled_in - unit_own * jnp.mean(scaled_in * unit_own, -1, keepdims=True)
    )
    gain_gate_part = jnp.sum(gain_gate_part, (0, 1))
    grad_taps = jnp.swapaxes(tap_rows[:, :CONV, :], 0, 1).reshape(CONV, heads * QKV)
    grad_gain_gate, grad_gain_in, grad_gain_ffn = lax.psum(
        (gain_gate_part, gain_in_part, gain_ffn_part), "tp"
    )

    def reduced(grad, axis):
        piece = lax.psum_scatter(
            grad.astype(bf16), ("shard", "ctx"), scatter_dimension=axis, tiled=True
        )
        return lax.all_gather(piece, "ctx", axis=axis, tiled=True).astype(f32)

    sum_taps, sum_rates, sum_bias, sum_gain_gate = lax.psum(
        (grad_taps, grad_rates, grad_bias, grad_gain_gate), ("shard", "ctx")
    )
    return (
        layer_rows.astype(bf16),
        token_grad,
        reduced(grad_in, 0),
        reduced(grad_gates, 0),
        sum_taps,
        sum_rates,
        sum_bias,
        sum_gain_gate,
        reduced(grad_out, 1),
        reduced(grad_gate, 0),
        reduced(grad_up, 0),
        reduced(grad_down, 1),
        reduced(grad_gain_in, 0),
        reduced(grad_gain_ffn, 0),
    )


def ffn_kernel(part_a, part_b, d_rows, weights, *refs):
    rows_out, hidden_out, d_pair_out, back_a, back_b, down_a, down_b = refs[-7:]
    units = weights.shape[1] // 3
    main = units // 128 * 128
    pair, down = weights.at[:, : 2 * units], weights.at[:, 2 * units :]
    half = part_a.shape[0]
    rows = jnp.concatenate([part_a[...], part_b[...]], axis=0)
    rows_out[...] = rows
    acts = mm(rows, pair[...])
    d_hidden = mm(d_rows[...], down[...])

    def through_gate(gate_act, up_act, d_act):
        sig = sigmoid(gate_act)
        swish = gate_act * sig
        d_gate = d_act * up_act * sig * (1.0 + gate_act * (1.0 - sig))
        return (swish * up_act).astype(bf16), d_gate.astype(bf16), (d_act * swish).astype(bf16)

    hidden, d_gate, d_up = through_gate(acts[:, :main], acts[:, main : 2 * main], d_hidden[:, :main])
    d_pair = [d_gate, d_up]
    if units > main:
        last = 2 * main + units - main
        tail, d_gate, d_up = through_gate(
            acts[:, 2 * main : last], acts[:, last:], d_hidden[:, main:]
        )
        hidden = jnp.concatenate([hidden, tail], axis=1)
        d_pair = d_pair + [d_gate, d_up]
    hidden_out[...] = hidden
    d_pair = jnp.concatenate(d_pair, axis=1)
    d_pair_out[...] = d_pair
    back = mm(d_pair, pair[...], (1, 1)).astype(bf16)
    through = mm(hidden, down[...], (1, 1)).astype(bf16)
    back_a[...] = back[:half]
    back_b[...] = back[half:]
    down_a[...] = through[:half]
    down_b[...] = through[half:]


def paired(gate, up):
    main = gate.shape[1] // 128 * 128
    return jnp.concatenate([gate[:, :main], up[:, :main], gate[:, main:], up[:, main:]], axis=1)


def unpaired(pair):
    units = pair.shape[1] // 2
    main = units // 128 * 128
    last = main + units
    gate = jnp.concatenate([pair[:, :main], pair[:, 2 * main : last]], axis=1)
    return gate, jnp.concatenate([pair[:, main : 2 * main], pair[:, last:]], axis=1)


def feed_forward(part_a, part_b, d_rows, weights, carried):
    half, width = part_a.shape
    units = weights.shape[1] // 3
    index = 1 if carried else 0

    def whole(*shape):
        return pl.BlockSpec(shape, lambda i: (0, 0))

    def placed(columns):
        return pl.BlockSpec((2 * half, columns), lambda i: (index, 0))

    return pl.pallas_call(
        ffn_kernel,
        grid=(1,),
        in_specs=[
            whole(half, width), whole(half, width), placed(width), whole(*weights.shape),
        ]
        + [pl.BlockSpec(memory_space=pl.ANY)] * len(carried),
        out_specs=[placed(width), placed(units), placed(2 * units)] + [whole(half, width)] * 4,
        out_shape=[
            jax.ShapeDtypeStruct((4 * half, columns), bf16) for columns in (width, units, 2 * units)
        ]
        + [jax.ShapeDtypeStruct((half, width), bf16)] * 4,
        input_output_aliases={4 + i: i for i in range(len(carried))},
        compiler_params=pltpu.CompilerParams(
            dimension_semantics=("arbitrary",), vmem_limit_bytes=56 * 1024 * 1024
        ),
        cost_estimate=cost(9.0),
        name="feed_forward",
    )(part_a, part_b, d_rows, weights, *carried)


def input_back_kernel(d_first, d_last, d_logits, weights, gates, *outs):
    split = d_first.shape[1]
    total = (
        mm(d_first[...], weights[:, :split], (1, 1))
        + mm(d_last[...], weights[:, split : 2 * split], (1, 1))
        + mm(d_logits[...], gates[...], (0, 0))
    ).astype(bf16)
    for i, out in enumerate(outs):

        @pl.when(pl.program_id(0) == i)
        def _(out=out):
            out[...] = total


def input_back(d_first, d_last, d_logits, weights, gates):
    full = d_first.shape[0]
    count = full // 4
    width = weights.shape[0]

    def whole(array):
        return pl.BlockSpec(array.shape, lambda i: (0, 0))

    return pl.pallas_call(
        input_back_kernel,
        grid=(4,),
        in_specs=[
            pl.BlockSpec((count, d_first.shape[1]), lambda i: (i, 0)),
            pl.BlockSpec((count, d_last.shape[1]), lambda i: (i, 0)),
            pl.BlockSpec((d_logits.shape[0], count), lambda i: (0, i)),
            whole(weights),
            whole(gates),
        ],
        out_specs=[pl.BlockSpec((count, width), lambda i: (0, 0))] * 4,
        out_shape=[jax.ShapeDtypeStruct((count, width), bf16)] * 4,
        compiler_params=pltpu.CompilerParams(
            dimension_semantics=("arbitrary",), vmem_limit_bytes=56 * 1024 * 1024
        ),
        cost_estimate=cost(5.0),
        name="input_back",
    )(d_first, d_last, d_logits, weights, gates)


def ffn_grads_kernel(rows, d_pair, d_rows, hidden, out):
    out[...] = jnp.concatenate(
        [mm(rows[...], d_pair[...], (0, 0)), mm(d_rows[...], hidden[...], (0, 0))], axis=1
    ).astype(bf16)


def ffn_grads(rows, d_pair, d_rows, hidden):
    full, width = rows.shape
    count = width // 4
    wide = d_pair.shape[1] + hidden.shape[1]

    def columns():
        return pl.BlockSpec((full, count), lambda i: (0, i))

    def whole(array):
        return pl.BlockSpec(array.shape, lambda i: (0, 0))

    return pl.pallas_call(
        ffn_grads_kernel,
        grid=(4,),
        in_specs=[columns(), whole(d_pair), columns(), whole(hidden)],
        out_specs=pl.BlockSpec((count, wide), lambda i: (i, 0)),
        out_shape=jax.ShapeDtypeStruct((width, wide), bf16),
        compiler_params=pltpu.CompilerParams(
            dimension_semantics=("arbitrary",), vmem_limit_bytes=56 * 1024 * 1024
        ),
        cost_estimate=cost(10.0),
        name="ffn_grads",
    )(rows, d_pair, d_rows, hidden)


def both_grads_kernel(rows, d_rows, weights, part_0, part_1, part_2, part_3, gated, out, sums):
    grad = mm(rows[...], d_rows[...], (0, 0))
    columns = jnp.sum(grad * weights[...].astype(f32), -1, keepdims=True)
    lanes = jnp.concatenate([columns, jnp.zeros((columns.shape[0], 127), f32)], axis=1)
    sums[...] = jnp.transpose(lanes)[0:8]
    branch = jnp.concatenate([part_0[...], part_1[...], part_2[...], part_3[...]], axis=0)
    out[...] = jnp.concatenate([grad, mm(branch, gated[...], (0, 0))], axis=1).astype(bf16)


def both_grads(rows, d_rows, weights, parts, gated):
    full, width = rows.shape
    columns = d_rows.shape[1]
    count = width // 4
    wide = columns + gated.shape[1]
    return pl.pallas_call(
        both_grads_kernel,
        grid=(4,),
        in_specs=[
            pl.BlockSpec((full, count), lambda i: (0, i)),
            pl.BlockSpec((full, columns), lambda i: (0, 0)),
            pl.BlockSpec((count, columns), lambda i: (i, 0)),
        ]
        + [pl.BlockSpec((parts[0].shape[0], count), lambda i: (0, i))] * 4
        + [pl.BlockSpec(gated.shape, lambda i: (0, 0))],
        out_specs=[
            pl.BlockSpec((count, wide), lambda i: (i, 0)),
            pl.BlockSpec((8, count), lambda i: (0, i)),
        ],
        out_shape=[
            jax.ShapeDtypeStruct((width, wide), bf16),
            jax.ShapeDtypeStruct((8, width), f32),
        ],
        compiler_params=pltpu.CompilerParams(
            dimension_semantics=("arbitrary",), vmem_limit_bytes=56 * 1024 * 1024
        ),
        cost_estimate=cost(8.0),
        name="both_grads",
    )(rows, d_rows, weights, *parts, gated)


def input_grad_kernel(
    shard, rows, d_rows, weights, left_a, left_b, left_send, right_a, right_b, right_send, part
):
    grad = mm(rows[...], d_rows[...], (0, 0))
    sums = jnp.sum(grad * weights[...].astype(f32), -1, keepdims=True)
    lanes = jnp.concatenate([sums, jnp.zeros((sums.shape[0], 127), f32)], axis=1)
    part[...] = jnp.transpose(lanes)[0:8]
    low = grad.astype(bf16)
    count = low.shape[0]
    cut = left_a.shape[1]
    left, right = low[:, :cut], low[:, cut:]
    step = pl.program_id(0)

    @pl.when(step == 0)
    def _():
        left_a[...] = left
        right_a[...] = right

    @pl.when(step == 1)
    def _():
        left_send[:count] = left
        right_b[...] = right

    @pl.when(step == 2)
    def _():
        left_b[...] = left
        right_send[:count] = right

    @pl.when(step == 3)
    def _():
        left_send[count:] = left
        right_send[count:] = right


def input_grad(shard, rows, d_rows, weights, head):
    full, width = rows.shape
    columns = d_rows.shape[1]
    count = width // 4
    cut = columns // 256 * 128

    def whole(*shape):
        return pl.BlockSpec(shape, lambda i, place: (0, 0))

    shapes = [
        (count, cut), (count, cut), (2 * count, cut),
        (count, columns - cut), (count, columns - cut), (2 * count, columns - cut),
    ]
    return pl.pallas_call(
        input_grad_kernel,
        grid_spec=pltpu.PrefetchScalarGridSpec(
            num_scalar_prefetch=1,
            grid=(4,),
            in_specs=[
                pl.BlockSpec((full, count), lambda i, place: (0, place[0] ^ i)),
                whole(full, columns),
                pl.BlockSpec((count, columns), lambda i, place: (place[0] ^ i, head)),
            ],
            out_specs=[whole(*shape) for shape in shapes]
            + [pl.BlockSpec((8, count), lambda i, place: (0, place[0] ^ i))],
        ),
        out_shape=[jax.ShapeDtypeStruct(shape, bf16) for shape in shapes]
        + [jax.ShapeDtypeStruct((8, width), f32)],
        compiler_params=pltpu.CompilerParams(
            dimension_semantics=("arbitrary",), vmem_limit_bytes=56 * 1024 * 1024
        ),
        cost_estimate=cost(4.0),
        name="input_grad",
    )(shard, rows, d_rows, weights)


def branch_back_kernel(
    places, rows, part_0, part_1, part_2, part_3, weights, mixer, og, gain, qe, m,
    d_out, d_og_out, n_out, start_out, gain_out, d_gated,
):
    count = part_0.shape[0]
    for i, part in enumerate((part_0, part_1, part_2, part_3)):
        d_gated[0, i * count : (i + 1) * count, :] = mm(part[...], weights[...])
    norm_back_kernel(
        places, rows, d_gated, mixer, og, gain, qe, m, d_out, d_og_out, n_out, start_out, gain_out
    )


def branch_back(places, rows, parts, weights, mixer, projected, gain, qe, m):
    seqs, heads, chunks = qe.shape[:3]
    length = chunks * CHUNK
    count, width = parts[0].shape
    return pl.pallas_call(
        branch_back_kernel,
        grid=(heads, seqs),
        in_specs=[
            smem(),
            per_unit(2 * chunks, CHUNK),
        ]
        + [pl.BlockSpec((count, width), lambda h, s: (0, 0))] * 4
        + [
            pl.BlockSpec((width, DV), lambda h, s: (0, h)),
            pl.BlockSpec((1, length, DV), lambda h, s: (s, 0, h)),
            pl.BlockSpec((1, length, 256), lambda h, s: (s, 0, 3 * h + 2)),
            pl.BlockSpec((1, DV), lambda h, s: (0, 0)),
            per_unit(chunks, CHUNK, DK),
            per_unit(chunks, DK, DK),
        ],
        out_specs=[
            per_unit(chunks, CHUNK, DV),
            per_unit(length, DV),
            per_unit(chunks, DK, DV),
            per_unit(DK, DV),
            pl.BlockSpec((1, 8, DV), lambda h, s: (h, 0, 0)),
        ],
        out_shape=[
            jax.ShapeDtypeStruct((seqs, heads, chunks, CHUNK, DV), bf16),
            jax.ShapeDtypeStruct((seqs, heads, length, DV), bf16),
            jax.ShapeDtypeStruct((seqs, heads, chunks, DK, DV), f32),
            jax.ShapeDtypeStruct((seqs, heads, DK, DV), f32),
            jax.ShapeDtypeStruct((heads, 8, DV), f32),
        ],
        scratch_shapes=[pltpu.VMEM((1, length, DV), f32)],
        compiler_params=params(),
        cost_estimate=cost(5.0 * heads),
        name="branch_back",
    )(places, rows, *parts, weights, mixer, projected, gain, qe, m)


def widened(block):
    return jnp.pad(block, ((0, 0), (0, -block.shape[1] % 128)))


def local_paired(
    tokens,
    proj_in,
    proj_gates,
    conv_taps,
    log_rates,
    rate_bias,
    gate_gain,
    proj_out,
    ffn_gate,
    ffn_up,
    ffn_down,
    gain_in,
    gain_ffn,
    cotangent,
):
    seqs, length, width = tokens.shape
    heads = log_rates.shape[0]
    units = ffn_gate.shape[1]
    core = lax.axis_index("ctx")
    place = lax.axis_index("tp")
    shard = lax.axis_index("shard")
    tp_count = lax.axis_size("tp")
    shards = lax.axis_size("shard")
    seq = place // 2
    half = place % 2
    quarter = length // 2
    share = length // tp_count
    full = 2 * length
    chunks = full // CHUNK
    route = []
    for j in range(tp_count):
        route.append((j, (j % 2) * tp_count + j // 2))
        route.append((tp_count + j, (j % 2) * tp_count + 2 + j // 2))
    route_back = [(b, a) for a, b in route]
    pairs = [(i, i ^ 1) for i in range(tp_count)]
    pairs_x = [(i, i ^ 1) for i in range(shards)]
    pairs_y = [(i, i ^ 2) for i in range(shards)]
    odd_x = shard % 2 == 1
    odd_y = shard // 2 == 1

    def hold(*values):
        return lax.optimization_barrier(values)

    def swap_core(block):
        with jax.named_scope("swap_core"):
            return lax.ppermute(block, "ctx", [(0, 1), (1, 0)])

    def swap_chip(block):
        with jax.named_scope("swap_chip"):
            return lax.ppermute(block, "tp", pairs)

    def swap_x(block):
        with jax.named_scope("swap_x"):
            return lax.ppermute(block, "shard", pairs_x)

    def swap_y(block):
        with jax.named_scope("swap_y"):
            return lax.ppermute(block, "shard", pairs_y)

    def to_users(block):
        with jax.named_scope("to_users"):
            return lax.ppermute(block, ("ctx", "tp"), route)

    def to_owners(block):
        with jax.named_scope("to_owners"):
            return lax.ppermute(block, ("ctx", "tp"), route_back)

    def both_cores(block):
        return block.astype(f32) + swap_core(block).astype(f32)

    def add(kept, got):
        return (kept.astype(f32) + got.astype(f32)).astype(bf16)

    def group_rows(mine, got):
        return jnp.concatenate(
            [mine[:quarter], got[:quarter], mine[quarter:], got[quarter:]], axis=0
        )

    def own_rows(rows):
        sequence = lax.dynamic_index_in_dim(rows, seq, 0, keepdims=False)
        mine = lax.dynamic_slice_in_dim(sequence, half * quarter, quarter, 0)
        other = lax.dynamic_slice_in_dim(sequence, (1 - half) * quarter, quarter, 0)
        return jnp.concatenate([mine, other], axis=0)

    def swap_sides(mine):
        return swap_x(mine), swap_y(mine)

    def swap_fourth(from_x, from_y):
        count = from_x.shape[0] // 2
        return swap_x(from_y[:count]), swap_y(from_x[count:])

    def ordered(odd, mine, theirs):
        return jnp.concatenate([jnp.where(odd, theirs, mine), jnp.where(odd, mine, theirs)], axis=0)

    def assembled(mine, sides, fourth):
        across = jnp.concatenate(fourth, axis=0)
        return ordered(
            odd_y, ordered(odd_x, mine, sides[0]), ordered(odd_x, sides[1], across)
        )

    def blocks(grad, *places_xor):
        rows = grad.shape[0] // shards
        return jnp.concatenate(
            [lax.dynamic_slice_in_dim(grad, (shard ^ p) * rows, rows, 0) for p in places_xor],
            axis=0,
        )

    def scatter_first(grad):
        cut = grad.shape[1] // 256 * 128
        left, right = grad[:, :cut], grad[:, cut:]
        return (
            blocks(left, 0, 2),
            swap_x(blocks(left, 1, 3)),
            blocks(right, 0, 1),
            swap_y(blocks(right, 2, 3)),
        )

    def scatter_second(left, left_got, right, right_got):
        rows = left.shape[0] // 2
        left = add(left, left_got)
        right = add(right, right_got)
        return left[:rows], swap_y(left[rows:]), right[:rows], swap_x(right[rows:])

    def scatter_end(left, left_got, right, right_got):
        return jnp.concatenate([add(left, left_got), add(right, right_got)], axis=1)

    def quarters(rows, weights):
        return [
            dot(rows[i * quarter : (i + 1) * quarter], weights, (1, 1)) for i in (3, 2, 1, 0)
        ]

    def piece_first(left_a, left_b, left_send, right_a, right_b, right_send):
        return left_a, left_b, swap_x(left_send), right_a, right_b, swap_y(right_send)

    def piece_second(left_a, left_b, left_got, right_a, right_b, right_got):
        rows = left_a.shape[0]
        left_on = swap_y(add(left_b, left_got[rows:]))
        right_on = swap_x(add(right_b, right_got[rows:]))
        return left_a, left_got, left_on, right_a, right_got, right_on

    def piece_end(left_a, left_got, left_on, right_a, right_got, right_on):
        rows = left_a.shape[0]

        def total(mine, got, on):
            return (mine.astype(f32) + got[:rows].astype(f32) + on.astype(f32)).astype(bf16)

        return jnp.concatenate(
            [total(left_a, left_got, left_on), total(right_a, right_got, right_on)], axis=1
        )

    small = jnp.concatenate(
        [
            conv_taps.astype(f32),
            jnp.pad(jnp.stack([log_rates, rate_bias]), ((0, 2), (0, conv_taps.shape[1] - heads))),
        ],
        axis=0,
    )
    inner = heads * HEAD
    block = proj_in.shape[0]
    gates_block = jnp.pad(
        proj_gates.T, ((0, 16 - 2 * heads), (0, inner - block))
    )
    mine_in = to_users(jnp.concatenate([proj_in, gates_block], axis=0))
    mine_rows = own_rows(tokens)
    got_rows = swap_core(mine_rows)
    gains = lax.all_gather(jnp.stack([gain_in, gain_ffn]), "shard", axis=1, tiled=True)
    mine_d = own_rows(cotangent)
    got_d = swap_core(mine_d)
    mine_pair = paired(ffn_gate, ffn_up)
    mine_in, mine_rows, got_rows, gains, mine_d, got_d, small, mine_out, mine_pair, mine_down = hold(
        mine_in, mine_rows, got_rows, gains, mine_d, got_d, small, proj_out.T, mine_pair,
        ffn_down.T,
    )
    in_sides = swap_sides(mine_in)
    small = to_users(small)
    mine_out = to_users(mine_out)
    mine_down = to_users(mine_down)
    gains = gains.astype(f32)
    gain_in_f, gain_ffn_f = gains[0:1], gains[1:2]
    inputs_f = group_rows(mine_rows, got_rows).astype(f32)
    scale_in = lax.rsqrt(jnp.mean(inputs_f * inputs_f, -1, keepdims=True) + epsilon)
    normed_in = (inputs_f * scale_in * gain_in_f).astype(bf16)
    d_out = group_rows(mine_d, got_d)
    in_sides, small, mine_out, normed_in, d_out, mine_pair, mine_down = hold(
        in_sides, small, mine_out, normed_in, d_out, mine_pair, mine_down
    )
    in_fourth = swap_fourth(*in_sides)
    mine_pair = to_users(mine_pair)
    whole_out = lax.all_gather(mine_out, "shard", axis=0, tiled=True)
    in_fourth, normed_in = hold(in_fourth, normed_in)
    whole_in = assembled(
        mine_in[:block],
        [side[:block] for side in in_sides],
        [jnp.concatenate(in_fourth, axis=0)[:block]],
    )
    gate_rows = [
        rows_of[block : block + 8, :block]
        for rows_of in (mine_in, *in_sides, jnp.concatenate(in_fourth, axis=0))
    ]

    def side_by_side(odd, mine, theirs):
        return jnp.concatenate(
            [jnp.where(odd, theirs, mine), jnp.where(odd, mine, theirs)], axis=1
        )

    gates_rows = side_by_side(
        odd_y,
        side_by_side(odd_x, gate_rows[0], gate_rows[1]),
        side_by_side(odd_x, gate_rows[2], gate_rows[3]),
    )
    projected = dot(normed_in, whole_in).astype(bf16).reshape(1, full, inner)
    logits = dot(gates_rows, normed_in, (1, 1))[: 2 * heads]
    logits = logits.reshape(1, 2 * heads, chunks, CHUNK)
    projected, logits, gates_rows, mine_ffn = hold(
        projected, logits, gates_rows, jnp.concatenate([mine_pair, mine_down], axis=1)
    )
    weights_ffn = lax.all_gather(mine_ffn, "shard", axis=0, tiled=True)

    taps = small[:CONV]
    log_rates_here, rate_bias_here = small[CONV, :heads], small[CONV + 1, :heads]
    halo = jnp.zeros((1, HALO, inner), bf16)
    chunk = jnp.arange(chunks, dtype=jnp.int32)
    per_quarter = quarter // CHUNK
    true_quarter = chunk // per_quarter
    places = (
        2 * ((true_quarter % 2) ^ half) + ((true_quarter // 2) ^ core)
    ) * per_quarter + chunk % per_quarter
    no_state = jnp.zeros((1, heads, DK, DV), f32)
    gain_row = gate_gain.reshape(1, DV)
    source = (projected, halo, logits, taps, log_rates_here, rate_bias_here)
    prepared = prepare(places, *source, False)[:11]
    q, k, v, rows, t, w, u, qe, m, b, own_out = prepared
    gated, mixer, states = mixer_output(
        places, (rows, qe, m, b, own_out), no_state, projected, gain_row
    )
    gated = gated.reshape(full, heads * DV)
    far_b, far_a, near_b, near_a = quarters(gated, whole_out)
    far_got = swap_core(far_b.astype(bf16))
    near_got = swap_core(near_b.astype(bf16))
    far_sum, near_a, near_got = hold(add(far_a, far_got), near_a, near_got)
    far_sum = swap_chip(far_sum)
    middle = inputs_f[:quarter] + (near_a + near_got.astype(f32) + far_sum.astype(f32))
    scale_mid = lax.rsqrt(jnp.mean(middle * middle, -1, keepdims=True) + epsilon)
    unit_mid = middle * scale_mid

    mine_mid = (unit_mid * gain_ffn_f).astype(bf16)
    far_mid = swap_chip(mine_mid)
    near_mid = swap_core(mine_mid)
    near = feed_forward(mine_mid, near_mid, d_out, weights_ffn, ())
    far_mid, near = hold(far_mid, near)
    near_a, near_b, near_down_a, near_down_b = near[3:]
    near_got = swap_core(near_b)
    far = feed_forward(
        far_mid, swap_core(far_mid), d_out, weights_ffn, tuple(near[:3])
    )
    normed_mid, hidden, d_pair, far_a, far_b, far_down_a, far_down_b = far
    far_got = swap_core(far_b)
    far_sum, near_got, normed_mid, hidden, d_pair = hold(
        add(far_a, far_got), near_got, normed_mid, hidden, d_pair
    )
    far_sum = swap_chip(far_sum)
    far_down_got = swap_core(far_down_b)
    near_down_got = swap_core(near_down_b)
    grad_ffn = ffn_grads(normed_mid, d_pair, d_out, hidden)
    far_sum, grad_ffn, far_down_got, near_down_got = hold(
        far_sum, grad_ffn, far_down_got, near_down_got
    )
    piece_ffn = lax.psum_scatter(grad_ffn, "shard", scatter_dimension=0, tiled=True)
    d_mid_norm = near_a.astype(f32) + near_got.astype(f32) + far_sum.astype(f32)
    scaled_mid = d_mid_norm * gain_ffn_f
    d_middle = d_out[:quarter].astype(f32) + scale_mid * (
        scaled_mid - unit_mid * jnp.mean(scaled_mid * unit_mid, -1, keepdims=True)
    )
    d_low = d_middle.astype(bf16)
    far_low = swap_chip(d_low)
    near_low = swap_core(d_low)
    far_low, near_low, far_down_a, far_down_got = hold(
        far_low, near_low, far_down_a, far_down_got
    )
    d_parts = (d_low, near_low, far_low, swap_core(far_low))

    far_down_sum = swap_chip(add(far_down_a, far_down_got))
    branch = branch_back(places, rows, d_parts, whole_out, mixer, projected, gain_row, qe, m)
    branch, gated = hold(branch, gated)
    d_mixer, d_og, n, _, gain_gate_part = branch

    def head_grads(h, d_mixer):
        d_projected, _, _, d_logits, rate_rows, tap_rows = mixer_grads(
            places, *source, q, k, v, rows, t, w, u, m, states, d_mixer, n, no_state, d_og,
            start=h, count=1,
        )
        return d_projected.reshape(full, HEAD), d_logits, rate_rows, tap_rows

    even = half == 0
    first = seq == 0
    send_a = [(0, 0), (1, 2), (2, 1), (3, 3)]
    send_b = [(0, 1), (1, 3), (2, 0), (3, 2)]

    def to_outputs(mine):
        low, high = mine[:share], mine[share:]
        with jax.named_scope("to_outputs"):
            got_a = lax.ppermute(jnp.where(first, low, high), "tp", send_a)
            got_b = lax.ppermute(jnp.where(first, high, low), "tp", send_b)
        return got_a, got_b

    def stacked(got_a, got_b):
        return jnp.stack([jnp.where(even, got_a, got_b), jnp.where(even, got_b, got_a)])

    place_x = shard.reshape(1).astype(jnp.int32)
    first_head = head_grads(0, d_mixer)
    first_head, d_mixer, far_down_sum = hold(first_head, d_mixer, far_down_sum)
    grad_both, part_first = both_grads(normed_in, first_head[0], whole_in, d_parts, gated)
    grad_both, part_first, d_mixer, piece_ffn = hold(grad_both, part_first, d_mixer, piece_ffn)
    owned_pair = to_owners(piece_ffn[:, : 2 * hidden.shape[1]])
    piece_both = lax.psum_scatter(grad_both, "shard", scatter_dimension=0, tiled=True)
    layer_rows = (
        middle
        + near_down_a.astype(f32)
        + near_down_got.astype(f32)
        + far_down_sum.astype(f32)
    ).astype(bf16)

    last_head, owned_pair = hold(head_grads(1, d_mixer), owned_pair)

    owned_down = to_owners(piece_ffn[:, 2 * hidden.shape[1] :])
    *sent, part_last = input_grad(place_x, normed_in, last_head[0], whole_in, 1)
    sent, part_last, last_head, owned_down, layer_rows = hold(
        sent, part_last, last_head, owned_down, layer_rows
    )
    steps_last = piece_first(*sent)
    layer_got = to_outputs(layer_rows)
    logits_first = first_head[1].reshape(2, full)
    logits_last = last_head[1].reshape(2, full)
    d_logit_rows = jnp.concatenate(
        [logits_first, logits_last, jnp.zeros((8 - 2 * heads, full), f32)], axis=0
    ).astype(bf16)
    grad_gates = dot(d_logit_rows, normed_in)
    packed = jnp.concatenate(
        [
            jnp.concatenate([first_head[3][0], last_head[3][0]], axis=1),
            grad_gates,
            part_first + part_last + gates_rows.astype(f32) * grad_gates,
            jnp.concatenate(
                [
                    gain_gate_part[0], gain_gate_part[1], first_head[2][0, 0], last_head[2][0, 0],
                    first_head[1][0, 0], last_head[1][0, 0],
                ],
                axis=1,
            ),
        ],
        axis=0,
    )
    packed_got = swap_x(packed)
    backs = input_back(first_head[0], last_head[0], d_logit_rows, whole_in, gates_rows)
    backs, steps_last, layer_got, packed, packed_got, piece_both = hold(
        backs, steps_last, layer_got, packed, packed_got, piece_both
    )
    owned_both = to_owners(piece_both)
    near_a, near_b, far_a, far_b = backs
    far_got = swap_core(far_b)
    near_got = swap_core(near_b)
    steps_last = piece_second(*steps_last)
    packed = packed + packed_got
    packed_got = swap_y(packed)
    (
        far_sum, near_got, near_a, steps_last, packed, packed_got, owned_pair, owned_down, owned_both,
    ) = hold(
        add(far_a, far_got), near_got, near_a, steps_last, packed, packed_got, owned_pair,
        owned_down, owned_both,
    )
    far_sum = swap_chip(far_sum)
    piece_last = to_owners(piece_end(*steps_last))
    packed = packed + packed_got
    sum_pair = both_cores(owned_pair)
    sum_gate, sum_up = unpaired(sum_pair)
    far_sum, sum_gate, sum_up, near_a, owned_down, layer_got, piece_last, packed, owned_both = hold(
        far_sum, sum_gate, sum_up, near_a, owned_down, layer_got, piece_last, packed, owned_both
    )
    packed = to_owners(packed)
    d_in_norm = near_a.astype(f32) + near_got.astype(f32) + far_sum.astype(f32)
    unit_in = (inputs_f * scale_in)[:quarter]
    scaled_in = d_in_norm * gain_in_f
    token_rows = d_middle + scale_in[:quarter] * (
        scaled_in - unit_in * jnp.mean(scaled_in * unit_in, -1, keepdims=True)
    )
    token_got = to_outputs(token_rows.astype(bf16))
    packed = both_cores(packed)
    sum_down = both_cores(owned_down).T
    layer_out = stacked(*layer_got)
    sum_both = both_cores(owned_both)
    sum_out = sum_both[:, HEAD:].T
    sum_last = both_cores(piece_last)

    part_ffn = jnp.sum(ffn_gate.astype(f32) * sum_gate + ffn_up.astype(f32) * sum_up, 1)
    sum_taps, sum_gates, part_in, rest = (packed[8 * i : 8 * i + 8] for i in range(4))
    sum_gain = jnp.sum(rest[:, :DV] + rest[:, DV : 2 * DV], 0)
    sum_rates = jnp.sum(rest[:, 2 * DV :].reshape(8, 2 * heads, CHUNK), (0, 2))
    rows_here = gain_in.shape[0]

    def own_block(rows_of):
        return lax.dynamic_slice_in_dim(rows_of, shard * rows_here, rows_here, -1)

    over_blocks = jnp.concatenate([sum_gain, jnp.sum(own_block(part_in), 0), part_ffn])
    over_blocks = jnp.pad(over_blocks, (0, -over_blocks.shape[0] % 1024)).reshape(-1, 128)
    over_blocks = over_blocks + swap_chip(over_blocks)
    with jax.named_scope("swap_pair"):
        other_pair = lax.ppermute(over_blocks, "tp", [(i, i ^ 2) for i in range(tp_count)])
    over_blocks = (over_blocks + other_pair).reshape(-1)
    return (
        layer_out,
        stacked(*token_got).astype(f32),
        jnp.concatenate([sum_both[:, :HEAD], sum_last], axis=1),
        own_block(sum_gates)[: 2 * heads].T,
        sum_taps[:CONV],
        sum_rates[:heads],
        sum_rates[heads:],
        over_blocks[:DV],
        sum_out,
        sum_gate,
        sum_up,
        sum_down,
        over_blocks[DV : DV + rows_here] / gain_in.astype(f32),
        over_blocks[DV + rows_here : DV + 2 * rows_here] / gain_ffn.astype(f32),
    )


def solution(mesh):
    placed = (
        P("shard", "ctx", None),
        P("shard", "tp"),
        P("shard", "tp"),
        P(None, "tp"),
        P("tp"),
        P("tp"),
        P(),
        P("tp", "shard"),
        P("shard", "tp"),
        P("shard", "tp"),
        P("tp", "shard"),
        P("shard"),
        P("shard"),
        P("shard", "ctx", None),
    )
    shape = dict(mesh.shape)
    paired = (shape["shard"], shape["ctx"], shape["tp"]) == (4, 2, 4)

    def body(*arrays):
        seqs, length, _ = arrays[0].shape
        heads = arrays[4].shape[0]
        if paired and seqs == 2 and heads == 2 and length % (2 * CHUNK) == 0:
            return local_paired(*arrays)
        return local(*arrays)

    return jax.shard_map(
        body,
        mesh=mesh,
        in_specs=placed,
        out_specs=(
            P("shard", ("ctx", "tp"), None),
            P("shard", ("ctx", "tp"), None),
            P("shard", "tp"),
            P("shard", "tp"),
            P(None, "tp"),
            P("tp"),
            P("tp"),
            P(),
            P("tp", "shard"),
            P("shard", "tp"),
            P("shard", "tp"),
            P("tp", "shard"),
            P("shard"),
            P("shard"),
        ),
        check_vma=False,
    )
```

```python
import functools

import jax
import jax.numpy as jnp
from jax import lax
from jax.experimental import pallas as pl
from jax.experimental.pallas import tpu as pltpu
from jax.sharding import PartitionSpec as P

DK = 128
DV = 256
QKV = 2 * DK + DV
HEAD = QKV + DV
CONV = 4
CHUNK = 128
HALO = 16
ROWS = 8

epsilon = 1e-06
f32 = jnp.float32
bf16 = jnp.bfloat16


def mm(left, right, contract=(1, 0)):
    return lax.dot_general(
        left.astype(bf16),
        right.astype(bf16),
        (((contract[0],), (contract[1],)), ((), ())),
        preferred_element_type=f32,
    )


def mm_split(left, right):
    left_hi = left.astype(bf16)
    right_hi = right.astype(bf16)
    left_lo = left - left_hi.astype(f32)
    right_lo = right - right_hi.astype(f32)
    return mm(left_hi, right_hi) + (mm(left_hi, right_lo) + mm(left_lo, right_hi))


def mm_exact(left, right):
    return lax.dot_general(
        left,
        right,
        (((1,), (0,)), ((), ())),
        precision=lax.Precision.HIGHEST,
        preferred_element_type=f32,
    )


def iotas():
    row = lax.broadcasted_iota(jnp.int32, (CHUNK, CHUNK), 0)
    col = lax.broadcasted_iota(jnp.int32, (CHUNK, CHUNK), 1)
    return row, col


def pad_rows(block):
    missing = CHUNK - block.shape[0]
    return jnp.concatenate([block, jnp.zeros((missing, block.shape[1]), f32)], axis=0)


def softplus(values):
    return jnp.maximum(values, 0.0) + jnp.log1p(jnp.exp(-jnp.abs(values)))


def sigmoid(values):
    return 1.0 / (1.0 + jnp.exp(-values))


def place_of(places, c):
    return pl.ds(pl.multiple_of(places[c] * CHUNK, CHUNK), CHUNK)


def chunk_rows(places, logit_ref, chunks):
    def stacked(row):
        return jnp.concatenate(
            [logit_ref[0, row, pl.ds(places[c], 1), :] for c in range(chunks)], axis=0
        )

    return stacked(0), stacked(1)


def invert_units(lowers, row, col):
    eye = (row == col).astype(f32)
    same = (row // 16) == (col // 16)
    powers = [jnp.where(same, n, 0.0) for n in lowers]
    inverses = [eye - p for p in powers]
    for _ in range(3):
        powers = [mm_split(p, p) for p in powers]
        inverses = [x + mm_split(x, p) for x, p in zip(inverses, powers)]
    size = 16
    while size < CHUNK:
        joins = ((row // (2 * size)) == (col // (2 * size))) & ((row // size) != (col // size))
        middles = [mm_split(jnp.where(joins, n, 0.0), x) for n, x in zip(lowers, inverses)]
        inverses = [x - mm_split(x, m) for x, m in zip(inverses, middles)]
        size *= 2
    return inverses


def conv_into(places, scratch, x_qk, x_v, halo_qk, halo_v, taps_qk, taps_v, length):
    scratch[0:ROWS, 0 : 2 * DK] = halo_qk[0, HALO - ROWS :, :].astype(f32)
    scratch[0:ROWS, 2 * DK :] = halo_v[0, HALO - ROWS :, :].astype(f32)
    for c in range(length // CHUNK):
        body = slice(ROWS + c * CHUNK, ROWS + (c + 1) * CHUNK)
        scratch[body, 0 : 2 * DK] = x_qk[0, place_of(places, c), :].astype(f32)
        scratch[body, 2 * DK :] = x_v[0, place_of(places, c), :].astype(f32)
    taps = jnp.concatenate([taps_qk[...], taps_v[...]], axis=1).astype(f32)
    first = ROWS - CONV + 1
    mixed = taps[0:1, :] * scratch[first : first + length, :]
    for j in range(1, CONV):
        mixed = mixed + taps[j : j + 1, :] * scratch[first + j : first + j + length, :]
    return mixed, taps


def prep_kernel(
    places, rates, biases, x_qk, x_v, halo_qk, halo_v, logits, taps_qk, taps_v,
    q_out, k_out, v_out, rows_out, t_out, w_out, u_out, qe_out, m_out, b_out, p_out, end_out, map_out,
    scratch,
):
    head = pl.program_id(0)
    length = x_qk.shape[1]
    chunks = length // CHUNK
    mixed, _ = conv_into(
        places, scratch, x_qk, x_v, halo_qk, halo_v, taps_qk, taps_v, length
    )
    active = mixed * sigmoid(mixed)
    q_act = active[:, :DK]
    k_act = active[:, DK : 2 * DK]
    q_all = (
        q_act * lax.rsqrt(jnp.sum(q_act * q_act, -1, keepdims=True) + epsilon) * DK ** (-0.5)
    ).astype(bf16)
    k_all = (
        k_act * lax.rsqrt(jnp.sum(k_act * k_act, -1, keepdims=True) + epsilon)
    ).astype(bf16)
    v_all = active[:, 2 * DK :].astype(bf16)
    q_out[0, 0] = q_all
    k_out[0, 0] = k_all
    v_out[0, 0] = v_all
    decay_logit, strength_logit = chunk_rows(places, logits, chunks)
    decay = -jnp.exp(rates[head]) * softplus(decay_logit + biases[head])
    row, col = iotas()
    lower = row >= col
    strict = row > col
    total = mm_exact(pad_rows(decay)[: max(8, chunks)], (row <= col).astype(f32))[:chunks]
    strength = sigmoid(strength_logit)
    stacked = jnp.concatenate([total, strength], axis=0)
    rows_out[0, 0] = stacked
    columns = jnp.transpose(pad_rows(stacked))
    units = range(chunks)
    span = [slice(c * CHUNK, (c + 1) * CHUNK) for c in units]
    g_col = [columns[:, c : c + 1] for c in units]
    b_col = [columns[:, chunks + c : chunks + c + 1] for c in units]
    table = [
        jnp.where(lower, jnp.exp(jnp.where(lower, g_col[c] - total[c : c + 1, :], 0.0)), 0.0)
        for c in units
    ]
    q = [q_all[s] for s in span]
    k = [k_all[s] for s in span]
    gram = [mm(k[c], k[c], (1, 1)) for c in units]
    score = [mm(q[c], k[c], (1, 1)) * table[c] for c in units]
    lowers = [jnp.where(strict, b_col[c] * gram[c] * table[c], 0.0) for c in units]
    inverse = invert_units(lowers, row, col)
    grown = [jnp.exp(g_col[c]) for c in units]
    w = [mm(inverse[c], (b_col[c] * grown[c]) * k[c].astype(f32)) for c in units]
    u = [mm(inverse[c], b_col[c] * v_all[span[c]].astype(f32)) for c in units]
    qe = [grown[c] * q[c].astype(f32) - mm(score[c], w[c]) for c in units]
    own = [mm(score[c], u[c]) for c in units]
    last = [g_col[c][CHUNK - 1 :, :] for c in units]
    k_late = [jnp.exp(last[c] - g_col[c]) * k[c].astype(f32) for c in units]
    m = [-mm(k_late[c], w[c], (0, 0)) for c in units]
    b = [mm(k_late[c], u[c], (0, 0)) for c in units]
    state = b[0]
    for c in units:
        t_out[0, 0, c] = inverse[c].astype(bf16)
        w_out[0, 0, c] = w[c].astype(bf16)
        u_out[0, 0, c] = u[c]
        qe_out[0, 0, c] = qe[c].astype(bf16)
        m_out[0, 0, c] = m[c].astype(bf16)
        b_out[0, 0, c] = b[c]
        p_out[0, 0, c] = own[c]
        if c and end_out is not None:
            state = jnp.exp(last[c]) * state + mm(m[c], state) + b[c]
    if end_out is not None:
        end_out[0, 0] = state
    if map_out is not None:
        chain = (row == col).astype(f32)
        for c in units:
            chain = jnp.exp(last[c]) * chain + mm(m[c], chain)
        map_out[0, 0] = chain


def output_kernel(
    places, rows, qe, m, b, own, arriving, og, gain,
    gated_out, mixer_out, states_out,
):
    chunks = qe.shape[2]
    last = jnp.exp(rows[0, 0][0:chunks, CHUNK - 1 :])
    state = arriving[0, 0].astype(f32)
    gain_row = gain[...].astype(f32)
    for c in range(chunks):
        s = slice(c * CHUNK, (c + 1) * CHUNK)
        states_out[0, 0, c] = state.astype(bf16)
        out = mm(qe[0, 0, c], state) + own[0, 0, c]
        mixer_out[0, s, :] = out
        scale = lax.rsqrt(jnp.mean(out * out, -1, keepdims=True) + epsilon)
        gate = og[0, place_of(places, c), :].astype(f32)
        gated_out[0, place_of(places, c), :] = (out * scale * gain_row * (gate * sigmoid(gate))).astype(bf16)
        if c < chunks - 1:
            state = last[c : c + 1, :] * state + mm(m[0, 0, c], state) + b[0, 0, c]


def norm_back_kernel(
    places, rows, d_gated, mixer, og, gain, qe, m,
    d_out, d_og_out, n_out, start_out, gain_out,
):
    seq = pl.program_id(1)
    chunks = qe.shape[2]
    last = jnp.exp(rows[0, 0][0:chunks, CHUNK - 1 :])
    gain_row = gain[...].astype(f32)
    gain_sum = jnp.zeros((8, DV), f32)
    adds = []
    for c in range(chunks):
        s = slice(c * CHUNK, (c + 1) * CHUNK)
        out = mixer[0, s, :]
        gate = og[0, place_of(places, c), :].astype(f32)
        sig = sigmoid(gate)
        swish = gate * sig
        dg = d_gated[0, place_of(places, c), :].astype(f32)
        scale = lax.rsqrt(jnp.mean(out * out, -1, keepdims=True) + epsilon)
        unit = out * scale
        spread = dg * unit
        e = dg * (gain_row * swish)
        d_mix = scale * (e - unit * jnp.mean(e * unit, -1, keepdims=True))
        d_og_out[0, 0, s, :] = (spread * gain_row * (sig * (1.0 + gate * (1.0 - sig)))).astype(bf16)
        gain_sum = gain_sum + jnp.sum((spread * swish).reshape(CHUNK // 8, 8, DV), axis=0)
        d_low = d_mix.astype(bf16)
        d_out[0, 0, c] = d_low
        add = mm(qe[0, 0, c], d_low, (0, 0))
        n_out[0, 0, c] = add
        adds.append(add)
    if start_out is not None:
        back = adds[-1]
        for c in reversed(range(chunks - 1)):
            back = last[c : c + 1, :] * back + mm(m[0, 0, c], back, (0, 0)) + adds[c]
        start_out[0, 0] = back

    @pl.when(seq == 0)
    def _():
        gain_out[0] = gain_sum

    @pl.when(seq != 0)
    def _():
        gain_out[0] = gain_out[0] + gain_sum


def grad_kernel(
    start, places, rates, biases, x_qk, x_v, halo_qk, halo_v, logits, taps_qk, taps_v,
    q_in, k_in, v_in, rows, t_in, w_in, u_in, m_in, states, d_out, n_in, arriving, d_og,
    d_proj_out, d_halo_out, d_tail_out, d_logit_out, rate_out, taps_out,
    scratch, grads,
):
    head = pl.program_id(0) + start
    seq = pl.program_id(1)
    length = x_qk.shape[1]
    chunks = length // CHUNK
    units = range(chunks)
    row, col = iotas()
    lower = row >= col
    strict = row > col
    stacked = rows[0, 0]
    total = stacked[0:chunks]
    strength = stacked[chunks : 2 * chunks]
    columns = jnp.transpose(pad_rows(stacked))
    g_col = [columns[:, c : c + 1] for c in units]
    b_col = [columns[:, chunks + c : chunks + c + 1] for c in units]
    last = [g_col[c][CHUNK - 1 :, :] for c in units]
    ends = [None] * chunks
    back = arriving[0, 0].astype(f32)
    for c in reversed(units):
        ends[c] = back
        if c:
            back = jnp.exp(last[c]) * back + mm(m_in[0, 0, c], back, (0, 0)) + n_in[0, 0, c]
    span = [slice(c * CHUNK, (c + 1) * CHUNK) for c in units]
    table = [
        jnp.where(lower, jnp.exp(jnp.where(lower, g_col[c] - total[c : c + 1, :], 0.0)), 0.0)
        for c in units
    ]
    q = [q_in[0, 0, s, :] for s in span]
    k = [k_in[0, 0, s, :] for s in span]
    v = [v_in[0, 0, s, :] for s in span]
    k_f = [k[c].astype(f32) for c in units]
    q_f = [q[c].astype(f32) for c in units]
    t = [t_in[0, 0, c] for c in units]
    w = [w_in[0, 0, c] for c in units]
    u = [u_in[0, 0, c] for c in units]
    s_in = [states[0, 0, c] for c in units]
    d_o = [d_out[0, 0, c] for c in units]
    gram = [mm(k[c], k[c], (1, 1)) * table[c] for c in units]
    score = [mm(q[c], k[c], (1, 1)) * table[c] for c in units]
    grown = [jnp.exp(g_col[c]) for c in units]
    fade = [jnp.exp(last[c] - g_col[c]) for c in units]
    fresh = [u[c] - mm(w[c], s_in[c]) for c in units]
    k_late = [fade[c] * k_f[c] for c in units]
    d_fresh = [mm(score[c], d_o[c], (0, 0)) + mm(k_late[c], ends[c]) for c in units]
    d_score = [jnp.where(lower, mm(d_o[c], fresh[c], (1, 1)), 0.0) for c in units]
    d_q_grown = [mm(d_o[c], s_in[c], (1, 1)) for c in units]
    d_k_late = [mm(fresh[c], ends[c], (1, 1)) for c in units]
    d_w = [-mm(d_fresh[c], s_in[c], (1, 1)) for c in units]
    d_vb = [mm(t[c], d_fresh[c], (0, 0)) for c in units]
    d_kb = [mm(t[c], d_w[c], (0, 0)) for c in units]
    d_lower = [
        jnp.where(strict, -(mm(d_vb[c], u[c], (1, 1)) + mm(d_kb[c], w[c], (1, 1))), 0.0)
        for c in units
    ]
    d_score_t = [d_score[c] * table[c] for c in units]
    d_lower_b = [d_lower[c] * b_col[c] for c in units]
    d_gram = [d_lower_b[c] * table[c] for c in units]
    cols = []
    cols_b = []
    rows_g = []
    for c in units:
        s = span[c]
        paired = d_score[c] * score[c] + d_lower_b[c] * gram[c]
        late = k_late[c] * d_k_late[c]
        k_dot = grown[c] * (d_kb[c] * k_f[c])
        per_row = (
            paired + grown[c] * (q_f[c] * d_q_grown[c]) - late + b_col[c] * k_dot
        )
        cols.append(jnp.sum(per_row, -1, keepdims=True))
        v_f = v[c].astype(f32)
        v_dot = d_vb[c] * v_f
        cols_b.append(
            jnp.sum(
                d_lower[c] * gram[c] + k_dot + v_dot[:, :DK] + v_dot[:, DK:], -1, keepdims=True
            )
        )
        kept = s_in[c].astype(f32) * ends[c]
        whole = jnp.sum(
            jnp.sum(late, 0, keepdims=True)
            + jnp.exp(last[c]) * jnp.sum(kept[:, :DK] + kept[:, DK:], 0, keepdims=True),
            -1,
            keepdims=True,
        )
        rows_g.append((jnp.sum(paired, 0, keepdims=True), whole))
        d_q = mm(d_score_t[c], k[c]) + grown[c] * d_q_grown[c]
        d_k = (
            mm(d_score_t[c], q[c], (0, 0))
            + mm(d_gram[c], k[c])
            + mm(d_gram[c], k[c], (0, 0))
            + fade[c] * d_k_late[c]
            + (b_col[c] * grown[c]) * d_kb[c]
        )
        grads[ROWS + s.start : ROWS + s.stop, 0:DK] = d_q
        grads[ROWS + s.start : ROWS + s.stop, DK : 2 * DK] = d_k
        grads[ROWS + s.start : ROWS + s.stop, 2 * DK :] = b_col[c] * d_vb[c]
    wide = jnp.concatenate(
        cols + cols_b + [jnp.zeros((CHUNK, CHUNK - 2 * chunks), f32)], axis=1
    )
    tall = jnp.transpose(wide)
    d_total = tall[0:chunks] - jnp.concatenate([r for r, _ in rows_g], axis=0)
    d_strength = tall[chunks : 2 * chunks]
    d_decay = mm_exact(pad_rows(d_total)[: max(8, chunks)], lower.astype(f32))[:chunks]
    d_decay = d_decay + jnp.concatenate([w_ for _, w_ in rows_g], axis=0)
    decay_logit, _ = chunk_rows(places, logits, chunks)
    biased = decay_logit + biases[head]
    rate = jnp.exp(rates[head])
    d_logit = -d_decay * rate * sigmoid(biased)
    d_strength_logit = d_strength * strength * (1.0 - strength)
    for c in units:
        d_logit_out[0, 0, pl.ds(places[c], 1), :] = d_logit[c : c + 1, :]
        d_logit_out[0, 1, pl.ds(places[c], 1), :] = d_strength_logit[c : c + 1, :]
    rate_out[0, 0] = -d_decay * rate * softplus(biased)

    mixed, taps = conv_into(
        places, scratch, x_qk, x_v, halo_qk, halo_v, taps_qk, taps_v, length
    )
    sig = sigmoid(mixed)
    active = mixed * sig
    slope = sig * (1.0 + mixed * (1.0 - sig))

    def unnorm(act, grad, factor):
        scale = lax.rsqrt(jnp.sum(act * act, -1, keepdims=True) + epsilon)
        unit = act * scale
        return (factor * scale) * (grad - unit * jnp.sum(unit * grad, -1, keepdims=True))

    body = slice(ROWS, ROWS + length)
    grads[body, 0:DK] = (
        unnorm(active[:, :DK], grads[body, 0:DK], DK ** (-0.5)) * slope[:, :DK]
    )
    grads[body, DK : 2 * DK] = (
        unnorm(active[:, DK : 2 * DK], grads[body, DK : 2 * DK], 1.0) * slope[:, DK : 2 * DK]
    )
    grads[body, 2 * DK :] = grads[body, 2 * DK :] * slope[:, 2 * DK :]
    grads[0:ROWS, :] = jnp.zeros((ROWS, QKV), f32)
    grads[ROWS + length :, :] = jnp.zeros((ROWS, QKV), f32)
    d_x = None
    d_halo = None
    tap_rows = []
    d_conv = grads[body, :]
    first = ROWS - CONV + 1
    for j in range(CONV):
        ahead = CONV - 1 - j
        part = taps[j : j + 1, :] * grads[ROWS + ahead : ROWS + ahead + length, :]
        d_x = part if d_x is None else d_x + part
        edge = taps[j : j + 1, :] * grads[ahead : ahead + ROWS, :]
        d_halo = edge if d_halo is None else d_halo + edge
        tap_rows.append(
            jnp.sum(d_conv * scratch[first + j : first + j + length, :], 0, keepdims=True)
        )
    for c in units:
        d_proj_out[0, place_of(places, c), 0:QKV] = d_x[span[c]].astype(bf16)
        d_proj_out[0, place_of(places, c), QKV:] = d_og[0, 0, span[c], :]
    d_tail_out[0, 0] = d_x[length - ROWS :, :]
    d_halo_out[0, 0] = d_halo
    tap_rows = jnp.concatenate(tap_rows + [jnp.zeros((8 - CONV, QKV), f32)], axis=0)

    @pl.when(seq == 0)
    def _():
        taps_out[0] = tap_rows

    @pl.when(seq != 0)
    def _():
        taps_out[0] = taps_out[0] + tap_rows


def cost(micros):
    return pl.CostEstimate(
        flops=int(micros * 1e8), bytes_accessed=int(micros * 1e5), transcendentals=0
    )


def params():
    return pltpu.CompilerParams(
        dimension_semantics=("arbitrary", "arbitrary"), vmem_limit_bytes=56 * 1024 * 1024
    )


def smem():
    return pl.BlockSpec(memory_space=pltpu.SMEM)


def per_unit(*shape, start=0):
    zeros = (0,) * len(shape)
    return pl.BlockSpec((1, 1) + shape, lambda h, s: (s, h + start) + zeros)


def input_specs(length, start=0):
    return [
        smem(),
        smem(),
        smem(),
        pl.BlockSpec((1, length, 256), lambda h, s: (s, 0, 3 * (h + start))),
        pl.BlockSpec((1, length, 256), lambda h, s: (s, 0, 3 * (h + start) + 1)),
        pl.BlockSpec((1, HALO, 256), lambda h, s: (s, 0, 3 * (h + start))),
        pl.BlockSpec((1, HALO, 256), lambda h, s: (s, 0, 3 * (h + start) + 1)),
        pl.BlockSpec((1, 2, length // CHUNK, CHUNK), lambda h, s: (s, h + start, 0, 0)),
        pl.BlockSpec((CONV, 256), lambda h, s: (0, 2 * (h + start))),
        pl.BlockSpec((CONV, 256), lambda h, s: (0, 2 * (h + start) + 1)),
    ]


def prepare(places, projected, halo, logits, taps, rates, biases, with_map, with_end=True):
    seqs, length, _ = projected.shape
    heads = rates.shape[0]
    chunks = length // CHUNK

    def out(dtype, *shape):
        return jax.ShapeDtypeStruct((seqs, heads) + shape, dtype), per_unit(*shape)

    outs = [
        out(bf16, length, DK),
        out(bf16, length, DK),
        out(bf16, length, DV),
        out(f32, 2 * chunks, CHUNK),
        out(bf16, chunks, CHUNK, CHUNK),
        out(bf16, chunks, CHUNK, DK),
        out(f32, chunks, CHUNK, DV),
        out(bf16, chunks, CHUNK, DK),
        out(bf16, chunks, DK, DK),
        out(f32, chunks, DK, DV),
        out(f32, chunks, CHUNK, DV),
        out(f32, DK, DV),
    ]
    if with_map:
        outs.append(out(f32, DK, DK))
        kernel = prep_kernel
    elif with_end:

        def kernel(*refs):
            prep_kernel(*refs[:-1], None, refs[-1])

    else:
        outs.pop()

        def kernel(*refs):
            prep_kernel(*refs[:-1], None, None, refs[-1])

    results = pl.pallas_call(
        kernel,
        grid=(heads, seqs),
        in_specs=input_specs(length),
        out_specs=[spec for _, spec in outs],
        out_shape=[shape for shape, _ in outs],
        scratch_shapes=[pltpu.VMEM((length + ROWS, QKV), f32)],
        compiler_params=params(),
        cost_estimate=cost(9.0 * heads * seqs * chunks / 8),
        name="prepare",
    )(places, rates, biases, projected, projected, halo, halo, logits, taps, taps)
    return results if with_map else list(results) + [None]


def mixer_output(places, kept, arriving, projected, gain):
    rows, qe, m, b, own = kept
    seqs, heads, chunks = qe.shape[:3]
    length = chunks * CHUNK
    return pl.pallas_call(
        output_kernel,
        grid=(heads, seqs),
        in_specs=[
            smem(),
            per_unit(2 * chunks, CHUNK),
            per_unit(chunks, CHUNK, DK),
            per_unit(chunks, DK, DK),
            per_unit(chunks, DK, DV),
            per_unit(chunks, CHUNK, DV),
            per_unit(DK, DV),
            pl.BlockSpec((1, length, 256), lambda h, s: (s, 0, 3 * h + 2)),
            pl.BlockSpec((1, DV), lambda h, s: (0, 0)),
        ],
        out_specs=[
            pl.BlockSpec((1, length, DV), lambda h, s: (s, 0, h)),
            pl.BlockSpec((1, length, DV), lambda h, s: (s, 0, h)),
            per_unit(chunks, DK, DV),
        ],
        out_shape=[
            jax.ShapeDtypeStruct((seqs, length, heads * DV), bf16),
            jax.ShapeDtypeStruct((seqs, length, heads * DV), f32),
            jax.ShapeDtypeStruct((seqs, heads, chunks, DK, DV), bf16),
        ],
        compiler_params=params(),
        cost_estimate=cost(4.0 * heads * seqs * chunks / 8),
        name="mixer_output",
    )(places, rows, qe, m, b, own, arriving, projected, gain)


def norm_back(places, rows, d_gated, mixer, projected, gain, qe, m, start=0, count=None):
    seqs, heads, chunks = qe.shape[:3]
    length = chunks * CHUNK
    heads = count or heads
    return pl.pallas_call(
        norm_back_kernel,
        grid=(heads, seqs),
        in_specs=[
            smem(),
            per_unit(2 * chunks, CHUNK, start=start),
            pl.BlockSpec((1, length, DV), lambda h, s: (s, 0, h + start)),
            pl.BlockSpec((1, length, DV), lambda h, s: (s, 0, h + start)),
            pl.BlockSpec((1, length, 256), lambda h, s: (s, 0, 3 * (h + start) + 2)),
            pl.BlockSpec((1, DV), lambda h, s: (0, 0)),
            per_unit(chunks, CHUNK, DK, start=start),
            per_unit(chunks, DK, DK, start=start),
        ],
        out_specs=[
            per_unit(chunks, CHUNK, DV),
            per_unit(length, DV),
            per_unit(chunks, DK, DV),
            per_unit(DK, DV),
            pl.BlockSpec((1, 8, DV), lambda h, s: (h, 0, 0)),
        ],
        out_shape=[
            jax.ShapeDtypeStruct((seqs, heads, chunks, CHUNK, DV), bf16),
            jax.ShapeDtypeStruct((seqs, heads, length, DV), bf16),
            jax.ShapeDtypeStruct((seqs, heads, chunks, DK, DV), f32),
            jax.ShapeDtypeStruct((seqs, heads, DK, DV), f32),
            jax.ShapeDtypeStruct((heads, 8, DV), f32),
        ],
        compiler_params=params(),
        cost_estimate=cost(4.0 * heads * seqs * chunks / 8),
        name="norm_back",
    )(places, rows, d_gated, mixer, projected, gain, qe, m)


def mixer_grads(
    places, projected, halo, logits, taps, rates, biases, q, k, v, rows, t, w, u, m, states, d_out, n, arriving, d_og,
    start=0, count=None,
):
    seqs, length, _ = projected.shape
    heads = count or rates.shape[0]
    chunks = length // CHUNK
    return pl.pallas_call(
        functools.partial(grad_kernel, start),
        grid=(heads, seqs),
        in_specs=input_specs(length, start)
        + [
            per_unit(length, DK, start=start),
            per_unit(length, DK, start=start),
            per_unit(length, DV, start=start),
            per_unit(2 * chunks, CHUNK, start=start),
            per_unit(chunks, CHUNK, CHUNK, start=start),
            per_unit(chunks, CHUNK, DK, start=start),
            per_unit(chunks, CHUNK, DV, start=start),
            per_unit(chunks, DK, DK, start=start),
            per_unit(chunks, DK, DV, start=start),
            per_unit(chunks, CHUNK, DV, start=start),
            per_unit(chunks, DK, DV, start=start),
            per_unit(DK, DV, start=start),
            per_unit(length, DV, start=start),
        ],
        out_specs=[
            pl.BlockSpec((1, length, HEAD), lambda h, s: (s, 0, h)),
            per_unit(ROWS, QKV),
            per_unit(ROWS, QKV),
            pl.BlockSpec((1, 2, chunks, CHUNK), lambda h, s: (s, h, 0, 0)),
            per_unit(chunks, CHUNK),
            pl.BlockSpec((1, 8, QKV), lambda h, s: (h, 0, 0)),
        ],
        out_shape=[
            jax.ShapeDtypeStruct((seqs, length, heads * HEAD), bf16),
            jax.ShapeDtypeStruct((seqs, heads, ROWS, QKV), f32),
            jax.ShapeDtypeStruct((seqs, heads, ROWS, QKV), f32),
            jax.ShapeDtypeStruct((seqs, 2 * heads, chunks, CHUNK), f32),
            jax.ShapeDtypeStruct((seqs, heads, chunks, CHUNK), f32),
            jax.ShapeDtypeStruct((heads, 8, QKV), f32),
        ],
        scratch_shapes=[
            pltpu.VMEM((length + ROWS, QKV), f32),
            pltpu.VMEM((length + 2 * ROWS, QKV), f32),
        ],
        compiler_params=params(),
        cost_estimate=cost(10.0 * heads * seqs * chunks / 8),
        name="mixer_grads",
    )(
        places, rates, biases, projected, projected, halo, halo, logits, taps, taps,
        q, k, v, rows, t, w, u, m, states, d_out, n, arriving, d_og,
    )


def shifted(block, axis, distance):
    devices = range(lax.axis_size(axis))
    route = [(i - distance, i) for i in devices if i - distance in devices]
    return lax.ppermute(block, axis, route)


def relay(first, maps, distance):
    arriving = shifted(first.astype(bf16), "ctx", distance)
    for _ in range(lax.axis_size("ctx") - 2):
        leaving = first + maps(arriving.astype(f32))
        arriving = shifted(leaving.astype(bf16), "ctx", distance)
    return arriving


def dot(left, right, contract=(1, 0)):
    return lax.dot_general(
        left, right, (((contract[0],), (contract[1],)), ((), ())), preferred_element_type=f32
    )


def local(
    tokens,
    proj_in,
    proj_gates,
    conv_taps,
    log_rates,
    rate_bias,
    gate_gain,
    proj_out,
    ffn_gate,
    ffn_up,
    ffn_down,
    gain_in,
    gain_ffn,
    cotangent,
):
    seqs, length, width = tokens.shape
    row_count = seqs * length
    heads = log_rates.shape[0]
    chunks = length // CHUNK
    tp_count = lax.axis_size("tp")
    tp_place = lax.axis_index("tp")
    share = length // tp_count
    with_map = lax.axis_size("ctx") > 2

    def own(rows):
        return lax.dynamic_slice_in_dim(
            rows.reshape(seqs, length, rows.shape[-1]), tp_place * share, share, 1
        )

    def scatter_sum(partial):
        partial = partial.astype(bf16).reshape(seqs, length, width)
        return lax.psum_scatter(partial, "tp", scatter_dimension=1, tiled=True).astype(f32)

    def gather_rows(rows):
        return lax.all_gather(rows, "tp", axis=1, tiled=True).reshape(row_count, width)

    whole_in = lax.all_gather(proj_in, "shard", axis=0, tiled=True)
    whole_gates = lax.all_gather(proj_gates, "shard", axis=0, tiled=True)
    whole_out = lax.all_gather(proj_out, "shard", axis=1, tiled=True)
    whole_gate = lax.all_gather(ffn_gate, "shard", axis=0, tiled=True)
    whole_up = lax.all_gather(ffn_up, "shard", axis=0, tiled=True)
    whole_down = lax.all_gather(ffn_down, "shard", axis=1, tiled=True)
    gain_in_f = lax.all_gather(gain_in, "shard", axis=0, tiled=True).astype(f32)
    gain_ffn_f = lax.all_gather(gain_ffn, "shard", axis=0, tiled=True).astype(f32)

    inputs_f = tokens.reshape(row_count, width).astype(f32)
    scale_in = lax.rsqrt(jnp.mean(inputs_f * inputs_f, -1, keepdims=True) + epsilon)
    unit_in = inputs_f * scale_in
    normed_in = (unit_in * gain_in_f).astype(bf16)
    projected = dot(normed_in, whole_in).astype(bf16).reshape(seqs, length, heads * HEAD)
    logits = dot(whole_gates, normed_in, (0, 1)).reshape(
        2 * heads, seqs, chunks, CHUNK
    )
    logits = jnp.swapaxes(logits, 0, 1)
    halo = shifted(projected[:, length - HALO :, :], "ctx", 1)
    places = jnp.arange(chunks, dtype=jnp.int32)
    q, k, v, rows, t, w, u, qe, m, b, own_out, state_end, state_map = prepare(
        places, projected, halo, logits, conv_taps, log_rates, rate_bias, with_map
    )

    def map_forward(arriving):
        return jnp.einsum("shij,shjk->shik", state_map, arriving)

    def map_back(arriving):
        return jnp.einsum("shji,shjk->shik", state_map, arriving)

    arriving = relay(state_end, map_forward, 1)
    gain_row = gate_gain.reshape(1, DV)
    gated, mixer, states = mixer_output(
        places, (rows, qe, m, b, own_out), arriving, projected, gain_row
    )
    gated = gated.reshape(row_count, heads * DV)

    middle = own(inputs_f) + scatter_sum(dot(gated, whole_out))
    scale_mid = lax.rsqrt(jnp.mean(middle * middle, -1, keepdims=True) + epsilon)
    unit_mid = middle * scale_mid
    normed_mid = gather_rows((unit_mid * gain_ffn_f).astype(bf16))
    gate_act = dot(normed_mid, whole_gate)
    up_act = dot(normed_mid, whole_up)
    gate_sig = jax.nn.sigmoid(gate_act)
    gate_silu = gate_act * gate_sig
    hidden = (gate_silu * up_act).astype(bf16)
    d_out = cotangent.reshape(row_count, width)
    d_hidden = dot(d_out, whole_down, (1, 1))
    d_gate = (d_hidden * up_act * gate_sig * (1.0 + gate_act * (1.0 - gate_sig))).astype(bf16)
    d_up = (d_hidden * gate_silu).astype(bf16)
    d_mid_norm = scatter_sum(dot(d_gate, whole_gate, (1, 1)) + dot(d_up, whole_up, (1, 1)))
    layer_rows = middle + scatter_sum(dot(hidden, whole_down))
    grad_down = dot(hidden, d_out, (0, 0))
    grad_gate = dot(normed_mid, d_gate, (0, 0))
    grad_up = dot(normed_mid, d_up, (0, 0))
    gain_ffn_part = jnp.sum(d_mid_norm * unit_mid, (0, 1))
    scaled_mid = d_mid_norm * gain_ffn_f
    d_middle = own(cotangent).astype(f32) + scale_mid * (
        scaled_mid - unit_mid * jnp.mean(scaled_mid * unit_mid, -1, keepdims=True)
    )
    d_branch = gather_rows(d_middle.astype(bf16))
    grad_out = dot(gated, d_branch, (0, 0))
    d_gated = dot(d_branch, whole_out, (1, 1)).reshape(seqs, length, heads * DV)
    d_mixer, d_og, n, d_start, gain_gate_part = norm_back(
        places, rows, d_gated, mixer, projected, gain_row, qe, m
    )
    arriving_back = relay(d_start, map_back, -1)
    d_projected, d_halo, d_tail, d_logits, rate_rows, tap_rows = mixer_grads(
        places, projected, halo, logits, conv_taps, log_rates, rate_bias,
        q, k, v, rows, t, w, u, m, states, d_mixer, n, arriving_back, d_og,
    )
    later = shifted(d_halo, "ctx", -1)
    tail = (d_tail + later).astype(bf16)
    for h in range(heads):
        d_projected = lax.dynamic_update_slice(
            d_projected, tail[:, h], (0, length - ROWS, h * HEAD)
        )
    d_projected = d_projected.reshape(row_count, heads * HEAD)
    grad_bias = jnp.sum(d_logits[:, 0::2], (0, 2, 3))
    grad_rates = jnp.sum(rate_rows, (0, 2, 3))
    d_logit_rows = jnp.swapaxes(d_logits, 0, 1).reshape(2 * heads, row_count).astype(bf16)
    grad_in = dot(normed_in, d_projected, (0, 0))
    grad_gates = dot(normed_in, d_logit_rows, (0, 1))
    in_back = dot(d_projected, whole_in, (1, 1)) + dot(d_logit_rows, whole_gates, (0, 1))
    d_in_norm = scatter_sum(in_back)
    unit_own = own(unit_in)
    scale_own = own(scale_in)
    gain_in_part = jnp.sum(d_in_norm * unit_own, (0, 1))
    scaled_in = d_in_norm * gain_in_f
    token_grad = d_middle + scale_own * (
        scaled_in - unit_own * jnp.mean(scaled_in * unit_own, -1, keepdims=True)
    )
    gain_gate_part = jnp.sum(gain_gate_part, (0, 1))
    grad_taps = jnp.swapaxes(tap_rows[:, :CONV, :], 0, 1).reshape(CONV, heads * QKV)
    grad_gain_gate, grad_gain_in, grad_gain_ffn = lax.psum(
        (gain_gate_part, gain_in_part, gain_ffn_part), "tp"
    )

    def reduced(grad, axis):
        piece = lax.psum_scatter(
            grad.astype(bf16), ("shard", "ctx"), scatter_dimension=axis, tiled=True
        )
        return lax.all_gather(piece, "ctx", axis=axis, tiled=True).astype(f32)

    sum_taps, sum_rates, sum_bias, sum_gain_gate = lax.psum(
        (grad_taps, grad_rates, grad_bias, grad_gain_gate), ("shard", "ctx")
    )
    return (
        layer_rows.astype(bf16),
        token_grad,
        reduced(grad_in, 0),
        reduced(grad_gates, 0),
        sum_taps,
        sum_rates,
        sum_bias,
        sum_gain_gate,
        reduced(grad_out, 1),
        reduced(grad_gate, 0),
        reduced(grad_up, 0),
        reduced(grad_down, 1),
        reduced(grad_gain_in, 0),
        reduced(grad_gain_ffn, 0),
    )


def ffn_kernel(part_a, part_b, d_rows, weights, *refs):
    rows_out, hidden_out, d_pair_out, back_a, back_b, down_a, down_b = refs[-7:]
    units = weights.shape[1] // 3
    main = units // 128 * 128
    pair, down = weights.at[:, : 2 * units], weights.at[:, 2 * units :]
    half = part_a.shape[0]
    rows = jnp.concatenate([part_a[...], part_b[...]], axis=0)
    rows_out[...] = rows
    acts = mm(rows, pair[...])
    d_hidden = mm(d_rows[...], down[...])

    def through_gate(gate_act, up_act, d_act):
        sig = sigmoid(gate_act)
        swish = gate_act * sig
        d_gate = d_act * up_act * sig * (1.0 + gate_act * (1.0 - sig))
        return (swish * up_act).astype(bf16), d_gate.astype(bf16), (d_act * swish).astype(bf16)

    hidden, d_gate, d_up = through_gate(acts[:, :main], acts[:, main : 2 * main], d_hidden[:, :main])
    d_pair = [d_gate, d_up]
    if units > main:
        last = 2 * main + units - main
        tail, d_gate, d_up = through_gate(
            acts[:, 2 * main : last], acts[:, last:], d_hidden[:, main:]
        )
        hidden = jnp.concatenate([hidden, tail], axis=1)
        d_pair = d_pair + [d_gate, d_up]
    hidden_out[...] = hidden
    d_pair = jnp.concatenate(d_pair, axis=1)
    d_pair_out[...] = d_pair
    back = mm(d_pair, pair[...], (1, 1)).astype(bf16)
    through = mm(hidden, down[...], (1, 1)).astype(bf16)
    back_a[...] = back[:half]
    back_b[...] = back[half:]
    down_a[...] = through[:half]
    down_b[...] = through[half:]


def paired(gate, up):
    main = gate.shape[1] // 128 * 128
    return jnp.concatenate([gate[:, :main], up[:, :main], gate[:, main:], up[:, main:]], axis=1)


def unpaired(pair):
    units = pair.shape[1] // 2
    main = units // 128 * 128
    last = main + units
    gate = jnp.concatenate([pair[:, :main], pair[:, 2 * main : last]], axis=1)
    return gate, jnp.concatenate([pair[:, main : 2 * main], pair[:, last:]], axis=1)


def feed_forward(part_a, part_b, d_rows, weights, carried):
    half, width = part_a.shape
    units = weights.shape[1] // 3
    index = 1 if carried else 0

    def whole(*shape):
        return pl.BlockSpec(shape, lambda i: (0, 0))

    def placed(columns):
        return pl.BlockSpec((2 * half, columns), lambda i: (index, 0))

    return pl.pallas_call(
        ffn_kernel,
        grid=(1,),
        in_specs=[
            whole(half, width), whole(half, width), placed(width), whole(*weights.shape),
        ]
        + [pl.BlockSpec(memory_space=pl.ANY)] * len(carried),
        out_specs=[placed(width), placed(units), placed(2 * units)] + [whole(half, width)] * 4,
        out_shape=[
            jax.ShapeDtypeStruct((4 * half, columns), bf16) for columns in (width, units, 2 * units)
        ]
        + [jax.ShapeDtypeStruct((half, width), bf16)] * 4,
        input_output_aliases={4 + i: i for i in range(len(carried))},
        compiler_params=pltpu.CompilerParams(
            dimension_semantics=("arbitrary",), vmem_limit_bytes=56 * 1024 * 1024
        ),
        cost_estimate=cost(9.0),
        name="feed_forward",
    )(part_a, part_b, d_rows, weights, *carried)


def input_back_kernel(d_first, d_last, d_logits, weights, gates, *outs):
    split = d_first.shape[1]
    total = (
        mm(d_first[...], weights[:, :split], (1, 1))
        + mm(d_last[...], weights[:, split : 2 * split], (1, 1))
        + mm(d_logits[...], gates[...], (0, 0))
    ).astype(bf16)
    for i, out in enumerate(outs):

        @pl.when(pl.program_id(0) == i)
        def _(out=out):
            out[...] = total


def input_back(d_first, d_last, d_logits, weights, gates):
    full = d_first.shape[0]
    count = full // 4
    width = weights.shape[0]

    def whole(array):
        return pl.BlockSpec(array.shape, lambda i: (0, 0))

    return pl.pallas_call(
        input_back_kernel,
        grid=(4,),
        in_specs=[
            pl.BlockSpec((count, d_first.shape[1]), lambda i: (i, 0)),
            pl.BlockSpec((count, d_last.shape[1]), lambda i: (i, 0)),
            pl.BlockSpec((d_logits.shape[0], count), lambda i: (0, i)),
            whole(weights),
            whole(gates),
        ],
        out_specs=[pl.BlockSpec((count, width), lambda i: (0, 0))] * 4,
        out_shape=[jax.ShapeDtypeStruct((count, width), bf16)] * 4,
        compiler_params=pltpu.CompilerParams(
            dimension_semantics=("arbitrary",), vmem_limit_bytes=56 * 1024 * 1024
        ),
        cost_estimate=cost(5.0),
        name="input_back",
    )(d_first, d_last, d_logits, weights, gates)


def ffn_grads_kernel(rows, d_pair, d_rows, hidden, out):
    out[...] = jnp.concatenate(
        [mm(rows[...], d_pair[...], (0, 0)), mm(d_rows[...], hidden[...], (0, 0))], axis=1
    ).astype(bf16)


def ffn_grads(rows, d_pair, d_rows, hidden):
    full, width = rows.shape
    count = width // 4
    wide = d_pair.shape[1] + hidden.shape[1]

    def columns():
        return pl.BlockSpec((full, count), lambda i: (0, i))

    def whole(array):
        return pl.BlockSpec(array.shape, lambda i: (0, 0))

    return pl.pallas_call(
        ffn_grads_kernel,
        grid=(4,),
        in_specs=[columns(), whole(d_pair), columns(), whole(hidden)],
        out_specs=pl.BlockSpec((count, wide), lambda i: (i, 0)),
        out_shape=jax.ShapeDtypeStruct((width, wide), bf16),
        compiler_params=pltpu.CompilerParams(
            dimension_semantics=("arbitrary",), vmem_limit_bytes=56 * 1024 * 1024
        ),
        cost_estimate=cost(10.0),
        name="ffn_grads",
    )(rows, d_pair, d_rows, hidden)


def both_grads_kernel(rows, d_rows, weights, part_0, part_1, part_2, part_3, gated, out, sums):
    grad = mm(rows[...], d_rows[...], (0, 0))
    columns = jnp.sum(grad * weights[...].astype(f32), -1, keepdims=True)
    lanes = jnp.concatenate([columns, jnp.zeros((columns.shape[0], 127), f32)], axis=1)
    sums[...] = jnp.transpose(lanes)[0:8]
    branch = jnp.concatenate([part_0[...], part_1[...], part_2[...], part_3[...]], axis=0)
    out[...] = jnp.concatenate([grad, mm(branch, gated[...], (0, 0))], axis=1).astype(bf16)


def both_grads(rows, d_rows, weights, parts, gated):
    full, width = rows.shape
    columns = d_rows.shape[1]
    count = width // 4
    wide = columns + gated.shape[1]
    return pl.pallas_call(
        both_grads_kernel,
        grid=(4,),
        in_specs=[
            pl.BlockSpec((full, count), lambda i: (0, i)),
            pl.BlockSpec((full, columns), lambda i: (0, 0)),
            pl.BlockSpec((count, columns), lambda i: (i, 0)),
        ]
        + [pl.BlockSpec((parts[0].shape[0], count), lambda i: (0, i))] * 4
        + [pl.BlockSpec(gated.shape, lambda i: (0, 0))],
        out_specs=[
            pl.BlockSpec((count, wide), lambda i: (i, 0)),
            pl.BlockSpec((8, count), lambda i: (0, i)),
        ],
        out_shape=[
            jax.ShapeDtypeStruct((width, wide), bf16),
            jax.ShapeDtypeStruct((8, width), f32),
        ],
        compiler_params=pltpu.CompilerParams(
            dimension_semantics=("arbitrary",), vmem_limit_bytes=56 * 1024 * 1024
        ),
        cost_estimate=cost(8.0),
        name="both_grads",
    )(rows, d_rows, weights, *parts, gated)


def input_grad_kernel(
    shard, rows, d_rows, weights, left_a, left_b, left_send, right_a, right_b, right_send, part
):
    grad = mm(rows[...], d_rows[...], (0, 0))
    sums = jnp.sum(grad * weights[...].astype(f32), -1, keepdims=True)
    lanes = jnp.concatenate([sums, jnp.zeros((sums.shape[0], 127), f32)], axis=1)
    part[...] = jnp.transpose(lanes)[0:8]
    low = grad.astype(bf16)
    count = low.shape[0]
    cut = left_a.shape[1]
    left, right = low[:, :cut], low[:, cut:]
    step = pl.program_id(0)

    @pl.when(step == 0)
    def _():
        left_a[...] = left
        right_a[...] = right

    @pl.when(step == 1)
    def _():
        left_send[:count] = left
        right_b[...] = right

    @pl.when(step == 2)
    def _():
        left_b[...] = left
        right_send[:count] = right

    @pl.when(step == 3)
    def _():
        left_send[count:] = left
        right_send[count:] = right


def input_grad(shard, rows, d_rows, weights, head):
    full, width = rows.shape
    columns = d_rows.shape[1]
    count = width // 4
    cut = columns // 256 * 128

    def whole(*shape):
        return pl.BlockSpec(shape, lambda i, place: (0, 0))

    shapes = [
        (count, cut), (count, cut), (2 * count, cut),
        (count, columns - cut), (count, columns - cut), (2 * count, columns - cut),
    ]
    return pl.pallas_call(
        input_grad_kernel,
        grid_spec=pltpu.PrefetchScalarGridSpec(
            num_scalar_prefetch=1,
            grid=(4,),
            in_specs=[
                pl.BlockSpec((full, count), lambda i, place: (0, place[0] ^ i)),
                whole(full, columns),
                pl.BlockSpec((count, columns), lambda i, place: (place[0] ^ i, head)),
            ],
            out_specs=[whole(*shape) for shape in shapes]
            + [pl.BlockSpec((8, count), lambda i, place: (0, place[0] ^ i))],
        ),
        out_shape=[jax.ShapeDtypeStruct(shape, bf16) for shape in shapes]
        + [jax.ShapeDtypeStruct((8, width), f32)],
        compiler_params=pltpu.CompilerParams(
            dimension_semantics=("arbitrary",), vmem_limit_bytes=56 * 1024 * 1024
        ),
        cost_estimate=cost(4.0),
        name="input_grad",
    )(shard, rows, d_rows, weights)


def branch_back_kernel(
    places, rows, part_0, part_1, part_2, part_3, weights, mixer, og, gain, qe, m,
    d_out, d_og_out, n_out, gain_out, d_gated,
):
    count = part_0.shape[0]
    for i, part in enumerate((part_0, part_1, part_2, part_3)):
        d_gated[0, i * count : (i + 1) * count, :] = mm(part[...], weights[...])
    norm_back_kernel(
        places, rows, d_gated, mixer, og, gain, qe, m, d_out, d_og_out, n_out, None, gain_out
    )


def branch_back(places, rows, parts, weights, mixer, projected, gain, qe, m):
    seqs, heads, chunks = qe.shape[:3]
    length = chunks * CHUNK
    count, width = parts[0].shape
    return pl.pallas_call(
        branch_back_kernel,
        grid=(heads, seqs),
        in_specs=[
            smem(),
            per_unit(2 * chunks, CHUNK),
        ]
        + [pl.BlockSpec((count, width), lambda h, s: (0, 0))] * 4
        + [
            pl.BlockSpec((width, DV), lambda h, s: (0, h)),
            pl.BlockSpec((1, length, DV), lambda h, s: (s, 0, h)),
            pl.BlockSpec((1, length, 256), lambda h, s: (s, 0, 3 * h + 2)),
            pl.BlockSpec((1, DV), lambda h, s: (0, 0)),
            per_unit(chunks, CHUNK, DK),
            per_unit(chunks, DK, DK),
        ],
        out_specs=[
            per_unit(chunks, CHUNK, DV),
            per_unit(length, DV),
            per_unit(chunks, DK, DV),
            pl.BlockSpec((1, 8, DV), lambda h, s: (h, 0, 0)),
        ],
        out_shape=[
            jax.ShapeDtypeStruct((seqs, heads, chunks, CHUNK, DV), bf16),
            jax.ShapeDtypeStruct((seqs, heads, length, DV), bf16),
            jax.ShapeDtypeStruct((seqs, heads, chunks, DK, DV), f32),
            jax.ShapeDtypeStruct((heads, 8, DV), f32),
        ],
        scratch_shapes=[pltpu.VMEM((1, length, DV), f32)],
        compiler_params=params(),
        cost_estimate=cost(5.0 * heads),
        name="branch_back",
    )(places, rows, *parts, weights, mixer, projected, gain, qe, m)


def widened(block):
    return jnp.pad(block, ((0, 0), (0, -block.shape[1] % 128)))


def local_paired(
    tokens,
    proj_in,
    proj_gates,
    conv_taps,
    log_rates,
    rate_bias,
    gate_gain,
    proj_out,
    ffn_gate,
    ffn_up,
    ffn_down,
    gain_in,
    gain_ffn,
    cotangent,
):
    seqs, length, width = tokens.shape
    heads = log_rates.shape[0]
    units = ffn_gate.shape[1]
    core = lax.axis_index("ctx")
    place = lax.axis_index("tp")
    shard = lax.axis_index("shard")
    tp_count = lax.axis_size("tp")
    shards = lax.axis_size("shard")
    seq = place // 2
    half = place % 2
    quarter = length // 2
    share = length // tp_count
    full = 2 * length
    chunks = full // CHUNK
    route = []
    for j in range(tp_count):
        route.append((j, (j % 2) * tp_count + j // 2))
        route.append((tp_count + j, (j % 2) * tp_count + 2 + j // 2))
    route_back = [(b, a) for a, b in route]
    pairs = [(i, i ^ 1) for i in range(tp_count)]
    pairs_x = [(i, i ^ 1) for i in range(shards)]
    pairs_y = [(i, i ^ 2) for i in range(shards)]
    odd_x = shard % 2 == 1
    odd_y = shard // 2 == 1

    def hold(*values):
        return lax.optimization_barrier(values)

    def swap_core(block):
        with jax.named_scope("swap_core"):
            return lax.ppermute(block, "ctx", [(0, 1), (1, 0)])

    def swap_chip(block):
        with jax.named_scope("swap_chip"):
            return lax.ppermute(block, "tp", pairs)

    def swap_x(block):
        with jax.named_scope("swap_x"):
            return lax.ppermute(block, "shard", pairs_x)

    def swap_y(block):
        with jax.named_scope("swap_y"):
            return lax.ppermute(block, "shard", pairs_y)

    def to_users(block):
        with jax.named_scope("to_users"):
            return lax.ppermute(block, ("ctx", "tp"), route)

    def to_owners(block):
        with jax.named_scope("to_owners"):
            return lax.ppermute(block, ("ctx", "tp"), route_back)

    def both_cores(block):
        return block.astype(f32) + swap_core(block).astype(f32)

    def add(kept, got):
        return (kept.astype(f32) + got.astype(f32)).astype(bf16)

    def group_rows(mine, got):
        return jnp.concatenate(
            [mine[:quarter], got[:quarter], mine[quarter:], got[quarter:]], axis=0
        )

    def own_rows(rows):
        sequence = lax.dynamic_index_in_dim(rows, seq, 0, keepdims=False)
        mine = lax.dynamic_slice_in_dim(sequence, half * quarter, quarter, 0)
        other = lax.dynamic_slice_in_dim(sequence, (1 - half) * quarter, quarter, 0)
        return jnp.concatenate([mine, other], axis=0)

    def swap_sides(mine):
        return swap_x(mine), swap_y(mine)

    def swap_fourth(from_x, from_y):
        count = from_x.shape[0] // 2
        return swap_x(from_y[:count]), swap_y(from_x[count:])

    def ordered(odd, mine, theirs):
        return jnp.concatenate([jnp.where(odd, theirs, mine), jnp.where(odd, mine, theirs)], axis=0)

    def assembled(mine, sides, fourth):
        across = jnp.concatenate(fourth, axis=0)
        return ordered(
            odd_y, ordered(odd_x, mine, sides[0]), ordered(odd_x, sides[1], across)
        )

    def blocks(grad, *places_xor):
        rows = grad.shape[0] // shards
        return jnp.concatenate(
            [lax.dynamic_slice_in_dim(grad, (shard ^ p) * rows, rows, 0) for p in places_xor],
            axis=0,
        )

    def scatter_first(grad):
        cut = grad.shape[1] // 256 * 128
        left, right = grad[:, :cut], grad[:, cut:]
        return (
            blocks(left, 0, 2),
            swap_x(blocks(left, 1, 3)),
            blocks(right, 0, 1),
            swap_y(blocks(right, 2, 3)),
        )

    def scatter_second(left, left_got, right, right_got):
        rows = left.shape[0] // 2
        left = add(left, left_got)
        right = add(right, right_got)
        return left[:rows], swap_y(left[rows:]), right[:rows], swap_x(right[rows:])

    def scatter_end(left, left_got, right, right_got):
        return jnp.concatenate([add(left, left_got), add(right, right_got)], axis=1)

    def quarters(rows, weights):
        return [
            dot(rows[i * quarter : (i + 1) * quarter], weights, (1, 1)) for i in (3, 2, 1, 0)
        ]

    def piece_first(left_a, left_b, left_send, right_a, right_b, right_send):
        return left_a, left_b, swap_x(left_send), right_a, right_b, swap_y(right_send)

    def piece_second(left_a, left_b, left_got, right_a, right_b, right_got):
        rows = left_a.shape[0]
        left_on = swap_y(add(left_b, left_got[rows:]))
        right_on = swap_x(add(right_b, right_got[rows:]))
        return left_a, left_got, left_on, right_a, right_got, right_on

    def piece_end(left_a, left_got, left_on, right_a, right_got, right_on):
        rows = left_a.shape[0]

        def total(mine, got, on):
            return (mine.astype(f32) + got[:rows].astype(f32) + on.astype(f32)).astype(bf16)

        return jnp.concatenate(
            [total(left_a, left_got, left_on), total(right_a, right_got, right_on)], axis=1
        )

    small = jnp.concatenate(
        [
            conv_taps.astype(f32),
            jnp.pad(jnp.stack([log_rates, rate_bias]), ((0, 2), (0, conv_taps.shape[1] - heads))),
        ],
        axis=0,
    )
    inner = heads * HEAD
    block = proj_in.shape[0]
    gates_block = jnp.pad(
        proj_gates.T, ((0, 16 - 2 * heads), (0, inner - block))
    )
    mine_in = to_users(jnp.concatenate([proj_in, gates_block], axis=0))
    mine_rows = own_rows(tokens)
    got_rows = swap_core(mine_rows)
    gains = lax.all_gather(jnp.stack([gain_in, gain_ffn]), "shard", axis=1, tiled=True)
    mine_d = own_rows(cotangent)
    got_d = swap_core(mine_d)
    mine_pair = paired(ffn_gate, ffn_up)
    mine_in, mine_rows, got_rows, gains, mine_d, got_d, small, mine_out, mine_pair, mine_down = hold(
        mine_in, mine_rows, got_rows, gains, mine_d, got_d, small, proj_out.T, mine_pair,
        ffn_down.T,
    )
    in_sides = swap_sides(mine_in)
    small = to_users(small)
    mine_out = to_users(mine_out)
    mine_down = to_users(mine_down)
    gains = gains.astype(f32)
    gain_in_f, gain_ffn_f = gains[0:1], gains[1:2]
    inputs_f = group_rows(mine_rows, got_rows).astype(f32)
    scale_in = lax.rsqrt(jnp.mean(inputs_f * inputs_f, -1, keepdims=True) + epsilon)
    normed_in = (inputs_f * scale_in * gain_in_f).astype(bf16)
    d_out = group_rows(mine_d, got_d)
    in_sides, small, mine_out, normed_in, d_out, mine_pair, mine_down = hold(
        in_sides, small, mine_out, normed_in, d_out, mine_pair, mine_down
    )
    in_fourth = swap_fourth(*in_sides)
    mine_pair = to_users(mine_pair)
    whole_out = lax.all_gather(mine_out, "shard", axis=0, tiled=True)
    in_fourth, normed_in = hold(in_fourth, normed_in)
    whole_in = assembled(
        mine_in[:block],
        [side[:block] for side in in_sides],
        [jnp.concatenate(in_fourth, axis=0)[:block]],
    )
    gate_rows = [
        rows_of[block : block + 8, :block]
        for rows_of in (mine_in, *in_sides, jnp.concatenate(in_fourth, axis=0))
    ]

    def side_by_side(odd, mine, theirs):
        return jnp.concatenate(
            [jnp.where(odd, theirs, mine), jnp.where(odd, mine, theirs)], axis=1
        )

    gates_rows = side_by_side(
        odd_y,
        side_by_side(odd_x, gate_rows[0], gate_rows[1]),
        side_by_side(odd_x, gate_rows[2], gate_rows[3]),
    )
    projected = dot(normed_in, whole_in).astype(bf16).reshape(1, full, inner)
    logits = dot(gates_rows, normed_in, (1, 1))[: 2 * heads]
    logits = logits.reshape(1, 2 * heads, chunks, CHUNK)
    projected, logits, gates_rows, mine_ffn = hold(
        projected, logits, gates_rows, jnp.concatenate([mine_pair, mine_down], axis=1)
    )
    weights_ffn = lax.all_gather(mine_ffn, "shard", axis=0, tiled=True)

    taps = small[:CONV]
    log_rates_here, rate_bias_here = small[CONV, :heads], small[CONV + 1, :heads]
    halo = jnp.zeros((1, HALO, inner), bf16)
    chunk = jnp.arange(chunks, dtype=jnp.int32)
    per_quarter = quarter // CHUNK
    true_quarter = chunk // per_quarter
    places = (
        2 * ((true_quarter % 2) ^ half) + ((true_quarter // 2) ^ core)
    ) * per_quarter + chunk % per_quarter
    no_state = jnp.zeros((1, heads, DK, DV), f32)
    gain_row = gate_gain.reshape(1, DV)
    source = (projected, halo, logits, taps, log_rates_here, rate_bias_here)
    prepared = prepare(places, *source, False, False)[:11]
    q, k, v, rows, t, w, u, qe, m, b, own_out = prepared
    gated, mixer, states = mixer_output(
        places, (rows, qe, m, b, own_out), no_state, projected, gain_row
    )
    gated = gated.reshape(full, heads * DV)
    far_b, far_a, near_b, near_a = quarters(gated, whole_out)
    far_got = swap_core(far_b.astype(bf16))
    near_got = swap_core(near_b.astype(bf16))
    far_sum, near_a, near_got = hold(add(far_a, far_got), near_a, near_got)
    far_sum = swap_chip(far_sum)
    middle = inputs_f[:quarter] + (near_a + near_got.astype(f32) + far_sum.astype(f32))
    scale_mid = lax.rsqrt(jnp.mean(middle * middle, -1, keepdims=True) + epsilon)
    unit_mid = middle * scale_mid

    mine_mid = (unit_mid * gain_ffn_f).astype(bf16)
    far_mid = swap_chip(mine_mid)
    near_mid = swap_core(mine_mid)
    near = feed_forward(mine_mid, near_mid, d_out, weights_ffn, ())
    far_mid, near = hold(far_mid, near)
    near_a, near_b, near_down_a, near_down_b = near[3:]
    near_got = swap_core(near_b)
    far = feed_forward(
        far_mid, swap_core(far_mid), d_out, weights_ffn, tuple(near[:3])
    )
    normed_mid, hidden, d_pair, far_a, far_b, far_down_a, far_down_b = far
    far_got = swap_core(far_b)
    far_sum, near_got, normed_mid, hidden, d_pair = hold(
        add(far_a, far_got), near_got, normed_mid, hidden, d_pair
    )
    far_sum = swap_chip(far_sum)
    far_down_got = swap_core(far_down_b)
    near_down_got = swap_core(near_down_b)
    grad_ffn = ffn_grads(normed_mid, d_pair, d_out, hidden)
    far_sum, grad_ffn, far_down_got, near_down_got = hold(
        far_sum, grad_ffn, far_down_got, near_down_got
    )
    piece_ffn = lax.psum_scatter(grad_ffn, "shard", scatter_dimension=0, tiled=True)
    d_mid_norm = near_a.astype(f32) + near_got.astype(f32) + far_sum.astype(f32)
    scaled_mid = d_mid_norm * gain_ffn_f
    d_middle = d_out[:quarter].astype(f32) + scale_mid * (
        scaled_mid - unit_mid * jnp.mean(scaled_mid * unit_mid, -1, keepdims=True)
    )
    d_low = d_middle.astype(bf16)
    far_low = swap_chip(d_low)
    near_low = swap_core(d_low)
    far_low, near_low, far_down_a, far_down_got = hold(
        far_low, near_low, far_down_a, far_down_got
    )
    d_parts = (d_low, near_low, far_low, swap_core(far_low))

    far_down_sum = swap_chip(add(far_down_a, far_down_got))
    branch = branch_back(places, rows, d_parts, whole_out, mixer, projected, gain_row, qe, m)
    branch, gated = hold(branch, gated)
    d_mixer, d_og, n, gain_gate_part = branch

    def head_grads(h, d_mixer):
        d_projected, _, _, d_logits, rate_rows, tap_rows = mixer_grads(
            places, *source, q, k, v, rows, t, w, u, m, states, d_mixer, n, no_state, d_og,
            start=h, count=1,
        )
        return d_projected.reshape(full, HEAD), d_logits, rate_rows, tap_rows

    even = half == 0
    first = seq == 0
    send_a = [(0, 0), (1, 2), (2, 1), (3, 3)]
    send_b = [(0, 1), (1, 3), (2, 0), (3, 2)]

    def to_outputs(mine):
        low, high = mine[:share], mine[share:]
        with jax.named_scope("to_outputs"):
            got_a = lax.ppermute(jnp.where(first, low, high), "tp", send_a)
            got_b = lax.ppermute(jnp.where(first, high, low), "tp", send_b)
        return got_a, got_b

    def stacked(got_a, got_b):
        return jnp.stack([jnp.where(even, got_a, got_b), jnp.where(even, got_b, got_a)])

    place_x = shard.reshape(1).astype(jnp.int32)
    first_head = head_grads(0, d_mixer)
    first_head, d_mixer, far_down_sum = hold(first_head, d_mixer, far_down_sum)
    grad_both, part_first = both_grads(normed_in, first_head[0], whole_in, d_parts, gated)
    grad_both, part_first, d_mixer, piece_ffn = hold(grad_both, part_first, d_mixer, piece_ffn)
    owned_pair = to_owners(piece_ffn[:, : 2 * hidden.shape[1]])
    piece_both = lax.psum_scatter(grad_both, "shard", scatter_dimension=0, tiled=True)
    layer_rows = (
        middle
        + near_down_a.astype(f32)
        + near_down_got.astype(f32)
        + far_down_sum.astype(f32)
    ).astype(bf16)

    last_head, owned_pair = hold(head_grads(1, d_mixer), owned_pair)

    owned_down = to_owners(piece_ffn[:, 2 * hidden.shape[1] :])
    *sent, part_last = input_grad(place_x, normed_in, last_head[0], whole_in, 1)
    sent, part_last, last_head, owned_down, layer_rows = hold(
        sent, part_last, last_head, owned_down, layer_rows
    )
    steps_last = piece_first(*sent)
    layer_got = to_outputs(layer_rows)
    logits_first = first_head[1].reshape(2, full)
    logits_last = last_head[1].reshape(2, full)
    d_logit_rows = jnp.concatenate(
        [logits_first, logits_last, jnp.zeros((8 - 2 * heads, full), f32)], axis=0
    ).astype(bf16)
    grad_gates = dot(d_logit_rows, normed_in)
    packed = jnp.concatenate(
        [
            jnp.concatenate([first_head[3][0], last_head[3][0]], axis=1),
            grad_gates,
            part_first + part_last + gates_rows.astype(f32) * grad_gates,
            jnp.concatenate(
                [
                    gain_gate_part[0], gain_gate_part[1], first_head[2][0, 0], last_head[2][0, 0],
                    first_head[1][0, 0], last_head[1][0, 0],
                ],
                axis=1,
            ),
        ],
        axis=0,
    )
    packed_got = swap_x(packed)
    backs = input_back(first_head[0], last_head[0], d_logit_rows, whole_in, gates_rows)
    backs, steps_last, layer_got, packed, packed_got, piece_both = hold(
        backs, steps_last, layer_got, packed, packed_got, piece_both
    )
    owned_both = to_owners(piece_both)
    near_a, near_b, far_a, far_b = backs
    far_got = swap_core(far_b)
    near_got = swap_core(near_b)
    steps_last = piece_second(*steps_last)
    packed = packed + packed_got
    packed_got = swap_y(packed)
    (
        far_sum, near_got, near_a, steps_last, packed, packed_got, owned_pair, owned_down, owned_both,
    ) = hold(
        add(far_a, far_got), near_got, near_a, steps_last, packed, packed_got, owned_pair,
        owned_down, owned_both,
    )
    far_sum = swap_chip(far_sum)
    piece_last = piece_end(*steps_last)
    packed = packed + packed_got
    sum_pair = both_cores(owned_pair)
    sum_gate, sum_up = unpaired(sum_pair)
    far_sum, sum_gate, sum_up, near_a, owned_down, layer_got, piece_last, packed, owned_both = hold(
        far_sum, sum_gate, sum_up, near_a, owned_down, layer_got, piece_last, packed, owned_both
    )
    piece_last = to_owners(piece_last)
    packed = to_owners(packed)
    d_in_norm = near_a.astype(f32) + near_got.astype(f32) + far_sum.astype(f32)
    unit_in = (inputs_f * scale_in)[:quarter]
    scaled_in = d_in_norm * gain_in_f
    token_rows = d_middle + scale_in[:quarter] * (
        scaled_in - unit_in * jnp.mean(scaled_in * unit_in, -1, keepdims=True)
    )
    token_got = to_outputs(token_rows.astype(bf16))
    packed = both_cores(packed)
    sum_down = both_cores(owned_down).T
    layer_out = stacked(*layer_got)
    sum_both = both_cores(owned_both)
    sum_out = sum_both[:, HEAD:].T
    sum_last = both_cores(piece_last)

    part_ffn = jnp.sum(ffn_gate.astype(f32) * sum_gate + ffn_up.astype(f32) * sum_up, 1)
    sum_taps, sum_gates, part_in, rest = (packed[8 * i : 8 * i + 8] for i in range(4))
    sum_gain = jnp.sum(rest[:, :DV] + rest[:, DV : 2 * DV], 0)
    sum_rates = jnp.sum(rest[:, 2 * DV :].reshape(8, 2 * heads, CHUNK), (0, 2))
    rows_here = gain_in.shape[0]

    def own_block(rows_of):
        return lax.dynamic_slice_in_dim(rows_of, shard * rows_here, rows_here, -1)

    over_blocks = jnp.concatenate([sum_gain, jnp.sum(own_block(part_in), 0), part_ffn])
    over_blocks = jnp.pad(over_blocks, (0, -over_blocks.shape[0] % 1024)).reshape(-1, 128)
    over_blocks = over_blocks + swap_chip(over_blocks)
    with jax.named_scope("swap_pair"):
        other_pair = lax.ppermute(over_blocks, "tp", [(i, i ^ 2) for i in range(tp_count)])
    over_blocks = (over_blocks + other_pair).reshape(-1)
    return (
        layer_out,
        stacked(*token_got).astype(f32),
        jnp.concatenate([sum_both[:, :HEAD], sum_last], axis=1),
        own_block(sum_gates)[: 2 * heads].T,
        sum_taps[:CONV],
        sum_rates[:heads],
        sum_rates[heads:],
        over_blocks[:DV],
        sum_out,
        sum_gate,
        sum_up,
        sum_down,
        over_blocks[DV : DV + rows_here] / gain_in.astype(f32),
        over_blocks[DV + rows_here : DV + 2 * rows_here] / gain_ffn.astype(f32),
    )


def solution(mesh):
    placed = (
        P("shard", "ctx", None),
        P("shard", "tp"),
        P("shard", "tp"),
        P(None, "tp"),
        P("tp"),
        P("tp"),
        P(),
        P("tp", "shard"),
        P("shard", "tp"),
        P("shard", "tp"),
        P("tp", "shard"),
        P("shard"),
        P("shard"),
        P("shard", "ctx", None),
    )
    shape = dict(mesh.shape)
    paired = (shape["shard"], shape["ctx"], shape["tp"]) == (4, 2, 4)

    def body(*arrays):
        seqs, length, _ = arrays[0].shape
        heads = arrays[4].shape[0]
        if paired and seqs == 2 and heads == 2 and length % (2 * CHUNK) == 0:
            return local_paired(*arrays)
        return local(*arrays)

    return jax.shard_map(
        body,
        mesh=mesh,
        in_specs=placed,
        out_specs=(
            P("shard", ("ctx", "tp"), None),
            P("shard", ("ctx", "tp"), None),
            P("shard", "tp"),
            P("shard", "tp"),
            P(None, "tp"),
            P("tp"),
            P("tp"),
            P(),
            P("tp", "shard"),
            P("shard", "tp"),
            P("shard", "tp"),
            P("tp", "shard"),
            P("shard"),
            P("shard"),
        ),
        check_vma=False,
    )
```
